32 devices in a mesh: dp: 4 (over y, x), ctx: 8 (over z, core).
Axes of the slice: x: 2, y: 2, z: 4, core: 2. Of those that a mesh axis runs over, the one named last changes fastest.
Arguments:
- queries: bfloat16 [4, 2048, 2048], P('dp', 'ctx'), may hold values from -6 to 6
- keys: bfloat16 [4, 2048, 2048], P('dp', 'ctx'), may hold values from -6 to 6
- values: bfloat16 [4, 2048, 2048], P('dp', 'ctx'), may hold values from -6 to 6
- out_grad: bfloat16 [4, 2048, 2048], P('dp', 'ctx'), may hold values from -6 to 6
- segment_ids: int32 [4, 2048], P('dp', 'ctx'), may hold values from 0 to 31, never falling along the last dimension, each value on 1 to 256 neighbouring positions
- image_flags: int32 [4, 32], P('dp'), may hold values 0 or 1
- gain: float32 [2048], replicated, may hold values from 0.25 to 1.75
Outputs:
- output: bfloat16 [4, 2048, 2048], P('dp', 'ctx')
- grad_queries: bfloat16 [4, 2048, 2048], P('dp', 'ctx')
- grad_keys: bfloat16 [4, 2048, 2048], P('dp', 'ctx')
- grad_values: bfloat16 [4, 2048, 2048], P('dp', 'ctx')
- grad_gain: float32 [2048], P(('dp', 'ctx'))
The draws below stay inside these ranges and needn't reach their ends.
Inputs may be any that keep to these rules, and one draw needn't show every extreme that they name: `segment_ids`: along each sequence the ids never fall, every id from 0 to 31 occurs, and each segment covers 1 to 256 consecutive tokens; some segment covers exactly 256.
All inputs are finite; a program needn't handle non-finite values. No bound on the sum of `image_flags` on one device may be relied on, other than what follows from the above.
Results may differ from the reference program's by a relative error of at most 0.0085.
Values sent between devices are 32-bit elements; how exact they have to be, the bound alone decides.
No kernel may reach another device: no remote copies, remote signals or barrier semaphores. Data moves between devices by JAX's collectives and lax.ppermute only.
A program may use at most 128 MiB of HBM per device.

```python
import math
import jax
import jax.numpy as jnp
import numpy as np
from jax import lax

H = 32
E = 64
TOK_DEV = 256
TOKENS = 2048
SEQS = 4
SEGS = 32
N_CTX = 8


def plant(entries, own_key, low, high):
    index_at = [jax.random.randint(jax.random.fold_in(own_key, axis), (), 0, length) for axis, length in enumerate(entries.shape)]
    widest = entries.shape.index(max(entries.shape))
    next_to = index_at[:widest] + [(index_at[widest] + 1) % entries.shape[widest]] + index_at[widest + 1:]
    return entries.at[tuple(index_at)].set(low).at[tuple(next_to)].set(high)


def spiked(values, key, source, target, shards_of, factor):
    def block_of(position):
        return (jnp.arange(values.shape[position]) // (values.shape[position] // shards_of)).reshape((-1,) + (1,) * (values.ndim - 1 - position))

    one_side = jax.random.permutation(key, shards_of)[block_of(target)]
    far = (block_of(target) + shards_of // 2) % shards_of
    return jnp.where((block_of(source) == one_side) | (block_of(source) == far), factor * values, values)


def levels(stream_key, dims, pieces, low, largest):
    level = 1.0
    for axis_at, shards_of in pieces:
        steps = jax.random.uniform(jax.random.fold_in(jax.random.fold_in(stream_key, 6), axis_at), (shards_of,), jnp.float32, low / len(pieces), largest / len(pieces))
        level = level * jnp.repeat(jnp.exp(steps), dims[axis_at] // shards_of).reshape((-1,) + (1,) * (len(dims) - 1 - axis_at))
    return level


def length_profile(count, total, bound, lean):
    weights = [(1 << 20) // math.isqrt(grade ** lean) + 1 for grade in range(2, count + 1)]
    rest, counts = total - bound - (count - 1), [1] * (count - 1)
    while rest > 0:
        candidates = [i for i in range(count - 1) if counts[i] < bound]
        pool, left = sum([weights[i] for i in candidates]), rest
        for i in candidates:
            addition = min(bound - counts[i], max(1, left * weights[i] // pool), rest)
            counts[i] = counts[i] + addition
            rest = rest - addition
    return np.array([bound] + counts)


def uneven_parts(stream_key, amount, total, bound, lean):
    if amount == 2:
        one = jax.random.randint(stream_key, (), max(1, total - bound), min(bound, total - 1) + 1)
        return jnp.stack([one, total - one])
    sizes = jnp.asarray(length_profile(amount, total, bound, lean), jnp.int32)
    twos = (amount - 1) // 2
    giver, taker = sizes[1:1 + 2 * twos:2], sizes[2:2 + 2 * twos:2]
    slack = jnp.minimum(giver - 1, bound - taker)
    passed = jax.random.randint(jax.random.fold_in(stream_key, 1), (twos,), 0, 1 << 20) % (slack + 1)
    sizes = sizes.at[1:1 + 2 * twos:2].set(giver - passed).at[2:2 + 2 * twos:2].set(taker + passed)
    return sizes[jax.random.permutation(jax.random.fold_in(stream_key, 2), amount)]


def scatter_about(own_key, extent, scale, most, cuts=(), dtype=jnp.bfloat16):
    values = jax.random.normal(own_key, extent, jnp.float32) * scale
    if len(cuts) > 0:
        values = levels(own_key, extent, cuts, -0.22, 0.18) * values
    return jnp.clip(values, min=-most, max=most).astype(dtype)


def noise_with(key, dims, scale, most, cuts, heavy, dtype=jnp.bfloat16):
    drawn = scale * jax.random.normal(key, dims, jnp.float32)
    if cuts:
        drawn = drawn * levels(key, dims, cuts, -0.22, 0.18)
    return jnp.clip(spiked(drawn, jax.random.fold_in(key, 3), *heavy), -most, most).astype(dtype)


def setup_inputs(seed: int = 0) -> dict:
    key_of = jax.random.split(jax.random.key(seed), 8)
    queries = scatter_about(key_of[0], (SEQS, TOKENS, H * E), 1.0, 6.0, ((0, 4), (1, 8)))
    keys = scatter_about(key_of[1], (SEQS, TOKENS, H * E), 1.0, 6.0, ((0, 4), (1, 8)))
    values = scatter_about(key_of[2], (SEQS, TOKENS, H * E), 1.0, 6.0, ((0, 4), (1, 8)))
    out_grad = noise_with(key_of[3], (SEQS, TOKENS, H * E), 1.0, 6.0, ((0, 4), (1, 8)), (1, 2, 8, 2.0))
    segment_ids = jax.vmap(lambda own: jnp.searchsorted(jnp.cumsum(uneven_parts(own, SEGS, TOKENS, TOK_DEV, 1)), jnp.arange(TOKENS), side="right"))(jax.random.split(key_of[4], SEQS)).reshape((SEQS, TOKENS)).astype(jnp.int32)
    image_flags = plant((jax.random.randint(key_of[5], (SEQS, SEGS), 0, 2) < 1).astype(jnp.int32), jax.random.fold_in(key_of[5], 1), 0, 1)
    gain = jnp.clip(1.0 + 0.15 * jax.random.normal(key_of[6], (H * E,), jnp.float32), 0.25, 1.75)
    return dict(queries=queries, keys=keys, values=values, out_grad=out_grad, segment_ids=segment_ids, image_flags=image_flags, gain=gain)


def ein(form, a, b):
    return jnp.einsum(form, a, b, precision=lax.Precision.HIGHEST)

def per_sequence(items):
    queries, keys, values, out_grad, segment_ids, image_flags, gain = items
    q = queries.reshape(N_CTX, TOK_DEV, H, E).astype(jnp.float32)
    k = keys.reshape(N_CTX, TOK_DEV, H, E).astype(jnp.float32)
    v = values.reshape(N_CTX, TOK_DEV, H, E).astype(jnp.float32)
    dy = out_grad.reshape(N_CTX, TOK_DEV, H, E).astype(jnp.float32)
    seg = segment_ids.reshape(N_CTX, TOK_DEV)
    img = image_flags[segment_ids].reshape(N_CTX, TOK_DEV)
    pos = jnp.arange(TOK_DEV)
    causal = pos[:, None] >= pos[None, :]
    same = seg[:, :, None] == seg[:, None, :]
    mask = causal[None] | same & (img[:, :, None] == 1)
    zero_state = jnp.zeros((1, H, E, E), jnp.float32)
    none_id = jnp.full((1,), -1, jnp.int32)
    kv_local = ein('ntha,nthb->nhab', k, v)
    prefix = jnp.concatenate([zero_state, jnp.cumsum(kv_local, axis=0)[:-1]], axis=0)
    first = seg[:, 0]
    last = seg[:, -1]
    first_sel = seg == first[:, None]
    n_local = ein('ntha,nthb->nhab', jnp.where(first_sel[:, :, None, None], k, 0.0), v)
    n_next = jnp.concatenate([n_local[1:], zero_state], axis=0)
    first_next = jnp.concatenate([first[1:], none_id], axis=0)
    on_next = ((img == 1) & (seg == first_next[:, None])).astype(jnp.float32)[:, :, None, None]
    scores = ein('ntha,nsha->nhts', q, k)
    probs = lax.optimization_barrier(jnp.where(mask[:, None], scores, 0.0).astype(jnp.bfloat16)).astype(jnp.float32)
    attn = ein('ntha,nhab->nthb', q, prefix) + on_next * ein('ntha,nhab->nthb', q, n_next)
    attn = attn + ein('nhts,nshb->nthb', probs, v)
    g = gain.reshape(H, E)
    scale = lax.rsqrt(lax.optimization_barrier(jnp.mean(attn * attn, axis=-1, keepdims=True)) + 1e-06)
    normed = attn * scale
    output = (normed * g).astype(jnp.bfloat16)
    ga = dy * g
    da = scale * (ga - normed * lax.optimization_barrier(jnp.mean(ga * normed, axis=-1, keepdims=True)))
    db = lax.optimization_barrier(da.astype(jnp.bfloat16)).astype(jnp.float32)
    gain_part = lax.optimization_barrier(jnp.sum(dy * normed, axis=(0, 1))).reshape(H * E)
    qd_local = ein('ntha,nthb->nhab', q, db)
    reversed_sum = jnp.cumsum(qd_local[::-1], axis=0)[::-1]
    suffix = jnp.concatenate([reversed_sum[1:], zero_state], axis=0)
    last_sel = (seg == last[:, None]) & (img == 1)
    g_local = ein('ntha,nthb->nhab', jnp.where(last_sel[:, :, None, None], q, 0.0), db)
    g_prev = jnp.concatenate([zero_state, g_local[:-1]], axis=0)
    last_prev = jnp.concatenate([none_id, last[:-1]], axis=0)
    on_prev = (seg == last_prev[:, None]).astype(jnp.float32)[:, :, None, None]
    dscores = ein('nthb,nshb->nhts', db, v)
    dprobs = lax.optimization_barrier(jnp.where(mask[:, None], dscores, 0.0).astype(jnp.bfloat16)).astype(jnp.float32)
    grad_q = ein('nthb,nhab->ntha', db, prefix) + on_next * ein('nthb,nhab->ntha', db, n_next)
    grad_q = grad_q + ein('nhts,nsha->ntha', dprobs, k)
    grad_k = ein('nshb,nhab->nsha', v, suffix) + on_prev * ein('nshb,nhab->nsha', v, g_prev)
    grad_k = grad_k + ein('nhts,ntha->nsha', dprobs, q)
    grad_v = ein('nsha,nhab->nshb', k, suffix) + on_prev * ein('nsha,nhab->nshb', k, g_prev)
    grad_v = grad_v + ein('nhts,nthb->nshb', probs, db)
    shape = (TOKENS, H * E)
    return (output.reshape(shape), grad_q.astype(jnp.bfloat16).reshape(shape), grad_k.astype(jnp.bfloat16).reshape(shape), grad_v.astype(jnp.bfloat16).reshape(shape), gain_part)

def reference(queries, keys, values, out_grad, segment_ids, image_flags, gain):
    gains = jnp.broadcast_to(gain, (SEQS, H * E))
    results = lax.map(per_sequence, (queries, keys, values, out_grad, segment_ids, image_flags, gains))
    return (results[0], results[1], results[2], results[3], lax.optimization_barrier(jnp.sum(results[4], axis=0)))
```

```python
import functools

import jax
import jax.numpy as jnp
from jax import lax
from jax.experimental import pallas as pl
from jax.experimental.pallas import tpu as pltpu
from jax.sharding import PartitionSpec as P

E = 64
PAIR = 2 * E
GROUPS = 2
EXTRA = 8
F32 = jnp.float32
BF16 = jnp.bfloat16


def dot(a, b, ca, cb):
    return lax.dot_general(a, b, (((ca,), (cb,)), ((), ())), preferred_element_type=F32)


def low_lanes(rows, cols):
    lane = lax.broadcasted_iota(jnp.int32, (rows, cols), 1)
    return lane % PAIR < E


def fold(product):
    return jnp.where(low_lanes(E, product.shape[1]), product[:E], product[E:])


def split(state):
    high = state.astype(BF16)
    return high, (state - high.astype(F32)).astype(BF16)


def spread(state):
    low = low_lanes(*state.shape)
    zero = jnp.zeros_like(state)
    return jnp.concatenate([jnp.where(low, state, zero), jnp.where(low, zero, state)], axis=0)


def heads_of(pair):
    low = low_lanes(*pair.shape)
    zero = jnp.zeros_like(pair)
    return jnp.where(low, pair, zero), jnp.where(low, zero, pair)


def twice(x):
    return jnp.concatenate([x, x], axis=1)


def pair_at(ref, p):
    return ref[:, p * PAIR:(p + 1) * PAIR]


def rows_of(value, p):
    return value[p * E:(p + 1) * E]


def state_pair(a, b, sel):
    return fold(dot(a, jnp.concatenate([b, b * sel], axis=1), 0, 0))


def put_states(step, states, marks, keep, send, part):
    for p, state in enumerate(states):
        part[0, p * E:(p + 1) * E] = state[:, PAIR:]
    part[0, len(states) * E:] = jnp.broadcast_to(marks, (EXTRA, PAIR))

    @pl.when(step == 0)
    def _():
        for p, state in enumerate(states):
            keep[p * E:(p + 1) * E] = state[:, :PAIR]

    @pl.when(step == 1)
    def _():
        for p, state in enumerate(states):
            send[p * E:(p + 1) * E] = state[:, :PAIR]


def states_kernel(core, k, v, segs, keep, send, part):
    first = (segs[...] == segs[0:1]).astype(BF16)
    count = k.shape[1] // PAIR
    states = [state_pair(pair_at(k, p), pair_at(v, p), first) for p in range(count)]
    put_states(pl.program_id(0), states, segs[0:1], keep, send, part)


def local_kernel(core, q, k, v, mask, attn, probs):
    m = mask[...]
    for p in range(q.shape[1] // PAIR):
        kp = pair_at(k, p)
        total = None
        for h, (qh, vh) in enumerate(zip(heads_of(pair_at(q, p)), heads_of(pair_at(v, p)))):
            prob = dot(qh, kp, 1, 1).astype(BF16) * m
            probs[2 * p + h] = prob
            term = dot(prob, vh, 1, 0)
            total = term if total is None else total + term
        attn[:, p * PAIR:(p + 1) * PAIR] = total


def head_mean(x):
    high, low = split(x)
    ones = spread(jnp.full((E, PAIR), 1.0 / E, BF16))
    return dot(jnp.concatenate([high, low], axis=1), jnp.concatenate([ones, ones], axis=0), 1, 0)


def side_by_side(state, part):
    sh, sl = split(state)
    ph, pll = split(part)
    left = jnp.concatenate([spread(sh), spread(sl)], axis=0)
    right = jnp.concatenate([spread(ph), spread(pll)], axis=0)
    return jnp.concatenate([left, right], axis=1)


def stacked(state, part):
    sh, sl = split(state)
    ph, pll = split(part)
    top = jnp.concatenate([spread(sh), spread(sl)], axis=1)
    bottom = jnp.concatenate([spread(ph), spread(pll)], axis=1)
    return jnp.concatenate([top, bottom], axis=0)


def norm_kernel(core, q, dy, local, gain, segs, imgs, pre_keep, pre_recv, nxt, *rest):
    out, dab, gsum, keep, send, part = rest[-6:]
    step = pl.program_id(0)
    count = q.shape[1] // PAIR
    prefix = jnp.where(step == 0, pre_keep[...], pre_recv[...])
    on_next = (imgs[...] == nxt[0, count * E:count * E + 1]).astype(F32)
    last = (imgs[...] == segs[segs.shape[0] - 1:]).astype(BF16)
    states = []
    for p in range(count):
        lanes = slice(p * PAIR, (p + 1) * PAIR)
        qp = q[:, lanes]
        far = dot(twice(qp), side_by_side(rows_of(prefix, p), nxt[0, p * E:(p + 1) * E]), 1, 0)
        attn = local[:, lanes] + far[:, :PAIR] + on_next * far[:, PAIR:]
        scale = lax.rsqrt(head_mean(attn * attn) + 1e-06)
        normed = attn * scale
        g = gain[:, lanes]
        out[:, lanes] = (normed * g).astype(BF16)
        dyp = dy[:, lanes].astype(F32)
        gsum[:, lanes] = jnp.sum(dyp * normed, axis=0, keepdims=True)
        ga = dyp * g
        da = (scale * (ga - normed * head_mean(ga * normed))).astype(BF16)
        dab[:, lanes] = da
        states.append(state_pair(qp, da, last))
    put_states(step, states, segs[segs.shape[0] - 1:], keep, send, part)


def inner_kernel(core, q, k, v, dab, probs, mask, imgs, pre_keep, pre_recv, nxt, *rest):
    gq, gk, gv = rest[-3:]
    step = pl.program_id(0)
    count = q.shape[1] // PAIR
    m = mask[...]
    prefix = jnp.where(step == 0, pre_keep[...], pre_recv[...])
    on_next = (imgs[...] == nxt[0, count * E:count * E + 1]).astype(F32)
    for p in range(count):
        lanes = slice(p * PAIR, (p + 1) * PAIR)
        da = dab[:, lanes]
        vp = v[:, lanes]
        far = dot(twice(da), stacked(rows_of(prefix, p), nxt[0, p * E:(p + 1) * E]), 1, 1)
        tq = far[:, :PAIR] + on_next * far[:, PAIR:]
        tk = tv = None
        das = heads_of(da)
        for h, (qh, kh, dh) in enumerate(zip(heads_of(q[:, lanes]), heads_of(k[:, lanes]), das)):
            dprob = dot(dh, vp, 1, 1).astype(BF16) * m
            tq = tq + dot(dprob, kh, 1, 0)
            a = dot(dprob, qh, 0, 0)
            b = dot(probs[2 * p + h], dh, 0, 0)
            tk = a if tk is None else tk + a
            tv = b if tv is None else tv + b
        gq[:, lanes] = tq.astype(BF16)
        gk[:, lanes] = tk
        gv[:, lanes] = tv


def outer_kernel(core, k, v, gk_in, gv_in, segs, suf_keep, suf_recv, prv, *rest):
    gk, gv = rest[-2:]
    step = pl.program_id(0)
    count = k.shape[1] // PAIR
    suffix = jnp.where(step == 0, suf_keep[...], suf_recv[...])
    on_prev = (segs[...] == prv[0, count * E:count * E + 1]).astype(F32)
    for p in range(count):
        lanes = slice(p * PAIR, (p + 1) * PAIR)
        s = rows_of(suffix, p)
        g = prv[0, p * E:(p + 1) * E]
        far = dot(twice(v[:, lanes]), stacked(s, g), 1, 1)
        gk[:, lanes] = (gk_in[:, lanes] + far[:, :PAIR] + on_prev * far[:, PAIR:]).astype(BF16)
        far = dot(twice(k[:, lanes]), side_by_side(s, g), 1, 0)
        gv[:, lanes] = (gv_in[:, lanes] + far[:, :PAIR] + on_prev * far[:, PAIR:]).astype(BF16)


def partner(x, axis, bit):
    route = [(i, i ^ (1 << bit)) for i in range(lax.axis_size(axis))]
    return lax.ppermute(x, axis, route)


def shifted(x, distance):
    count = lax.axis_size("ctx")
    return lax.ppermute(x, "ctx", [(i, i + distance) for i in range(count) if 0 <= i + distance < count])


def chips_before(own, towards):
    chips = lax.axis_size("ctx") // 2
    if chips > 8:
        total = shifted(own, 2 * towards)
        span = 1
        while span < chips:
            total = total + shifted(total, 2 * towards * span)
            span *= 2
        return total
    before = jnp.zeros_like(own)
    for hop in range(chips - 1):
        source = hop if towards == 1 else chips - 1 - hop
        route = [(2 * source + c, 2 * (source + towards) + c) for c in range(2)]
        before = before + lax.ppermute(own + before, "ctx", route)
    return before


def scan(keep, send, towards):
    core = lax.axis_index("ctx") & 1
    received = partner(send, "ctx", 0)
    before = chips_before(keep + received, towards)
    is_source = core == (0 if towards == 1 else 1)
    mine = jnp.where(is_source, before, before + received)
    theirs = partner(jnp.where(is_source, before + keep, before), "ctx", 0)
    return mine, theirs


def scatter_sum(x):
    devices = lax.axis_size("dp") * lax.axis_size("ctx")
    x = x.reshape(devices, -1)
    for axis in ("dp", "ctx"):
        for bit in reversed(range(lax.axis_size(axis).bit_length() - 1)):
            upper = lax.axis_index(axis) >> bit & 1 == 1
            half = x.shape[0] // 2
            low, high = x[:half], x[half:]
            x = jnp.where(upper, high, low) + partner(jnp.where(upper, low, high), axis, bit)
    return x.reshape(-1)


def on_device(queries, keys, values, out_grad, segment_ids, image_flags, gain):
    rows, width = queries.shape[1:]
    q, k, v, dy = (x[0] for x in (queries, keys, values, out_grad))
    seg = segment_ids[0]
    table = image_flags[0]
    gain_row = gain.reshape(1, width)
    core = (lax.axis_index("ctx") & 1).reshape(1).astype(jnp.int32)
    onehot = seg[:, None] == jnp.arange(table.shape[0], dtype=jnp.int32)[None, :]
    img = jnp.sum(jnp.where(onehot, table[None, :], 0), axis=1)
    imgseg = jnp.where(img == 1, seg, -1)
    pos = jnp.arange(rows)
    mask = (pos[:, None] >= pos[None, :]) | (imgseg[:, None] == seg[None, :])
    mask = mask.astype(BF16)
    segs = jnp.broadcast_to(seg.astype(F32)[:, None], (rows, PAIR))
    imgs = jnp.broadcast_to(imgseg.astype(F32)[:, None], (rows, PAIR))

    lanes = width // GROUPS // 2
    half_rows = lanes // PAIR * E
    heads = lanes // E

    def call(kernel, group, ins, outs, alias, flops):
        def wide(i, c):
            return (0, 2 * group + (i + c[0]) % 2)

        def own(i, c):
            return (0, (i + c[0]) % 2)

        def whole(i, c):
            return (0, 0)

        specs = {
            "wide": pl.BlockSpec((rows, lanes), wide),
            "block": pl.BlockSpec((rows, lanes), own),
            "row": pl.BlockSpec((1, lanes), wide),
            "rowblock": pl.BlockSpec((1, lanes), own),
            "half": pl.BlockSpec((half_rows, PAIR), whole),
            "part": pl.BlockSpec((1, half_rows + EXTRA, PAIR), lambda i, c: ((i + c[0]) % 2, 0, 0)),
            "segs": pl.BlockSpec((rows, PAIR), whole),
            "mask": pl.BlockSpec((rows, rows), whole),
            "probs": pl.BlockSpec((heads, rows, rows), lambda i, c: ((i + c[0]) % 2, 0, 0)),
            "any": pl.BlockSpec(memory_space=pl.ANY),
        }
        shapes = {
            "wide": (rows, width),
            "block": (rows, 2 * lanes),
            "rowblock": (1, 2 * lanes),
            "half": (half_rows, PAIR),
            "part": (2, half_rows + EXTRA, PAIR),
            "probs": (2 * heads, rows, rows),
        }
        operands = [x for _, x in ins]
        kinds = [kind for kind, _ in ins]
        aliases = {}
        for out_at, x in alias:
            if x is not None:
                aliases[1 + len(operands)] = out_at
                operands.append(x)
                kinds.append("any")
        out_shape = [jax.ShapeDtypeStruct(shapes[kind], dtype) for kind, dtype in outs]
        moved = sum(rows * 2 * lanes * 2 for kind in kinds if kind in ("wide", "block"))
        moved += sum(rows * 2 * lanes * 2 for kind, _ in outs if kind in ("wide", "block"))
        return pl.pallas_call(
            kernel,
            grid_spec=pltpu.PrefetchScalarGridSpec(
                num_scalar_prefetch=1,
                grid=(2,),
                in_specs=[specs[kind] for kind in kinds],
                out_specs=[specs[kind] for kind, _ in outs],
            ),
            out_shape=out_shape,
            input_output_aliases=aliases,
            compiler_params=pltpu.CompilerParams(vmem_limit_bytes=40 * 2**20),
            cost_estimate=pl.CostEstimate(flops=flops, bytes_accessed=moved, transcendentals=0),
        )(core, *operands)

    unit = 2 * rows * rows * PAIR * 2 * heads
    prefix, nexts = [], []
    for g in range(GROUPS):
        keep, send, n = call(
            states_kernel, g, [("wide", k), ("wide", v), ("segs", segs)],
            [("half", F32), ("half", F32), ("part", F32)], [], unit)
        prefix.append(scan(keep, send, 1))
        nexts.append(shifted(n, -1))
    local = [
        call(local_kernel, g, [("wide", q), ("wide", k), ("wide", v), ("mask", mask)],
             [("block", F32), ("probs", BF16)], [], 4 * unit)
        for g in range(GROUPS)
    ]
    output = grad_q = grad_k = grad_v = None
    suffix, prevs, inner, gsums = [], [], [], []
    for g in range(GROUPS):
        attn, probs = local[g]
        output, dab, gsum, keep, send, part = call(
            norm_kernel, g,
            [("wide", q), ("wide", dy), ("block", attn), ("row", gain_row), ("segs", segs), ("segs", imgs),
             ("half", prefix[g][0]), ("half", prefix[g][1]), ("part", nexts[g])],
            [("wide", BF16), ("block", BF16), ("rowblock", F32), ("half", F32), ("half", F32), ("part", F32)],
            [(0, output)], 2 * unit)
        gsums.append(gsum)
        suffix.append(scan(keep, send, -1))
        prevs.append(shifted(part, 1))
        grad_q, gk, gv = call(
            inner_kernel, g,
            [("wide", q), ("wide", k), ("wide", v), ("block", dab), ("probs", probs), ("mask", mask), ("segs", imgs),
             ("half", prefix[g][0]), ("half", prefix[g][1]), ("part", nexts[g])],
            [("wide", BF16), ("block", F32), ("block", F32)],
            [(0, grad_q)], 8 * unit)
        inner.append((gk, gv))
    grad_gain = scatter_sum(jnp.concatenate(gsums, axis=1))
    for g in range(GROUPS):
        gk, gv = inner[g]
        grad_k, grad_v = call(
            outer_kernel, g,
            [("wide", k), ("wide", v), ("block", gk), ("block", gv), ("segs", segs),
             ("half", suffix[g][0]), ("half", suffix[g][1]), ("part", prevs[g])],
            [("wide", BF16), ("wide", BF16)],
            [(0, grad_k), (1, grad_v)], 2 * unit)
    return output[None], grad_q[None], grad_k[None], grad_v[None], grad_gain


def solution(mesh):
    return jax.shard_map(
        on_device,
        mesh=mesh,
        in_specs=(
            P("dp", "ctx", None),
            P("dp", "ctx", None),
            P("dp", "ctx", None),
            P("dp", "ctx", None),
            P("dp", "ctx"),
            P("dp", None),
            P(),
        ),
        out_specs=(
            P("dp", "ctx", None),
            P("dp", "ctx", None),
            P("dp", "ctx", None),
            P("dp", "ctx", None),
            P(("dp", "ctx")),
        ),
        check_vma=False,
    )
```

```python
import functools

import jax
import jax.numpy as jnp
from jax import lax
from jax.experimental import pallas as pl
from jax.experimental.pallas import tpu as pltpu
from jax.sharding import PartitionSpec as P

E = 64
PAIR = 2 * E
GROUPS = 2
EXTRA = 8
F32 = jnp.float32
BF16 = jnp.bfloat16


def dot(a, b, ca, cb):
    return lax.dot_general(a, b, (((ca,), (cb,)), ((), ())), preferred_element_type=F32)


def low_lanes(rows, cols):
    lane = lax.broadcasted_iota(jnp.int32, (rows, cols), 1)
    return lane % PAIR < E


def fold(product):
    return jnp.where(low_lanes(E, product.shape[1]), product[:E], product[E:])


def split(state):
    high = state.astype(BF16)
    return high, (state - high.astype(F32)).astype(BF16)


def spread(state):
    low = low_lanes(*state.shape)
    zero = jnp.zeros_like(state)
    return jnp.concatenate([jnp.where(low, state, zero), jnp.where(low, zero, state)], axis=0)


def heads_of(pair):
    low = low_lanes(*pair.shape)
    zero = jnp.zeros_like(pair)
    return jnp.where(low, pair, zero), jnp.where(low, zero, pair)


def twice(x):
    return jnp.concatenate([x, x], axis=1)


def pair_at(ref, p):
    return ref[:, p * PAIR:(p + 1) * PAIR]


def rows_of(value, p):
    return value[p * E:(p + 1) * E]


def state_pair(a, b, sel):
    return fold(dot(a, jnp.concatenate([b, b * sel], axis=1), 0, 0))


def put_states(step, states, marks, keep, send, part):
    for p, state in enumerate(states):
        part[0, p * E:(p + 1) * E] = state[:, PAIR:]
    part[0, len(states) * E:] = jnp.broadcast_to(marks, (EXTRA, PAIR))

    @pl.when(step == 0)
    def _():
        for p, state in enumerate(states):
            keep[p * E:(p + 1) * E] = state[:, :PAIR]

    @pl.when(step == 1)
    def _():
        for p, state in enumerate(states):
            send[p * E:(p + 1) * E] = state[:, :PAIR]


def states_kernel(core, k, v, segs, keep, send, part):
    first = (segs[...] == segs[0:1]).astype(BF16)
    count = k.shape[1] // PAIR
    states = [state_pair(pair_at(k, p), pair_at(v, p), first) for p in range(count)]
    put_states(pl.program_id(0), states, segs[0:1], keep, send, part)


def local_kernel(core, q, k, v, mask, attn, probs):
    m = mask[...]
    for p in range(q.shape[1] // PAIR):
        kp = pair_at(k, p)
        total = None
        for h, (qh, vh) in enumerate(zip(heads_of(pair_at(q, p)), heads_of(pair_at(v, p)))):
            prob = dot(qh, kp, 1, 1).astype(BF16) * m
            probs[2 * p + h] = prob
            term = dot(prob, vh, 1, 0)
            total = term if total is None else total + term
        attn[:, p * PAIR:(p + 1) * PAIR] = total


def head_mean(x):
    high, low = split(x)
    ones = spread(jnp.full((E, PAIR), 1.0 / E, BF16))
    return dot(jnp.concatenate([high, low], axis=1), jnp.concatenate([ones, ones], axis=0), 1, 0)


def side_by_side(state, part):
    sh, sl = split(state)
    ph, pll = split(part)
    left = jnp.concatenate([spread(sh), spread(sl)], axis=0)
    right = jnp.concatenate([spread(ph), spread(pll)], axis=0)
    return jnp.concatenate([left, right], axis=1)


def stacked(state, part):
    sh, sl = split(state)
    ph, pll = split(part)
    top = jnp.concatenate([spread(sh), spread(sl)], axis=1)
    bottom = jnp.concatenate([spread(ph), spread(pll)], axis=1)
    return jnp.concatenate([top, bottom], axis=0)


def norm_kernel(core, q, dy, local, gain, segs, imgs, pre_keep, pre_recv, nxt, *rest):
    out, dab, gsum, keep, send, part = rest[-6:]
    step = pl.program_id(0)
    count = q.shape[1] // PAIR
    prefix = jnp.where(step == 0, pre_keep[...], pre_recv[...])
    on_next = (imgs[...] == nxt[0, count * E:count * E + 1]).astype(F32)
    last = (imgs[...] == segs[segs.shape[0] - 1:]).astype(BF16)
    pairs = [slice(p * PAIR, (p + 1) * PAIR) for p in range(count)]
    fars = [
        dot(twice(q[:, at]), side_by_side(rows_of(prefix, p), nxt[0, p * E:(p + 1) * E]), 1, 0)
        for p, at in enumerate(pairs)
    ]
    attns = [local[:, at] + far[:, :PAIR] + on_next * far[:, PAIR:] for at, far in zip(pairs, fars)]
    squares = [head_mean(attn * attn) for attn in attns]
    scales = [lax.rsqrt(square + 1e-06) for square in squares]
    normeds = [attn * scale for attn, scale in zip(attns, scales)]
    gas = [dy[:, at].astype(F32) * gain[:, at] for at in pairs]
    means = [head_mean(ga * normed) for ga, normed in zip(gas, normeds)]
    das = [
        (scale * (ga - normed * mean)).astype(BF16)
        for scale, ga, normed, mean in zip(scales, gas, normeds, means)
    ]
    states = [state_pair(q[:, at], da, last) for at, da in zip(pairs, das)]
    for at, normed, da in zip(pairs, normeds, das):
        dab[:, at] = da
        out[:, at] = (normed * gain[:, at]).astype(BF16)
        gsum[:, at] = jnp.sum(dy[:, at].astype(F32) * normed, axis=0, keepdims=True)
    put_states(step, states, segs[segs.shape[0] - 1:], keep, send, part)


def inner_kernel(core, q, k, v, dab, probs, mask, imgs, pre_keep, pre_recv, nxt, *rest):
    gq, gk, gv = rest[-3:]
    step = pl.program_id(0)
    count = q.shape[1] // PAIR
    m = mask[...]
    prefix = jnp.where(step == 0, pre_keep[...], pre_recv[...])
    on_next = (imgs[...] == nxt[0, count * E:count * E + 1]).astype(F32)
    for p in range(count):
        lanes = slice(p * PAIR, (p + 1) * PAIR)
        da = dab[:, lanes]
        vp = v[:, lanes]
        far = dot(twice(da), stacked(rows_of(prefix, p), nxt[0, p * E:(p + 1) * E]), 1, 1)
        tq = far[:, :PAIR] + on_next * far[:, PAIR:]
        tk = tv = None
        das = heads_of(da)
        for h, (qh, kh, dh) in enumerate(zip(heads_of(q[:, lanes]), heads_of(k[:, lanes]), das)):
            dprob = dot(dh, vp, 1, 1).astype(BF16) * m
            tq = tq + dot(dprob, kh, 1, 0)
            a = dot(dprob, qh, 0, 0)
            b = dot(probs[2 * p + h], dh, 0, 0)
            tk = a if tk is None else tk + a
            tv = b if tv is None else tv + b
        gq[:, lanes] = tq.astype(BF16)
        gk[:, lanes] = tk
        gv[:, lanes] = tv


def outer_kernel(core, k, v, gk_in, gv_in, segs, suf_keep, suf_recv, prv, *rest):
    gk, gv = rest[-2:]
    step = pl.program_id(0)
    count = k.shape[1] // PAIR
    suffix = jnp.where(step == 0, suf_keep[...], suf_recv[...])
    on_prev = (segs[...] == prv[0, count * E:count * E + 1]).astype(F32)
    for p in range(count):
        lanes = slice(p * PAIR, (p + 1) * PAIR)
        s = rows_of(suffix, p)
        g = prv[0, p * E:(p + 1) * E]
        far = dot(twice(v[:, lanes]), stacked(s, g), 1, 1)
        gk[:, lanes] = (gk_in[:, lanes] + far[:, :PAIR] + on_prev * far[:, PAIR:]).astype(BF16)
        far = dot(twice(k[:, lanes]), side_by_side(s, g), 1, 0)
        gv[:, lanes] = (gv_in[:, lanes] + far[:, :PAIR] + on_prev * far[:, PAIR:]).astype(BF16)


def partner(x, axis, bit):
    route = [(i, i ^ (1 << bit)) for i in range(lax.axis_size(axis))]
    return lax.ppermute(x, axis, route)


def shifted(x, distance):
    count = lax.axis_size("ctx")
    return lax.ppermute(x, "ctx", [(i, i + distance) for i in range(count) if 0 <= i + distance < count])


def chips_before(own, towards):
    chips = lax.axis_size("ctx") // 2
    if chips > 8:
        total = shifted(own, 2 * towards)
        span = 1
        while span < chips:
            total = total + shifted(total, 2 * towards * span)
            span *= 2
        return total
    before = jnp.zeros_like(own)
    for hop in range(chips - 1):
        source = hop if towards == 1 else chips - 1 - hop
        route = [(2 * source + c, 2 * (source + towards) + c) for c in range(2)]
        before = before + lax.ppermute(own + before, "ctx", route)
    return before


def scan(keep, send, towards):
    core = lax.axis_index("ctx") & 1
    received = partner(send, "ctx", 0)
    before = chips_before(keep + received, towards)
    is_source = core == (0 if towards == 1 else 1)
    mine = jnp.where(is_source, before, before + received)
    theirs = partner(jnp.where(is_source, before + keep, before), "ctx", 0)
    return mine, theirs


def scatter_sum(x):
    axes = ("dp", "ctx")
    devices = lax.axis_size("dp") * lax.axis_size("ctx")
    terms = lax.all_to_all(x.reshape(devices, -1), axes, 0, 0, tiled=True)
    return jnp.sum(terms, axis=0)


def on_device(queries, keys, values, out_grad, segment_ids, image_flags, gain):
    rows, width = queries.shape[1:]
    q, k, v, dy = (x[0] for x in (queries, keys, values, out_grad))
    seg = segment_ids[0]
    table = image_flags[0]
    gain_row = gain.reshape(1, width)
    core = (lax.axis_index("ctx") & 1).reshape(1).astype(jnp.int32)
    onehot = seg[:, None] == jnp.arange(table.shape[0], dtype=jnp.int32)[None, :]
    img = jnp.sum(jnp.where(onehot, table[None, :], 0), axis=1)
    imgseg = jnp.where(img == 1, seg, -1)
    pos = jnp.arange(rows)
    mask = (pos[:, None] >= pos[None, :]) | (imgseg[:, None] == seg[None, :])
    mask = mask.astype(BF16)
    segs = jnp.broadcast_to(seg.astype(F32)[:, None], (rows, PAIR))
    imgs = jnp.broadcast_to(imgseg.astype(F32)[:, None], (rows, PAIR))

    lanes = width // GROUPS // 2
    half_rows = lanes // PAIR * E
    heads = lanes // E

    def call(kernel, group, ins, outs, alias, micros):
        def wide(i, c):
            return (0, 2 * group + (i + c[0]) % 2)

        def own(i, c):
            return (0, (i + c[0]) % 2)

        def whole(i, c):
            return (0, 0)

        specs = {
            "wide": pl.BlockSpec((rows, lanes), wide),
            "block": pl.BlockSpec((rows, lanes), own),
            "row": pl.BlockSpec((1, lanes), wide),
            "rowblock": pl.BlockSpec((1, lanes), own),
            "half": pl.BlockSpec((half_rows, PAIR), whole),
            "part": pl.BlockSpec((1, half_rows + EXTRA, PAIR), lambda i, c: ((i + c[0]) % 2, 0, 0)),
            "segs": pl.BlockSpec((rows, PAIR), whole),
            "mask": pl.BlockSpec((rows, rows), whole),
            "probs": pl.BlockSpec((heads, rows, rows), lambda i, c: ((i + c[0]) % 2, 0, 0)),
            "any": pl.BlockSpec(memory_space=pl.ANY),
        }
        shapes = {
            "wide": (rows, width),
            "block": (rows, 2 * lanes),
            "rowblock": (1, 2 * lanes),
            "half": (half_rows, PAIR),
            "part": (2, half_rows + EXTRA, PAIR),
            "probs": (2 * heads, rows, rows),
        }
        operands = [x for _, x in ins]
        kinds = [kind for kind, _ in ins]
        aliases = {}
        for out_at, x in alias:
            if x is not None:
                aliases[1 + len(operands)] = out_at
                operands.append(x)
                kinds.append("any")
        out_shape = [jax.ShapeDtypeStruct(shapes[kind], dtype) for kind, dtype in outs]
        moved = sum(rows * 2 * lanes * 2 for kind in kinds if kind in ("wide", "block"))
        moved += sum(rows * 2 * lanes * 2 for kind, _ in outs if kind in ("wide", "block"))
        return pl.pallas_call(
            kernel,
            grid_spec=pltpu.PrefetchScalarGridSpec(
                num_scalar_prefetch=1,
                grid=(2,),
                in_specs=[specs[kind] for kind in kinds],
                out_specs=[specs[kind] for kind, _ in outs],
            ),
            out_shape=out_shape,
            input_output_aliases=aliases,
            compiler_params=pltpu.CompilerParams(vmem_limit_bytes=16 * 2**20),
            cost_estimate=pl.CostEstimate(flops=int(micros * 1.15e9), bytes_accessed=moved, transcendentals=0),
        )(core, *operands)

    prefix, nexts = [], []
    for g in range(GROUPS):
        keep, send, n = call(
            states_kernel, g, [("wide", k), ("wide", v), ("segs", segs)],
            [("half", F32), ("half", F32), ("part", F32)], [], 1.4)
        prefix.append(scan(keep, send, 1))
        nexts.append(shifted(n, -1))
    local = [
        call(local_kernel, g, [("wide", q), ("wide", k), ("wide", v), ("mask", mask)],
             [("block", F32), ("probs", BF16)], [], 2.3)
        for g in range(GROUPS)
    ]
    output = grad_q = grad_k = grad_v = None
    suffix, prevs, inner, gsums = [], [], [], []
    for g in range(GROUPS):
        attn, probs = local[g]
        output, dab, gsum, keep, send, part = call(
            norm_kernel, g,
            [("wide", q), ("wide", dy), ("block", attn), ("row", gain_row), ("segs", segs), ("segs", imgs),
             ("half", prefix[g][0]), ("half", prefix[g][1]), ("part", nexts[g])],
            [("wide", BF16), ("block", BF16), ("rowblock", F32), ("half", F32), ("half", F32), ("part", F32)],
            [(0, output)], 4.0)
        gsums.append(gsum)
        suffix.append(scan(keep, send, -1))
        prevs.append(shifted(part, 1))
        grad_q, gk, gv = call(
            inner_kernel, g,
            [("wide", q), ("wide", k), ("wide", v), ("block", dab), ("probs", probs), ("mask", mask), ("segs", imgs),
             ("half", prefix[g][0]), ("half", prefix[g][1]), ("part", nexts[g])],
            [("wide", BF16), ("block", F32), ("block", F32)],
            [(0, grad_q)], 5.5)
        inner.append((gk, gv))
    grad_gain = scatter_sum(jnp.concatenate(gsums, axis=1))
    for g in range(GROUPS):
        gk, gv = inner[g]
        grad_k, grad_v = call(
            outer_kernel, g,
            [("wide", k), ("wide", v), ("block", gk), ("block", gv), ("segs", segs),
             ("half", suffix[g][0]), ("half", suffix[g][1]), ("part", prevs[g])],
            [("wide", BF16), ("wide", BF16)],
            [(0, grad_k), (1, grad_v)], 2.1)
    return output[None], grad_q[None], grad_k[None], grad_v[None], grad_gain


def solution(mesh):
    return jax.shard_map(
        on_device,
        mesh=mesh,
        in_specs=(
            P("dp", "ctx", None),
            P("dp", "ctx", None),
            P("dp", "ctx", None),
            P("dp", "ctx", None),
            P("dp", "ctx"),
            P("dp", None),
            P(),
        ),
        out_specs=(
            P("dp", "ctx", None),
            P("dp", "ctx", None),
            P("dp", "ctx", None),
            P("dp", "ctx", None),
            P(("dp", "ctx")),
        ),
        check_vma=False,
    )
```

```python
import functools

import jax
import jax.numpy as jnp
from jax import lax
from jax.experimental import pallas as pl
from jax.experimental.pallas import tpu as pltpu
from jax.sharding import PartitionSpec as P

E = 64
PAIR = 2 * E
GROUPS = 2
EXTRA = 8
VMEM = 10 * 2**20
F32 = jnp.float32
BF16 = jnp.bfloat16


def dot(a, b, ca, cb):
    return lax.dot_general(a, b, (((ca,), (cb,)), ((), ())), preferred_element_type=F32)


def low_lanes(rows, cols):
    lane = lax.broadcasted_iota(jnp.int32, (rows, cols), 1)
    return lane % PAIR < E


def fold(product):
    return jnp.where(low_lanes(E, product.shape[1]), product[:E], product[E:])


def split(state):
    high = state.astype(BF16)
    return high, (state - high.astype(F32)).astype(BF16)


def spread(state):
    low = low_lanes(*state.shape)
    zero = jnp.zeros_like(state)
    return jnp.concatenate([jnp.where(low, state, zero), jnp.where(low, zero, state)], axis=0)


def heads_of(pair):
    low = low_lanes(*pair.shape)
    zero = jnp.zeros_like(pair)
    return jnp.where(low, pair, zero), jnp.where(low, zero, pair)


def twice(x):
    return jnp.concatenate([x, x], axis=1)


def pair_at(ref, p):
    return ref[:, p * PAIR:(p + 1) * PAIR]


def rows_of(value, p):
    return value[p * E:(p + 1) * E]


def state_pair(a, b):
    return fold(dot(a, b, 0, 0))


def edge(seg, table, last):
    row = seg[...]
    count = row.shape[1]
    own = row[:, count - 1:] if last else row[:, :1]
    size = jnp.sum((row == own).astype(F32), axis=1, keepdims=True)
    at = lax.broadcasted_iota(jnp.int32, (count, PAIR), 0).astype(F32)
    rows = at >= count - size if last else at < size
    ids = lax.broadcasted_iota(jnp.int32, table.shape, 1)
    flag = jnp.sum(jnp.where(ids == own, table[...], 0).astype(F32), axis=1, keepdims=True)
    return rows, own.astype(F32), flag


def states_kernel(group, core, k, v, *rest):
    keep, send, k_buf, v_buf, sems = rest[-5:]
    lanes = k_buf.shape[2]
    copies = []
    for half in (1, 0):
        at = pl.multiple_of((2 * group + (half + core[0]) % 2) * lanes, lanes)
        for i, (array, buf) in enumerate(((k, k_buf), (v, v_buf))):
            copies.append(pltpu.make_async_copy(array.at[:, pl.ds(at, lanes)], buf.at[half], sems.at[half, i]))
    for copy in copies:
        copy.start()
    for half, out in ((1, send), (0, keep)):
        copies.pop(0).wait()
        copies.pop(0).wait()
        for p in range(lanes // PAIR):
            at = slice(p * PAIR, (p + 1) * PAIR)
            out[p * E:(p + 1) * E] = state_pair(k_buf[half, :, at], v_buf[half, :, at])


def part_kernel(last, a, b, seg, table, *rest):
    out = rest[-1]
    count = a.shape[1] // PAIR
    rows, own, flag = edge(seg, table, last)
    sel = rows.astype(F32) * jnp.where(flag == 1, 1.0, 0.0) if last else rows.astype(F32)
    sel = sel.astype(BF16)
    for p in range(count):
        out[0, p * E:(p + 1) * E] = state_pair(pair_at(a, p), pair_at(b, p) * sel)
    out[0, count * E:] = jnp.broadcast_to(own, (EXTRA, PAIR))


def local_kernel(core, q, k, v, mask, *rest):
    attn, token = rest[-2:]
    m = mask[...]
    token[...] = jnp.zeros_like(token)
    for p in range(q.shape[1] // PAIR):
        kp = pair_at(k, p)
        total = None
        for qh, vh in zip(heads_of(pair_at(q, p)), heads_of(pair_at(v, p))):
            prob = dot(qh, kp, 1, 1).astype(BF16) * m
            term = dot(prob, vh, 1, 0)
            total = term if total is None else total + term
        attn[:, p * PAIR:(p + 1) * PAIR] = total


def head_mean(x):
    high, low = split(x)
    ones = spread(jnp.full((E, PAIR), 1.0 / E, BF16))
    return dot(jnp.concatenate([high, low], axis=1), jnp.concatenate([ones, ones], axis=0), 1, 0)


def side_by_side(state, part):
    sh, sl = split(state)
    ph, pll = split(part)
    left = jnp.concatenate([spread(sh), spread(sl)], axis=0)
    right = jnp.concatenate([spread(ph), spread(pll)], axis=0)
    return jnp.concatenate([left, right], axis=1)


def stacked(state, part):
    sh, sl = split(state)
    ph, pll = split(part)
    top = jnp.concatenate([spread(sh), spread(sl)], axis=1)
    bottom = jnp.concatenate([spread(ph), spread(pll)], axis=1)
    return jnp.concatenate([top, bottom], axis=0)


def on_rows(seg, table, last, part, count):
    rows, own, flag = edge(seg, table, last)
    met = part[0, count * E:count * E + 1] == own
    if last:
        met = met & (flag == 1)
    return rows.astype(F32) * met.astype(F32)


def norm_kernel(core, q, dy, local, gain, seg, table, pre_keep, pre_recv, nxt, *rest):
    out, dab, gsum, keep, send = rest[-5:]
    step = pl.program_id(0)
    count = q.shape[1] // PAIR
    prefix = jnp.where(step == 0, pre_keep[...], pre_recv[...])
    on_next = on_rows(seg, table, True, nxt, count)
    pairs = [slice(p * PAIR, (p + 1) * PAIR) for p in range(count)]
    fars = [
        dot(twice(q[:, at]), side_by_side(rows_of(prefix, p), nxt[0, p * E:(p + 1) * E]), 1, 0)
        for p, at in enumerate(pairs)
    ]
    attns = [local[:, at] + far[:, :PAIR] + on_next * far[:, PAIR:] for at, far in zip(pairs, fars)]
    squares = [head_mean(attn * attn) for attn in attns]
    scales = [lax.rsqrt(square + 1e-06) for square in squares]
    normeds = [attn * scale for attn, scale in zip(attns, scales)]
    gas = [dy[:, at].astype(F32) * gain[:, at] for at in pairs]
    means = [head_mean(ga * normed) for ga, normed in zip(gas, normeds)]
    das = [
        (scale * (ga - normed * mean)).astype(BF16)
        for scale, ga, normed, mean in zip(scales, gas, normeds, means)
    ]
    states = [state_pair(q[:, at], da) for at, da in zip(pairs, das)]
    for at, normed, da in zip(pairs, normeds, das):
        dab[:, at] = da
        out[:, at] = (normed * gain[:, at]).astype(BF16)
        gsum[:, at] = jnp.sum(dy[:, at].astype(F32) * normed, axis=0, keepdims=True)

    @pl.when(step == 0)
    def _():
        for p, state in enumerate(states):
            keep[p * E:(p + 1) * E] = state

    @pl.when(step == 1)
    def _():
        for p, state in enumerate(states):
            send[p * E:(p + 1) * E] = state


def inner_kernel(core, q, k, v, dab, mask, mask_t, seg, table, pre_keep, pre_recv, nxt, *rest):
    gq, gk, gv, token = rest[-4:]
    step = pl.program_id(0)
    count = q.shape[1] // PAIR
    m, mt = mask[...], mask_t[...]
    token[...] = jnp.zeros_like(token)
    prefix = jnp.where(step == 0, pre_keep[...], pre_recv[...])
    on_next = on_rows(seg, table, True, nxt, count)
    for p in range(count):
        lanes = slice(p * PAIR, (p + 1) * PAIR)
        da = dab[:, lanes]
        kp, vp = k[:, lanes], v[:, lanes]
        far = dot(twice(da), stacked(rows_of(prefix, p), nxt[0, p * E:(p + 1) * E]), 1, 1)
        tq = far[:, :PAIR] + on_next * far[:, PAIR:]
        tk = tv = None
        for qh, kh, dh in zip(heads_of(q[:, lanes]), heads_of(kp), heads_of(da)):
            dprob = dot(dh, vp, 1, 1).astype(BF16) * m
            prob_t = dot(kp, qh, 1, 1).astype(BF16) * mt
            tq = tq + dot(dprob, kh, 1, 0)
            a = dot(dprob, qh, 0, 0)
            b = dot(prob_t, dh, 1, 0)
            tk = a if tk is None else tk + a
            tv = b if tv is None else tv + b
        gq[:, lanes] = tq.astype(BF16)
        gk[:, lanes] = tk
        gv[:, lanes] = tv


def outer_kernel(core, k, v, gk_in, gv_in, seg, table, suf_keep, suf_recv, prv, *rest):
    gk, gv = rest[-2:]
    step = pl.program_id(0)
    count = k.shape[1] // PAIR
    suffix = jnp.where(step == 0, suf_keep[...], suf_recv[...])
    on_prev = on_rows(seg, table, False, prv, count)
    for p in range(count):
        lanes = slice(p * PAIR, (p + 1) * PAIR)
        s = rows_of(suffix, p)
        g = prv[0, p * E:(p + 1) * E]
        far = dot(twice(v[:, lanes]), stacked(s, g), 1, 1)
        gk[:, lanes] = (gk_in[:, lanes] + far[:, :PAIR] + on_prev * far[:, PAIR:]).astype(BF16)
        far = dot(twice(k[:, lanes]), side_by_side(s, g), 1, 0)
        gv[:, lanes] = (gv_in[:, lanes] + far[:, :PAIR] + on_prev * far[:, PAIR:]).astype(BF16)


def partner(x, axis, bit):
    route = [(i, i ^ (1 << bit)) for i in range(lax.axis_size(axis))]
    return lax.ppermute(x, axis, route)


def shifted(x, distance):
    count = lax.axis_size("ctx")
    return lax.ppermute(x, "ctx", [(i, i + distance) for i in range(count) if 0 <= i + distance < count])


def chips_before(owns, towards, works):
    chips = lax.axis_size("ctx") // 2
    if chips > 8:
        for work in works:
            work(owns)
        totals = [shifted(own, 2 * towards) for own in owns]
        span = 1
        while span < chips:
            totals = [total + shifted(total, 2 * towards * span) for total in totals]
            span *= 2
        return totals
    befores = [None] * len(owns)
    for hop in range(max(chips - 1, len(works))):
        totals = [own if before is None else own + before for own, before in zip(owns, befores)]
        source = hop if towards == 1 else chips - 1 - hop
        token = works[hop](totals) if hop < len(works) else 0.0
        if hop < chips - 1:
            route = [(2 * source + c, 2 * (source + towards) + c) for c in range(2)]
            arrived = [lax.ppermute(total, "ctx", route) + token for total in totals]
            befores = [a if before is None else before + a for before, a in zip(befores, arrived)]
    return befores


def within_chip(keep, send):
    received = partner(send, "ctx", 0)
    return received, keep + received


def to_cores(before, keep, received, towards):
    is_source = lax.axis_index("ctx") & 1 == (0 if towards == 1 else 1)
    mine = jnp.where(is_source, before, before + received)
    return mine, partner(jnp.where(is_source, before + keep, before), "ctx", 0)


def scatter_sum(x):
    axes = ("dp", "ctx")
    devices = lax.axis_size("dp") * lax.axis_size("ctx")
    terms = lax.all_to_all(x.reshape(devices, -1), axes, 0, 0, tiled=True)
    return jnp.sum(terms, axis=0)


def on_device(queries, keys, values, out_grad, segment_ids, image_flags, gain):
    rows, width = queries.shape[1:]
    q, k, v, dy = (x[0] for x in (queries, keys, values, out_grad))
    seg = segment_ids[0]
    table = image_flags[0]
    gain_row = gain.reshape(1, width)
    core = (lax.axis_index("ctx") & 1).reshape(1).astype(jnp.int32)
    onehot = seg[:, None] == jnp.arange(table.shape[0], dtype=jnp.int32)[None, :]
    img = jnp.sum(jnp.where(onehot, table[None, :], 0), axis=1)
    imgseg = jnp.where(img == 1, seg, -1)
    pos = jnp.arange(rows)
    mask = ((pos[:, None] >= pos[None, :]) | (imgseg[:, None] == seg[None, :])).astype(BF16)
    mask_t = ((pos[:, None] <= pos[None, :]) | (seg[:, None] == imgseg[None, :])).astype(BF16)

    lanes = width // GROUPS // 2
    half_rows = lanes // PAIR * E
    heads = lanes // E

    def call(kernel, group, ins, outs, micros, after=(), alias=(), scratch=(), steps=(2,), prefetch=True):
        def at(i, c=None):
            return (i + c[0]) % 2 if prefetch else i

        def wide(*args):
            return (0, 2 * group + at(*args))

        def own(*args):
            return (0, at(*args))

        def whole(*args):
            return (0, 0)

        def part(*args):
            return (2 * group + at(*args), 0, 0)

        specs = {
            "wide": pl.BlockSpec((rows, lanes), wide),
            "block": pl.BlockSpec((rows, lanes), own),
            "row": pl.BlockSpec((1, lanes), wide),
            "rowblock": pl.BlockSpec((1, lanes), own),
            "half": pl.BlockSpec((half_rows, PAIR), whole),
            "part": pl.BlockSpec((1, half_rows + EXTRA, PAIR), part),
            "seg": pl.BlockSpec((1, rows), whole),
            "table": pl.BlockSpec((1, table.shape[0]), whole),
            "mask": pl.BlockSpec((rows, rows), whole),
            "token": pl.BlockSpec((8, PAIR), whole),
            "any": pl.BlockSpec(memory_space=pl.ANY),
            "hbm": pl.BlockSpec(memory_space=pltpu.HBM),
        }
        shapes = {
            "wide": (rows, width),
            "block": (rows, 2 * lanes),
            "rowblock": (1, 2 * lanes),
            "half": (half_rows, PAIR),
            "part": (2 * GROUPS, half_rows + EXTRA, PAIR),
            "token": (8, PAIR),
        }
        operands = [x for _, x in ins] + list(after)
        kinds = [kind for kind, _ in ins] + ["any"] * len(after)
        aliases = {}
        for out_at, x in alias:
            if x is not None:
                aliases[prefetch + len(operands)] = out_at
                operands.append(x)
                kinds.append("any")
        out_shape = [jax.ShapeDtypeStruct(shapes[kind], dtype) for kind, dtype in outs]
        moved = sum(rows * 2 * lanes * 2 for kind in kinds if kind in ("wide", "block"))
        moved += sum(rows * 2 * lanes * 2 for kind, _ in outs if kind in ("wide", "block"))
        return pl.pallas_call(
            kernel,
            grid_spec=pltpu.PrefetchScalarGridSpec(
                num_scalar_prefetch=int(prefetch),
                grid=steps,
                in_specs=[specs[kind] for kind in kinds],
                out_specs=[specs[kind] for kind, _ in outs],
                scratch_shapes=scratch,
            ),
            out_shape=out_shape,
            input_output_aliases=aliases,
            compiler_params=pltpu.CompilerParams(vmem_limit_bytes=VMEM),
            cost_estimate=pl.CostEstimate(flops=int(micros * 1.15e9), bytes_accessed=moved, transcendentals=0),
        )(*([core] if prefetch else []), *operands)

    edges = [("seg", segment_ids), ("table", image_flags)]
    groups = range(GROUPS)

    def phase(pieces, towards, works):
        befores = chips_before([own for _, _, own in pieces], towards, works)
        return [to_cores(before, keep, received, towards) for before, (keep, received, _) in zip(befores, pieces)]

    pieces = []
    buffers = [pltpu.VMEM((2, rows, lanes), BF16)] * 2 + [pltpu.SemaphoreType.DMA((2, 2))]
    for g in groups:
        keep, send = call(
            functools.partial(states_kernel, g), g, [("hbm", k), ("hbm", v)],
            [("half", F32), ("half", F32)], 1.2, scratch=buffers, steps=())
        pieces.append((keep, *within_chip(keep, send)))

    found = {}

    def early_work(g):
        def work(totals):
            if g == 0:
                found["nxt"], = call(
                    functools.partial(part_kernel, False), 0, [("wide", k), ("wide", v), *edges],
                    [("part", F32)], 2.0, after=totals, steps=(2 * GROUPS,), prefetch=False)
                totals = [found["nxt"]]
            found["local", g], token = call(
                local_kernel, g, [("wide", q), ("wide", k), ("wide", v), ("mask", mask)],
                [("block", F32), ("token", F32)], 2.3, after=totals)
            return token[:1, :1]
        return work

    prefix = phase(pieces, 1, [early_work(g) for g in groups])
    nxt = shifted(found["nxt"], -1)

    output = dab = grad_q = grad_k = grad_v = None
    pieces, gsums = [], []
    for g in groups:
        output, dab, gsum, keep, send = call(
            norm_kernel, g,
            [("wide", q), ("wide", dy), ("block", found["local", g]), ("row", gain_row), *edges,
             ("half", prefix[g][0]), ("half", prefix[g][1]), ("part", nxt)],
            [("wide", BF16), ("wide", BF16), ("rowblock", F32), ("half", F32), ("half", F32)],
            3.0, after=[own for _, _, own in pieces], alias=[(0, output), (1, dab)])
        gsums.append(gsum)
        pieces.append((keep, *within_chip(keep, send)))

    def late_work(g):
        def work(totals):
            if g == 0:
                found["prv"], = call(
                    functools.partial(part_kernel, True), 0, [("wide", q), ("wide", dab), *edges],
                    [("part", F32)], 2.0, after=totals, steps=(2 * GROUPS,), prefetch=False)
                totals = [found["prv"]]
            found["gq"], gk, gv, token = call(
                inner_kernel, g,
                [("wide", q), ("wide", k), ("wide", v), ("wide", dab), ("mask", mask), ("mask", mask_t), *edges,
                 ("half", prefix[g][0]), ("half", prefix[g][1]), ("part", nxt)],
                [("wide", BF16), ("block", F32), ("block", F32), ("token", F32)],
                5.5, after=totals, alias=[(0, found.get("gq"))])
            found["inner", g] = gk, gv
            return token[:1, :1]
        return work

    suffix = phase(pieces, -1, [late_work(g) for g in groups])
    prv = shifted(found["prv"], 1)
    grad_q = found["gq"]
    grad_gain = scatter_sum(jnp.concatenate(gsums, axis=1))
    for g in groups:
        gk, gv = found["inner", g]
        grad_k, grad_v = call(
            outer_kernel, g,
            [("wide", k), ("wide", v), ("block", gk), ("block", gv), *edges,
             ("half", suffix[g][0]), ("half", suffix[g][1]), ("part", prv)],
            [("wide", BF16), ("wide", BF16)],
            2.1, alias=[(0, grad_k), (1, grad_v)])
    return output[None], grad_q[None], grad_k[None], grad_v[None], grad_gain


def solution(mesh):
    return jax.shard_map(
        on_device,
        mesh=mesh,
        in_specs=(
            P("dp", "ctx", None),
            P("dp", "ctx", None),
            P("dp", "ctx", None),
            P("dp", "ctx", None),
            P("dp", "ctx"),
            P("dp", None),
            P(),
        ),
        out_specs=(
            P("dp", "ctx", None),
            P("dp", "ctx", None),
            P("dp", "ctx", None),
            P("dp", "ctx", None),
            P(("dp", "ctx")),
        ),
        check_vma=False,
    )
```

```python
import functools

import jax
import jax.numpy as jnp
from jax import lax
from jax.experimental import pallas as pl
from jax.experimental.pallas import tpu as pltpu
from jax.sharding import PartitionSpec as P

E = 64
PAIR = 2 * E
GROUPS = 2
EXTRA = 8
VMEM = 10 * 2**20
F32 = jnp.float32
BF16 = jnp.bfloat16


def dot(a, b, ca, cb):
    return lax.dot_general(a, b, (((ca,), (cb,)), ((), ())), preferred_element_type=F32)


def low_lanes(rows, cols):
    lane = lax.broadcasted_iota(jnp.int32, (rows, cols), 1)
    return lane % PAIR < E


def fold(product):
    return jnp.where(low_lanes(E, product.shape[1]), product[:E], product[E:])


def split(state):
    high = state.astype(BF16)
    return high, (state - high.astype(F32)).astype(BF16)


def spread(state):
    low = low_lanes(*state.shape)
    zero = jnp.zeros_like(state)
    return jnp.concatenate([jnp.where(low, state, zero), jnp.where(low, zero, state)], axis=0)


def heads_of(pair):
    low = low_lanes(*pair.shape)
    zero = jnp.zeros_like(pair)
    return jnp.where(low, pair, zero), jnp.where(low, zero, pair)


def twice(x):
    return jnp.concatenate([x, x], axis=1)


def pair_at(ref, p):
    return ref[:, p * PAIR:(p + 1) * PAIR]


def rows_of(value, p):
    return value[p * E:(p + 1) * E]


def state_pair(a, b):
    return fold(dot(a, b, 0, 0))


def edge(seg, table, last):
    row = seg[...]
    count = row.shape[1]
    own = row[:, count - 1:] if last else row[:, :1]
    size = jnp.sum((row == own).astype(F32), axis=1, keepdims=True)
    at = lax.broadcasted_iota(jnp.int32, (count, PAIR), 0).astype(F32)
    rows = at >= count - size if last else at < size
    ids = lax.broadcasted_iota(jnp.int32, table.shape, 1)
    flag = jnp.sum(jnp.where(ids == own, table[...], 0).astype(F32), axis=1, keepdims=True)
    return rows, own.astype(F32), flag


def states_kernel(group, core, k, v, *rest):
    keep, send, k_buf, v_buf, sems = rest[-5:]
    lanes = k_buf.shape[2]
    copies = []
    for half in (1, 0):
        at = pl.multiple_of((2 * group + (half + core[0]) % 2) * lanes, lanes)
        for i, (array, buf) in enumerate(((k, k_buf), (v, v_buf))):
            copies.append(pltpu.make_async_copy(array.at[:, pl.ds(at, lanes)], buf.at[half], sems.at[half, i]))
    for copy in copies:
        copy.start()
    for half, out in ((1, send), (0, keep)):
        copies.pop(0).wait()
        copies.pop(0).wait()
        for p in range(lanes // PAIR):
            at = slice(p * PAIR, (p + 1) * PAIR)
            out[p * E:(p + 1) * E] = state_pair(k_buf[half, :, at], v_buf[half, :, at])


def part_kernel(last, a, b, seg, table, *rest):
    out = rest[-1]
    count = a.shape[1] // PAIR
    rows, own, flag = edge(seg, table, last)
    sel = rows.astype(F32) * jnp.where(flag == 1, 1.0, 0.0) if last else rows.astype(F32)
    sel = sel.astype(BF16)
    for p in range(count):
        out[0, p * E:(p + 1) * E] = state_pair(pair_at(a, p), pair_at(b, p) * sel)
    out[0, count * E:] = jnp.broadcast_to(own, (EXTRA, PAIR))


def local_kernel(core, q, k, v, mask, *rest):
    attn, token = rest[-2:]
    m = mask[...]
    token[...] = jnp.zeros_like(token)
    for p in range(q.shape[1] // PAIR):
        kp = pair_at(k, p)
        total = None
        for qh, vh in zip(heads_of(pair_at(q, p)), heads_of(pair_at(v, p))):
            prob = dot(qh, kp, 1, 1).astype(BF16) * m
            term = dot(prob, vh, 1, 0)
            total = term if total is None else total + term
        attn[:, p * PAIR:(p + 1) * PAIR] = total


def head_mean(x):
    high, low = split(x)
    ones = spread(jnp.full((E, PAIR), 1.0 / E, BF16))
    return dot(jnp.concatenate([high, low], axis=1), jnp.concatenate([ones, ones], axis=0), 1, 0)


def side_by_side(state, part):
    sh, sl = split(state)
    ph, pll = split(part)
    left = jnp.concatenate([spread(sh), spread(sl)], axis=0)
    right = jnp.concatenate([spread(ph), spread(pll)], axis=0)
    return jnp.concatenate([left, right], axis=1)


def stacked(state, part):
    sh, sl = split(state)
    ph, pll = split(part)
    top = jnp.concatenate([spread(sh), spread(sl)], axis=1)
    bottom = jnp.concatenate([spread(ph), spread(pll)], axis=1)
    return jnp.concatenate([top, bottom], axis=0)


def on_rows(seg, table, last, part, count):
    rows, own, flag = edge(seg, table, last)
    met = part[0, count * E:count * E + 1] == own
    if last:
        met = met & (flag == 1)
    return rows.astype(F32) * met.astype(F32)


def norm_kernel(core, q, dy, local, gain, seg, table, pre_keep, pre_recv, nxt, *rest):
    out, dab, gsum, keep, send = rest[-5:]
    step = pl.program_id(0)
    count = q.shape[1] // PAIR
    prefix = jnp.where(step == 0, pre_keep[...], pre_recv[...])
    on_next = on_rows(seg, table, True, nxt, count)
    pairs = [slice(p * PAIR, (p + 1) * PAIR) for p in range(count)]
    fars = [
        dot(twice(q[:, at]), side_by_side(rows_of(prefix, p), nxt[0, p * E:(p + 1) * E]), 1, 0)
        for p, at in enumerate(pairs)
    ]
    attns = [local[:, at] + far[:, :PAIR] + on_next * far[:, PAIR:] for at, far in zip(pairs, fars)]
    squares = [head_mean(attn * attn) for attn in attns]
    scales = [lax.rsqrt(square + 1e-06) for square in squares]
    normeds = [attn * scale for attn, scale in zip(attns, scales)]
    gas = [dy[:, at].astype(F32) * gain[:, at] for at in pairs]
    means = [head_mean(ga * normed) for ga, normed in zip(gas, normeds)]
    das = [
        (scale * (ga - normed * mean)).astype(BF16)
        for scale, ga, normed, mean in zip(scales, gas, normeds, means)
    ]
    states = [state_pair(q[:, at], da) for at, da in zip(pairs, das)]
    for at, normed, da in zip(pairs, normeds, das):
        dab[:, at] = da
        out[:, at] = (normed * gain[:, at]).astype(BF16)
        gsum[:, at] = jnp.sum(dy[:, at].astype(F32) * normed, axis=0, keepdims=True)

    @pl.when(step == 0)
    def _():
        for p, state in enumerate(states):
            keep[p * E:(p + 1) * E] = state

    @pl.when(step == 1)
    def _():
        for p, state in enumerate(states):
            send[p * E:(p + 1) * E] = state


def inner_kernel(core, q, k, v, dab, mask, mask_t, seg, table, pre_keep, pre_recv, nxt, *rest):
    gq, gk, gv, token = rest[-4:]
    step = pl.program_id(0)
    count = q.shape[1] // PAIR
    m, mt = mask[...], mask_t[...]
    token[...] = jnp.zeros_like(token)
    prefix = jnp.where(step == 0, pre_keep[...], pre_recv[...])
    on_next = on_rows(seg, table, True, nxt, count)
    for p in range(count):
        lanes = slice(p * PAIR, (p + 1) * PAIR)
        da = dab[:, lanes]
        kp, vp = k[:, lanes], v[:, lanes]
        far = dot(twice(da), stacked(rows_of(prefix, p), nxt[0, p * E:(p + 1) * E]), 1, 1)
        tq = far[:, :PAIR] + on_next * far[:, PAIR:]
        tk = tv = None
        for qh, kh, dh in zip(heads_of(q[:, lanes]), heads_of(kp), heads_of(da)):
            dprob = dot(dh, vp, 1, 1).astype(BF16) * m
            prob_t = dot(kp, qh, 1, 1).astype(BF16) * mt
            tq = tq + dot(dprob, kh, 1, 0)
            a = dot(dprob, qh, 0, 0)
            b = dot(prob_t, dh, 1, 0)
            tk = a if tk is None else tk + a
            tv = b if tv is None else tv + b
        gq[:, lanes] = tq.astype(BF16)
        gk[:, lanes] = tk
        gv[:, lanes] = tv


def outer_kernel(core, k, v, gk_in, gv_in, seg, table, suf_keep, suf_recv, prv, *rest):
    gk, gv = rest[-2:]
    step = pl.program_id(0)
    count = k.shape[1] // PAIR
    suffix = jnp.where(step == 0, suf_keep[...], suf_recv[...])
    on_prev = on_rows(seg, table, False, prv, count)
    for p in range(count):
        lanes = slice(p * PAIR, (p + 1) * PAIR)
        s = rows_of(suffix, p)
        g = prv[0, p * E:(p + 1) * E]
        far = dot(twice(v[:, lanes]), stacked(s, g), 1, 1)
        gk[:, lanes] = (gk_in[:, lanes] + far[:, :PAIR] + on_prev * far[:, PAIR:]).astype(BF16)
        far = dot(twice(k[:, lanes]), side_by_side(s, g), 1, 0)
        gv[:, lanes] = (gv_in[:, lanes] + far[:, :PAIR] + on_prev * far[:, PAIR:]).astype(BF16)


def partner(x, axis, bit):
    route = [(i, i ^ (1 << bit)) for i in range(lax.axis_size(axis))]
    return lax.ppermute(x, axis, route)


def shifted(x, distance):
    count = lax.axis_size("ctx")
    return lax.ppermute(x, "ctx", [(i, i + distance) for i in range(count) if 0 <= i + distance < count])


def chips_before(owns, towards, works):
    chips = lax.axis_size("ctx") // 2
    if chips > 8:
        for work in works:
            work(owns)
        totals = [shifted(own, 2 * towards) for own in owns]
        span = 1
        while span < chips:
            totals = [total + shifted(total, 2 * towards * span) for total in totals]
            span *= 2
        return totals
    befores = [None] * len(owns)
    for hop in range(max(chips - 1, len(works))):
        totals = [own if before is None else own + before for own, before in zip(owns, befores)]
        source = hop if towards == 1 else chips - 1 - hop
        token = works[hop](totals) if hop < len(works) else jnp.zeros((1, PAIR), F32)
        if hop < chips - 1:
            route = [(2 * source + c, 2 * (source + towards) + c) for c in range(2)]
            arrived = [lax.ppermute(total, "ctx", route) + token for total in totals]
            befores = [a if before is None else before + a for before, a in zip(befores, arrived)]
    return befores


def within_chip(keep, send):
    received = partner(send, "ctx", 0)
    return received, keep + received


def to_cores(before, keep, received, towards):
    is_source = lax.axis_index("ctx") & 1 == (0 if towards == 1 else 1)
    mine = jnp.where(is_source, before, before + received)
    return mine, partner(jnp.where(is_source, before + keep, before), "ctx", 0)


def in_hbm(x):
    return pltpu.with_memory_space_constraint(x, pltpu.HBM)


def scatter_sum(x):
    axes = ("dp", "ctx")
    terms = lax.all_gather(x[0], axes)
    count = x.shape[1] // terms.shape[0]
    own = lax.dynamic_slice_in_dim(terms, lax.axis_index(axes) * count, count, 1)
    return jnp.sum(own, axis=0)


def on_device(queries, keys, values, out_grad, segment_ids, image_flags, gain):
    rows, width = queries.shape[1:]
    q, k, v, dy = (x[0] for x in (queries, keys, values, out_grad))
    seg = segment_ids[0]
    table = image_flags[0]
    gain_row = gain.reshape(1, width)
    core = (lax.axis_index("ctx") & 1).reshape(1).astype(jnp.int32)
    onehot = seg[:, None] == jnp.arange(table.shape[0], dtype=jnp.int32)[None, :]
    img = jnp.sum(jnp.where(onehot, table[None, :], 0), axis=1)
    imgseg = jnp.where(img == 1, seg, -1)
    pos = jnp.arange(rows)
    mask = ((pos[:, None] >= pos[None, :]) | (imgseg[:, None] == seg[None, :])).astype(BF16)
    mask_t = ((pos[:, None] <= pos[None, :]) | (seg[:, None] == imgseg[None, :])).astype(BF16)

    lanes = width // GROUPS // 2
    half_rows = lanes // PAIR * E
    heads = lanes // E

    def call(kernel, group, ins, outs, micros, after=(), alias=(), scratch=(), steps=(2,), prefetch=True):
        def at(i, c=None):
            return (i + c[0]) % 2 if prefetch else i

        def wide(*args):
            return (0, 2 * group + at(*args))

        def own(*args):
            return (0, at(*args))

        def whole(*args):
            return (0, 0)

        def part(*args):
            return (2 * group + at(*args), 0, 0)

        specs = {
            "wide": pl.BlockSpec((rows, lanes), wide),
            "block": pl.BlockSpec((rows, lanes), own),
            "row": pl.BlockSpec((1, lanes), wide),
            "rowblock": pl.BlockSpec((1, lanes), own),
            "half": pl.BlockSpec((half_rows, PAIR), whole),
            "part": pl.BlockSpec((1, half_rows + EXTRA, PAIR), part),
            "seg": pl.BlockSpec((1, rows), whole),
            "table": pl.BlockSpec((1, table.shape[0]), whole),
            "mask": pl.BlockSpec((rows, rows), whole),
            "token": pl.BlockSpec((1, PAIR), whole),
            "after2": pl.BlockSpec((8, PAIR), whole),
            "after3": pl.BlockSpec((1, 8, PAIR), lambda *args: (0, 0, 0)),
            "any": pl.BlockSpec(memory_space=pl.ANY),
            "hbm": pl.BlockSpec(memory_space=pltpu.HBM),
        }
        shapes = {
            "wide": (rows, width),
            "block": (rows, 2 * lanes),
            "rowblock": (1, 2 * lanes),
            "half": (half_rows, PAIR),
            "part": (2 * GROUPS, half_rows + EXTRA, PAIR),
            "token": (1, PAIR),
        }
        operands = [x for _, x in ins] + list(after)
        kinds = [kind for kind, _ in ins] + [f"after{x.ndim}" for x in after]
        aliases = {}
        for out_at, x in alias:
            if x is not None:
                aliases[prefetch + len(operands)] = out_at
                operands.append(x)
                kinds.append("any")
        out_shape = [
            pltpu.HBM(shapes[kind], dtype) if kind in ("block", "wide") else jax.ShapeDtypeStruct(shapes[kind], dtype)
            for kind, dtype in outs
        ]
        moved = sum(rows * 2 * lanes * 2 for kind in kinds if kind in ("wide", "block"))
        moved += sum(rows * 2 * lanes * 2 for kind, _ in outs if kind in ("wide", "block"))
        return pl.pallas_call(
            kernel,
            grid_spec=pltpu.PrefetchScalarGridSpec(
                num_scalar_prefetch=int(prefetch),
                grid=steps,
                in_specs=[specs[kind] for kind in kinds],
                out_specs=[specs[kind] for kind, _ in outs],
                scratch_shapes=scratch,
            ),
            out_shape=out_shape,
            input_output_aliases=aliases,
            compiler_params=pltpu.CompilerParams(vmem_limit_bytes=VMEM),
            cost_estimate=pl.CostEstimate(flops=int(micros * 1.15e9), bytes_accessed=moved, transcendentals=0),
        )(*([core] if prefetch else []), *operands)

    edges = [("seg", segment_ids), ("table", image_flags)]
    groups = range(GROUPS)

    def phase(pieces, towards, works):
        befores = chips_before([own for _, _, own in pieces], towards, works)
        return [to_cores(before, keep, received, towards) for before, (keep, received, _) in zip(befores, pieces)]

    pieces = []
    buffers = [pltpu.VMEM((2, rows, lanes), BF16)] * 2 + [pltpu.SemaphoreType.DMA((2, 2))]
    for g in groups:
        keep, send = call(
            functools.partial(states_kernel, g), g, [("hbm", in_hbm(k)), ("hbm", in_hbm(v))],
            [("half", F32), ("half", F32)], 1.2, scratch=buffers, steps=())
        pieces.append((keep, *within_chip(keep, send)))

    found = {}

    def early_work(g):
        def work(totals):
            if g == 0:
                found["nxt"], = call(
                    functools.partial(part_kernel, False), 0, [("wide", k), ("wide", v), *edges],
                    [("part", F32)], 2.0, after=totals, steps=(2 * GROUPS,), prefetch=False)
                totals = [found["nxt"]]
            found["local", g], token = call(
                local_kernel, g, [("wide", q), ("wide", k), ("wide", v), ("mask", mask)],
                [("block", F32), ("token", F32)], 2.3, after=totals)
            return token
        return work

    prefix = phase(pieces, 1, [early_work(g) for g in groups])
    nxt = shifted(found["nxt"], -1)

    output = dab = grad_q = grad_k = grad_v = None
    pieces, gsums = [], []
    for g in groups:
        output, dab, gsum, keep, send = call(
            norm_kernel, g,
            [("wide", q), ("wide", dy), ("block", found["local", g]), ("row", gain_row), *edges,
             ("half", prefix[g][0]), ("half", prefix[g][1]), ("part", nxt)],
            [("wide", BF16), ("wide", BF16), ("rowblock", F32), ("half", F32), ("half", F32)],
            3.0, after=[own for _, _, own in pieces], alias=[(0, output), (1, dab)])
        gsums.append(gsum)
        pieces.append((keep, *within_chip(keep, send)))

    def late_work(g):
        def work(totals):
            if g == 0:
                found["prv"], = call(
                    functools.partial(part_kernel, True), 0, [("wide", q), ("wide", dab), *edges],
                    [("part", F32)], 2.0, after=totals, steps=(2 * GROUPS,), prefetch=False)
                totals = [found["prv"]]
            found["gq"], gk, gv, token = call(
                inner_kernel, g,
                [("wide", q), ("wide", k), ("wide", v), ("wide", dab), ("mask", mask), ("mask", mask_t), *edges,
                 ("half", prefix[g][0]), ("half", prefix[g][1]), ("part", nxt)],
                [("wide", BF16), ("block", F32), ("block", F32), ("token", F32)],
                5.5, after=totals, alias=[(0, found.get("gq"))])
            found["inner", g] = gk, gv
            return token
        return work

    suffix = phase(pieces, -1, [late_work(g) for g in groups])
    prv = shifted(found["prv"], 1)
    grad_q = found["gq"]
    grad_gain = scatter_sum(jnp.concatenate(gsums, axis=1))
    for g in groups:
        gk, gv = found["inner", g]
        grad_k, grad_v = call(
            outer_kernel, g,
            [("wide", k), ("wide", v), ("block", gk), ("block", gv), *edges,
             ("half", suffix[g][0]), ("half", suffix[g][1]), ("part", prv)],
            [("wide", BF16), ("wide", BF16)],
            2.1, alias=[(0, grad_k), (1, grad_v)])
    return output[None], grad_q[None], grad_k[None], grad_v[None], grad_gain


def solution(mesh):
    return jax.shard_map(
        on_device,
        mesh=mesh,
        in_specs=(
            P("dp", "ctx", None),
            P("dp", "ctx", None),
            P("dp", "ctx", None),
            P("dp", "ctx", None),
            P("dp", "ctx"),
            P("dp", None),
            P(),
        ),
        out_specs=(
            P("dp", "ctx", None),
            P("dp", "ctx", None),
            P("dp", "ctx", None),
            P("dp", "ctx", None),
            P(("dp", "ctx")),
        ),
        check_vma=False,
    )
```

```python
import functools

import jax
import jax.numpy as jnp
from jax import lax
from jax.experimental import pallas as pl
from jax.experimental.pallas import tpu as pltpu
from jax.sharding import PartitionSpec as P

E = 64
PAIR = 2 * E
GROUPS = 2
EXTRA = 8
VMEM = 10 * 2**20
F32 = jnp.float32
BF16 = jnp.bfloat16


def dot(a, b, ca, cb):
    return lax.dot_general(a, b, (((ca,), (cb,)), ((), ())), preferred_element_type=F32)


def low_lanes(rows, cols):
    lane = lax.broadcasted_iota(jnp.int32, (rows, cols), 1)
    return lane % PAIR < E


def fold(product):
    return jnp.where(low_lanes(E, product.shape[1]), product[:E], product[E:])


def split(state):
    high = state.astype(BF16)
    return high, (state - high.astype(F32)).astype(BF16)


def spread(state):
    low = low_lanes(*state.shape)
    zero = jnp.zeros_like(state)
    return jnp.concatenate([jnp.where(low, state, zero), jnp.where(low, zero, state)], axis=0)


def heads_of(pair):
    low = low_lanes(*pair.shape)
    zero = jnp.zeros_like(pair)
    return jnp.where(low, pair, zero), jnp.where(low, zero, pair)


def twice(x):
    return jnp.concatenate([x, x], axis=1)


def pair_at(ref, p):
    return ref[:, p * PAIR:(p + 1) * PAIR]


def rows_of(value, p):
    return value[p * E:(p + 1) * E]


def state_pair(a, b):
    return fold(dot(a, b, 0, 0))


def edge(seg, table, last):
    row = seg[...]
    count = row.shape[1]
    own = row[:, count - 1:] if last else row[:, :1]
    size = jnp.sum((row == own).astype(F32), axis=1, keepdims=True)
    at = lax.broadcasted_iota(jnp.int32, (count, PAIR), 0).astype(F32)
    rows = at >= count - size if last else at < size
    ids = lax.broadcasted_iota(jnp.int32, table.shape, 1)
    flag = jnp.sum(jnp.where(ids == own, table[...], 0).astype(F32), axis=1, keepdims=True)
    return rows, own.astype(F32), flag


def states_kernel(group, core, k, v, *rest):
    keep, send, k_buf, v_buf, sems = rest[-5:]
    lanes = k_buf.shape[2]
    copies = []
    for half in (1, 0):
        at = pl.multiple_of((2 * group + (half + core[0]) % 2) * lanes, lanes)
        for i, (array, buf) in enumerate(((k, k_buf), (v, v_buf))):
            copies.append(pltpu.make_async_copy(array.at[:, pl.ds(at, lanes)], buf.at[half], sems.at[half, i]))
    for copy in copies:
        copy.start()
    for half, out in ((1, send), (0, keep)):
        copies.pop(0).wait()
        copies.pop(0).wait()
        for p in range(lanes // PAIR):
            at = slice(p * PAIR, (p + 1) * PAIR)
            out[p * E:(p + 1) * E] = state_pair(k_buf[half, :, at], v_buf[half, :, at])


def part_kernel(last, a, b, seg, table, *rest):
    out, token = rest[-2:]
    token[...] = jnp.zeros_like(token)
    count = a.shape[1] // PAIR
    rows, own, flag = edge(seg, table, last)
    sel = rows.astype(F32) * jnp.where(flag == 1, 1.0, 0.0) if last else rows.astype(F32)
    sel = sel.astype(BF16)
    for p in range(count):
        out[0, p * E:(p + 1) * E] = state_pair(pair_at(a, p), pair_at(b, p) * sel)
    out[0, count * E:] = jnp.broadcast_to(own, (EXTRA, PAIR))


def local_kernel(core, q, k, v, mask, *rest):
    attn, token = rest[-2:]
    m = mask[...]
    token[...] = jnp.zeros_like(token)
    for p in range(q.shape[1] // PAIR):
        kp = pair_at(k, p)
        total = None
        for qh, vh in zip(heads_of(pair_at(q, p)), heads_of(pair_at(v, p))):
            prob = dot(qh, kp, 1, 1).astype(BF16) * m
            term = dot(prob, vh, 1, 0)
            total = term if total is None else total + term
        attn[:, p * PAIR:(p + 1) * PAIR] = total


def head_mean(x):
    high, low = split(x)
    ones = spread(jnp.full((E, PAIR), 1.0 / E, BF16))
    return dot(jnp.concatenate([high, low], axis=1), jnp.concatenate([ones, ones], axis=0), 1, 0)


def side_by_side(state, part):
    sh, sl = split(state)
    ph, pll = split(part)
    left = jnp.concatenate([spread(sh), spread(sl)], axis=0)
    right = jnp.concatenate([spread(ph), spread(pll)], axis=0)
    return jnp.concatenate([left, right], axis=1)


def stacked(state, part):
    sh, sl = split(state)
    ph, pll = split(part)
    top = jnp.concatenate([spread(sh), spread(sl)], axis=1)
    bottom = jnp.concatenate([spread(ph), spread(pll)], axis=1)
    return jnp.concatenate([top, bottom], axis=0)


def on_rows(seg, table, last, part, count):
    rows, own, flag = edge(seg, table, last)
    met = part[0, count * E:count * E + 1] == own
    if last:
        met = met & (flag == 1)
    return rows.astype(F32) * met.astype(F32)


def norm_kernel(core, q, dy, local, gain, seg, table, pre_keep, pre_recv, nxt, *rest):
    out, dab, gsum, keep, send = rest[-5:]
    step = pl.program_id(0)
    count = q.shape[1] // PAIR
    prefix = jnp.where(step == 0, pre_keep[...], pre_recv[...])
    on_next = on_rows(seg, table, True, nxt, count)
    pairs = [slice(p * PAIR, (p + 1) * PAIR) for p in range(count)]
    fars = [
        dot(twice(q[:, at]), side_by_side(rows_of(prefix, p), nxt[0, p * E:(p + 1) * E]), 1, 0)
        for p, at in enumerate(pairs)
    ]
    attns = [local[:, at] + far[:, :PAIR] + on_next * far[:, PAIR:] for at, far in zip(pairs, fars)]
    squares = [head_mean(attn * attn) for attn in attns]
    scales = [lax.rsqrt(square + 1e-06) for square in squares]
    normeds = [attn * scale for attn, scale in zip(attns, scales)]
    gas = [dy[:, at].astype(F32) * gain[:, at] for at in pairs]
    means = [head_mean(ga * normed) for ga, normed in zip(gas, normeds)]
    das = [
        (scale * (ga - normed * mean)).astype(BF16)
        for scale, ga, normed, mean in zip(scales, gas, normeds, means)
    ]
    states = [state_pair(q[:, at], da) for at, da in zip(pairs, das)]
    for at, normed, da in zip(pairs, normeds, das):
        dab[:, at] = da
        out[:, at] = (normed * gain[:, at]).astype(BF16)
        gsum[:, at] = jnp.sum(dy[:, at].astype(F32) * normed, axis=0, keepdims=True)

    @pl.when(step == 0)
    def _():
        for p, state in enumerate(states):
            keep[p * E:(p + 1) * E] = state

    @pl.when(step == 1)
    def _():
        for p, state in enumerate(states):
            send[p * E:(p + 1) * E] = state


def inner_kernel(core, q, k, v, dab, mask, mask_t, seg, table, pre_keep, pre_recv, nxt, *rest):
    gq, gk, gv, token = rest[-4:]
    step = pl.program_id(0)
    count = q.shape[1] // PAIR
    m, mt = mask[...], mask_t[...]
    token[...] = jnp.zeros_like(token)
    prefix = jnp.where(step == 0, pre_keep[...], pre_recv[...])
    on_next = on_rows(seg, table, True, nxt, count)
    for p in range(count):
        lanes = slice(p * PAIR, (p + 1) * PAIR)
        da = dab[:, lanes]
        kp, vp = k[:, lanes], v[:, lanes]
        far = dot(twice(da), stacked(rows_of(prefix, p), nxt[0, p * E:(p + 1) * E]), 1, 1)
        tq = far[:, :PAIR] + on_next * far[:, PAIR:]
        tk = tv = None
        for qh, kh, dh in zip(heads_of(q[:, lanes]), heads_of(kp), heads_of(da)):
            dprob = dot(dh, vp, 1, 1).astype(BF16) * m
            prob_t = dot(kp, qh, 1, 1).astype(BF16) * mt
            tq = tq + dot(dprob, kh, 1, 0)
            a = dot(dprob, qh, 0, 0)
            b = dot(prob_t, dh, 1, 0)
            tk = a if tk is None else tk + a
            tv = b if tv is None else tv + b
        gq[:, lanes] = tq.astype(BF16)
        gk[:, lanes] = tk
        gv[:, lanes] = tv


def outer_kernel(core, k, v, gk_in, gv_in, seg, table, suf_keep, suf_recv, prv, *rest):
    gk, gv = rest[-2:]
    step = pl.program_id(0)
    count = k.shape[1] // PAIR
    suffix = jnp.where(step == 0, suf_keep[...], suf_recv[...])
    on_prev = on_rows(seg, table, False, prv, count)
    for p in range(count):
        lanes = slice(p * PAIR, (p + 1) * PAIR)
        s = rows_of(suffix, p)
        g = prv[0, p * E:(p + 1) * E]
        far = dot(twice(v[:, lanes]), stacked(s, g), 1, 1)
        gk[:, lanes] = (gk_in[:, lanes] + far[:, :PAIR] + on_prev * far[:, PAIR:]).astype(BF16)
        far = dot(twice(k[:, lanes]), side_by_side(s, g), 1, 0)
        gv[:, lanes] = (gv_in[:, lanes] + far[:, :PAIR] + on_prev * far[:, PAIR:]).astype(BF16)


def partner(x, axis, bit):
    route = [(i, i ^ (1 << bit)) for i in range(lax.axis_size(axis))]
    return lax.ppermute(x, axis, route)


def shifted(x, distance):
    count = lax.axis_size("ctx")
    return lax.ppermute(x, "ctx", [(i, i + distance) for i in range(count) if 0 <= i + distance < count])


def chips_before(owns, towards, works):
    chips = lax.axis_size("ctx") // 2
    if chips > 8:
        for work in works:
            work(owns)
        totals = [shifted(own, 2 * towards) for own in owns]
        span = 1
        while span < chips:
            totals = [total + shifted(total, 2 * towards * span) for total in totals]
            span *= 2
        return totals
    befores = [None] * len(owns)
    for hop in range(max(chips - 1, len(works))):
        totals = [own if before is None else own + before for own, before in zip(owns, befores)]
        source = hop if towards == 1 else chips - 1 - hop
        token = works[hop](totals) if hop < len(works) else jnp.zeros((1, PAIR), F32)
        if hop < chips - 1:
            target = source + towards
            mate = {source: target, target: source}
            route = [(2 * z + c, 2 * mate.get(z, z) + c) for z in range(chips) for c in range(2)]
            is_target = lax.axis_index("ctx") // 2 == target
            arrived = [jnp.where(is_target, lax.ppermute(total, "ctx", route), 0.0) + token for total in totals]
            befores = [a if before is None else before + a for before, a in zip(befores, arrived)]
    return befores


def within_chip(keep, send):
    received = partner(send, "ctx", 0)
    return received, keep + received


def to_cores(before, keep, received, towards):
    is_source = lax.axis_index("ctx") & 1 == (0 if towards == 1 else 1)
    mine = jnp.where(is_source, before, before + received)
    return mine, partner(jnp.where(is_source, before + keep, before), "ctx", 0)


def in_hbm(x):
    return pltpu.with_memory_space_constraint(x, pltpu.HBM)


def scatter_sum(x, token):
    axes = ("dp", "ctx")
    devices = lax.axis_size("dp") * lax.axis_size("ctx")
    x = x.reshape(devices, -1)
    terms = lax.all_to_all(x + token[:, :x.shape[1]], axes, 0, 0, tiled=True)
    return jnp.sum(terms, axis=0)


def on_device(queries, keys, values, out_grad, segment_ids, image_flags, gain):
    rows, width = queries.shape[1:]
    q, k, v, dy = (x[0] for x in (queries, keys, values, out_grad))
    seg = segment_ids[0]
    table = image_flags[0]
    gain_row = gain.reshape(1, width)
    core = (lax.axis_index("ctx") & 1).reshape(1).astype(jnp.int32)
    onehot = seg[:, None] == jnp.arange(table.shape[0], dtype=jnp.int32)[None, :]
    img = jnp.sum(jnp.where(onehot, table[None, :], 0), axis=1)
    imgseg = jnp.where(img == 1, seg, -1)
    pos = jnp.arange(rows)
    mask = ((pos[:, None] >= pos[None, :]) | (imgseg[:, None] == seg[None, :])).astype(BF16)
    mask_t = ((pos[:, None] <= pos[None, :]) | (seg[:, None] == imgseg[None, :])).astype(BF16)

    lanes = width // GROUPS // 2
    half_rows = lanes // PAIR * E
    heads = lanes // E

    def call(kernel, group, ins, outs, micros, after=(), alias=(), scratch=(), steps=(2,), prefetch=True):
        def at(i, c=None):
            return (i + c[0]) % 2 if prefetch else i

        def wide(*args):
            return (0, 2 * group + at(*args))

        def own(*args):
            return (0, at(*args))

        def whole(*args):
            return (0, 0)

        def part(*args):
            return (2 * group + at(*args), 0, 0)

        specs = {
            "wide": pl.BlockSpec((rows, lanes), wide),
            "block": pl.BlockSpec((rows, lanes), own),
            "row": pl.BlockSpec((1, lanes), wide),
            "rowblock": pl.BlockSpec((1, lanes), own),
            "half": pl.BlockSpec((half_rows, PAIR), whole),
            "part": pl.BlockSpec((1, half_rows + EXTRA, PAIR), part),
            "seg": pl.BlockSpec((1, rows), whole),
            "table": pl.BlockSpec((1, table.shape[0]), whole),
            "mask": pl.BlockSpec((rows, rows), whole),
            "token": pl.BlockSpec((1, PAIR), whole),
            "after2": pl.BlockSpec((8, PAIR), whole),
            "after3": pl.BlockSpec((1, 8, PAIR), lambda *args: (0, 0, 0)),
            "any": pl.BlockSpec(memory_space=pl.ANY),
            "hbm": pl.BlockSpec(memory_space=pltpu.HBM),
        }
        shapes = {
            "wide": (rows, width),
            "block": (rows, 2 * lanes),
            "rowblock": (1, 2 * lanes),
            "half": (half_rows, PAIR),
            "part": (2 * GROUPS, half_rows + EXTRA, PAIR),
            "token": (1, PAIR),
        }
        operands = [x for _, x in ins] + list(after)
        kinds = [kind for kind, _ in ins] + [f"after{x.ndim}" for x in after]
        aliases = {}
        for out_at, x in alias:
            if x is not None:
                aliases[prefetch + len(operands)] = out_at
                operands.append(x)
                kinds.append("any")
        out_shape = [
            pltpu.HBM(shapes[kind], dtype) if kind in ("block", "wide") else jax.ShapeDtypeStruct(shapes[kind], dtype)
            for kind, dtype in outs
        ]
        moved = sum(rows * 2 * lanes * 2 for kind in kinds if kind in ("wide", "block"))
        moved += sum(rows * 2 * lanes * 2 for kind, _ in outs if kind in ("wide", "block"))
        return pl.pallas_call(
            kernel,
            grid_spec=pltpu.PrefetchScalarGridSpec(
                num_scalar_prefetch=int(prefetch),
                grid=steps,
                in_specs=[specs[kind] for kind in kinds],
                out_specs=[specs[kind] for kind, _ in outs],
                scratch_shapes=scratch,
            ),
            out_shape=out_shape,
            input_output_aliases=aliases,
            compiler_params=pltpu.CompilerParams(vmem_limit_bytes=VMEM),
            cost_estimate=pl.CostEstimate(flops=int(micros * 1.15e9), bytes_accessed=moved, transcendentals=0),
        )(*([core] if prefetch else []), *operands)

    edges = [("seg", segment_ids), ("table", image_flags)]
    groups = range(GROUPS)

    def phase(pieces, towards, works):
        befores = chips_before([own for _, _, own in pieces], towards, works)
        return [to_cores(before, keep, received, towards) for before, (keep, received, _) in zip(befores, pieces)]

    pieces = []
    buffers = [pltpu.VMEM((2, rows, lanes), BF16)] * 2 + [pltpu.SemaphoreType.DMA((2, 2))]
    for g in groups:
        keep, send = call(
            functools.partial(states_kernel, g), g, [("hbm", in_hbm(k)), ("hbm", in_hbm(v))],
            [("half", F32), ("half", F32)], 1.2, scratch=buffers, steps=())
        pieces.append((keep, *within_chip(keep, send)))

    found = {}

    def early_parts(totals):
        found["nxt"], token = call(
            functools.partial(part_kernel, False), 0, [("wide", k), ("wide", v), *edges],
            [("part", F32), ("token", F32)], 2.0, after=totals, steps=(2 * GROUPS,), prefetch=False)
        return token

    def local_of(g):
        def work(totals):
            found["local", g], token = call(
                local_kernel, g, [("wide", q), ("wide", k), ("wide", v), ("mask", mask)],
                [("block", F32), ("token", F32)], 2.3, after=totals)
            return token
        return work

    prefix = phase(pieces, 1, [early_parts, *map(local_of, groups)])
    nxt = shifted(found["nxt"], -1)

    output = dab = grad_q = grad_k = grad_v = None
    pieces, gsums = [], []
    for g in groups:
        output, dab, gsum, keep, send = call(
            norm_kernel, g,
            [("wide", q), ("wide", dy), ("block", found["local", g]), ("row", gain_row), *edges,
             ("half", prefix[g][0]), ("half", prefix[g][1]), ("part", nxt)],
            [("wide", BF16), ("wide", BF16), ("rowblock", F32), ("half", F32), ("half", F32)],
            3.0, after=[own for _, _, own in pieces], alias=[(0, output), (1, dab)])
        gsums.append(gsum)
        pieces.append((keep, *within_chip(keep, send)))

    def late_parts(totals):
        found["prv"], token = call(
            functools.partial(part_kernel, True), 0, [("wide", q), ("wide", dab), *edges],
            [("part", F32), ("token", F32)], 2.0, after=totals, steps=(2 * GROUPS,), prefetch=False)
        return token

    def inner_of(g):
        def work(totals):
            found["gq"], gk, gv, token = call(
                inner_kernel, g,
                [("wide", q), ("wide", k), ("wide", v), ("wide", dab), ("mask", mask), ("mask", mask_t), *edges,
                 ("half", prefix[g][0]), ("half", prefix[g][1]), ("part", nxt)],
                [("wide", BF16), ("block", F32), ("block", F32), ("token", F32)],
                5.5, after=totals, alias=[(0, found.get("gq"))])
            found["inner", g] = gk, gv
            found["token"] = token
            return token
        return work

    suffix = phase(pieces, -1, [late_parts, *map(inner_of, groups)])
    prv = shifted(found["prv"], 1)
    grad_q = found["gq"]
    grad_gain = scatter_sum(jnp.concatenate(gsums, axis=1), found["token"])
    for g in groups:
        gk, gv = found["inner", g]
        grad_k, grad_v = call(
            outer_kernel, g,
            [("wide", k), ("wide", v), ("block", gk), ("block", gv), *edges,
             ("half", suffix[g][0]), ("half", suffix[g][1]), ("part", prv)],
            [("wide", BF16), ("wide", BF16)],
            2.1, alias=[(0, grad_k), (1, grad_v)])
    return output[None], grad_q[None], grad_k[None], grad_v[None], grad_gain


def solution(mesh):
    return jax.shard_map(
        on_device,
        mesh=mesh,
        in_specs=(
            P("dp", "ctx", None),
            P("dp", "ctx", None),
            P("dp", "ctx", None),
            P("dp", "ctx", None),
            P("dp", "ctx"),
            P("dp", None),
            P(),
        ),
        out_specs=(
            P("dp", "ctx", None),
            P("dp", "ctx", None),
            P("dp", "ctx", None),
            P("dp", "ctx", None),
            P(("dp", "ctx")),
        ),
        check_vma=False,
    )
```

```python
import functools

import jax
import jax.numpy as jnp
from jax import lax
from jax.experimental import pallas as pl
from jax.experimental.pallas import tpu as pltpu
from jax.sharding import PartitionSpec as P

E = 64
PAIR = 2 * E
GROUPS = 2
EXTRA = 8
VMEM = 10 * 2**20
PINNED = ("block", "wide", "part")
F32 = jnp.float32
BF16 = jnp.bfloat16


def dot(a, b, ca, cb):
    return lax.dot_general(a, b, (((ca,), (cb,)), ((), ())), preferred_element_type=F32)


def low_lanes(rows, cols):
    lane = lax.broadcasted_iota(jnp.int32, (rows, cols), 1)
    return lane % PAIR < E


def fold(product):
    return jnp.where(low_lanes(E, product.shape[1]), product[:E], product[E:])


def split(state):
    high = state.astype(BF16)
    return high, (state - high.astype(F32)).astype(BF16)


def spread(state):
    low = low_lanes(*state.shape)
    zero = jnp.zeros_like(state)
    return jnp.concatenate([jnp.where(low, state, zero), jnp.where(low, zero, state)], axis=0)


def heads_of(pair):
    low = low_lanes(*pair.shape)
    zero = jnp.zeros_like(pair)
    return jnp.where(low, pair, zero), jnp.where(low, zero, pair)


def twice(x):
    return jnp.concatenate([x, x], axis=1)


def pair_at(ref, p):
    return ref[:, p * PAIR:(p + 1) * PAIR]


def rows_of(value, p):
    return value[p * E:(p + 1) * E]


def state_pair(a, b):
    return fold(dot(a, b, 0, 0))


def edge(seg, table, last):
    row = seg[...]
    count = row.shape[1]
    own = row[:, count - 1:] if last else row[:, :1]
    size = jnp.sum((row == own).astype(F32), axis=1, keepdims=True)
    at = lax.broadcasted_iota(jnp.int32, (count, PAIR), 0).astype(F32)
    rows = at >= count - size if last else at < size
    ids = lax.broadcasted_iota(jnp.int32, table.shape, 1)
    flag = jnp.sum(jnp.where(ids == own, table[...], 0).astype(F32), axis=1, keepdims=True)
    return rows, own.astype(F32), flag


def states_kernel(group, core, k, v, *rest):
    keep, send, zero, k_buf, v_buf, sems = rest[-6:]
    lanes = k_buf.shape[2]
    copies = []
    for half in (1, 0):
        at = pl.multiple_of((2 * group + (half + core[0]) % 2) * lanes, lanes)
        for i, (array, buf) in enumerate(((k, k_buf), (v, v_buf))):
            copies.append(pltpu.make_async_copy(array.at[:, pl.ds(at, lanes)], buf.at[half], sems.at[half, i]))
    for copy in copies:
        copy.start()
    zero[...] = jnp.zeros_like(zero)
    for half, out in ((1, send), (0, keep)):
        copies.pop(0).wait()
        copies.pop(0).wait()
        for p in range(lanes // PAIR):
            at = slice(p * PAIR, (p + 1) * PAIR)
            out[p * E:(p + 1) * E] = state_pair(k_buf[half, :, at], v_buf[half, :, at])


def part_kernel(a, b, seg, table, *rest):
    out, token = rest[-2:]
    token[...] = jnp.zeros_like(token)
    count = a.shape[1] // PAIR
    rows, own, _ = edge(seg, table, False)
    sel = rows.astype(BF16)
    for p in range(count):
        out[0, p * E:(p + 1) * E] = state_pair(pair_at(a, p), pair_at(b, p) * sel)
    out[0, count * E:] = jnp.broadcast_to(own, (EXTRA, PAIR))


def local_kernel(core, q, k, v, mask, *rest):
    attn, token = rest[-2:]
    m = mask[...]
    token[...] = jnp.zeros_like(token)
    for p in range(q.shape[1] // PAIR):
        kp = pair_at(k, p)
        total = None
        for qh, vh in zip(heads_of(pair_at(q, p)), heads_of(pair_at(v, p))):
            prob = dot(qh, kp, 1, 1).astype(BF16) * m
            term = dot(prob, vh, 1, 0)
            total = term if total is None else total + term
        attn[:, p * PAIR:(p + 1) * PAIR] = total


def head_mean(x):
    high, low = split(x)
    ones = spread(jnp.full((E, PAIR), 1.0 / E, BF16))
    return dot(jnp.concatenate([high, low], axis=1), jnp.concatenate([ones, ones], axis=0), 1, 0)


def side_by_side(state, part):
    sh, sl = split(state)
    ph, pll = split(part)
    left = jnp.concatenate([spread(sh), spread(sl)], axis=0)
    right = jnp.concatenate([spread(ph), spread(pll)], axis=0)
    return jnp.concatenate([left, right], axis=1)


def stacked(state, part):
    sh, sl = split(state)
    ph, pll = split(part)
    top = jnp.concatenate([spread(sh), spread(sl)], axis=1)
    bottom = jnp.concatenate([spread(ph), spread(pll)], axis=1)
    return jnp.concatenate([top, bottom], axis=0)


def on_rows(seg, table, last, part, count):
    rows, own, flag = edge(seg, table, last)
    met = part[0, count * E:count * E + 1] == own
    if last:
        met = met & (flag == 1)
    return rows.astype(F32) * met.astype(F32)


def norm_kernel(core, q, dy, local, gain, seg, table, pre_keep, pre_recv, nxt, *rest):
    out, dab, part, gsum, keep, send = rest[-6:]
    step = pl.program_id(0)
    count = q.shape[1] // PAIR
    prefix = jnp.where(step == 0, pre_keep[...], pre_recv[...])
    on_next = on_rows(seg, table, True, nxt, count)
    last, own, flag = edge(seg, table, True)
    last = (last.astype(F32) * jnp.where(flag == 1, 1.0, 0.0)).astype(BF16)
    pairs = [slice(p * PAIR, (p + 1) * PAIR) for p in range(count)]
    fars = [
        dot(twice(q[:, at]), side_by_side(rows_of(prefix, p), nxt[0, p * E:(p + 1) * E]), 1, 0)
        for p, at in enumerate(pairs)
    ]
    attns = [local[:, at] + far[:, :PAIR] + on_next * far[:, PAIR:] for at, far in zip(pairs, fars)]
    squares = [head_mean(attn * attn) for attn in attns]
    scales = [lax.rsqrt(square + 1e-06) for square in squares]
    normeds = [attn * scale for attn, scale in zip(attns, scales)]
    gas = [dy[:, at].astype(F32) * gain[:, at] for at in pairs]
    means = [head_mean(ga * normed) for ga, normed in zip(gas, normeds)]
    das = [
        (scale * (ga - normed * mean)).astype(BF16)
        for scale, ga, normed, mean in zip(scales, gas, normeds, means)
    ]
    states = [state_pair(q[:, at], jnp.concatenate([da, da * last], axis=1)) for at, da in zip(pairs, das)]
    part[0, count * E:] = jnp.broadcast_to(own, (EXTRA, PAIR))
    for p, (at, normed, da) in enumerate(zip(pairs, normeds, das)):
        part[0, p * E:(p + 1) * E] = states[p][:, PAIR:]
        dab[:, at] = da
        out[:, at] = (normed * gain[:, at]).astype(BF16)
        gsum[0, p:p + 1] = jnp.sum(dy[:, at].astype(F32) * normed, axis=0, keepdims=True)

    @pl.when(step == 0)
    def _():
        for p, state in enumerate(states):
            keep[p * E:(p + 1) * E] = state[:, :PAIR]

    @pl.when(step == 1)
    def _():
        for p, state in enumerate(states):
            send[p * E:(p + 1) * E] = state[:, :PAIR]


def inner_kernel(core, q, k, v, dab, mask, mask_t, seg, table, pre_keep, pre_recv, nxt, *rest):
    gq, gk, gv, token = rest[-4:]
    step = pl.program_id(0)
    count = q.shape[1] // PAIR
    m, mt = mask[...], mask_t[...]
    token[...] = jnp.zeros_like(token)
    prefix = jnp.where(step == 0, pre_keep[...], pre_recv[...])
    on_next = on_rows(seg, table, True, nxt, count)
    for p in range(count):
        lanes = slice(p * PAIR, (p + 1) * PAIR)
        da = dab[:, lanes]
        kp, vp = k[:, lanes], v[:, lanes]
        far = dot(twice(da), stacked(rows_of(prefix, p), nxt[0, p * E:(p + 1) * E]), 1, 1)
        tq = far[:, :PAIR] + on_next * far[:, PAIR:]
        tk = tv = None
        for qh, kh, dh in zip(heads_of(q[:, lanes]), heads_of(kp), heads_of(da)):
            dprob = dot(dh, vp, 1, 1).astype(BF16) * m
            prob_t = dot(kp, qh, 1, 1).astype(BF16) * mt
            tq = tq + dot(dprob, kh, 1, 0)
            a = dot(dprob, qh, 0, 0)
            b = dot(prob_t, dh, 1, 0)
            tk = a if tk is None else tk + a
            tv = b if tv is None else tv + b
        gq[:, lanes] = tq.astype(BF16)
        gk[:, lanes] = tk
        gv[:, lanes] = tv


def outer_kernel(core, k, v, gk_in, gv_in, seg, table, suf_keep, suf_recv, prv, *rest):
    gk, gv, token = rest[-3:]
    token[...] = jnp.zeros_like(token)
    step = pl.program_id(0)
    count = k.shape[1] // PAIR
    suffix = jnp.where(step == 0, suf_keep[...], suf_recv[...])
    on_prev = on_rows(seg, table, False, prv, count)
    for p in range(count):
        lanes = slice(p * PAIR, (p + 1) * PAIR)
        s = rows_of(suffix, p)
        g = prv[0, p * E:(p + 1) * E]
        far = dot(twice(v[:, lanes]), stacked(s, g), 1, 1)
        gk[:, lanes] = (gk_in[:, lanes] + far[:, :PAIR] + on_prev * far[:, PAIR:]).astype(BF16)
        far = dot(twice(k[:, lanes]), side_by_side(s, g), 1, 0)
        gv[:, lanes] = (gv_in[:, lanes] + far[:, :PAIR] + on_prev * far[:, PAIR:]).astype(BF16)


def partner(x, axis, bit):
    route = [(i, i ^ (1 << bit)) for i in range(lax.axis_size(axis))]
    return lax.ppermute(x, axis, route)


def shifted(x, distance):
    count = lax.axis_size("ctx")
    return lax.ppermute(x, "ctx", [(i, i + distance) for i in range(count) if 0 <= i + distance < count])


def chip_rank(towards):
    chip = lax.axis_index("ctx") // 2
    return chip if towards == 1 else lax.axis_size("ctx") // 2 - 1 - chip


def chips_before(own, towards):
    chips = lax.axis_size("ctx") // 2
    total = shifted(own, 2 * towards)
    span = 1
    while span < chips:
        total = total + shifted(total, 2 * towards * span)
        span *= 2
    return total


def pick(rank, cases):
    value = cases[-1][1]
    for at, case in cases[:-1]:
        value = jnp.where(rank == at, case, value)
    return value


def chain_load(owns, arrived, step, towards):
    chips = lax.axis_size("ctx") // 2
    cases = [(step - g, own) for g, own in enumerate(owns) if 0 <= step - g <= chips - 2]
    load = pick(chip_rank(towards), cases)
    return load if arrived is None else load + arrived


def chain_step(load, step, towards):
    chips = lax.axis_size("ctx") // 2
    route = []
    for rank in range(chips - 1):
        if 0 <= step - rank < GROUPS:
            chip = rank if towards == 1 else chips - 1 - rank
            route += [(2 * chip + c, 2 * (chip + towards) + c) for c in range(2)]
    return lax.ppermute(load, "ctx", route)


def chain_result(arrivals, group, towards):
    chips = lax.axis_size("ctx") // 2
    cases = [(rank, arrivals[group + rank - 1]) for rank in range(1, chips)]
    return pick(chip_rank(towards), cases + [(0, jnp.zeros_like(arrivals[0]))])


def within_chip(keep, send):
    received = partner(send, "ctx", 0)
    return keep, received, keep + received


def to_cores(before, piece, towards):
    keep, received, _ = piece
    is_source = lax.axis_index("ctx") & 1 == (0 if towards == 1 else 1)
    mine = jnp.where(is_source, before, before + received)
    return mine, partner(jnp.where(is_source, before + keep, before), "ctx", 0)


def in_hbm(x):
    return pltpu.with_memory_space_constraint(x, pltpu.HBM)


def scatter_sum(x, axis):
    for bit in reversed(range(lax.axis_size(axis).bit_length() - 1)):
        upper = lax.axis_index(axis) >> bit & 1 == 1
        low, high = jnp.split(x, 2, axis=0 if x.shape[0] > 1 else 1)
        x = jnp.where(upper, high, low) + partner(jnp.where(upper, low, high), axis, bit)
    return x


def on_device(queries, keys, values, out_grad, segment_ids, image_flags, gain):
    rows, width = queries.shape[1:]
    q, k, v, dy = (x[0] for x in (queries, keys, values, out_grad))
    table = image_flags[0]
    gain_row = gain.reshape(1, width)
    core = (lax.axis_index("ctx") & 1).reshape(1).astype(jnp.int32)
    lanes = width // GROUPS // 2
    half_rows = lanes // PAIR * E
    heads = lanes // E

    def call(kernel, group, ins, outs, micros, after=(), alias=(), scratch=(), steps=(2,), prefetch=True):
        def at(i, c=None):
            return (i + c[0]) % 2 if prefetch else i

        def wide(*args):
            return (0, 2 * group + at(*args))

        def own(*args):
            return (0, at(*args))

        def whole(*args):
            return (0, 0)

        def part(*args):
            return (2 * group + at(*args), 0, 0)

        specs = {
            "wide": pl.BlockSpec((rows, lanes), wide),
            "block": pl.BlockSpec((rows, lanes), own),
            "row": pl.BlockSpec((1, lanes), wide),
            "sums": pl.BlockSpec((1, lanes // PAIR, PAIR), part),
            "zero": pl.BlockSpec((1, rows), whole),
            "half": pl.BlockSpec((half_rows, PAIR), whole),
            "part": pl.BlockSpec((1, half_rows + EXTRA, PAIR), part),
            "seg": pl.BlockSpec((1, rows), whole),
            "table": pl.BlockSpec((1, table.shape[0]), whole),
            "mask": pl.BlockSpec((rows, rows), whole),
            "token": pl.BlockSpec((1, PAIR), whole),
            "after2": pl.BlockSpec((8, PAIR), whole),
            "after3": pl.BlockSpec((1, 8, PAIR), lambda *args: (0, 0, 0)),
            "any": pl.BlockSpec(memory_space=pl.ANY),
            "hbm": pl.BlockSpec(memory_space=pltpu.HBM),
        }
        shapes = {
            "wide": (rows, width),
            "block": (rows, 2 * lanes),
            "sums": (2 * GROUPS, lanes // PAIR, PAIR),
            "zero": (1, rows),
            "half": (half_rows, PAIR),
            "part": (2 * GROUPS, half_rows + EXTRA, PAIR),
            "token": (1, PAIR),
        }
        operands = [x for _, x in ins] + list(after)
        kinds = [kind for kind, _ in ins] + [f"after{x.ndim}" for x in after]
        aliases = {}
        for out_at, x in alias:
            if x is not None:
                aliases[prefetch + len(operands)] = out_at
                operands.append(x)
                kinds.append("any")
        out_shape = [
            pltpu.HBM(shapes[kind], dtype) if kind in PINNED and (kind != "block" or len(outs) == 2) else jax.ShapeDtypeStruct(shapes[kind], dtype)
            for kind, dtype in outs
        ]
        moved = sum(rows * 2 * lanes * 2 for kind in kinds if kind in ("wide", "block"))
        moved += sum(rows * 2 * lanes * 2 for kind, _ in outs if kind in ("wide", "block"))
        return pl.pallas_call(
            kernel,
            grid_spec=pltpu.PrefetchScalarGridSpec(
                num_scalar_prefetch=int(prefetch),
                grid=steps,
                in_specs=[specs[kind] for kind in kinds],
                out_specs=[specs[kind] for kind, _ in outs],
                scratch_shapes=scratch,
            ),
            out_shape=out_shape,
            input_output_aliases=aliases,
            compiler_params=pltpu.CompilerParams(vmem_limit_bytes=VMEM),
            cost_estimate=pl.CostEstimate(flops=int(micros * 1.15e9), bytes_accessed=moved, transcendentals=0),
        )(*([core] if prefetch else []), *operands)

    edges = [("seg", segment_ids), ("table", image_flags)]
    groups = range(GROUPS)
    chips = lax.axis_size("ctx") // 2
    chained = GROUPS < chips <= 8
    buffers = [pltpu.VMEM((2, rows, lanes), BF16)] * 2 + [pltpu.SemaphoreType.DMA((2, 2))]

    def own_states(g, after):
        keep, send, zero = call(
            functools.partial(states_kernel, g), g, [("hbm", in_hbm(k)), ("hbm", in_hbm(v))],
            [("half", F32), ("half", F32), ("zero", jnp.int32)], 1.2, after=after, scratch=buffers, steps=(1,))
        return within_chip(keep, send), zero

    def local_attn(g, after):
        return call(
            local_kernel, g, [("wide", q), ("wide", k), ("wide", v), ("mask", mask)],
            [("block", F32), ("token", F32)], 2.3, after=after)

    def norm(g, prefix, before, after):
        output, dab, prv, gsum, keep, send = call(
            norm_kernel, g,
            [("wide", q), ("wide", dy), ("block", local[g][0]), ("row", gain_row), *edges,
             ("half", prefix[0]), ("half", prefix[1]), ("part", nxt)],
            [("wide", BF16), ("wide", BF16), ("part", F32), ("sums", F32), ("half", F32), ("half", F32)],
            3.0, after=after, alias=list(enumerate(before)))
        return (output, dab, prv, gsum), within_chip(keep, send)

    def inner(g, before, after):
        return call(
            inner_kernel, g,
            [("wide", q), ("wide", k), ("wide", v), ("wide", in_hbm(dab)), ("mask", mask), ("mask", mask_t), *edges,
             ("half", prefix[g][0]), ("half", prefix[g][1]), ("part", nxt)],
            [("wide", BF16), ("block", F32), ("block", F32), ("token", F32)], 6.0, after=after, alias=[(0, before)])

    def outer(g, suffix, before, after):
        return call(
            outer_kernel, g,
            [("wide", k), ("wide", v), ("block", inners[g][1]), ("block", inners[g][2]), *edges,
             ("half", suffix[0]), ("half", suffix[1]), ("part", prv)],
            [("wide", BF16), ("wide", BF16), ("token", F32)], 2.1, after=after, alias=list(enumerate(before)))

    steps = chips - 2 + GROUPS
    owns, arrivals, local, prefix = [], [], [], []
    piece, zero = own_states(0, [])
    owns.append(piece)
    for g in groups[1:]:
        piece, zero = own_states(g, [owns[0][2]])
        owns.append(piece)
    seg = (segment_ids + zero)[0]
    onehot = seg[:, None] == jnp.arange(table.shape[0], dtype=jnp.int32)[None, :]
    img = jnp.sum(jnp.where(onehot, table[None, :], 0), axis=1)
    imgseg = jnp.where(img == 1, seg, -1)
    pos = jnp.arange(rows)
    mask = ((pos[:, None] >= pos[None, :]) | (imgseg[:, None] == seg[None, :])).astype(BF16)
    mask_t = ((pos[:, None] <= pos[None, :]) | (seg[:, None] == imgseg[None, :])).astype(BF16)
    sums = [piece[2] for piece in owns]
    load = chain_load(sums, None, 0, 1) if chained else sums[0]
    local.append(local_attn(0, [load, sums[-1]]))
    token = local[0][1]
    nexts = None
    for step in range(steps if chained else GROUPS):
        if chained:
            arrivals.append(chain_step(load, step, 1))
        if step + 1 < steps and chained:
            load = chain_load(sums, arrivals[-1] + token, step + 1, 1)
        if step == 0:
            nexts, token = call(
                part_kernel, 0, [("wide", k), ("wide", v), *edges],
                [("part", F32), ("token", F32)], 2.0, after=[load], steps=(2 * GROUPS,), prefetch=False)
            nxt = shifted(nexts, -1)
        elif step < GROUPS:
            local.append(local_attn(step, [load, nexts]))
            token = local[step][1]
        else:
            token = jnp.zeros((1, PAIR), F32)
    befores = [chain_result(arrivals, g, 1) if chained else chips_before(sums[g], 1) for g in groups]
    prefix = [to_cores(before, piece, 1) for before, piece in zip(befores, owns)]

    norms, owns, arrivals = [None] * 4, [], []
    for g in groups:
        norms, piece = norm(g, prefix[g], norms, [piece[2] for piece in owns])
        owns.append(piece)
    output, dab, prv, gsum = norms
    prv = shifted(prv, 1)
    sums = [piece[2] for piece in owns]
    inners, outers, suffix = [], [None] * 2, []
    token = None
    for step in range(steps if chained else GROUPS):
        if chained:
            arrived = arrivals[-1] if arrivals else None
            load = chain_load(sums, arrived if token is None else arrived + token, step, -1)
            arrivals.append(chain_step(load, step, -1))
        else:
            load = sums[-1]
        if 1 <= step <= GROUPS:
            inners.append(inner(step - 1, inners[-1][0] if inners else None, [load, norms[2]]))
            token = inners[-1][3]
    while len(inners) < GROUPS:
        inners.append(inner(len(inners), inners[-1][0] if inners else None, [load]))
    gain_sum = scatter_sum(gsum.reshape(-1, PAIR) + inners[0][3], "dp")
    grad_gain = scatter_sum(gain_sum + inners[-1][3], "ctx").reshape(-1)
    grad_q = inners[-1][0]
    for g in groups:
        if g and chained:
            arrivals[-1] = arrivals[-1] + token
        before = chain_result(arrivals, g, -1) if chained else chips_before(sums[g], -1)
        *outers, token = outer(g, to_cores(before, owns[g], -1), outers, [])
    grad_k, grad_v = outers
    return output[None], grad_q[None], grad_k[None], grad_v[None], grad_gain


def solution(mesh):
    return jax.shard_map(
        on_device,
        mesh=mesh,
        in_specs=(
            P("dp", "ctx", None),
            P("dp", "ctx", None),
            P("dp", "ctx", None),
            P("dp", "ctx", None),
            P("dp", "ctx"),
            P("dp", None),
            P(),
        ),
        out_specs=(
            P("dp", "ctx", None),
            P("dp", "ctx", None),
            P("dp", "ctx", None),
            P("dp", "ctx", None),
            P(("dp", "ctx")),
        ),
        check_vma=False,
    )
```

```python
import functools

import jax
import jax.numpy as jnp
from jax import lax
from jax.experimental import pallas as pl
from jax.experimental.pallas import tpu as pltpu
from jax.sharding import PartitionSpec as P

E = 64
PAIR = 2 * E
GROUPS = 2
EXTRA = 8
VMEM = 10 * 2**20
SUB = 2
PINNED = ("block", "wide")
F32 = jnp.float32
BF16 = jnp.bfloat16


def dot(a, b, ca, cb):
    return lax.dot_general(a, b, (((ca,), (cb,)), ((), ())), preferred_element_type=F32)


def low_lanes(rows, cols):
    lane = lax.broadcasted_iota(jnp.int32, (rows, cols), 1)
    return lane % PAIR < E


def fold(product):
    return jnp.where(low_lanes(E, product.shape[1]), product[:E], product[E:])


def split(state):
    high = state.astype(BF16)
    return high, (state - high.astype(F32)).astype(BF16)


def spread(state):
    low = low_lanes(*state.shape)
    zero = jnp.zeros_like(state)
    return jnp.concatenate([jnp.where(low, state, zero), jnp.where(low, zero, state)], axis=0)


def heads_of(pair):
    low = low_lanes(*pair.shape)
    zero = jnp.zeros_like(pair)
    return jnp.where(low, pair, zero), jnp.where(low, zero, pair)


def twice(x):
    return jnp.concatenate([x, x], axis=1)


def pair_at(ref, p):
    return ref[:, p * PAIR:(p + 1) * PAIR]


def rows_at(p):
    return pl.ds(pl.multiple_of(p * E, E), E)


def own_or_received(keep, received, own, p):
    return jnp.where(own, keep[rows_at(p)], received[rows_at(p)])


def state_pair(a, b):
    return fold(dot(a, b, 0, 0))


def edge(seg, table, last):
    row = seg[...]
    count = row.shape[1]
    own = row[:, count - 1:] if last else row[:, :1]
    size = jnp.sum((row == own).astype(F32), axis=1, keepdims=True)
    at = lax.broadcasted_iota(jnp.int32, (count, PAIR), 0).astype(F32)
    rows = at >= count - size if last else at < size
    ids = lax.broadcasted_iota(jnp.int32, table.shape, 1)
    flag = jnp.sum(jnp.where(ids == own, table[...], 0).astype(F32), axis=1, keepdims=True)
    return rows, own.astype(F32), flag


def states_kernel(core, k, v, *rest):
    keep, send, zero, k_buf, v_buf, sems = rest[-6:]
    lanes = k_buf.shape[2]
    count = lanes // PAIR
    copies = []
    for half in (1, 0):
        for group in range(GROUPS):
            at = pl.multiple_of((2 * group + (half + core[0]) % 2) * lanes, lanes)
            slot = 2 * group + half
            for i, (array, buf) in enumerate(((k, k_buf), (v, v_buf))):
                copies.append(pltpu.make_async_copy(array.at[:, pl.ds(at, lanes)], buf.at[slot], sems.at[slot, i]))
    for copy in copies:
        copy.start()
    zero[...] = jnp.zeros_like(zero)
    for half, out in ((1, send), (0, keep)):
        for group in range(GROUPS):
            copies.pop(0).wait()
            copies.pop(0).wait()
            for p in range(count):
                at = slice(p * PAIR, (p + 1) * PAIR)
                row = (group * count + p) * E
                out[row:row + E] = state_pair(k_buf[2 * group + half, :, at], v_buf[2 * group + half, :, at])


def part_kernel(a, b, seg, table, *rest):
    out, token = rest[-2:]
    token[...] = jnp.zeros_like(token)
    count = a.shape[1] // PAIR
    rows, own, _ = edge(seg, table, False)
    sel = rows.astype(BF16)
    for p in range(count):
        out[0, p * E:(p + 1) * E] = state_pair(pair_at(a, p), pair_at(b, p) * sel)
    out[0, count * E:] = jnp.broadcast_to(own, (EXTRA, PAIR))


def local_kernel(core, q, k, v, mask, *rest):
    attn, token = rest[-2:]
    m = mask[...]
    token[...] = jnp.zeros_like(token)
    for p in range(q.shape[1] // PAIR):
        kp = pair_at(k, p)
        total = None
        for qh, vh in zip(heads_of(pair_at(q, p)), heads_of(pair_at(v, p))):
            prob = dot(qh, kp, 1, 1).astype(BF16) * m
            term = dot(prob, vh, 1, 0)
            total = term if total is None else total + term
        attn[:, p * PAIR:(p + 1) * PAIR] = total


def head_mean(x):
    high, low = split(x)
    ones = spread(jnp.full((E, PAIR), 1.0 / E, BF16))
    return dot(jnp.concatenate([high, low], axis=1), jnp.concatenate([ones, ones], axis=0), 1, 0)


def side_by_side(state, part):
    sh, sl = split(state)
    ph, pll = split(part)
    left = jnp.concatenate([spread(sh), spread(sl)], axis=0)
    right = jnp.concatenate([spread(ph), spread(pll)], axis=0)
    return jnp.concatenate([left, right], axis=1)


def stacked(state, part):
    sh, sl = split(state)
    ph, pll = split(part)
    top = jnp.concatenate([spread(sh), spread(sl)], axis=1)
    bottom = jnp.concatenate([spread(ph), spread(pll)], axis=1)
    return jnp.concatenate([top, bottom], axis=0)


def on_rows(seg, table, last, part):
    rows, own, flag = edge(seg, table, last)
    met = part[0, part.shape[1] - EXTRA:part.shape[1] - EXTRA + 1] == own
    if last:
        met = met & (flag == 1)
    return rows.astype(F32) * met.astype(F32)


def norm_kernel(core, q, dy, local, gain, seg, table, pre_keep, pre_recv, nxt, *rest):
    out, dab, part, gsum, keep, send, token = rest[-7:]
    token[...] = jnp.zeros_like(token)
    step = pl.program_id(0)
    count = q.shape[1] // PAIR
    on_next = on_rows(seg, table, True, nxt)
    last, own, flag = edge(seg, table, True)
    last = (last.astype(F32) * jnp.where(flag == 1, 1.0, 0.0)).astype(BF16)
    pairs = [slice(p * PAIR, (p + 1) * PAIR) for p in range(count)]
    fars = [
        dot(twice(q[:, at]), side_by_side(own_or_received(pre_keep, pre_recv, step == 0, p), nxt[0, rows_at(p)]), 1, 0)
        for p, at in enumerate(pairs)
    ]
    attns = [local[:, at] + far[:, :PAIR] + on_next * far[:, PAIR:] for at, far in zip(pairs, fars)]
    squares = [head_mean(attn * attn) for attn in attns]
    scales = [lax.rsqrt(square + 1e-06) for square in squares]
    normeds = [attn * scale for attn, scale in zip(attns, scales)]
    gas = [dy[:, at].astype(F32) * gain[:, at] for at in pairs]
    means = [head_mean(ga * normed) for ga, normed in zip(gas, normeds)]
    das = [
        (scale * (ga - normed * mean)).astype(BF16)
        for scale, ga, normed, mean in zip(scales, gas, normeds, means)
    ]
    states = [state_pair(q[:, at], jnp.concatenate([da, da * last], axis=1)) for at, da in zip(pairs, das)]
    part[0, count * E:] = jnp.broadcast_to(own, (EXTRA, PAIR))
    for p, (at, normed, da) in enumerate(zip(pairs, normeds, das)):
        part[0, p * E:(p + 1) * E] = states[p][:, PAIR:]
        dab[:, at] = da
        out[:, at] = (normed * gain[:, at]).astype(BF16)
        gsum[0, p:p + 1] = jnp.sum(dy[:, at].astype(F32) * normed, axis=0, keepdims=True)

    @pl.when(step == 0)
    def _():
        for p, state in enumerate(states):
            keep[p * E:(p + 1) * E] = state[:, :PAIR]

    @pl.when(step == 1)
    def _():
        for p, state in enumerate(states):
            send[p * E:(p + 1) * E] = state[:, :PAIR]


def inner_kernel(core, q, k, v, dab, mask, mask_t, seg, table, pre_keep, pre_recv, nxt, *rest):
    gq, gk, gv, token = rest[-4:]
    step = pl.program_id(0)
    count = q.shape[1] // PAIR
    m, mt = mask[...], mask_t[...]
    token[...] = jnp.zeros_like(token)
    on_next = on_rows(seg, table, True, nxt)
    for p in range(count):
        at = step % SUB * count + p
        lanes = slice(p * PAIR, (p + 1) * PAIR)
        da = dab[:, lanes]
        kp, vp = k[:, lanes], v[:, lanes]
        far = dot(twice(da), stacked(own_or_received(pre_keep, pre_recv, step < SUB, at), nxt[0, rows_at(at)]), 1, 1)
        tq = far[:, :PAIR] + on_next * far[:, PAIR:]
        tk = tv = None
        for qh, kh, dh in zip(heads_of(q[:, lanes]), heads_of(kp), heads_of(da)):
            dprob = dot(dh, vp, 1, 1).astype(BF16) * m
            prob_t = dot(kp, qh, 1, 1).astype(BF16) * mt
            tq = tq + dot(dprob, kh, 1, 0)
            a = dot(dprob, qh, 0, 0)
            b = dot(prob_t, dh, 1, 0)
            tk = a if tk is None else tk + a
            tv = b if tv is None else tv + b
        gq[:, lanes] = tq.astype(BF16)
        gk[:, lanes] = tk
        gv[:, lanes] = tv


def outer_kernel(core, k, v, gk_in, gv_in, seg, table, suf_keep, suf_recv, prv, *rest):
    gk, gv, token = rest[-3:]
    token[...] = jnp.zeros_like(token)
    step = pl.program_id(0)
    count = k.shape[1] // PAIR
    on_prev = on_rows(seg, table, False, prv)
    for p in range(count):
        lanes = slice(p * PAIR, (p + 1) * PAIR)
        at = step % SUB * count + p
        s = own_or_received(suf_keep, suf_recv, step < SUB, at)
        g = prv[0, rows_at(at)]
        far = dot(twice(v[:, lanes]), stacked(s, g), 1, 1)
        gk[:, lanes] = (gk_in[:, lanes] + far[:, :PAIR] + on_prev * far[:, PAIR:]).astype(BF16)
        far = dot(twice(k[:, lanes]), side_by_side(s, g), 1, 0)
        gv[:, lanes] = (gv_in[:, lanes] + far[:, :PAIR] + on_prev * far[:, PAIR:]).astype(BF16)


def partner(x, axis, bit):
    route = [(i, i ^ (1 << bit)) for i in range(lax.axis_size(axis))]
    return lax.ppermute(x, axis, route)


def shifted(x, distance):
    count = lax.axis_size("ctx")
    return lax.ppermute(x, "ctx", [(i, i + distance) for i in range(count) if 0 <= i + distance < count])


def nought(x):
    return jnp.minimum(jnp.abs(x), 0.0)


def chip_rank(towards):
    chip = lax.axis_index("ctx") // 2
    return chip if towards == 1 else lax.axis_size("ctx") // 2 - 1 - chip


def chips_before(own, towards):
    chips = lax.axis_size("ctx") // 2
    total = shifted(own, 2 * towards)
    span = 1
    while span < chips:
        total = total + shifted(total, 2 * towards * span)
        span *= 2
    return total


def pick(rank, cases):
    value = cases[-1][1]
    for at, case in cases[:-1]:
        value = jnp.where(rank == at, case, value)
    return value


def chain_load(owns, arrived, step, towards):
    chips = lax.axis_size("ctx") // 2
    cases = [(step - g, own) for g, own in enumerate(owns) if 0 <= step - g <= chips - 2]
    load = pick(chip_rank(towards), cases)
    return load if arrived is None else load + arrived


def chain_step(load, step, towards):
    chips = lax.axis_size("ctx") // 2
    route = []
    for rank in range(chips - 1):
        if 0 <= step - rank < GROUPS:
            chip = rank if towards == 1 else chips - 1 - rank
            route += [(2 * chip + c, 2 * (chip + towards) + c) for c in range(2)]
    return lax.ppermute(load, "ctx", route)


def chain_result(arrivals, group, towards):
    chips = lax.axis_size("ctx") // 2
    cases = [(rank, arrivals[group + rank - 1]) for rank in range(1, chips)]
    return pick(chip_rank(towards), cases + [(0, jnp.zeros_like(arrivals[0]))])


def within_chip(keep, send):
    received = partner(send, "ctx", 0)
    return keep, received, keep + received


def to_cores(before, piece, towards):
    keep, received, _ = piece
    is_source = lax.axis_index("ctx") & 1 == (0 if towards == 1 else 1)
    mine = jnp.where(is_source, before, before + received)
    return mine, partner(jnp.where(is_source, before + keep, before), "ctx", 0)


def in_hbm(x):
    return pltpu.with_memory_space_constraint(x, pltpu.HBM)


def scatter_step(x, axis, bit):
    upper = lax.axis_index(axis) >> bit & 1 == 1
    low, high = jnp.split(x, 2, axis=0 if x.shape[0] > 1 else 1)
    return jnp.where(upper, high, low) + partner(jnp.where(upper, low, high), axis, bit)


def on_device(queries, keys, values, out_grad, segment_ids, image_flags, gain):
    rows, width = queries.shape[1:]
    q, k, v, dy = (x[0] for x in (queries, keys, values, out_grad))
    table = image_flags[0]
    gain_row = gain.reshape(1, width)
    core = (lax.axis_index("ctx") & 1).reshape(1).astype(jnp.int32)
    lanes = width // GROUPS // 2
    half_rows = lanes // PAIR * E
    heads = lanes // E

    def call(kernel, group, ins, outs, micros, after=(), alias=(), scratch=(), sub=1, prefetch=True, steps=None):
        def half_of(i, c=None):
            return (i // sub + c[0]) % 2 if prefetch else i // sub

        def wide(*args):
            return (0, (2 * group + half_of(*args)) * sub + args[0] % sub)

        def own(*args):
            return (0, half_of(*args) * sub + args[0] % sub)

        def whole(*args):
            return (0, 0)

        def part(*args):
            return (half_of(*args), 0, 0)

        specs = {
            "wide": pl.BlockSpec((rows, lanes // sub), wide),
            "block": pl.BlockSpec((rows, lanes // sub), own),
            "row": pl.BlockSpec((1, lanes // sub), wide),
            "sums": pl.BlockSpec((1, lanes // PAIR, PAIR), part),
            "zero": pl.BlockSpec((1, rows), whole),
            "half": pl.BlockSpec((half_rows, PAIR), whole),
            "all": pl.BlockSpec((GROUPS * half_rows, PAIR), whole),
            "part": pl.BlockSpec((1, half_rows + EXTRA, PAIR), part),
            "seg": pl.BlockSpec((1, rows), whole),
            "table": pl.BlockSpec((1, table.shape[0]), whole),
            "mask": pl.BlockSpec((rows, rows), whole),
            "token": pl.BlockSpec((1, PAIR), whole),
            "after2": pl.BlockSpec((8, PAIR), whole),
            "after3": pl.BlockSpec((1, 8, PAIR), lambda *args: (0, 0, 0)),
            "any": pl.BlockSpec(memory_space=pl.ANY),
            "hbm": pl.BlockSpec(memory_space=pltpu.HBM),
        }
        shapes = {
            "wide": (rows, width),
            "block": (rows, 2 * lanes),
            "sums": (2, lanes // PAIR, PAIR),
            "zero": (1, rows),
            "half": (half_rows, PAIR),
            "all": (GROUPS * half_rows, PAIR),
            "part": (2, half_rows + EXTRA, PAIR),
            "token": (1, PAIR),
        }
        operands = [in_hbm(x) if kind in PINNED else x for kind, x in ins] + list(after)
        kinds = [kind for kind, _ in ins] + [f"after{x.ndim}" for x in after]
        aliases = {}
        for out_at, x in alias:
            if x is not None:
                aliases[prefetch + len(operands)] = out_at
                operands.append(x)
                kinds.append("any")
        out_shape = [
            pltpu.HBM(shapes[kind], dtype) if kind in PINNED else jax.ShapeDtypeStruct(shapes[kind], dtype)
            for kind, dtype in outs
        ]
        moved = sum(rows * 2 * lanes * 2 for kind in kinds if kind in ("wide", "block"))
        moved += sum(rows * 2 * lanes * 2 for kind, _ in outs if kind in ("wide", "block"))
        return pl.pallas_call(
            kernel,
            grid_spec=pltpu.PrefetchScalarGridSpec(
                num_scalar_prefetch=int(prefetch),
                grid=steps or (2 * sub,),
                in_specs=[specs[kind] for kind in kinds],
                out_specs=[specs[kind] for kind, _ in outs],
                scratch_shapes=scratch,
            ),
            out_shape=out_shape,
            input_output_aliases=aliases,
            compiler_params=pltpu.CompilerParams(vmem_limit_bytes=VMEM),
            cost_estimate=pl.CostEstimate(flops=int(micros * 1.15e9), bytes_accessed=moved, transcendentals=0),
        )(*([core] if prefetch else []), *operands)

    edges = [("seg", segment_ids), ("table", image_flags)]
    groups = range(GROUPS)
    chips = lax.axis_size("ctx") // 2
    chained = GROUPS < chips <= 8

    def local_attn(g, after):
        return call(
            local_kernel, g, [("wide", q), ("wide", k), ("wide", v), ("mask", mask)],
            [("block", F32), ("token", F32)], 3.0, after=after, sub=SUB)

    def first_part(g, after):
        return call(
            part_kernel, g, [("wide", k), ("wide", v), *edges],
            [("part", F32), ("token", F32)], 1.3, after=after, prefetch=False)

    def norm(g, prefix, before, after):
        output, dab, prv, gsum, keep, send, token = call(
            norm_kernel, g,
            [("wide", q), ("wide", dy), ("block", local[g]), ("row", gain_row), *edges,
             ("half", prefix[0]), ("half", prefix[1]), ("part", nxt[g])],
            [("wide", BF16), ("wide", BF16), ("part", F32), ("sums", F32), ("half", F32), ("half", F32), ("token", F32)],
            3.9, after=after, alias=list(enumerate(before)))
        return (output, dab), prv, gsum, within_chip(keep, send), token

    def inner(g, before, after):
        return call(
            inner_kernel, g,
            [("wide", q), ("wide", k), ("wide", v), ("wide", dab), ("mask", mask), ("mask", mask_t), *edges,
             ("half", prefix[g][0]), ("half", prefix[g][1]), ("part", nxt[g])],
            [("wide", BF16), ("block", F32), ("block", F32), ("token", F32)],
            6.0, after=after, alias=[(0, before)], sub=SUB)

    def outer(g, suffix, before, after):
        return call(
            outer_kernel, g,
            [("wide", k), ("wide", v), ("block", inners[g][1]), ("block", inners[g][2]), *edges,
             ("half", suffix[0]), ("half", suffix[1]), ("part", prv[g])],
            [("wide", BF16), ("wide", BF16), ("token", F32)], 2.5, after=after, alias=list(enumerate(before)), sub=SUB)

    last = chips - 3 + GROUPS
    buffers = [pltpu.VMEM((2 * GROUPS, rows, lanes), BF16)] * 2 + [pltpu.SemaphoreType.DMA((2 * GROUPS, 2))]
    keep, send, zero = call(
        states_kernel, 0, [("hbm", in_hbm(k)), ("hbm", in_hbm(v))],
        [("all", F32), ("all", F32), ("zero", jnp.int32)], 3.0, scratch=buffers, steps=(1,))
    keep, received, total = within_chip(keep, send)
    owns = [tuple(x[g * half_rows:(g + 1) * half_rows] for x in (keep, received, total)) for g in groups]
    sums = [own for _, _, own in owns]
    seg = (segment_ids + zero)[0]
    onehot = seg[:, None] == jnp.arange(table.shape[0], dtype=jnp.int32)[None, :]
    img = jnp.sum(jnp.where(onehot, table[None, :], 0), axis=1)
    imgseg = jnp.where(img == 1, seg, -1)
    pos = jnp.arange(rows)
    mask = ((pos[:, None] >= pos[None, :]) | (imgseg[:, None] == seg[None, :])).astype(BF16)
    mask_t = ((pos[:, None] <= pos[None, :]) | (seg[:, None] == imgseg[None, :])).astype(BF16)

    local, nxt, arrivals = [], [], []
    load = sums[0]
    parts, tokens = zip(*[first_part(g, [load]) for g in groups])
    token = sum(tokens)
    for step in range(last + 1 if chained else GROUPS + 1):
        if chained:
            arrivals.append(chain_step(load, step, 1))
        if 1 <= step <= GROUPS:
            nxt.append(shifted(parts[step - 1], -1))
            attn, token = local_attn(step - 1, [load])
            local.append(attn)
            token = token + nought(nxt[-1][0, :1])
        if step < last and chained:
            load = chain_load(sums, arrivals[-1] + token, step + 1, 1)
    output, prefix, prv, gsums, pieces = [None] * 2, [], [], [], []
    for g in groups:
        if g and chained:
            arrivals[-1] = arrivals[-1] + token
        before = chain_result(arrivals, g, 1) if chained else chips_before(sums[g], 1)
        prefix.append(to_cores(before, owns[g], 1))
        output, part, gsum, piece, token = norm(g, prefix[g], output, [load])
        prv.append(part)
        gsums.append(gsum)
        pieces.append(piece)
    output, dab = output

    owns = pieces
    sums = [own for _, _, own in owns]
    arrivals, inners, outers = [], [], [None] * 2
    gain_sum = jnp.concatenate(gsums, axis=0).reshape(-1, PAIR)
    bits = [(axis, bit) for axis in ("dp", "ctx") for bit in reversed(range(lax.axis_size(axis).bit_length() - 1))]
    load, token = sums[0], None
    for step in range(last + 1 if chained else GROUPS + 1):
        if chained:
            if step:
                load = chain_load(sums, arrivals[-1] + token, step, -1)
            arrivals.append(chain_step(load, step, -1))
        token = None
        if bits and step < 4:
            gain_sum = scatter_step(gain_sum + nought(load[:1]), *bits.pop(0))
            token = nought(gain_sum[:1])
        if 1 <= step <= GROUPS:
            prv[step - 1] = shifted(prv[step - 1], 1)
            tie = nought(prv[step - 1][0, :1])
            token = tie if token is None else token + tie
        if step < GROUPS:
            inners.append(inner(step, inners[-1][0] if inners else None, [load, sums[-1]]))
            token = token + inners[-1][3]
    for g in groups:
        if g and chained:
            arrivals[-1] = arrivals[-1] + token
        before = chain_result(arrivals, g, -1) if chained else chips_before(sums[g], -1)
        *outers, done = outer(g, to_cores(before, owns[g], -1), outers, [load])
        token = done if token is None else token + done
    for axis, bit in bits:
        gain_sum = scatter_step(gain_sum, axis, bit)
    grad_q = inners[-1][0]
    grad_k, grad_v = outers
    grad_gain = gain_sum.reshape(-1)
    return output[None], grad_q[None], grad_k[None], grad_v[None], grad_gain


def solution(mesh):
    return jax.shard_map(
        on_device,
        mesh=mesh,
        in_specs=(
            P("dp", "ctx", None),
            P("dp", "ctx", None),
            P("dp", "ctx", None),
            P("dp", "ctx", None),
            P("dp", "ctx"),
            P("dp", None),
            P(),
        ),
        out_specs=(
            P("dp", "ctx", None),
            P("dp", "ctx", None),
            P("dp", "ctx", None),
            P("dp", "ctx", None),
            P(("dp", "ctx")),
        ),
        check_vma=False,
    )
```

```python
import functools

import jax
import jax.numpy as jnp
from jax import lax
from jax.experimental import pallas as pl
from jax.experimental.pallas import tpu as pltpu
from jax.sharding import PartitionSpec as P

E = 64
PAIR = 2 * E
GROUPS = 2
EXTRA = 8
VMEM = 10 * 2**20
SUB = 2
F32 = jnp.float32
BF16 = jnp.bfloat16


def dot(a, b, ca, cb):
    return lax.dot_general(a, b, (((ca,), (cb,)), ((), ())), preferred_element_type=F32)


def low_lanes(rows, cols):
    lane = lax.broadcasted_iota(jnp.int32, (rows, cols), 1)
    return lane % PAIR < E


def fold(product):
    return jnp.where(low_lanes(E, product.shape[1]), product[:E], product[E:])


def split(state):
    high = state.astype(BF16)
    return high, (state - high.astype(F32)).astype(BF16)


def spread(state):
    low = low_lanes(*state.shape)
    zero = jnp.zeros_like(state)
    return jnp.concatenate([jnp.where(low, state, zero), jnp.where(low, zero, state)], axis=0)


def heads_of(pair):
    low = low_lanes(*pair.shape)
    zero = jnp.zeros_like(pair)
    return jnp.where(low, pair, zero), jnp.where(low, zero, pair)


def twice(x):
    return jnp.concatenate([x, x], axis=1)


def pair_at(ref, p):
    return ref[:, p * PAIR:(p + 1) * PAIR]


def rows_at(p):
    return pl.ds(pl.multiple_of(p * E, E), E)


def own_or_received(keep, received, own, p):
    return jnp.where(own, keep[rows_at(p)], received[rows_at(p)])


def state_pair(a, b):
    return fold(dot(a, b, 0, 0))


def edge(seg, table, last):
    row = seg[...]
    count = row.shape[1]
    own = row[:, count - 1:] if last else row[:, :1]
    size = jnp.sum((row == own).astype(F32), axis=1, keepdims=True)
    at = lax.broadcasted_iota(jnp.int32, (count, PAIR), 0).astype(F32)
    rows = at >= count - size if last else at < size
    ids = lax.broadcasted_iota(jnp.int32, table.shape, 1)
    flag = jnp.sum(jnp.where(ids == own, table[...], 0).astype(F32), axis=1, keepdims=True)
    return rows, own.astype(F32), flag


def lanes_at(base, p):
    return pl.ds(pl.multiple_of(base + p * PAIR, PAIR), PAIR)


def place(group, core, lanes, sub):
    step = pl.program_id(0)
    half = (step // sub + core[0]) % 2
    base = half * lanes + step % sub * (lanes // sub)
    return half, base, 2 * group * lanes + base


def states_kernel(core, k_in, v_in, keep, send, zero, k, v, sems):
    lanes = k.shape[1] // GROUPS // 2
    count = lanes // PAIR
    copies = []
    for half in (1, 0):
        for group in range(GROUPS):
            slot = 2 * group + half
            at = pl.ds(pl.multiple_of((2 * group + (half + core[0]) % 2) * lanes, lanes), lanes)
            for i, (array, buf) in enumerate(((k_in, k), (v_in, v))):
                copies.append(pltpu.make_async_copy(array.at[:, at], buf.at[:, at], sems.at[slot, i]))
    for copy in copies:
        copy.start()
    zero[...] = jnp.zeros_like(zero)
    for half, out in ((1, send), (0, keep)):
        for group in range(GROUPS):
            copies.pop(0).wait()
            copies.pop(0).wait()
            base = (2 * group + (half + core[0]) % 2) * lanes
            for p in range(count):
                at = lanes_at(base, p)
                row = (group * count + p) * E
                out[row:row + E] = state_pair(k[:, at], v[:, at])


def part_kernel(q_in, dy_in, k, v, seg, table, *rest):
    *outs, q, dy, token, sems = rest[-GROUPS - 4:]
    copies = [pltpu.make_async_copy(a, b, sems.at[i]) for i, (a, b) in enumerate(((q_in, q), (dy_in, dy)))]
    for copy in copies:
        copy.start()
    token[...] = jnp.zeros_like(token)
    count = k.shape[1] // GROUPS // 2 // PAIR
    rows, own, _ = edge(seg, table, False)
    sel = rows.astype(BF16)
    for i in range(2 * GROUPS):
        out = outs[i // 2]
        for p in range(count):
            out[i % 2, p * E:(p + 1) * E] = state_pair(pair_at(k, i * count + p), pair_at(v, i * count + p) * sel)
        out[i % 2, count * E:] = jnp.broadcast_to(own, (EXTRA, PAIR))
    for copy in copies:
        copy.wait()


def local_kernel(group, core, q, k, v, mask, mask_t, *rest):
    attn, probs, token = rest[-3:]
    lanes = q.shape[1] // GROUPS // 2
    half, base, wide = place(group, core, lanes, 1)
    m, mt = mask[...], mask_t[...]
    token[...] = jnp.zeros_like(token)
    for p in range(lanes // PAIR):
        at = lanes_at(wide, p)
        kp = k[:, at]
        total = None
        for h, (qh, vh) in enumerate(zip(heads_of(q[:, at]), heads_of(v[:, at]))):
            prob = dot(qh, kp, 1, 1).astype(BF16) * m
            probs[half * (lanes // E) + 2 * p + h] = dot(kp, qh, 1, 1).astype(BF16) * mt
            term = dot(prob, vh, 1, 0)
            total = term if total is None else total + term
        attn[:, lanes_at(base, p)] = total


def head_mean(x):
    high, low = split(x)
    ones = spread(jnp.full((E, PAIR), 1.0 / E, BF16))
    return dot(jnp.concatenate([high, low], axis=1), jnp.concatenate([ones, ones], axis=0), 1, 0)


def side_by_side(state, part):
    sh, sl = split(state)
    ph, pll = split(part)
    left = jnp.concatenate([spread(sh), spread(sl)], axis=0)
    right = jnp.concatenate([spread(ph), spread(pll)], axis=0)
    return jnp.concatenate([left, right], axis=1)


def stacked(state, part):
    sh, sl = split(state)
    ph, pll = split(part)
    top = jnp.concatenate([spread(sh), spread(sl)], axis=1)
    bottom = jnp.concatenate([spread(ph), spread(pll)], axis=1)
    return jnp.concatenate([top, bottom], axis=0)


def on_rows(seg, table, last, part):
    rows, own, flag = edge(seg, table, last)
    met = part[0, part.shape[1] - EXTRA:part.shape[1] - EXTRA + 1] == own
    if last:
        met = met & (flag == 1)
    return rows.astype(F32) * met.astype(F32)


def norm_kernel(group, core, q, dy, local, gain, seg, table, pre_keep, pre_recv, nxt, *rest):
    out, dab, part, gsum, keep, send, token = rest[-7:]
    token[...] = jnp.zeros_like(token)
    step = pl.program_id(0)
    lanes = out.shape[1]
    count = lanes // PAIR
    _, base, wide = place(group, core, lanes, 1)
    on_next = on_rows(seg, table, True, nxt)
    last, own, flag = edge(seg, table, True)
    last = (last.astype(F32) * jnp.where(flag == 1, 1.0, 0.0)).astype(BF16)
    pairs = [slice(p * PAIR, (p + 1) * PAIR) for p in range(count)]
    bases = [lanes_at(base, p) for p in range(count)]
    wides = [lanes_at(wide, p) for p in range(count)]
    fars = [
        dot(twice(q[:, at]), side_by_side(own_or_received(pre_keep, pre_recv, step == 0, p), nxt[0, rows_at(p)]), 1, 0)
        for p, at in enumerate(wides)
    ]
    attns = [local[:, at] + far[:, :PAIR] + on_next * far[:, PAIR:] for at, far in zip(bases, fars)]
    squares = [head_mean(attn * attn) for attn in attns]
    scales = [lax.rsqrt(square + 1e-06) for square in squares]
    normeds = [attn * scale for attn, scale in zip(attns, scales)]
    gas = [dy[:, at].astype(F32) * gain[:, pair] for at, pair in zip(wides, pairs)]
    means = [head_mean(ga * normed) for ga, normed in zip(gas, normeds)]
    das = [
        (scale * (ga - normed * mean)).astype(BF16)
        for scale, ga, normed, mean in zip(scales, gas, normeds, means)
    ]
    states = [state_pair(q[:, at], jnp.concatenate([da, da * last], axis=1)) for at, da in zip(wides, das)]
    part[0, count * E:] = jnp.broadcast_to(own, (EXTRA, PAIR))
    for p, (at, normed, da) in enumerate(zip(pairs, normeds, das)):
        part[0, p * E:(p + 1) * E] = states[p][:, PAIR:]
        dab[:, bases[p]] = da
        out[:, at] = (normed * gain[:, at]).astype(BF16)
        gsum[0, p:p + 1] = jnp.sum(dy[:, wides[p]].astype(F32) * normed, axis=0, keepdims=True)

    @pl.when(step == 0)
    def _():
        for p, state in enumerate(states):
            keep[p * E:(p + 1) * E] = state[:, :PAIR]

    @pl.when(step == 1)
    def _():
        for p, state in enumerate(states):
            send[p * E:(p + 1) * E] = state[:, :PAIR]


def inner_kernel(group, core, q, k, v, dab, probs, mask, seg, table, pre_keep, pre_recv, nxt, *rest):
    gq, gk, gv, token = rest[-4:]
    step = pl.program_id(0)
    lanes = dab.shape[1] // 2
    count = lanes // SUB // PAIR
    half, base, wide = place(group, core, lanes, SUB)
    m = mask[...]
    token[...] = jnp.zeros_like(token)
    on_next = on_rows(seg, table, True, nxt)
    for p in range(count):
        in_half = step % SUB * count + p
        at = lanes_at(wide, p)
        da = dab[:, lanes_at(base, p)]
        vp = v[:, at]
        far = dot(
            twice(da),
            stacked(own_or_received(pre_keep, pre_recv, step < SUB, in_half), nxt[0, rows_at(in_half)]), 1, 1)
        tq = far[:, :PAIR] + on_next * far[:, PAIR:]
        tk = tv = None
        for h, (qh, kh, dh) in enumerate(zip(heads_of(q[:, at]), heads_of(k[:, at]), heads_of(da))):
            dprob = dot(dh, vp, 1, 1).astype(BF16) * m
            tq = tq + dot(dprob, kh, 1, 0)
            a = dot(dprob, qh, 0, 0)
            b = dot(probs[half * (lanes // E) + 2 * in_half + h], dh, 1, 0)
            tk = a if tk is None else tk + a
            tv = b if tv is None else tv + b
        gq[:, p * PAIR:(p + 1) * PAIR] = tq.astype(BF16)
        gk[:, lanes_at(base, p)] = tk
        gv[:, lanes_at(base, p)] = tv


def outer_kernel(group, core, k, v, gk_in, gv_in, seg, table, suf_keep, suf_recv, prv, *rest):
    gk, gv, token = rest[-3:]
    step = pl.program_id(0)
    lanes = gk_in.shape[1] // 2
    count = lanes // SUB // PAIR
    _, base, wide = place(group, core, lanes, SUB)
    token[...] = jnp.zeros_like(token)
    on_prev = on_rows(seg, table, False, prv)
    for p in range(count):
        in_half = step % SUB * count + p
        here, own, at = slice(p * PAIR, (p + 1) * PAIR), lanes_at(base, p), lanes_at(wide, p)
        s = own_or_received(suf_keep, suf_recv, step < SUB, in_half)
        g = prv[0, rows_at(in_half)]
        far = dot(twice(v[:, at]), stacked(s, g), 1, 1)
        gk[:, here] = (gk_in[:, own] + far[:, :PAIR] + on_prev * far[:, PAIR:]).astype(BF16)
        far = dot(twice(k[:, at]), side_by_side(s, g), 1, 0)
        gv[:, here] = (gv_in[:, own] + far[:, :PAIR] + on_prev * far[:, PAIR:]).astype(BF16)


def partner(x, axis, bit):
    route = [(i, i ^ (1 << bit)) for i in range(lax.axis_size(axis))]
    return lax.ppermute(x, axis, route)


def shifted(x, distance):
    count = lax.axis_size("ctx")
    return lax.ppermute(x, "ctx", [(i, i + distance) for i in range(count) if 0 <= i + distance < count])


def nought(x):
    return jnp.minimum(jnp.abs(x), 0.0)


def chip_rank(towards):
    chip = lax.axis_index("ctx") // 2
    return chip if towards == 1 else lax.axis_size("ctx") // 2 - 1 - chip


def chips_before(own, towards):
    chips = lax.axis_size("ctx") // 2
    total = shifted(own, 2 * towards)
    span = 1
    while span < chips:
        total = total + shifted(total, 2 * towards * span)
        span *= 2
    return total


def pick(rank, cases):
    value = cases[-1][1]
    for at, case in cases[:-1]:
        value = jnp.where(rank == at, case, value)
    return value


def chain_load(owns, starts, arrived, step, towards):
    chips = lax.axis_size("ctx") // 2
    cases = [(step - at, own) for own, at in zip(owns, starts) if 0 <= step - at <= chips - 2]
    load = pick(chip_rank(towards), cases)
    return load if arrived is None else load + arrived


def chain_step(load, starts, step, towards):
    chips = lax.axis_size("ctx") // 2
    route = []
    for rank in range(chips - 1):
        if step - rank in starts:
            chip = rank if towards == 1 else chips - 1 - rank
            route += [(2 * chip + c, 2 * (chip + towards) + c) for c in range(2)]
    return lax.ppermute(load, "ctx", route)


def chain_result(arrivals, start, towards):
    chips = lax.axis_size("ctx") // 2
    cases = [(rank, arrivals[start + rank - 1]) for rank in range(1, chips)]
    return pick(chip_rank(towards), cases + [(0, jnp.zeros_like(arrivals[0]))])


def within_chip(keep, send):
    received = partner(send, "ctx", 0)
    return keep, received, keep + received


def to_cores(before, piece, towards):
    keep, received, _ = piece
    is_source = lax.axis_index("ctx") & 1 == (0 if towards == 1 else 1)
    mine = jnp.where(is_source, before, before + received)
    return mine, partner(jnp.where(is_source, before + keep, before), "ctx", 0)


def pinned(x, space):
    return pltpu.with_memory_space_constraint(x, space)


def scatter_step(x, axis, bit):
    upper = lax.axis_index(axis) >> bit & 1 == 1
    low, high = jnp.split(x, 2, axis=0 if x.shape[0] > 1 else 1)
    return jnp.where(upper, high, low) + partner(jnp.where(upper, low, high), axis, bit)


def on_device(queries, keys, values, out_grad, segment_ids, image_flags, gain):
    rows, width = queries.shape[1:]
    q, k, v, dy = (x[0] for x in (queries, keys, values, out_grad))
    table = image_flags[0]
    gain_row = gain.reshape(1, width)
    core = (lax.axis_index("ctx") & 1).reshape(1).astype(jnp.int32)
    lanes = width // GROUPS // 2
    half_rows = lanes // PAIR * E
    heads = lanes // E

    def call(kernel, group, ins, outs, after=(), alias=(), scratch=(), sub=1, steps=None):
        def half_of(i, c):
            return (i // sub + c[0]) % 2

        def wide(i, c):
            return (0, (2 * group + half_of(i, c)) * sub + i % sub)

        def whole(*args):
            return (0, 0)

        def part(i, c):
            return (half_of(i, c), 0, 0)

        specs = {
            "vmem": pl.BlockSpec(memory_space=pltpu.VMEM),
            "hbm": pl.BlockSpec(memory_space=pltpu.HBM),
            "wide": pl.BlockSpec((rows, lanes // sub), wide),
            "row": pl.BlockSpec((1, lanes // sub), wide),
            "sums": pl.BlockSpec((1, lanes // PAIR, PAIR), part),
            "zero": pl.BlockSpec((1, rows), whole),
            "half": pl.BlockSpec((half_rows, PAIR), whole),
            "all": pl.BlockSpec((GROUPS * half_rows, PAIR), whole),
            "part": pl.BlockSpec((1, half_rows + EXTRA, PAIR), part),
            "parts": pl.BlockSpec((2, half_rows + EXTRA, PAIR), lambda *args: (0, 0, 0)),
            "seg": pl.BlockSpec((1, rows), whole),
            "table": pl.BlockSpec((1, table.shape[0]), whole),
            "mask": pl.BlockSpec((rows, rows), whole),
            "token": pl.BlockSpec((1, PAIR), whole),
            "after2": pl.BlockSpec((8, PAIR), whole),
            "after3": pl.BlockSpec((1, 8, PAIR), lambda *args: (0, 0, 0)),
            "any": pl.BlockSpec(memory_space=pl.ANY),
        }
        shapes = {
            "wide": (rows, width),
            "sums": (2, lanes // PAIR, PAIR),
            "zero": (1, rows),
            "half": (half_rows, PAIR),
            "all": (GROUPS * half_rows, PAIR),
            "part": (2, half_rows + EXTRA, PAIR),
            "parts": (2, half_rows + EXTRA, PAIR),
            "token": (1, PAIR),
        }
        spaces = {"vmem": pltpu.VMEM, "hbm": pltpu.HBM}
        operands = [pinned(x, spaces[kind]) if kind in spaces else x for kind, x in ins] + list(after)
        kinds = [kind for kind, _ in ins] + [f"after{x.ndim}" for x in after]
        aliases = {}
        for out_at, x in alias:
            if x is not None:
                aliases[1 + len(operands)] = out_at
                operands.append(x)
                kinds.append("any")
        out_shape = [
            pltpu.VMEM(*shape, dtype) if kind == "vmem" else jax.ShapeDtypeStruct(shapes[kind], dtype)
            for kind, dtype, *shape in outs
        ]
        return pl.pallas_call(
            kernel,
            grid_spec=pltpu.PrefetchScalarGridSpec(
                num_scalar_prefetch=1,
                grid=steps or (2 * sub,),
                in_specs=[specs[kind] for kind in kinds],
                out_specs=[specs[kind] for kind, *_ in outs],
                scratch_shapes=scratch,
            ),
            out_shape=out_shape,
            input_output_aliases=aliases,
            compiler_params=pltpu.CompilerParams(vmem_limit_bytes=VMEM),
            cost_estimate=pl.CostEstimate(flops=1, bytes_accessed=1, transcendentals=0),
        )(core, *operands)

    edges = [("seg", segment_ids), ("table", image_flags)]
    groups = range(GROUPS)
    chips = lax.axis_size("ctx") // 2
    chained = GROUPS < chips <= 8

    whole, group_of = (rows, width), (rows, 2 * lanes)

    def local_attn(g, after):
        return call(
            functools.partial(local_kernel, g), g,
            [("vmem", q), ("vmem", k), ("vmem", v), ("mask", mask), ("mask", mask_t)],
            [("vmem", F32, group_of), ("vmem", BF16, (2 * heads, rows, rows)), ("token", F32)], after=after)

    def norm(g, prefix, before, after):
        output, dab, prv, gsum, keep, send, token = call(
            functools.partial(norm_kernel, g), g,
            [("vmem", q), ("vmem", dy), ("vmem", local[g][0]), ("row", gain_row), *edges,
             ("half", prefix[0]), ("half", prefix[1]), ("part", nxt[g])],
            [("wide", BF16), ("vmem", BF16, group_of), ("part", F32), ("sums", F32), ("half", F32), ("half", F32),
             ("token", F32)],
            after=after, alias=[(0, before)])
        return output, dab, prv, gsum, (keep, send), token

    def inner(g, before, after):
        return call(
            functools.partial(inner_kernel, g), g,
            [("vmem", q), ("vmem", k), ("vmem", v), ("vmem", norms[g][1]), ("vmem", local[g][1]), ("mask", mask), *edges,
             ("half", prefix[g][0]), ("half", prefix[g][1]), ("part", nxt[g])],
            [("wide", BF16), ("vmem", F32, group_of), ("vmem", F32, group_of), ("token", F32)],
            after=after, alias=[(0, before)], sub=SUB)

    def outer(g, suffix, before, after):
        return call(
            functools.partial(outer_kernel, g), g,
            [("vmem", k), ("vmem", v), ("vmem", inners[g][1]), ("vmem", inners[g][2]), *edges,
             ("half", suffix[0]), ("half", suffix[1]), ("part", prv[g])],
            [("wide", BF16), ("wide", BF16), ("token", F32)], after=after, alias=list(enumerate(before)), sub=SUB)

    keep, send, zero, k, v = call(
        states_kernel, 0, [("hbm", k), ("hbm", v)],
        [("all", F32), ("all", F32), ("zero", jnp.int32), ("vmem", BF16, whole), ("vmem", BF16, whole)],
        scratch=[pltpu.SemaphoreType.DMA((2 * GROUPS, 2))], steps=(1,))
    keep, received, total = within_chip(keep, send)
    owns = [tuple(x[g * half_rows:(g + 1) * half_rows] for x in (keep, received, total)) for g in groups]
    sums = [own for _, _, own in owns]
    seg = (segment_ids + zero)[0]
    onehot = seg[:, None] == jnp.arange(table.shape[0], dtype=jnp.int32)[None, :]
    img = jnp.sum(jnp.where(onehot, table[None, :], 0), axis=1)
    imgseg = jnp.where(img == 1, seg, -1)
    pos = jnp.arange(rows)
    mask = ((pos[:, None] >= pos[None, :]) | (imgseg[:, None] == seg[None, :])).astype(BF16)
    mask_t = ((pos[:, None] <= pos[None, :]) | (seg[:, None] == imgseg[None, :])).astype(BF16)

    local, nxt, arrivals = [], [], []
    starts = list(groups)
    last = chips - 2 + starts[-1]
    load = sums[0]
    *parts, q, dy, token = call(
        lambda core, *refs: part_kernel(*refs), 0, [("hbm", q), ("hbm", dy), ("vmem", k), ("vmem", v), *edges],
        [("parts", F32)] * GROUPS + [("vmem", BF16, whole), ("vmem", BF16, whole), ("token", F32)],
        after=[load], scratch=[pltpu.SemaphoreType.DMA((2,))], steps=(1,))
    for step in range(last + 1 if chained else GROUPS + 1):
        if chained:
            arrivals.append(chain_step(load, starts, step, 1))
        if 1 <= step <= GROUPS:
            nxt.append(shifted(parts[step - 1], -1))
            *attn, token = local_attn(step - 1, [load])
            local.append(attn)
            token = token + nought(nxt[-1][0, :1])
        if step < last and chained:
            load = chain_load(sums, starts, arrivals[-1] + token, step + 1, 1)
    prefix, norms = [], []
    before = chain_result(arrivals, starts[0], 1) if chained else chips_before(sums[0], 1)
    prefix.append(to_cores(before, owns[0], 1))
    norms.append(norm(0, prefix[0], None, [load]))

    ins, ins_starts, ins_arrivals = owns, starts, arrivals
    owns = [within_chip(*norms[0][4])]
    sums = [owns[0][2]]
    load = sums[0]
    for g in groups[1:]:
        if chained:
            ins_arrivals[-1] = ins_arrivals[-1] + norms[-1][5]
        before = chain_result(ins_arrivals, ins_starts[g], 1) if chained else chips_before(ins[g][2], 1)
        prefix.append(to_cores(before, ins[g], 1))
        norms.append(norm(g, prefix[g], norms[-1][0], [load]))
        owns.append(within_chip(*norms[-1][4]))
        sums.append(owns[-1][2])
    output = norms[-1][0]
    prv = [n[2] for n in norms]
    gain_sum = jnp.concatenate([n[3] for n in norms], axis=0).reshape(-1, PAIR)
    bits = [(axis, bit) for axis in ("dp", "ctx") for bit in reversed(range(lax.axis_size(axis).bit_length() - 1))]
    arrivals, inners, outers = [], [], [None] * 2
    starts = [0] + [g + 1 for g in groups[1:]]
    last = chips - 2 + starts[-1]
    token = norms[-1][5]
    for step in range(last + 1 if chained else GROUPS + 1):
        if chained:
            if step:
                load = chain_load(sums, starts, arrivals[-1] + token, step, -1)
            arrivals.append(chain_step(load, starts, step, -1))
        if step == 0:
            prv[0] = shifted(prv[0], 1)
            token = token + nought(prv[0][0, :1])
            continue
        token = jnp.zeros((1, PAIR), F32)
        if 2 <= step and len(bits) > 2:
            gain_sum = scatter_step(gain_sum + nought(load[:1]), *bits.pop(0))
            token = token + nought(gain_sum[:1])
        if step == GROUPS + 1 or (not chained and step == 1):
            for g in groups[1:]:
                prv[g] = shifted(prv[g] + nought(load[:1]), 1)
                token = token + nought(prv[g][0, :1])
        if step <= GROUPS:
            inners.append(inner(step - 1, inners[-1][0] if inners else None, [load]))
            token = token + inners[-1][3]
    for g in groups:
        if g and chained:
            arrivals[-1] = arrivals[-1] + token
        before = chain_result(arrivals, starts[g], -1) if chained else chips_before(sums[g], -1)
        *outers, done = outer(g, to_cores(before, owns[g], -1), outers, [])
        token = token + done
    for axis, bit in bits:
        gain_sum = scatter_step(gain_sum, axis, bit)
    grad_q = inners[-1][0]
    grad_k, grad_v = outers
    grad_gain = gain_sum.reshape(-1)
    return output[None], grad_q[None], grad_k[None], grad_v[None], grad_gain


def solution(mesh):
    return jax.shard_map(
        on_device,
        mesh=mesh,
        in_specs=(
            P("dp", "ctx", None),
            P("dp", "ctx", None),
            P("dp", "ctx", None),
            P("dp", "ctx", None),
            P("dp", "ctx"),
            P("dp", None),
            P(),
        ),
        out_specs=(
            P("dp", "ctx", None),
            P("dp", "ctx", None),
            P("dp", "ctx", None),
            P("dp", "ctx", None),
            P(("dp", "ctx")),
        ),
        check_vma=False,
    )
```

```python
import functools

import jax
import jax.numpy as jnp
from jax import lax
from jax.experimental import pallas as pl
from jax.experimental.pallas import tpu as pltpu
from jax.sharding import PartitionSpec as P

E = 64
PAIR = 2 * E
GROUPS = 2
EXTRA = 8
VMEM = 10 * 2**20
SUB = 2
F32 = jnp.float32
BF16 = jnp.bfloat16


def dot(a, b, ca, cb):
    return lax.dot_general(a, b, (((ca,), (cb,)), ((), ())), preferred_element_type=F32)


def low_lanes(rows, cols):
    lane = lax.broadcasted_iota(jnp.int32, (rows, cols), 1)
    return lane % PAIR < E


def fold(product):
    return jnp.where(low_lanes(E, product.shape[1]), product[:E], product[E:])


def split(state):
    high = state.astype(BF16)
    return high, (state - high.astype(F32)).astype(BF16)


def spread(state):
    low = low_lanes(*state.shape)
    zero = jnp.zeros_like(state)
    return jnp.concatenate([jnp.where(low, state, zero), jnp.where(low, zero, state)], axis=0)


def heads_of(pair):
    low = low_lanes(*pair.shape)
    zero = jnp.zeros_like(pair)
    return jnp.where(low, pair, zero), jnp.where(low, zero, pair)


def twice(x):
    return jnp.concatenate([x, x], axis=1)


def pair_at(ref, p):
    return ref[:, p * PAIR:(p + 1) * PAIR]


def rows_at(p):
    return pl.ds(pl.multiple_of(p * E, E), E)


def own_or_received(keep, received, own, p):
    return jnp.where(own, keep[rows_at(p)], received[rows_at(p)])


def state_pair(a, b):
    return fold(dot(a, b, 0, 0))


def edge(seg, table, last):
    row = seg[...]
    count = row.shape[1]
    own = row[:, count - 1:] if last else row[:, :1]
    size = jnp.sum((row == own).astype(F32), axis=1, keepdims=True)
    at = lax.broadcasted_iota(jnp.int32, (count, PAIR), 0).astype(F32)
    rows = at >= count - size if last else at < size
    ids = lax.broadcasted_iota(jnp.int32, table.shape, 1)
    flag = jnp.sum(jnp.where(ids == own, table[...], 0).astype(F32), axis=1, keepdims=True)
    return rows, own.astype(F32), flag


def lanes_at(base, p):
    return pl.ds(pl.multiple_of(base + p * PAIR, PAIR), PAIR)


def place(group, core, lanes, sub):
    step = pl.program_id(0)
    half = (step // sub + core[0]) % 2
    base = half * lanes + step % sub * (lanes // sub)
    return half, base, 2 * group * lanes + base


def states_kernel(position, k_in, v_in, keep, send, zero, k, v, core_row, chip_row, ctx_row, dp_row, sems):
    core = position
    for i, row in enumerate((core_row, chip_row, ctx_row, dp_row)):
        row[...] = jnp.full(row.shape, position[i], jnp.int32)
    lanes = k.shape[1] // GROUPS // 2
    count = lanes // PAIR
    copies = []
    for half in (1, 0):
        for group in range(GROUPS):
            slot = 2 * group + half
            at = pl.ds(pl.multiple_of((2 * group + (half + core[0]) % 2) * lanes, lanes), lanes)
            for i, (array, buf) in enumerate(((k_in, k), (v_in, v))):
                copies.append(pltpu.make_async_copy(array.at[:, at], buf.at[:, at], sems.at[slot, i]))
    for copy in copies:
        copy.start()
    zero[...] = jnp.zeros_like(zero)
    for half, out in ((1, send), (0, keep)):
        for group in range(GROUPS):
            copies.pop(0).wait()
            copies.pop(0).wait()
            base = (2 * group + (half + core[0]) % 2) * lanes
            for p in range(count):
                at = lanes_at(base, p)
                row = (group * count + p) * E
                out[row:row + E] = state_pair(k[:, at], v[:, at])


def part_kernel(q_in, dy_in, k, v, seg, table, *rest):
    *outs, q, dy, token, sems = rest[-GROUPS - 4:]
    copies = [pltpu.make_async_copy(a, b, sems.at[i]) for i, (a, b) in enumerate(((q_in, q), (dy_in, dy)))]
    for copy in copies:
        copy.start()
    token[...] = jnp.zeros_like(token)
    count = k.shape[1] // GROUPS // 2 // PAIR
    rows, own, _ = edge(seg, table, False)
    sel = rows.astype(BF16)
    for i in range(2 * GROUPS):
        out = outs[i // 2]
        for p in range(count):
            out[i % 2, p * E:(p + 1) * E] = state_pair(pair_at(k, i * count + p), pair_at(v, i * count + p) * sel)
        out[i % 2, count * E:] = jnp.broadcast_to(own, (EXTRA, PAIR))
    for copy in copies:
        copy.wait()


def local_kernel(group, core, q, k, v, mask, mask_t, *rest):
    attn, probs, token = rest[-3:]
    lanes = q.shape[1] // GROUPS // 2
    half, base, wide = place(group, core, lanes, 1)
    m, mt = mask[...], mask_t[...]
    token[...] = jnp.zeros_like(token)
    for p in range(lanes // PAIR):
        at = lanes_at(wide, p)
        kp = k[:, at]
        total = None
        for h, (qh, vh) in enumerate(zip(heads_of(q[:, at]), heads_of(v[:, at]))):
            prob = dot(qh, kp, 1, 1).astype(BF16) * m
            probs[half * (lanes // E) + 2 * p + h] = dot(kp, qh, 1, 1).astype(BF16) * mt
            term = dot(prob, vh, 1, 0)
            total = term if total is None else total + term
        attn[:, lanes_at(base, p)] = total


def head_mean(x):
    high, low = split(x)
    ones = spread(jnp.full((E, PAIR), 1.0 / E, BF16))
    return dot(jnp.concatenate([high, low], axis=1), jnp.concatenate([ones, ones], axis=0), 1, 0)


def side_by_side(state, part):
    sh, sl = split(state)
    ph, pll = split(part)
    left = jnp.concatenate([spread(sh), spread(sl)], axis=0)
    right = jnp.concatenate([spread(ph), spread(pll)], axis=0)
    return jnp.concatenate([left, right], axis=1)


def stacked(state, part):
    sh, sl = split(state)
    ph, pll = split(part)
    top = jnp.concatenate([spread(sh), spread(sl)], axis=1)
    bottom = jnp.concatenate([spread(ph), spread(pll)], axis=1)
    return jnp.concatenate([top, bottom], axis=0)


def on_rows(seg, table, last, part):
    rows, own, flag = edge(seg, table, last)
    met = part[0, part.shape[1] - EXTRA:part.shape[1] - EXTRA + 1] == own
    if last:
        met = met & (flag == 1)
    return rows.astype(F32) * met.astype(F32)


def norm_kernel(group, core, q, dy, local, gain, seg, table, pre_keep, pre_recv, nxt, *rest):
    out, dab, part, gsum, keep, send, token = rest[-7:]
    token[...] = jnp.zeros_like(token)
    step = pl.program_id(0)
    lanes = out.shape[1]
    count = lanes // PAIR
    _, base, wide = place(group, core, lanes, 1)
    on_next = on_rows(seg, table, True, nxt)
    last, own, flag = edge(seg, table, True)
    last = (last.astype(F32) * jnp.where(flag == 1, 1.0, 0.0)).astype(BF16)
    pairs = [slice(p * PAIR, (p + 1) * PAIR) for p in range(count)]
    bases = [lanes_at(base, p) for p in range(count)]
    wides = [lanes_at(wide, p) for p in range(count)]
    fars = [
        dot(twice(q[:, at]), side_by_side(own_or_received(pre_keep, pre_recv, step == 0, p), nxt[0, rows_at(p)]), 1, 0)
        for p, at in enumerate(wides)
    ]
    attns = [local[:, at] + far[:, :PAIR] + on_next * far[:, PAIR:] for at, far in zip(bases, fars)]
    squares = [head_mean(attn * attn) for attn in attns]
    scales = [lax.rsqrt(square + 1e-06) for square in squares]
    normeds = [attn * scale for attn, scale in zip(attns, scales)]
    gas = [dy[:, at].astype(F32) * gain[:, pair] for at, pair in zip(wides, pairs)]
    means = [head_mean(ga * normed) for ga, normed in zip(gas, normeds)]
    das = [
        (scale * (ga - normed * mean)).astype(BF16)
        for scale, ga, normed, mean in zip(scales, gas, normeds, means)
    ]
    states = [state_pair(q[:, at], jnp.concatenate([da, da * last], axis=1)) for at, da in zip(wides, das)]
    part[0, count * E:] = jnp.broadcast_to(own, (EXTRA, PAIR))
    for p, (at, normed, da) in enumerate(zip(pairs, normeds, das)):
        part[0, p * E:(p + 1) * E] = states[p][:, PAIR:]
        dab[:, bases[p]] = da
        out[:, at] = (normed * gain[:, at]).astype(BF16)
        gsum[0, p:p + 1] = jnp.sum(dy[:, wides[p]].astype(F32) * normed, axis=0, keepdims=True)

    @pl.when(step == 0)
    def _():
        for p, state in enumerate(states):
            keep[p * E:(p + 1) * E] = state[:, :PAIR]

    @pl.when(step == 1)
    def _():
        for p, state in enumerate(states):
            send[p * E:(p + 1) * E] = state[:, :PAIR]


def inner_kernel(group, core, q, k, v, dab, probs, mask, seg, table, pre_keep, pre_recv, nxt, *rest):
    gq, gk, gv, token = rest[-4:]
    step = pl.program_id(0)
    lanes = dab.shape[1] // 2
    count = lanes // SUB // PAIR
    half, base, wide = place(group, core, lanes, SUB)
    m = mask[...]
    token[...] = jnp.zeros_like(token)
    on_next = on_rows(seg, table, True, nxt)
    for p in range(count):
        in_half = step % SUB * count + p
        at = lanes_at(wide, p)
        da = dab[:, lanes_at(base, p)]
        vp = v[:, at]
        far = dot(
            twice(da),
            stacked(own_or_received(pre_keep, pre_recv, step < SUB, in_half), nxt[0, rows_at(in_half)]), 1, 1)
        tq = far[:, :PAIR] + on_next * far[:, PAIR:]
        tk = tv = None
        for h, (qh, kh, dh) in enumerate(zip(heads_of(q[:, at]), heads_of(k[:, at]), heads_of(da))):
            dprob = dot(dh, vp, 1, 1).astype(BF16) * m
            tq = tq + dot(dprob, kh, 1, 0)
            a = dot(dprob, qh, 0, 0)
            b = dot(probs[half * (lanes // E) + 2 * in_half + h], dh, 1, 0)
            tk = a if tk is None else tk + a
            tv = b if tv is None else tv + b
        gq[:, p * PAIR:(p + 1) * PAIR] = tq.astype(BF16)
        gk[:, lanes_at(base, p)] = tk
        gv[:, lanes_at(base, p)] = tv


def outer_kernel(group, core, k, v, gk_in, gv_in, seg, table, suf_keep, suf_recv, prv, *rest):
    gk, gv, token = rest[-3:]
    step = pl.program_id(0)
    lanes = gk_in.shape[1] // 2
    count = lanes // SUB // PAIR
    _, base, wide = place(group, core, lanes, SUB)
    token[...] = jnp.zeros_like(token)
    on_prev = on_rows(seg, table, False, prv)
    for p in range(count):
        in_half = step % SUB * count + p
        here, own, at = slice(p * PAIR, (p + 1) * PAIR), lanes_at(base, p), lanes_at(wide, p)
        s = own_or_received(suf_keep, suf_recv, step < SUB, in_half)
        g = prv[0, rows_at(in_half)]
        far = dot(twice(v[:, at]), stacked(s, g), 1, 1)
        gk[:, here] = (gk_in[:, own] + far[:, :PAIR] + on_prev * far[:, PAIR:]).astype(BF16)
        far = dot(twice(k[:, at]), side_by_side(s, g), 1, 0)
        gv[:, here] = (gv_in[:, own] + far[:, :PAIR] + on_prev * far[:, PAIR:]).astype(BF16)


def partner(x, axis, bit):
    route = [(i, i ^ (1 << bit)) for i in range(lax.axis_size(axis))]
    return lax.ppermute(x, axis, route)


def shifted(x, distance):
    count = lax.axis_size("ctx")
    return lax.ppermute(x, "ctx", [(i, i + distance) for i in range(count) if 0 <= i + distance < count])


def nought(x):
    return jnp.minimum(jnp.abs(x), 0.0)


def chip_rank(chip, towards):
    return chip if towards == 1 else lax.axis_size("ctx") // 2 - 1 - chip


def chips_before(own, towards):
    chips = lax.axis_size("ctx") // 2
    total = shifted(own, 2 * towards)
    span = 1
    while span < chips:
        total = total + shifted(total, 2 * towards * span)
        span *= 2
    return total


def pick(rank, cases):
    value = cases[-1][1]
    for at, case in cases[:-1]:
        value = jnp.where(rank == at, case, value)
    return value


def chain_load(chip, owns, starts, arrived, step, towards):
    chips = lax.axis_size("ctx") // 2
    cases = [(step - at, own) for own, at in zip(owns, starts) if 0 <= step - at <= chips - 2]
    load = pick(chip_rank(chip, towards), cases)
    return load if arrived is None else load + arrived


def chain_step(load, starts, step, towards):
    chips = lax.axis_size("ctx") // 2
    route = []
    for rank in range(chips - 1):
        if step - rank in starts:
            chip = rank if towards == 1 else chips - 1 - rank
            route += [(2 * chip + c, 2 * (chip + towards) + c) for c in range(2)]
    return lax.ppermute(load, "ctx", route)


def chain_result(chip, arrivals, start, towards):
    chips = lax.axis_size("ctx") // 2
    cases = [(rank, arrivals[start + rank - 1]) for rank in range(1, chips)]
    return pick(chip_rank(chip, towards), cases + [(0, jnp.zeros_like(arrivals[0]))])


def within_chip(keep, send):
    received = partner(send, "ctx", 0)
    return keep, received, keep + received


def to_cores(core, before, piece, towards):
    keep, received, _ = piece
    is_source = core == (0 if towards == 1 else 1)
    mine = jnp.where(is_source, before, before + received)
    return mine, partner(jnp.where(is_source, before + keep, before), "ctx", 0)


def pinned(x, space):
    return pltpu.with_memory_space_constraint(x, space)


def scatter_step(x, at, axis, bit):
    low, high = jnp.split(x, 2, axis=0 if x.shape[0] > 1 else 1)
    upper = (at >> bit & 1 == 1)[:, :low.shape[1]]
    return jnp.where(upper, high, low) + partner(jnp.where(upper, low, high), axis, bit)


def on_device(queries, keys, values, out_grad, segment_ids, image_flags, gain):
    rows, width = queries.shape[1:]
    q, k, v, dy = (x[0] for x in (queries, keys, values, out_grad))
    table = image_flags[0]
    gain_row = gain.reshape(1, width)
    ctx = lax.axis_index("ctx")
    core = jnp.stack([ctx & 1, ctx >> 1, ctx, lax.axis_index("dp")]).astype(jnp.int32)
    lanes = width // GROUPS // 2
    half_rows = lanes // PAIR * E
    heads = lanes // E

    def call(kernel, group, ins, outs, after=(), alias=(), scratch=(), sub=1, steps=None):
        def half_of(i, c):
            return (i // sub + c[0]) % 2

        def wide(i, c):
            return (0, (2 * group + half_of(i, c)) * sub + i % sub)

        def whole(*args):
            return (0, 0)

        def part(i, c):
            return (half_of(i, c), 0, 0)

        specs = {
            "vmem": pl.BlockSpec(memory_space=pltpu.VMEM),
            "hbm": pl.BlockSpec(memory_space=pltpu.HBM),
            "wide": pl.BlockSpec((rows, lanes // sub), wide),
            "row": pl.BlockSpec((1, lanes // sub), wide),
            "sums": pl.BlockSpec((1, lanes // PAIR, PAIR), part),
            "zero": pl.BlockSpec((1, rows), whole),
            "half": pl.BlockSpec((half_rows, PAIR), whole),
            "all": pl.BlockSpec((GROUPS * half_rows, PAIR), whole),
            "part": pl.BlockSpec((1, half_rows + EXTRA, PAIR), part),
            "parts": pl.BlockSpec((2, half_rows + EXTRA, PAIR), lambda *args: (0, 0, 0)),
            "seg": pl.BlockSpec((1, rows), whole),
            "table": pl.BlockSpec((1, table.shape[0]), whole),
            "mask": pl.BlockSpec((rows, rows), whole),
            "token": pl.BlockSpec((1, PAIR), whole),
            "after2": pl.BlockSpec((8, PAIR), whole),
            "after3": pl.BlockSpec((1, 8, PAIR), lambda *args: (0, 0, 0)),
            "any": pl.BlockSpec(memory_space=pl.ANY),
        }
        shapes = {
            "wide": (rows, width),
            "sums": (2, lanes // PAIR, PAIR),
            "zero": (1, rows),
            "half": (half_rows, PAIR),
            "all": (GROUPS * half_rows, PAIR),
            "part": (2, half_rows + EXTRA, PAIR),
            "parts": (2, half_rows + EXTRA, PAIR),
            "token": (1, PAIR),
        }
        spaces = {"vmem": pltpu.VMEM, "hbm": pltpu.HBM}
        operands = [pinned(x, spaces[kind]) if kind in spaces else x for kind, x in ins] + list(after)
        kinds = [kind for kind, _ in ins] + [f"after{x.ndim}" for x in after]
        aliases = {}
        for out_at, x in alias:
            if x is not None:
                aliases[1 + len(operands)] = out_at
                operands.append(x)
                kinds.append("any")
        out_shape = [
            pltpu.VMEM(*shape, dtype) if kind == "vmem" else jax.ShapeDtypeStruct(shapes[kind], dtype)
            for kind, dtype, *shape in outs
        ]
        return pl.pallas_call(
            kernel,
            grid_spec=pltpu.PrefetchScalarGridSpec(
                num_scalar_prefetch=1,
                grid=steps or (2 * sub,),
                in_specs=[specs[kind] for kind in kinds],
                out_specs=[specs[kind] for kind, *_ in outs],
                scratch_shapes=scratch,
            ),
            out_shape=out_shape,
            input_output_aliases=aliases,
            compiler_params=pltpu.CompilerParams(vmem_limit_bytes=VMEM),
            cost_estimate=pl.CostEstimate(flops=1, bytes_accessed=1, transcendentals=0),
        )(core, *operands)

    edges = [("seg", segment_ids), ("table", image_flags)]
    groups = range(GROUPS)
    chips = lax.axis_size("ctx") // 2
    chained = GROUPS < chips <= 8

    whole, group_of = (rows, width), (rows, 2 * lanes)

    def local_attn(g, after):
        return call(
            functools.partial(local_kernel, g), g,
            [("vmem", q), ("vmem", k), ("vmem", v), ("mask", mask), ("mask", mask_t)],
            [("vmem", F32, group_of), ("vmem", BF16, (2 * heads, rows, rows)), ("token", F32)], after=after)

    def norm(g, prefix, before, after):
        output, dab, prv, gsum, keep, send, token = call(
            functools.partial(norm_kernel, g), g,
            [("vmem", q), ("vmem", dy), ("vmem", local[g][0]), ("row", gain_row), *edges,
             ("half", prefix[0]), ("half", prefix[1]), ("part", nxt[g])],
            [("wide", BF16), ("vmem", BF16, group_of), ("part", F32), ("sums", F32), ("half", F32), ("half", F32),
             ("token", F32)],
            after=after, alias=[(0, before)])
        return output, dab, prv, gsum, (keep, send), token

    def inner(g, before, after):
        return call(
            functools.partial(inner_kernel, g), g,
            [("vmem", q), ("vmem", k), ("vmem", v), ("vmem", norms[g][1]), ("vmem", local[g][1]), ("mask", mask), *edges,
             ("half", prefix[g][0]), ("half", prefix[g][1]), ("part", nxt[g])],
            [("wide", BF16), ("vmem", F32, group_of), ("vmem", F32, group_of), ("token", F32)],
            after=after, alias=[(0, before)], sub=SUB)

    def outer(g, suffix, before, after):
        return call(
            functools.partial(outer_kernel, g), g,
            [("vmem", k), ("vmem", v), ("vmem", inners[g][1]), ("vmem", inners[g][2]), *edges,
             ("half", suffix[0]), ("half", suffix[1]), ("part", prv[g])],
            [("wide", BF16), ("wide", BF16), ("token", F32)], after=after, alias=list(enumerate(before)), sub=SUB)

    keep, send, zero, k, v, core_row, chip_row, ctx_row, dp_row = call(
        states_kernel, 0, [("hbm", k), ("hbm", v)],
        [("all", F32), ("all", F32), ("zero", jnp.int32), ("vmem", BF16, whole), ("vmem", BF16, whole)]
        + [("token", jnp.int32)] * 4,
        scratch=[pltpu.SemaphoreType.DMA((2 * GROUPS, 2))], steps=(1,))
    at = {"ctx": ctx_row, "dp": dp_row}
    keep, received, total = within_chip(keep, send)
    owns = [tuple(x[g * half_rows:(g + 1) * half_rows] for x in (keep, received, total)) for g in groups]
    sums = [own for _, _, own in owns]
    seg = (segment_ids + zero)[0]
    onehot = seg[:, None] == jnp.arange(table.shape[0], dtype=jnp.int32)[None, :]
    img = jnp.sum(jnp.where(onehot, table[None, :], 0), axis=1)
    imgseg = jnp.where(img == 1, seg, -1)
    pos = jnp.arange(rows)
    mask = ((pos[:, None] >= pos[None, :]) | (imgseg[:, None] == seg[None, :])).astype(BF16)
    mask_t = ((pos[:, None] <= pos[None, :]) | (seg[:, None] == imgseg[None, :])).astype(BF16)

    local, nxt, arrivals = [], [], []
    starts = list(groups)
    last = chips - 2 + starts[-1]
    load = sums[0]
    *parts, q, dy, token = call(
        lambda core, *refs: part_kernel(*refs), 0, [("hbm", q), ("hbm", dy), ("vmem", k), ("vmem", v), *edges],
        [("parts", F32)] * GROUPS + [("vmem", BF16, whole), ("vmem", BF16, whole), ("token", F32)],
        after=[load], scratch=[pltpu.SemaphoreType.DMA((2,))], steps=(1,))
    for step in range(last + 1 if chained else GROUPS + 1):
        if chained:
            arrivals.append(chain_step(load, starts, step, 1))
        if 1 <= step <= GROUPS:
            nxt.append(shifted(parts[step - 1], -1))
            *attn, token = local_attn(step - 1, [load])
            local.append(attn)
            token = token + nought(nxt[-1][0, :1])
        if step < last and chained:
            load = chain_load(chip_row, sums, starts, arrivals[-1] + token, step + 1, 1)
    prefix, norms = [], []
    before = chain_result(chip_row, arrivals, starts[0], 1) if chained else chips_before(sums[0], 1)
    prefix.append(to_cores(core_row, before, owns[0], 1))
    norms.append(norm(0, prefix[0], None, [load]))

    ins, ins_starts, ins_arrivals = owns, starts, arrivals
    owns = [within_chip(*norms[0][4])]
    sums = [owns[0][2]]
    load = sums[0]
    for g in groups[1:]:
        if chained:
            ins_arrivals[-1] = ins_arrivals[-1] + norms[-1][5]
        before = chain_result(chip_row, ins_arrivals, ins_starts[g], 1) if chained else chips_before(ins[g][2], 1)
        prefix.append(to_cores(core_row, before, ins[g], 1))
        norms.append(norm(g, prefix[g], norms[-1][0], [load]))
        owns.append(within_chip(*norms[-1][4]))
        sums.append(owns[-1][2])
    output = norms[-1][0]
    prv = [n[2] for n in norms]
    gain_sum = jnp.concatenate([n[3] for n in norms], axis=0).reshape(-1, PAIR)
    bits = [(axis, bit) for axis in ("dp", "ctx") for bit in reversed(range(lax.axis_size(axis).bit_length() - 1))]
    arrivals, inners, outers = [], [], [None] * 2
    starts = [0] + [g + 1 for g in groups[1:]]
    last = chips - 2 + starts[-1]
    token = norms[-1][5]
    for step in range(last + 1 if chained else GROUPS + 1):
        if chained:
            if step:
                load = chain_load(chip_row, sums, starts, arrivals[-1] + token, step, -1)
            arrivals.append(chain_step(load, starts, step, -1))
        if step == 0:
            prv[0] = shifted(prv[0], 1)
            token = token + nought(prv[0][0, :1])
            continue
        token = jnp.zeros((1, PAIR), F32)
        if 2 <= step and len(bits) > 2:
            gain_sum = scatter_step(gain_sum + nought(load[:1]), at[bits[0][0]], *bits.pop(0))
            token = token + nought(gain_sum[:1])
        if step == GROUPS + 1 or (not chained and step == 1):
            for g in groups[1:]:
                prv[g] = shifted(prv[g] + nought(load[:1]), 1)
                token = token + nought(prv[g][0, :1])
        if step <= GROUPS:
            inners.append(inner(step - 1, inners[-1][0] if inners else None, [load]))
            token = token + inners[-1][3]
    for g in groups:
        if g and chained:
            arrivals[-1] = arrivals[-1] + token
        before = chain_result(chip_row, arrivals, starts[g], -1) if chained else chips_before(sums[g], -1)
        *outers, done = outer(g, to_cores(core_row, before, owns[g], -1), outers, [])
        token = token + done
    for axis, bit in bits:
        gain_sum = scatter_step(gain_sum, at[axis], axis, bit)
    grad_q = inners[-1][0]
    grad_k, grad_v = outers
    grad_gain = gain_sum.reshape(-1)
    return output[None], grad_q[None], grad_k[None], grad_v[None], grad_gain


def solution(mesh):
    return jax.shard_map(
        on_device,
        mesh=mesh,
        in_specs=(
            P("dp", "ctx", None),
            P("dp", "ctx", None),
            P("dp", "ctx", None),
            P("dp", "ctx", None),
            P("dp", "ctx"),
            P("dp", None),
            P(),
        ),
        out_specs=(
            P("dp", "ctx", None),
            P("dp", "ctx", None),
            P("dp", "ctx", None),
            P("dp", "ctx", None),
            P(("dp", "ctx")),
        ),
        check_vma=False,
    )
```

```python
import functools

import jax
import jax.numpy as jnp
from jax import lax
from jax.experimental import pallas as pl
from jax.experimental.pallas import tpu as pltpu
from jax.sharding import PartitionSpec as P

E = 64
PAIR = 2 * E
GROUPS = 2
EXTRA = 8
PAD = 32
VMEM = 10 * 2**20
SUB = 2
F32 = jnp.float32
BF16 = jnp.bfloat16


def dot(a, b, ca, cb):
    return lax.dot_general(a, b, (((ca,), (cb,)), ((), ())), preferred_element_type=F32)


def low_lanes(rows, cols):
    lane = lax.broadcasted_iota(jnp.int32, (rows, cols), 1)
    return lane % PAIR < E


def fold(product):
    return jnp.where(low_lanes(E, product.shape[1]), product[:E], product[E:])


def split(state):
    high = state.astype(BF16)
    return high, (state - high.astype(F32)).astype(BF16)


def spread(state):
    low = low_lanes(*state.shape)
    zero = jnp.zeros_like(state)
    return jnp.concatenate([jnp.where(low, state, zero), jnp.where(low, zero, state)], axis=0)


def heads_of(pair):
    low = low_lanes(*pair.shape)
    zero = jnp.zeros_like(pair)
    return jnp.where(low, pair, zero), jnp.where(low, zero, pair)


def twice(x):
    return jnp.concatenate([x, x], axis=1)


def pair_at(ref, p):
    return ref[:, p * PAIR:(p + 1) * PAIR]


def rows_at(base, p):
    return pl.ds(pl.multiple_of(base + p * E, E), E)


def twice(x):
    return jnp.concatenate([x, x], axis=1)


def pair_at(ref, p):
    return ref[:, p * PAIR:(p + 1) * PAIR]


def rows_at(base, p):
    return pl.ds(pl.multiple_of(base + p * E, E), E)


def own_or_received(keep, received, own, p):
    return jnp.where(own, keep[rows_at(p)], received[rows_at(p)])


def state_pair(a, b):
    return fold(dot(a, b, 0, 0))


def edge(seg, table, last):
    row = seg[...]
    count = row.shape[1]
    own = row[:, count - 1:] if last else row[:, :1]
    size = jnp.sum((row == own).astype(F32), axis=1, keepdims=True)
    at = lax.broadcasted_iota(jnp.int32, (count, PAIR), 0).astype(F32)
    rows = at >= count - size if last else at < size
    ids = lax.broadcasted_iota(jnp.int32, table.shape, 1)
    flag = jnp.sum(jnp.where(ids == own, table[...], 0).astype(F32), axis=1, keepdims=True)
    return rows, own.astype(F32), flag


def lanes_at(base, p):
    return pl.ds(pl.multiple_of(base + p * PAIR, PAIR), PAIR)


def place(sel, core, lanes, sub):
    step = pl.program_id(0)
    group, part = step // sub, step % sub
    half = (sel + core[0]) % 2
    base = group * lanes + part * (lanes // sub)
    return group, base, base + (group + half) * lanes, base // PAIR * E


def states_kernel(position, k_in, v_in, keep, send, zero, k, v, core_row, ctx_row, dp_row, sems):
    for i, row in enumerate((core_row, ctx_row, dp_row)):
        row[...] = jnp.full(row.shape, position[i], jnp.int32)
    lanes = k.shape[1] // GROUPS // 2
    count = lanes // PAIR
    copies = []
    for sel in (1, 0):
        for group in range(GROUPS):
            base = (2 * group + (sel + position[0]) % 2) * lanes
            at = pl.ds(pl.multiple_of(base, lanes), lanes)
            for i, (array, buf) in enumerate(((k_in, k), (v_in, v))):
                copies.append(pltpu.make_async_copy(array.at[:, at], buf.at[:, at], sems.at[2 * group + sel, i]))
    for copy in copies:
        copy.start()
    zero[...] = jnp.zeros_like(zero)
    for sel, out in ((1, send), (0, keep)):
        out[GROUPS * count * E:] = jnp.zeros((PAD, PAIR), F32)
        for group in range(GROUPS):
            copies.pop(0).wait()
            copies.pop(0).wait()
            base = (2 * group + (sel + position[0]) % 2) * lanes
            for p in range(count):
                at = lanes_at(base, p)
                row = (group * count + p) * E
                out[row:row + E] = state_pair(k[:, at], v[:, at])


def part_kernel(core, q_in, dy_in, k, v, seg, table, *rest):
    *outs, q, dy, token, sems = rest[-6:]
    copies = [pltpu.make_async_copy(a, b, sems.at[i]) for i, (a, b) in enumerate(((q_in, q), (dy_in, dy)))]
    for copy in copies:
        copy.start()
    token[...] = jnp.zeros_like(token)
    lanes = k.shape[1] // GROUPS // 2
    count = lanes // PAIR
    rows, own, _ = edge(seg, table, False)
    keep = rows.astype(BF16)
    for sel, out in enumerate(outs):
        for group in range(GROUPS):
            base = (2 * group + (sel + core[0]) % 2) * lanes
            for p in range(count):
                at = lanes_at(base, p)
                out[group, p * E:(p + 1) * E] = state_pair(k[:, at], v[:, at] * keep)
            out[group, count * E:] = jnp.broadcast_to(own, (EXTRA, PAIR))
    for copy in copies:
        copy.wait()


def local_kernel(sel, core, q, k, v, mask, mask_t, *rest):
    attn, probs, token = rest[-3:]
    lanes = attn.shape[1] // GROUPS
    group, base, wide, _ = place(sel, core, lanes, 1)
    m, mt = mask[...], mask_t[...]
    token[...] = jnp.zeros_like(token)
    for p in range(lanes // PAIR):
        at = lanes_at(wide, p)
        kp = k[:, at]
        total = None
        for h, (qh, vh) in enumerate(zip(heads_of(q[:, at]), heads_of(v[:, at]))):
            prob = dot(qh, kp, 1, 1).astype(BF16) * m
            probs[group * (lanes // E) + 2 * p + h] = dot(kp, qh, 1, 1).astype(BF16) * mt
            term = dot(prob, vh, 1, 0)
            total = term if total is None else total + term
        attn[:, lanes_at(base, p)] = total


def head_mean(x):
    high, low = split(x)
    ones = spread(jnp.full((E, PAIR), 1.0 / E, BF16))
    return dot(jnp.concatenate([high, low], axis=1), jnp.concatenate([ones, ones], axis=0), 1, 0)


def side_by_side(state, part):
    sh, sl = split(state)
    ph, pll = split(part)
    left = jnp.concatenate([spread(sh), spread(sl)], axis=0)
    right = jnp.concatenate([spread(ph), spread(pll)], axis=0)
    return jnp.concatenate([left, right], axis=1)


def stacked(state, part):
    sh, sl = split(state)
    ph, pll = split(part)
    top = jnp.concatenate([spread(sh), spread(sl)], axis=1)
    bottom = jnp.concatenate([spread(ph), spread(pll)], axis=1)
    return jnp.concatenate([top, bottom], axis=0)


def on_rows(seg, table, last, part):
    rows, own, flag = edge(seg, table, last)
    met = part[0, part.shape[1] - EXTRA:part.shape[1] - EXTRA + 1] == own
    if last:
        met = met & (flag == 1)
    return rows.astype(F32) * met.astype(F32)


def norm_kernel(sel, core, q, dy, local, gain, seg, table, prefix, nxt, *rest):
    out, dab, part, gsum, total, token = rest[-6:]
    token[...] = jnp.zeros_like(token)
    lanes = out.shape[1]
    count = lanes // PAIR
    _, base, wide, row = place(sel, core, lanes, 1)
    on_next = on_rows(seg, table, True, nxt)
    last, own, flag = edge(seg, table, True)
    last = (last.astype(F32) * jnp.where(flag == 1, 1.0, 0.0)).astype(BF16)
    pairs = [slice(p * PAIR, (p + 1) * PAIR) for p in range(count)]
    bases = [lanes_at(base, p) for p in range(count)]
    wides = [lanes_at(wide, p) for p in range(count)]
    fars = [
        dot(twice(q[:, at]), side_by_side(prefix[rows_at(row, p)], nxt[0, rows_at(0, p)]), 1, 0)
        for p, at in enumerate(wides)
    ]
    attns = [local[:, at] + far[:, :PAIR] + on_next * far[:, PAIR:] for at, far in zip(bases, fars)]
    squares = [head_mean(attn * attn) for attn in attns]
    scales = [lax.rsqrt(square + 1e-06) for square in squares]
    normeds = [attn * scale for attn, scale in zip(attns, scales)]
    gas = [dy[:, at].astype(F32) * gain[:, pair] for at, pair in zip(wides, pairs)]
    means = [head_mean(ga * normed) for ga, normed in zip(gas, normeds)]
    das = [
        (scale * (ga - normed * mean)).astype(BF16)
        for scale, ga, normed, mean in zip(scales, gas, normeds, means)
    ]
    states = [state_pair(q[:, at], jnp.concatenate([da, da * last], axis=1)) for at, da in zip(wides, das)]
    part[0, count * E:] = jnp.broadcast_to(own, (EXTRA, PAIR))
    total[GROUPS * count * E:] = jnp.zeros((PAD, PAIR), F32)
    for p, (at, normed, da) in enumerate(zip(pairs, normeds, das)):
        total[rows_at(row, p)] = states[p][:, :PAIR]
        part[0, p * E:(p + 1) * E] = states[p][:, PAIR:]
        dab[:, bases[p]] = da
        out[:, at] = (normed * gain[:, at]).astype(BF16)
        gsum[0, p:p + 1] = jnp.sum(dy[:, wides[p]].astype(F32) * normed, axis=0, keepdims=True)


def inner_kernel(sel, core, q, k, v, dab, probs, mask, seg, table, prefix, nxt, *rest):
    gq, gk, gv, token = rest[-4:]
    lanes = dab.shape[1] // GROUPS
    count = lanes // SUB // PAIR
    group, base, wide, row = place(sel, core, lanes, SUB)
    m = mask[...]
    token[...] = jnp.zeros_like(token)
    on_next = on_rows(seg, table, True, nxt)
    first = row - group * (lanes // 2)
    for p in range(count):
        at = lanes_at(wide, p)
        da = dab[:, lanes_at(base, p)]
        vp = v[:, at]
        far = dot(twice(da), stacked(prefix[rows_at(row, p)], nxt[0, rows_at(first, p)]), 1, 1)
        tq = far[:, :PAIR] + on_next * far[:, PAIR:]
        tk = tv = None
        for h, (qh, kh, dh) in enumerate(zip(heads_of(q[:, at]), heads_of(k[:, at]), heads_of(da))):
            dprob = dot(dh, vp, 1, 1).astype(BF16) * m
            tq = tq + dot(dprob, kh, 1, 0)
            a = dot(dprob, qh, 0, 0)
            b = dot(probs[row // (E // 2) + 2 * p + h], dh, 1, 0)
            tk = a if tk is None else tk + a
            tv = b if tv is None else tv + b
        gq[:, p * PAIR:(p + 1) * PAIR] = tq.astype(BF16)
        gk[:, lanes_at(base, p)] = tk
        gv[:, lanes_at(base, p)] = tv


def outer_kernel(sel, core, k, v, gk_in, gv_in, seg, table, suffix, prv, *rest):
    gk, gv, token = rest[-3:]
    lanes = gk_in.shape[1] // GROUPS
    count = lanes // SUB // PAIR
    group, base, wide, row = place(sel, core, lanes, SUB)
    token[...] = jnp.zeros_like(token)
    on_prev = on_rows(seg, table, False, prv)
    first = row - group * (lanes // 2)
    for p in range(count):
        here, own, at = slice(p * PAIR, (p + 1) * PAIR), lanes_at(base, p), lanes_at(wide, p)
        s = suffix[rows_at(row, p)]
        g = prv[0, rows_at(first, p)]
        far = dot(twice(v[:, at]), stacked(s, g), 1, 1)
        gk[:, here] = (gk_in[:, own] + far[:, :PAIR] + on_prev * far[:, PAIR:]).astype(BF16)
        far = dot(twice(k[:, at]), side_by_side(s, g), 1, 0)
        gv[:, here] = (gv_in[:, own] + far[:, :PAIR] + on_prev * far[:, PAIR:]).astype(BF16)


def partner(x, axis, bit):
    route = [(i, i ^ (1 << bit)) for i in range(lax.axis_size(axis))]
    return lax.ppermute(x, axis, route)


def shifted(x, distance):
    count = lax.axis_size("ctx")
    return lax.ppermute(x, "ctx", [(i, i + distance) for i in range(count) if 0 <= i + distance < count])


def nought(x):
    return jnp.minimum(jnp.abs(x), 0.0)


def within_chip(keep, send):
    received = partner(send, "ctx", 0)
    return keep, received, keep + received


def to_cores(core, before, piece, towards):
    keep, received, _ = piece
    is_source = core == (0 if towards == 1 else 1)
    mine = jnp.where(is_source, before, before + received)
    return mine, partner(jnp.where(is_source, before + keep, before), "ctx", 0)


def pinned(x, space):
    return pltpu.with_memory_space_constraint(x, space)


def scatter_step(x, at, axis, bit):
    low, high = jnp.split(x, 2, axis=1)
    upper = (at >> bit & 1 == 1)[:, :low.shape[1]]
    return jnp.where(upper, high, low) + partner(jnp.where(upper, low, high), axis, bit)


def scatter_stage(pieces, at, axis, low):
    def chosen(index):
        value = pieces[0]
        for i, piece in enumerate(pieces[1:]):
            value = jnp.where(index == i + 1, piece, value)
        return value

    own = at >> low & (len(pieces) - 1)
    total = chosen(own)
    for flip in range(1, len(pieces)):
        route = [(i, i ^ (flip << low)) for i in range(lax.axis_size(axis))]
        total = total + lax.ppermute(chosen(own ^ flip), axis, route)
    return total


def on_device(queries, keys, values, out_grad, segment_ids, image_flags, gain):
    rows, width = queries.shape[1:]
    q, k, v, dy = (x[0] for x in (queries, keys, values, out_grad))
    table = image_flags[0]
    gain_row = gain.reshape(1, width)
    ctx = lax.axis_index("ctx")
    core = jnp.stack([ctx & 1, ctx, lax.axis_index("dp")]).astype(jnp.int32)
    lanes = width // GROUPS // 2
    half_rows = lanes // PAIR * E
    heads = lanes // E

    def call(kernel, sel, ins, outs, after=(), alias=(), scratch=(), sub=1, steps=None):
        def wide(i, c):
            return (0, (i // sub * 2 + (sel + c[0]) % 2) * sub + i % sub)

        def whole(*args):
            return (0, 0)

        def part(i, c):
            return (i // sub, 0, 0)

        specs = {
            "vmem": pl.BlockSpec(memory_space=pltpu.VMEM),
            "hbm": pl.BlockSpec(memory_space=pltpu.HBM),
            "wide": pl.BlockSpec((rows, lanes // sub), wide),
            "row": pl.BlockSpec((1, lanes // sub), wide),
            "sums": pl.BlockSpec((1, lanes // PAIR, PAIR), part),
            "zero": pl.BlockSpec((1, rows), whole),
            "all": pl.BlockSpec((GROUPS * half_rows + PAD, PAIR), whole),
            "part": pl.BlockSpec((1, half_rows + EXTRA, PAIR), part),
            "parts": pl.BlockSpec((GROUPS, half_rows + EXTRA, PAIR), lambda *args: (0, 0, 0)),
            "seg": pl.BlockSpec((1, rows), whole),
            "table": pl.BlockSpec((1, table.shape[0]), whole),
            "mask": pl.BlockSpec((rows, rows), whole),
            "token": pl.BlockSpec((1, PAIR), whole),
            "after2": pl.BlockSpec((8, PAIR), whole),
            "after3": pl.BlockSpec((1, 8, PAIR), lambda *args: (0, 0, 0)),
            "any": pl.BlockSpec(memory_space=pl.ANY),
        }
        shapes = {
            "wide": (rows, width),
            "sums": (GROUPS, lanes // PAIR, PAIR),
            "zero": (1, rows),
            "all": (GROUPS * half_rows + PAD, PAIR),
            "part": (GROUPS, half_rows + EXTRA, PAIR),
            "parts": (GROUPS, half_rows + EXTRA, PAIR),
            "token": (1, PAIR),
        }
        spaces = {"vmem": pltpu.VMEM, "hbm": pltpu.HBM}
        operands = [pinned(x, spaces[kind]) if kind in spaces else x for kind, x in ins] + list(after)
        kinds = [kind for kind, _ in ins] + [f"after{x.ndim}" for x in after]
        aliases = {}
        for out_at, x in alias:
            if x is not None:
                aliases[1 + len(operands)] = out_at
                operands.append(x)
                kinds.append("any")
        out_shape = [
            pltpu.VMEM(*shape, dtype) if kind == "vmem" else jax.ShapeDtypeStruct(shapes[kind], dtype)
            for kind, dtype, *shape in outs
        ]
        return pl.pallas_call(
            kernel,
            grid_spec=pltpu.PrefetchScalarGridSpec(
                num_scalar_prefetch=1,
                grid=steps or (GROUPS * sub,),
                in_specs=[specs[kind] for kind in kinds],
                out_specs=[specs[kind] for kind, *_ in outs],
                scratch_shapes=scratch,
            ),
            out_shape=out_shape,
            input_output_aliases=aliases,
            compiler_params=pltpu.CompilerParams(vmem_limit_bytes=VMEM),
            cost_estimate=pl.CostEstimate(flops=1, bytes_accessed=1, transcendentals=0),
        )(core, *operands)

    edges = [("seg", segment_ids), ("table", image_flags)]
    chips = lax.axis_size("ctx") // 2
    whole, part_of = (rows, width), (rows, width // 2)

    def local_attn(sel, after):
        return call(
            functools.partial(local_kernel, sel), sel,
            [("vmem", q), ("vmem", k), ("vmem", v), ("mask", mask), ("mask", mask_t)],
            [("vmem", F32, part_of), ("vmem", BF16, (GROUPS * heads, rows, rows)), ("token", F32)], after=after)

    def norm(sel, before, after):
        return call(
            functools.partial(norm_kernel, sel), sel,
            [("vmem", q), ("vmem", dy), ("vmem", local[sel][0]), ("row", gain_row), *edges,
             ("all", prefix[sel]), ("part", nxt[sel])],
            [("wide", BF16), ("vmem", BF16, part_of), ("part", F32), ("sums", F32), ("all", F32), ("token", F32)],
            after=after, alias=[(0, before)])

    def inner(sel, before, after):
        return call(
            functools.partial(inner_kernel, sel), sel,
            [("vmem", q), ("vmem", k), ("vmem", v), ("vmem", norms[sel][1]), ("vmem", local[sel][1]), ("mask", mask),
             *edges, ("all", prefix[sel]), ("part", nxt[sel])],
            [("wide", BF16), ("vmem", F32, part_of), ("vmem", F32, part_of), ("token", F32)],
            after=after, alias=[(0, before)], sub=SUB)

    def outer(sel, before, after):
        return call(
            functools.partial(outer_kernel, sel), sel,
            [("vmem", k), ("vmem", v), ("vmem", inners[sel][1]), ("vmem", inners[sel][2]), *edges,
             ("all", suffix[sel]), ("part", prv[sel])],
            [("wide", BF16), ("wide", BF16), ("token", F32)], after=after, alias=list(enumerate(before)), sub=SUB)

    def summed_before(own, towards, works):
        load, before, span = own, None, 1
        while span < chips:
            arrived = shifted(load, 2 * towards * span)
            if works:
                arrived = arrived + works.pop(0)(load)
            before = arrived if before is None else before + arrived
            load = load + arrived
            span *= 2
        for work in works:
            before = before + work(load)
        return before

    keep, send, zero, k, v, core_row, ctx_row, dp_row = call(
        states_kernel, 0, [("hbm", k), ("hbm", v)],
        [("all", F32), ("all", F32), ("zero", jnp.int32), ("vmem", BF16, whole), ("vmem", BF16, whole)]
        + [("token", jnp.int32)] * 3,
        scratch=[pltpu.SemaphoreType.DMA((2 * GROUPS, 2))], steps=(1,))
    piece = within_chip(keep, send)
    seg = (segment_ids + zero)[0]
    onehot = seg[:, None] == jnp.arange(table.shape[0], dtype=jnp.int32)[None, :]
    img = jnp.sum(jnp.where(onehot, table[None, :], 0), axis=1)
    imgseg = jnp.where(img == 1, seg, -1)
    pos = jnp.arange(rows)
    mask = ((pos[:, None] >= pos[None, :]) | (imgseg[:, None] == seg[None, :])).astype(BF16)
    mask_t = ((pos[:, None] <= pos[None, :]) | (seg[:, None] == imgseg[None, :])).astype(BF16)

    parts = call(
        part_kernel, 0, [("hbm", q), ("hbm", dy), ("vmem", k), ("vmem", v), *edges],
        [("parts", F32)] * 2 + [("vmem", BF16, whole), ("vmem", BF16, whole), ("token", F32)],
        after=[piece[2]], scratch=[pltpu.SemaphoreType.DMA((2,))], steps=(1,))
    *parts, q, dy, _ = parts
    local, nxt = [], []

    def first_work(load):
        *made, token = local_attn(0, [parts[0]])
        local.append(made)
        return token

    def second_work(load):
        for part in reversed(parts):
            nxt.append(shifted(part + nought(load[:1]), -1))
        *made, token = local_attn(1, [load])
        local.append(made)
        return token + nought(nxt[0][0, :1]) + nought(nxt[1][0, :1])

    before = summed_before(piece[2], 1, [first_work, second_work])
    prefix = to_cores(core_row, before, piece, 1)
    norms = [norm(0, None, [])]
    norms.append(norm(1, norms[0][0], [norms[0][4]]))
    output = norms[1][0]
    piece = within_chip(norms[0][4], norms[1][4])
    sums = [jnp.where(core_row == sel, norms[0][3], norms[1][3]) for sel in range(2)]
    gain_sum = [[jnp.stack(sums, axis=1).reshape(-1, PAIR)]]
    inners, prv = [], []

    def third_work(load):
        x = (gain_sum[0][0] + nought(load[:1])).reshape(4, 4, PAIR)
        top = lax.axis_size("ctx").bit_length() - 3
        gain_sum.append(scatter_stage([x[:, i] for i in range(4)], ctx_row, "ctx", top))
        inners.append(inner(0, None, [load]))
        return inners[0][3] + nought(gain_sum[-1][:1])

    def fourth_work(load):
        x = gain_sum[-1] + nought(load[:1])
        gain_sum.append(scatter_stage([x[i:i + 1] for i in range(4)], dp_row, "dp", 0))
        for part in (norms[1][2], norms[0][2]):
            prv.append(shifted(part + nought(load[:1]), 1))
        inners.append(inner(1, inners[0][0], [load]))
        return inners[1][3] + nought(gain_sum[-1]) + nought(prv[0][0, :1]) + nought(prv[1][0, :1])

    before = summed_before(piece[2], -1, [third_work, fourth_work])
    suffix = to_cores(core_row, before, piece, -1)
    outers = outer(0, [None] * 2, [])
    grad_k, grad_v, _ = outer(1, outers[:2], [])
    grad_q = inners[1][0]
    grad_gain = gain_sum[-1]
    for bit in reversed(range(lax.axis_size("ctx").bit_length() - 3)):
        grad_gain = scatter_step(grad_gain, ctx_row, "ctx", bit)
    grad_gain = grad_gain.reshape(-1)
    return output[None], grad_q[None], grad_k[None], grad_v[None], grad_gain


def solution(mesh):
    return jax.shard_map(
        on_device,
        mesh=mesh,
        in_specs=(
            P("dp", "ctx", None),
            P("dp", "ctx", None),
            P("dp", "ctx", None),
            P("dp", "ctx", None),
            P("dp", "ctx"),
            P("dp", None),
            P(),
        ),
        out_specs=(
            P("dp", "ctx", None),
            P("dp", "ctx", None),
            P("dp", "ctx", None),
            P("dp", "ctx", None),
            P(("dp", "ctx")),
        ),
        check_vma=False,
    )
```

```python
import functools

import jax
import jax.numpy as jnp
from jax import lax
from jax.experimental import pallas as pl
from jax.experimental.pallas import tpu as pltpu
from jax.sharding import PartitionSpec as P

E = 64
PAIR = 2 * E
GROUPS = 2
EXTRA = 8
VMEM = 10 * 2**20
SUB = 2
F32 = jnp.float32
BF16 = jnp.bfloat16


def dot(a, b, ca, cb):
    return lax.dot_general(a, b, (((ca,), (cb,)), ((), ())), preferred_element_type=F32)


def low_lanes(rows, cols):
    lane = lax.broadcasted_iota(jnp.int32, (rows, cols), 1)
    return lane % PAIR < E


def fold(product):
    return jnp.where(low_lanes(E, product.shape[1]), product[:E], product[E:])


def split(state):
    high = state.astype(BF16)
    return high, (state - high.astype(F32)).astype(BF16)


def spread(state):
    low = low_lanes(*state.shape)
    zero = jnp.zeros_like(state)
    return jnp.concatenate([jnp.where(low, state, zero), jnp.where(low, zero, state)], axis=0)


def heads_of(pair):
    low = low_lanes(*pair.shape)
    zero = jnp.zeros_like(pair)
    return jnp.where(low, pair, zero), jnp.where(low, zero, pair)


def twice(x):
    return jnp.concatenate([x, x], axis=1)


def pair_at(ref, p):
    return ref[:, p * PAIR:(p + 1) * PAIR]


def rows_at(base, p):
    return pl.ds(pl.multiple_of(base + p * E, E), E)


def twice(x):
    return jnp.concatenate([x, x], axis=1)


def pair_at(ref, p):
    return ref[:, p * PAIR:(p + 1) * PAIR]


def rows_at(base, p):
    return pl.ds(pl.multiple_of(base + p * E, E), E)


def own_or_received(keep, received, own, p):
    return jnp.where(own, keep[rows_at(p)], received[rows_at(p)])


def state_pair(a, b):
    return fold(dot(a, b, 0, 0))


def edge(seg, table, last):
    row = seg[...]
    count = row.shape[1]
    own = row[:, count - 1:] if last else row[:, :1]
    size = jnp.sum((row == own).astype(F32), axis=1, keepdims=True)
    at = lax.broadcasted_iota(jnp.int32, (count, PAIR), 0).astype(F32)
    rows = at >= count - size if last else at < size
    ids = lax.broadcasted_iota(jnp.int32, table.shape, 1)
    flag = jnp.sum(jnp.where(ids == own, table[...], 0).astype(F32), axis=1, keepdims=True)
    return rows, own.astype(F32), flag


def lanes_at(base, p):
    return pl.ds(pl.multiple_of(base + p * PAIR, PAIR), PAIR)


def place(sel, core, lanes, sub):
    step = pl.program_id(0)
    group, part = step // sub, step % sub
    half = (sel + core[0]) % 2
    base = group * lanes + part * (lanes // sub)
    return group, base, base + (group + half) * lanes, base // PAIR * E


def states_kernel(core, ctx, dp, k_in, v_in, keep, send, zero, k, v, core_row, ctx_row, dp_row, sems):
    for row, index in ((core_row, core), (ctx_row, ctx), (dp_row, dp)):
        row[...] = jnp.full(row.shape, index[0], jnp.int32)
    lanes = k.shape[1] // GROUPS // 2
    count = lanes // PAIR
    copies = []
    for sel in (1, 0):
        for group in range(GROUPS):
            base = (2 * group + (sel + core[0]) % 2) * lanes
            at = pl.ds(pl.multiple_of(base, lanes), lanes)
            for i, (array, buf) in enumerate(((k_in, k), (v_in, v))):
                copies.append(pltpu.make_async_copy(array.at[:, at], buf.at[:, at], sems.at[2 * group + sel, i]))
    for copy in copies:
        copy.start()
    zero[...] = jnp.zeros_like(zero)
    for sel, out in ((1, send), (0, keep)):
        for group in range(GROUPS):
            copies.pop(0).wait()
            copies.pop(0).wait()
            base = (2 * group + (sel + core[0]) % 2) * lanes
            for p in range(count):
                at = lanes_at(base, p)
                row = (group * count + p) * E
                out[row:row + E] = state_pair(k[:, at], v[:, at])


def part_kernel(core, q_in, dy_in, k, v, seg, table, *rest):
    *outs, q, dy, token, sems = rest[-6:]
    copies = [pltpu.make_async_copy(a, b, sems.at[i]) for i, (a, b) in enumerate(((q_in, q), (dy_in, dy)))]
    for copy in copies:
        copy.start()
    token[...] = jnp.zeros_like(token)
    lanes = k.shape[1] // GROUPS // 2
    count = lanes // PAIR
    rows, own, _ = edge(seg, table, False)
    keep = rows.astype(BF16)
    for sel, out in enumerate(outs):
        for group in range(GROUPS):
            base = (2 * group + (sel + core[0]) % 2) * lanes
            for p in range(count):
                at = lanes_at(base, p)
                out[group, p * E:(p + 1) * E] = state_pair(k[:, at], v[:, at] * keep)
            out[group, count * E:] = jnp.broadcast_to(own, (EXTRA, PAIR))
    for copy in copies:
        copy.wait()


def local_kernel(sel, core, q, k, v, mask, mask_t, *rest):
    attn, probs, token = rest[-3:]
    lanes = attn.shape[1] // GROUPS
    group, base, wide, _ = place(sel, core, lanes, 1)
    m, mt = mask[...], mask_t[...]
    token[...] = jnp.zeros_like(token)
    for p in range(lanes // PAIR):
        at = lanes_at(wide, p)
        kp = k[:, at]
        total = None
        for h, (qh, vh) in enumerate(zip(heads_of(q[:, at]), heads_of(v[:, at]))):
            prob = dot(qh, kp, 1, 1).astype(BF16) * m
            probs[group * (lanes // E) + 2 * p + h] = dot(kp, qh, 1, 1).astype(BF16) * mt
            term = dot(prob, vh, 1, 0)
            total = term if total is None else total + term
        attn[:, lanes_at(base, p)] = total


def head_mean(x):
    high, low = split(x)
    ones = spread(jnp.full((E, PAIR), 1.0 / E, BF16))
    return dot(jnp.concatenate([high, low], axis=1), jnp.concatenate([ones, ones], axis=0), 1, 0)


def side_by_side(state, part):
    sh, sl = split(state)
    ph, pll = split(part)
    left = jnp.concatenate([spread(sh), spread(sl)], axis=0)
    right = jnp.concatenate([spread(ph), spread(pll)], axis=0)
    return jnp.concatenate([left, right], axis=1)


def stacked(state, part):
    sh, sl = split(state)
    ph, pll = split(part)
    top = jnp.concatenate([spread(sh), spread(sl)], axis=1)
    bottom = jnp.concatenate([spread(ph), spread(pll)], axis=1)
    return jnp.concatenate([top, bottom], axis=0)


def on_rows(seg, table, last, part):
    rows, own, flag = edge(seg, table, last)
    met = part[0, part.shape[1] - EXTRA:part.shape[1] - EXTRA + 1] == own
    if last:
        met = met & (flag == 1)
    return rows.astype(F32) * met.astype(F32)


def norm_kernel(sel, core, q, dy, local, gain, seg, table, prefix, nxt, *rest):
    out, dab, part, gsum, total, token = rest[-6:]
    token[...] = jnp.zeros_like(token)
    lanes = out.shape[1]
    count = lanes // PAIR
    _, base, wide, row = place(sel, core, lanes, 1)
    on_next = on_rows(seg, table, True, nxt)
    last, own, flag = edge(seg, table, True)
    last = (last.astype(F32) * jnp.where(flag == 1, 1.0, 0.0)).astype(BF16)
    pairs = [slice(p * PAIR, (p + 1) * PAIR) for p in range(count)]
    bases = [lanes_at(base, p) for p in range(count)]
    wides = [lanes_at(wide, p) for p in range(count)]
    fars = [
        dot(twice(q[:, at]), side_by_side(prefix[rows_at(row, p)], nxt[0, rows_at(0, p)]), 1, 0)
        for p, at in enumerate(wides)
    ]
    attns = [local[:, at] + far[:, :PAIR] + on_next * far[:, PAIR:] for at, far in zip(bases, fars)]
    squares = [head_mean(attn * attn) for attn in attns]
    scales = [lax.rsqrt(square + 1e-06) for square in squares]
    normeds = [attn * scale for attn, scale in zip(attns, scales)]
    gas = [dy[:, at].astype(F32) * gain[:, pair] for at, pair in zip(wides, pairs)]
    means = [head_mean(ga * normed) for ga, normed in zip(gas, normeds)]
    das = [
        (scale * (ga - normed * mean)).astype(BF16)
        for scale, ga, normed, mean in zip(scales, gas, normeds, means)
    ]
    states = [state_pair(q[:, at], jnp.concatenate([da, da * last], axis=1)) for at, da in zip(wides, das)]
    part[0, count * E:] = jnp.broadcast_to(own, (EXTRA, PAIR))
    for p, (at, normed, da) in enumerate(zip(pairs, normeds, das)):
        total[rows_at(row, p)] = states[p][:, :PAIR]
        part[0, p * E:(p + 1) * E] = states[p][:, PAIR:]
        dab[:, bases[p]] = da
        out[:, at] = (normed * gain[:, at]).astype(BF16)
        gsum[0, p:p + 1] = jnp.sum(dy[:, wides[p]].astype(F32) * normed, axis=0, keepdims=True)


def inner_kernel(sel, core, q, k, v, dab, probs, mask, seg, table, prefix, nxt, *rest):
    gq, gk, gv, token = rest[-4:]
    lanes = dab.shape[1] // GROUPS
    count = lanes // SUB // PAIR
    group, base, wide, row = place(sel, core, lanes, SUB)
    m = mask[...]
    token[...] = jnp.zeros_like(token)
    on_next = on_rows(seg, table, True, nxt)
    first = row - group * (lanes // 2)
    for p in range(count):
        at = lanes_at(wide, p)
        da = dab[:, lanes_at(base, p)]
        vp = v[:, at]
        far = dot(twice(da), stacked(prefix[rows_at(row, p)], nxt[0, rows_at(first, p)]), 1, 1)
        tq = far[:, :PAIR] + on_next * far[:, PAIR:]
        tk = tv = None
        for h, (qh, kh, dh) in enumerate(zip(heads_of(q[:, at]), heads_of(k[:, at]), heads_of(da))):
            dprob = dot(dh, vp, 1, 1).astype(BF16) * m
            tq = tq + dot(dprob, kh, 1, 0)
            a = dot(dprob, qh, 0, 0)
            b = dot(probs[row // (E // 2) + 2 * p + h], dh, 1, 0)
            tk = a if tk is None else tk + a
            tv = b if tv is None else tv + b
        gq[:, p * PAIR:(p + 1) * PAIR] = tq.astype(BF16)
        gk[:, lanes_at(base, p)] = tk
        gv[:, lanes_at(base, p)] = tv


def outer_kernel(sel, core, k, v, gk_in, gv_in, seg, table, suffix, prv, *rest):
    gk, gv, token = rest[-3:]
    lanes = gk_in.shape[1] // GROUPS
    count = lanes // SUB // PAIR
    group, base, wide, row = place(sel, core, lanes, SUB)
    token[...] = jnp.zeros_like(token)
    on_prev = on_rows(seg, table, False, prv)
    first = row - group * (lanes // 2)
    for p in range(count):
        here, own, at = slice(p * PAIR, (p + 1) * PAIR), lanes_at(base, p), lanes_at(wide, p)
        s = suffix[rows_at(row, p)]
        g = prv[0, rows_at(first, p)]
        far = dot(twice(v[:, at]), stacked(s, g), 1, 1)
        gk[:, here] = (gk_in[:, own] + far[:, :PAIR] + on_prev * far[:, PAIR:]).astype(BF16)
        far = dot(twice(k[:, at]), side_by_side(s, g), 1, 0)
        gv[:, here] = (gv_in[:, own] + far[:, :PAIR] + on_prev * far[:, PAIR:]).astype(BF16)


def partner(x, axis, bit):
    route = [(i, i ^ (1 << bit)) for i in range(lax.axis_size(axis))]
    return lax.ppermute(x, axis, route)


def shifted(x, distance):
    count = lax.axis_size("ctx")
    return lax.ppermute(x, "ctx", [(i, i + distance) for i in range(count) if 0 <= i + distance < count])


def nought(x):
    return jnp.minimum(jnp.abs(x), 0.0)


def within_chip(keep, send):
    received = partner(send, "ctx", 0)
    return keep, received, keep + received


def to_cores(core, before, piece, towards):
    keep, received, _ = piece
    is_source = core == (0 if towards == 1 else 1)
    mine = jnp.where(is_source, before, before + received)
    return mine, partner(jnp.where(is_source, before + keep, before), "ctx", 0)


def pinned(x, space):
    return pltpu.with_memory_space_constraint(x, space)


def scatter_step(x, at, axis, bit):
    low, high = jnp.split(x, 2, axis=0 if x.shape[0] > 1 else 1)
    upper = (at >> bit & 1 == 1)[:, :low.shape[1]]
    return jnp.where(upper, high, low) + partner(jnp.where(upper, low, high), axis, bit)


def on_device(queries, keys, values, out_grad, segment_ids, image_flags, gain):
    rows, width = queries.shape[1:]
    q, k, v, dy = (x[0] for x in (queries, keys, values, out_grad))
    table = image_flags[0]
    gain_row = gain.reshape(1, width)
    ctx = lax.axis_index("ctx")
    core, ctx, dp = (x.reshape(1).astype(jnp.int32) for x in (ctx & 1, ctx, lax.axis_index("dp")))
    lanes = width // GROUPS // 2
    half_rows = lanes // PAIR * E
    heads = lanes // E

    def call(kernel, sel, ins, outs, after=(), alias=(), scratch=(), sub=1, steps=None, scalars=None):
        scalars = scalars or [core]

        def wide(i, c, *_):
            return (0, (i // sub * 2 + (sel + c[0]) % 2) * sub + i % sub)

        def whole(*args):
            return (0, 0)

        def part(i, c, *_):
            return (i // sub, 0, 0)

        specs = {
            "vmem": pl.BlockSpec(memory_space=pltpu.VMEM),
            "hbm": pl.BlockSpec(memory_space=pltpu.HBM),
            "wide": pl.BlockSpec((rows, lanes // sub), wide),
            "row": pl.BlockSpec((1, lanes // sub), wide),
            "sums": pl.BlockSpec((1, lanes // PAIR, PAIR), part),
            "zero": pl.BlockSpec((1, rows), whole),
            "all": pl.BlockSpec((GROUPS * half_rows, PAIR), whole),
            "part": pl.BlockSpec((1, half_rows + EXTRA, PAIR), part),
            "parts": pl.BlockSpec((GROUPS, half_rows + EXTRA, PAIR), lambda *args: (0, 0, 0)),
            "seg": pl.BlockSpec((1, rows), whole),
            "table": pl.BlockSpec((1, table.shape[0]), whole),
            "mask": pl.BlockSpec((rows, rows), whole),
            "token": pl.BlockSpec((1, PAIR), whole),
            "after2": pl.BlockSpec((8, PAIR), whole),
            "after3": pl.BlockSpec((1, 8, PAIR), lambda *args: (0, 0, 0)),
            "any": pl.BlockSpec(memory_space=pl.ANY),
        }
        shapes = {
            "wide": (rows, width),
            "sums": (GROUPS, lanes // PAIR, PAIR),
            "zero": (1, rows),
            "all": (GROUPS * half_rows, PAIR),
            "part": (GROUPS, half_rows + EXTRA, PAIR),
            "parts": (GROUPS, half_rows + EXTRA, PAIR),
            "token": (1, PAIR),
        }
        spaces = {"vmem": pltpu.VMEM, "hbm": pltpu.HBM}
        operands = [pinned(x, spaces[kind]) if kind in spaces else x for kind, x in ins] + list(after)
        kinds = [kind for kind, _ in ins] + [f"after{x.ndim}" for x in after]
        aliases = {}
        for out_at, x in alias:
            if x is not None:
                aliases[len(scalars) + len(operands)] = out_at
                operands.append(x)
                kinds.append("any")
        out_shape = [
            pltpu.VMEM(*shape, dtype) if kind == "vmem" else jax.ShapeDtypeStruct(shapes[kind], dtype)
            for kind, dtype, *shape in outs
        ]
        return pl.pallas_call(
            kernel,
            grid_spec=pltpu.PrefetchScalarGridSpec(
                num_scalar_prefetch=len(scalars),
                grid=steps or (GROUPS * sub,),
                in_specs=[specs[kind] for kind in kinds],
                out_specs=[specs[kind] for kind, *_ in outs],
                scratch_shapes=scratch,
            ),
            out_shape=out_shape,
            input_output_aliases=aliases,
            compiler_params=pltpu.CompilerParams(vmem_limit_bytes=VMEM),
            cost_estimate=pl.CostEstimate(flops=1, bytes_accessed=1, transcendentals=0),
        )(*scalars, *operands)

    edges = [("seg", segment_ids), ("table", image_flags)]
    chips = lax.axis_size("ctx") // 2
    whole, part_of = (rows, width), (rows, width // 2)

    def local_attn(sel, after):
        return call(
            functools.partial(local_kernel, sel), sel,
            [("vmem", q), ("vmem", k), ("vmem", v), ("mask", mask), ("mask", mask_t)],
            [("vmem", F32, part_of), ("vmem", BF16, (GROUPS * heads, rows, rows)), ("token", F32)], after=after)

    def norm(sel, before, after):
        return call(
            functools.partial(norm_kernel, sel), sel,
            [("vmem", q), ("vmem", dy), ("vmem", local[sel][0]), ("row", gain_row), *edges,
             ("all", prefix[sel]), ("part", nxt[sel])],
            [("wide", BF16), ("vmem", BF16, part_of), ("part", F32), ("sums", F32), ("all", F32), ("token", F32)],
            after=after, alias=[(0, before)])

    def inner(sel, before, after):
        return call(
            functools.partial(inner_kernel, sel), sel,
            [("vmem", q), ("vmem", k), ("vmem", v), ("vmem", norms[sel][1]), ("vmem", local[sel][1]), ("mask", mask),
             *edges, ("all", prefix[sel]), ("part", nxt[sel])],
            [("wide", BF16), ("vmem", F32, part_of), ("vmem", F32, part_of), ("token", F32)],
            after=after, alias=[(0, before)], sub=SUB)

    def outer(sel, before, after):
        return call(
            functools.partial(outer_kernel, sel), sel,
            [("vmem", k), ("vmem", v), ("vmem", inners[sel][1]), ("vmem", inners[sel][2]), *edges,
             ("all", suffix[sel]), ("part", prv[sel])],
            [("wide", BF16), ("wide", BF16), ("token", F32)], after=after, alias=list(enumerate(before)), sub=SUB)

    def summed_before(own, towards, works):
        load, before, span = own, None, 1
        while span < chips:
            arrived = shifted(load, 2 * towards * span)
            if works:
                arrived = arrived + works.pop(0)(load)
            before = arrived if before is None else before + arrived
            load = load + arrived
            span *= 2
        for work in works:
            before = before + work(load)
        return before

    keep, send, zero, k, v, core_row, ctx_row, dp_row = call(
        states_kernel, 0, [("hbm", k), ("hbm", v)],
        [("all", F32), ("all", F32), ("zero", jnp.int32), ("vmem", BF16, whole), ("vmem", BF16, whole)]
        + [("token", jnp.int32)] * 3,
        scratch=[pltpu.SemaphoreType.DMA((2 * GROUPS, 2))], steps=(1,), scalars=[core, ctx, dp])
    piece = within_chip(keep, send)
    seg = (segment_ids + zero)[0]
    onehot = seg[:, None] == jnp.arange(table.shape[0], dtype=jnp.int32)[None, :]
    img = jnp.sum(jnp.where(onehot, table[None, :], 0), axis=1)
    imgseg = jnp.where(img == 1, seg, -1)
    pos = jnp.arange(rows)
    mask = ((pos[:, None] >= pos[None, :]) | (imgseg[:, None] == seg[None, :])).astype(BF16)
    mask_t = ((pos[:, None] <= pos[None, :]) | (seg[:, None] == imgseg[None, :])).astype(BF16)

    parts = call(
        part_kernel, 0, [("hbm", q), ("hbm", dy), ("vmem", k), ("vmem", v), *edges],
        [("parts", F32)] * 2 + [("vmem", BF16, whole), ("vmem", BF16, whole), ("token", F32)],
        after=[piece[2]], scratch=[pltpu.SemaphoreType.DMA((2,))], steps=(1,))
    *parts, q, dy, _ = parts
    local, nxt = [], []

    def first_work(load):
        *made, token = local_attn(0, [parts[0]])
        local.append(made)
        return token

    def second_work(load):
        for part in reversed(parts):
            nxt.append(shifted(part + nought(load[:1]), -1))
        *made, token = local_attn(1, [load])
        local.append(made)
        return token

    before = summed_before(piece[2], 1, [first_work, second_work])
    prefix = to_cores(core_row, before, piece, 1)
    norms = [norm(0, None, [])]
    norms.append(norm(1, norms[0][0], [norms[0][4]]))
    output = norms[1][0]
    piece = within_chip(norms[0][4], norms[1][4])
    sums = [jnp.where(core_row == sel, norms[0][3], norms[1][3]) for sel in range(2)]
    gain_sum = [[jnp.stack(sums, axis=1).reshape(-1, PAIR)]]
    inners, prv = [], []

    def third_work(load):
        top = lax.axis_size("ctx").bit_length() - 2
        x = (gain_sum[0][0] + nought(load[:1])).reshape(4, 2, 2 * PAIR)
        x = scatter_step(x.swapaxes(0, 1).reshape(16, PAIR), ctx_row, "ctx", top)
        gain_sum.append(x)
        inners.append(inner(0, None, [load]))
        return inners[0][3]

    def fourth_work(load):
        for part in (norms[1][2], norms[0][2]):
            prv.append(shifted(part + nought(load[:1]), 1))
        inners.append(inner(1, inners[0][0], [load]))
        x = gain_sum[-1] + inners[1][3]
        for bit in (1, 0):
            x = scatter_step(x, dp_row, "dp", bit)
        gain_sum.append(x)
        return inners[1][3]

    before = summed_before(piece[2], -1, [third_work, fourth_work])
    suffix = to_cores(core_row, before, piece, -1)
    outers = outer(0, [None] * 2, [])
    grad_k, grad_v, _ = outer(1, outers[:2], [])
    grad_q = inners[1][0]
    grad_gain = gain_sum[-1]
    for bit in reversed(range(lax.axis_size("ctx").bit_length() - 2)):
        grad_gain = scatter_step(grad_gain, ctx_row, "ctx", bit)
    grad_gain = grad_gain.reshape(-1)
    return output[None], grad_q[None], grad_k[None], grad_v[None], grad_gain


def solution(mesh):
    return jax.shard_map(
        on_device,
        mesh=mesh,
        in_specs=(
            P("dp", "ctx", None),
            P("dp", "ctx", None),
            P("dp", "ctx", None),
            P("dp", "ctx", None),
            P("dp", "ctx"),
            P("dp", None),
            P(),
        ),
        out_specs=(
            P("dp", "ctx", None),
            P("dp", "ctx", None),
            P("dp", "ctx", None),
            P("dp", "ctx", None),
            P(("dp", "ctx")),
        ),
        check_vma=False,
    )
```

```python
import functools

import jax
import jax.numpy as jnp
from jax import lax
from jax.experimental import pallas as pl
from jax.experimental.pallas import tpu as pltpu
from jax.sharding import PartitionSpec as P

E = 64
PAIR = 2 * E
GROUPS = 2
EXTRA = 8
VMEM = 10 * 2**20
SUB = 2
F32 = jnp.float32
BF16 = jnp.bfloat16


def dot(a, b, ca, cb):
    return lax.dot_general(a, b, (((ca,), (cb,)), ((), ())), preferred_element_type=F32)


def low_lanes(rows, cols):
    lane = lax.broadcasted_iota(jnp.int32, (rows, cols), 1)
    return lane % PAIR < E


def fold(product):
    return jnp.where(low_lanes(E, product.shape[1]), product[:E], product[E:])


def split(state):
    high = state.astype(BF16)
    return high, (state - high.astype(F32)).astype(BF16)


def spread(state):
    low = low_lanes(*state.shape)
    zero = jnp.zeros_like(state)
    return jnp.concatenate([jnp.where(low, state, zero), jnp.where(low, zero, state)], axis=0)


def heads_of(pair):
    low = low_lanes(*pair.shape)
    zero = jnp.zeros_like(pair)
    return jnp.where(low, pair, zero), jnp.where(low, zero, pair)


def twice(x):
    return jnp.concatenate([x, x], axis=1)


def pair_at(ref, p):
    return ref[:, p * PAIR:(p + 1) * PAIR]


def rows_at(base, p):
    return pl.ds(pl.multiple_of(base + p * E, E), E)


def twice(x):
    return jnp.concatenate([x, x], axis=1)


def pair_at(ref, p):
    return ref[:, p * PAIR:(p + 1) * PAIR]


def rows_at(base, p):
    return pl.ds(pl.multiple_of(base + p * E, E), E)


def own_or_received(keep, received, own, p):
    return jnp.where(own, keep[rows_at(p)], received[rows_at(p)])


def state_pair(a, b):
    return fold(dot(a, b, 0, 0))


def edge(seg, table, last):
    row = seg[...]
    count = row.shape[1]
    own = row[:, count - 1:] if last else row[:, :1]
    size = jnp.sum((row == own).astype(F32), axis=1, keepdims=True)
    at = lax.broadcasted_iota(jnp.int32, (count, PAIR), 0).astype(F32)
    rows = at >= count - size if last else at < size
    ids = lax.broadcasted_iota(jnp.int32, table.shape, 1)
    flag = jnp.sum(jnp.where(ids == own, table[...], 0).astype(F32), axis=1, keepdims=True)
    return rows, own.astype(F32), flag


def lanes_at(base, p):
    return pl.ds(pl.multiple_of(base + p * PAIR, PAIR), PAIR)


def place(sel, core, lanes, sub):
    step = pl.program_id(0)
    group, part = step // sub, step % sub
    half = (sel + core[0]) % 2
    base = group * lanes + part * (lanes // sub)
    return group, base, base + (group + half) * lanes, base // PAIR * E


def states_kernel(core, ctx, dp, k_in, v_in, keep, send, zero, k, v, core_row, ctx_row, dp_row, sems):
    for row, index in ((core_row, core), (ctx_row, ctx), (dp_row, dp)):
        row[...] = jnp.full(row.shape, index[0], jnp.int32)
    lanes = k.shape[1] // GROUPS // 2
    count = lanes // PAIR
    copies = []
    for sel in (1, 0):
        for group in range(GROUPS):
            base = (2 * group + (sel + core[0]) % 2) * lanes
            at = pl.ds(pl.multiple_of(base, lanes), lanes)
            for i, (array, buf) in enumerate(((k_in, k), (v_in, v))):
                copies.append(pltpu.make_async_copy(array.at[:, at], buf.at[:, at], sems.at[2 * group + sel, i]))
    for copy in copies:
        copy.start()
    zero[...] = jnp.zeros_like(zero)
    for sel, out in ((1, send), (0, keep)):
        for group in range(GROUPS):
            copies.pop(0).wait()
            copies.pop(0).wait()
            base = (2 * group + (sel + core[0]) % 2) * lanes
            for p in range(count):
                at = lanes_at(base, p)
                row = (group * count + p) * E
                out[row:row + E] = state_pair(k[:, at], v[:, at])


def part_kernel(core, q_in, dy_in, k, v, seg, table, *rest):
    *outs, q, dy, token, sems = rest[-6:]
    copies = [pltpu.make_async_copy(a, b, sems.at[i]) for i, (a, b) in enumerate(((q_in, q), (dy_in, dy)))]
    for copy in copies:
        copy.start()
    token[...] = jnp.zeros_like(token)
    lanes = k.shape[1] // GROUPS // 2
    count = lanes // PAIR
    rows, own, _ = edge(seg, table, False)
    keep = rows.astype(BF16)
    for sel, out in enumerate(outs):
        for group in range(GROUPS):
            base = (2 * group + (sel + core[0]) % 2) * lanes
            for p in range(count):
                at = lanes_at(base, p)
                out[group, p * E:(p + 1) * E] = state_pair(k[:, at], v[:, at] * keep)
            out[group, count * E:] = jnp.broadcast_to(own, (EXTRA, PAIR))
    for copy in copies:
        copy.wait()


def local_kernel(sel, core, q, k, v, mask, mask_t, *rest):
    attn, probs, token = rest[-3:]
    lanes = attn.shape[1] // GROUPS
    group, base, wide, _ = place(sel, core, lanes, 1)
    m, mt = mask[...], mask_t[...]
    token[...] = jnp.zeros_like(token)
    for p in range(lanes // PAIR):
        at = lanes_at(wide, p)
        kp = k[:, at]
        total = None
        for h, (qh, vh) in enumerate(zip(heads_of(q[:, at]), heads_of(v[:, at]))):
            prob = dot(qh, kp, 1, 1).astype(BF16) * m
            probs[group * (lanes // E) + 2 * p + h] = dot(kp, qh, 1, 1).astype(BF16) * mt
            term = dot(prob, vh, 1, 0)
            total = term if total is None else total + term
        attn[:, lanes_at(base, p)] = total


def head_mean(x):
    high, low = split(x)
    ones = spread(jnp.full((E, PAIR), 1.0 / E, BF16))
    return dot(jnp.concatenate([high, low], axis=1), jnp.concatenate([ones, ones], axis=0), 1, 0)


def side_by_side(state, part):
    sh, sl = split(state)
    ph, pll = split(part)
    left = jnp.concatenate([spread(sh), spread(sl)], axis=0)
    right = jnp.concatenate([spread(ph), spread(pll)], axis=0)
    return jnp.concatenate([left, right], axis=1)


def stacked(state, part):
    sh, sl = split(state)
    ph, pll = split(part)
    top = jnp.concatenate([spread(sh), spread(sl)], axis=1)
    bottom = jnp.concatenate([spread(ph), spread(pll)], axis=1)
    return jnp.concatenate([top, bottom], axis=0)


def on_rows(seg, table, last, part):
    rows, own, flag = edge(seg, table, last)
    met = part[0, part.shape[1] - EXTRA:part.shape[1] - EXTRA + 1] == own
    if last:
        met = met & (flag == 1)
    return rows.astype(F32) * met.astype(F32)


def norm_kernel(sel, core, q, dy, local, gain, seg, table, prefix, nxt, *rest):
    out, dab, part, gsum, total, token = rest[-6:]
    token[...] = jnp.zeros_like(token)
    lanes = out.shape[1]
    count = lanes // PAIR
    _, base, wide, row = place(sel, core, lanes, 1)
    on_next = on_rows(seg, table, True, nxt)
    last, own, flag = edge(seg, table, True)
    last = (last.astype(F32) * jnp.where(flag == 1, 1.0, 0.0)).astype(BF16)
    pairs = [slice(p * PAIR, (p + 1) * PAIR) for p in range(count)]
    bases = [lanes_at(base, p) for p in range(count)]
    wides = [lanes_at(wide, p) for p in range(count)]
    fars = [
        dot(twice(q[:, at]), side_by_side(prefix[rows_at(row, p)], nxt[0, rows_at(0, p)]), 1, 0)
        for p, at in enumerate(wides)
    ]
    attns = [local[:, at] + far[:, :PAIR] + on_next * far[:, PAIR:] for at, far in zip(bases, fars)]
    squares = [head_mean(attn * attn) for attn in attns]
    scales = [lax.rsqrt(square + 1e-06) for square in squares]
    normeds = [attn * scale for attn, scale in zip(attns, scales)]
    gas = [dy[:, at].astype(F32) * gain[:, pair] for at, pair in zip(wides, pairs)]
    means = [head_mean(ga * normed) for ga, normed in zip(gas, normeds)]
    das = [
        (scale * (ga - normed * mean)).astype(BF16)
        for scale, ga, normed, mean in zip(scales, gas, normeds, means)
    ]
    states = [state_pair(q[:, at], jnp.concatenate([da, da * last], axis=1)) for at, da in zip(wides, das)]
    part[0, count * E:] = jnp.broadcast_to(own, (EXTRA, PAIR))
    for p, (at, normed, da) in enumerate(zip(pairs, normeds, das)):
        total[rows_at(row, p)] = states[p][:, :PAIR]
        part[0, p * E:(p + 1) * E] = states[p][:, PAIR:]
        dab[:, bases[p]] = da
        out[:, at] = (normed * gain[:, at]).astype(BF16)
        gsum[0, p:p + 1] = jnp.sum(dy[:, wides[p]].astype(F32) * normed, axis=0, keepdims=True)


def inner_kernel(sel, core, q, k, v, dab, probs, mask, seg, table, prefix, nxt, *rest):
    gq, gk, gv, token = rest[-4:]
    lanes = dab.shape[1] // GROUPS
    count = lanes // SUB // PAIR
    group, base, wide, row = place(sel, core, lanes, SUB)
    m = mask[...]
    token[...] = jnp.zeros_like(token)
    on_next = on_rows(seg, table, True, nxt)
    first = row - group * (lanes // 2)
    for p in range(count):
        at = lanes_at(wide, p)
        da = dab[:, lanes_at(base, p)]
        vp = v[:, at]
        far = dot(twice(da), stacked(prefix[rows_at(row, p)], nxt[0, rows_at(first, p)]), 1, 1)
        tq = far[:, :PAIR] + on_next * far[:, PAIR:]
        tk = tv = None
        for h, (qh, kh, dh) in enumerate(zip(heads_of(q[:, at]), heads_of(k[:, at]), heads_of(da))):
            dprob = dot(dh, vp, 1, 1).astype(BF16) * m
            tq = tq + dot(dprob, kh, 1, 0)
            a = dot(dprob, qh, 0, 0)
            b = dot(probs[row // (E // 2) + 2 * p + h], dh, 1, 0)
            tk = a if tk is None else tk + a
            tv = b if tv is None else tv + b
        gq[:, p * PAIR:(p + 1) * PAIR] = tq.astype(BF16)
        gk[:, lanes_at(base, p)] = tk
        gv[:, lanes_at(base, p)] = tv


def outer_kernel(sel, core, k, v, gk_in, gv_in, seg, table, suffix, prv, *rest):
    gk, gv, token = rest[-3:]
    lanes = gk_in.shape[1] // GROUPS
    count = lanes // SUB // PAIR
    group, base, wide, row = place(sel, core, lanes, SUB)
    token[...] = jnp.zeros_like(token)
    on_prev = on_rows(seg, table, False, prv)
    first = row - group * (lanes // 2)
    for p in range(count):
        here, own, at = slice(p * PAIR, (p + 1) * PAIR), lanes_at(base, p), lanes_at(wide, p)
        s = suffix[rows_at(row, p)]
        g = prv[0, rows_at(first, p)]
        far = dot(twice(v[:, at]), stacked(s, g), 1, 1)
        gk[:, here] = (gk_in[:, own] + far[:, :PAIR] + on_prev * far[:, PAIR:]).astype(BF16)
        far = dot(twice(k[:, at]), side_by_side(s, g), 1, 0)
        gv[:, here] = (gv_in[:, own] + far[:, :PAIR] + on_prev * far[:, PAIR:]).astype(BF16)


def partner(x, axis, bit):
    route = [(i, i ^ (1 << bit)) for i in range(lax.axis_size(axis))]
    return lax.ppermute(x, axis, route)


def shifted(x, distance):
    count = lax.axis_size("ctx")
    return lax.ppermute(x, "ctx", [(i, i + distance) for i in range(count) if 0 <= i + distance < count])


def nought(x):
    return jnp.minimum(jnp.abs(x), 0.0)


def within_chip(keep, send):
    received = partner(send, "ctx", 0)
    return keep, received, keep + received


def to_cores(core, before, piece, towards):
    keep, received, _ = piece
    is_source = core == (0 if towards == 1 else 1)
    mine = jnp.where(is_source, before, before + received)
    return mine, partner(jnp.where(is_source, before + keep, before), "ctx", 0)


def pinned(x, space):
    return pltpu.with_memory_space_constraint(x, space)


def scatter_step(x, at, axis, bit):
    low, high = jnp.split(x, 2, axis=0 if x.shape[0] > 1 else 1)
    upper = (at >> bit & 1 == 1)[:, :low.shape[-1]]
    return jnp.where(upper, high, low) + partner(jnp.where(upper, low, high), axis, bit)


def on_device(queries, keys, values, out_grad, segment_ids, image_flags, gain):
    rows, width = queries.shape[1:]
    q, k, v, dy = (x[0] for x in (queries, keys, values, out_grad))
    table = image_flags[0]
    gain_row = gain.reshape(1, width)
    ctx = lax.axis_index("ctx")
    core, ctx, dp = (x.reshape(1).astype(jnp.int32) for x in (ctx & 1, ctx, lax.axis_index("dp")))
    lanes = width // GROUPS // 2
    half_rows = lanes // PAIR * E
    heads = lanes // E

    def call(kernel, sel, ins, outs, after=(), alias=(), scratch=(), sub=1, steps=None, scalars=None):
        scalars = scalars or [core]

        def wide(i, c, *_):
            return (0, (i // sub * 2 + (sel + c[0]) % 2) * sub + i % sub)

        def whole(*args):
            return (0, 0)

        def part(i, c, *_):
            return (i // sub, 0, 0)

        specs = {
            "vmem": pl.BlockSpec(memory_space=pltpu.VMEM),
            "hbm": pl.BlockSpec(memory_space=pltpu.HBM),
            "wide": pl.BlockSpec((rows, lanes // sub), wide),
            "row": pl.BlockSpec((1, lanes // sub), wide),
            "sums": pl.BlockSpec((1, lanes // PAIR, PAIR), part),
            "zero": pl.BlockSpec((1, rows), whole),
            "all": pl.BlockSpec((GROUPS * half_rows, PAIR), whole),
            "part": pl.BlockSpec((1, half_rows + EXTRA, PAIR), part),
            "parts": pl.BlockSpec((GROUPS, half_rows + EXTRA, PAIR), lambda *args: (0, 0, 0)),
            "seg": pl.BlockSpec((1, rows), whole),
            "table": pl.BlockSpec((1, table.shape[0]), whole),
            "mask": pl.BlockSpec((rows, rows), whole),
            "token": pl.BlockSpec((1, PAIR), whole),
            "after2": pl.BlockSpec((8, PAIR), whole),
            "after3": pl.BlockSpec((1, 8, PAIR), lambda *args: (0, 0, 0)),
            "any": pl.BlockSpec(memory_space=pl.ANY),
        }
        shapes = {
            "wide": (rows, width),
            "sums": (GROUPS, lanes // PAIR, PAIR),
            "zero": (1, rows),
            "all": (GROUPS * half_rows, PAIR),
            "part": (GROUPS, half_rows + EXTRA, PAIR),
            "parts": (GROUPS, half_rows + EXTRA, PAIR),
            "token": (1, PAIR),
        }
        spaces = {"vmem": pltpu.VMEM, "hbm": pltpu.HBM}
        operands = [pinned(x, spaces[kind]) if kind in spaces else x for kind, x in ins] + list(after)
        kinds = [kind for kind, _ in ins] + [f"after{x.ndim}" for x in after]
        aliases = {}
        for out_at, x in alias:
            if x is not None:
                aliases[len(scalars) + len(operands)] = out_at
                operands.append(x)
                kinds.append("any")
        out_shape = [
            pltpu.VMEM(*shape, dtype) if kind == "vmem" else jax.ShapeDtypeStruct(shapes[kind], dtype)
            for kind, dtype, *shape in outs
        ]
        return pl.pallas_call(
            kernel,
            grid_spec=pltpu.PrefetchScalarGridSpec(
                num_scalar_prefetch=len(scalars),
                grid=steps or (GROUPS * sub,),
                in_specs=[specs[kind] for kind in kinds],
                out_specs=[specs[kind] for kind, *_ in outs],
                scratch_shapes=scratch,
            ),
            out_shape=out_shape,
            input_output_aliases=aliases,
            compiler_params=pltpu.CompilerParams(vmem_limit_bytes=VMEM),
            cost_estimate=pl.CostEstimate(flops=1, bytes_accessed=1, transcendentals=0),
        )(*scalars, *operands)

    edges = [("seg", segment_ids), ("table", image_flags)]
    chips = lax.axis_size("ctx") // 2
    whole, part_of = (rows, width), (rows, width // 2)

    def local_attn(sel, after):
        return call(
            functools.partial(local_kernel, sel), sel,
            [("vmem", q), ("vmem", k), ("vmem", v), ("mask", mask), ("mask", mask_t)],
            [("vmem", F32, part_of), ("vmem", BF16, (GROUPS * heads, rows, rows)), ("token", F32)], after=after)

    def norm(sel, before, after):
        return call(
            functools.partial(norm_kernel, sel), sel,
            [("vmem", q), ("vmem", dy), ("vmem", local[sel][0]), ("row", gain_row), *edges,
             ("all", prefix[sel]), ("part", nxt[sel])],
            [("wide", BF16), ("vmem", BF16, part_of), ("part", F32), ("sums", F32), ("all", F32), ("token", F32)],
            after=after, alias=[(0, before)])

    def inner(sel, before, after):
        return call(
            functools.partial(inner_kernel, sel), sel,
            [("vmem", q), ("vmem", k), ("vmem", v), ("vmem", norms[sel][1]), ("vmem", local[sel][1]), ("mask", mask),
             *edges, ("all", prefix[sel]), ("part", nxt[sel])],
            [("wide", BF16), ("vmem", F32, part_of), ("vmem", F32, part_of), ("token", F32)],
            after=after, alias=[(0, before)], sub=SUB)

    def outer(sel, before, after):
        return call(
            functools.partial(outer_kernel, sel), sel,
            [("vmem", k), ("vmem", v), ("vmem", inners[sel][1]), ("vmem", inners[sel][2]), *edges,
             ("all", suffix[sel]), ("part", prv[sel])],
            [("wide", BF16), ("wide", BF16), ("token", F32)], after=after, alias=list(enumerate(before)), sub=SUB)

    def summed_before(own, towards, works):
        load, before, span = own, None, 1
        while span < chips:
            arrived = shifted(load, 2 * towards * span)
            if works:
                arrived = arrived + works.pop(0)(load)
            before = arrived if before is None else before + arrived
            load = load + arrived
            span *= 2
        for work in works:
            before = before + work(load)
        return before

    keep, send, zero, k, v, core_row, ctx_row, dp_row = call(
        states_kernel, 0, [("hbm", k), ("hbm", v)],
        [("all", F32), ("all", F32), ("zero", jnp.int32), ("vmem", BF16, whole), ("vmem", BF16, whole)]
        + [("token", jnp.int32)] * 3,
        scratch=[pltpu.SemaphoreType.DMA((2 * GROUPS, 2))], steps=(1,), scalars=[core, ctx, dp])
    piece = within_chip(keep, send)
    seg = (segment_ids + zero)[0]
    onehot = seg[:, None] == jnp.arange(table.shape[0], dtype=jnp.int32)[None, :]
    img = jnp.sum(jnp.where(onehot, table[None, :], 0), axis=1)
    imgseg = jnp.where(img == 1, seg, -1)
    pos = jnp.arange(rows)
    mask = ((pos[:, None] >= pos[None, :]) | (imgseg[:, None] == seg[None, :])).astype(BF16)
    mask_t = ((pos[:, None] <= pos[None, :]) | (seg[:, None] == imgseg[None, :])).astype(BF16)

    parts = call(
        part_kernel, 0, [("hbm", q), ("hbm", dy), ("vmem", k), ("vmem", v), *edges],
        [("parts", F32)] * 2 + [("vmem", BF16, whole), ("vmem", BF16, whole), ("token", F32)],
        after=[piece[2]], scratch=[pltpu.SemaphoreType.DMA((2,))], steps=(1,))
    *parts, q, dy, _ = parts
    local, nxt = [], []

    def first_work(load):
        *made, token = local_attn(0, [parts[0]])
        local.append(made)
        return token

    def second_work(load):
        for part in reversed(parts):
            nxt.append(shifted(part + nought(load[:1]), -1))
        *made, token = local_attn(1, [load])
        local.append(made)
        return token

    before = summed_before(piece[2], 1, [first_work, second_work])
    prefix = to_cores(core_row, before, piece, 1)
    norms = [norm(0, None, [])]
    norms.append(norm(1, norms[0][0], [norms[0][4]]))
    output = norms[1][0]
    piece = within_chip(norms[0][4], norms[1][4])
    gain_sum = [jnp.concatenate([jnp.where(core_row == half, norms[0][3], norms[1][3]) for half in range(2)], axis=0)]
    gain_sum.append(scatter_step(gain_sum[-1], dp_row, "dp", 0))
    bits = list(reversed(range(lax.axis_size("ctx").bit_length() - 1)))
    inners, prv = [], []

    def third_work(load):
        x = scatter_step(gain_sum[-1] + nought(load[:1]), dp_row, "dp", 1)
        gain_sum.append(x.reshape(-1, PAIR))
        inners.append(inner(0, None, [load]))
        return inners[0][3]

    def fourth_work(load):
        gain_sum.append(scatter_step(gain_sum[-1] + nought(load[:1]), ctx_row, "ctx", bits[0]))
        for part in (norms[1][2], norms[0][2]):
            prv.append(shifted(part + nought(load[:1]), 1))
        inners.append(inner(1, inners[0][0], [load]))
        return inners[1][3]

    before = summed_before(piece[2], -1, [third_work, fourth_work])
    suffix = to_cores(core_row, before, piece, -1)
    outers = outer(0, [None] * 2, [])
    grad_gain = gain_sum[-1] + outers[2]
    for bit in bits[1:]:
        grad_gain = scatter_step(grad_gain, ctx_row, "ctx", bit)
    grad_k, grad_v, _ = outer(1, outers[:2], [])
    grad_gain = grad_gain.reshape(-1)
    grad_q = inners[1][0]
    return output[None], grad_q[None], grad_k[None], grad_v[None], grad_gain


def solution(mesh):
    return jax.shard_map(
        on_device,
        mesh=mesh,
        in_specs=(
            P("dp", "ctx", None),
            P("dp", "ctx", None),
            P("dp", "ctx", None),
            P("dp", "ctx", None),
            P("dp", "ctx"),
            P("dp", None),
            P(),
        ),
        out_specs=(
            P("dp", "ctx", None),
            P("dp", "ctx", None),
            P("dp", "ctx", None),
            P("dp", "ctx", None),
            P(("dp", "ctx")),
        ),
        check_vma=False,
    )
```

```python
import functools

import jax
import jax.numpy as jnp
from jax import lax
from jax.experimental import pallas as pl
from jax.experimental.pallas import tpu as pltpu
from jax.sharding import PartitionSpec as P

E = 64
PAIR = 2 * E
GROUPS = 2
EXTRA = 8
VMEM = 10 * 2**20
SUB = 2
F32 = jnp.float32
BF16 = jnp.bfloat16


def dot(a, b, ca, cb):
    return lax.dot_general(a, b, (((ca,), (cb,)), ((), ())), preferred_element_type=F32)


def low_lanes(rows, cols):
    lane = lax.broadcasted_iota(jnp.int32, (rows, cols), 1)
    return lane % PAIR < E


def fold(product):
    return jnp.where(low_lanes(E, product.shape[1]), product[:E], product[E:])


def split(state):
    high = state.astype(BF16)
    return high, (state - high.astype(F32)).astype(BF16)


def spread(state):
    low = low_lanes(*state.shape)
    zero = jnp.zeros_like(state)
    return jnp.concatenate([jnp.where(low, state, zero), jnp.where(low, zero, state)], axis=0)


def heads_of(pair):
    low = low_lanes(*pair.shape)
    zero = jnp.zeros_like(pair)
    return jnp.where(low, pair, zero), jnp.where(low, zero, pair)


def twice(x):
    return jnp.concatenate([x, x], axis=1)


def pair_at(ref, p):
    return ref[:, p * PAIR:(p + 1) * PAIR]


def rows_at(base, p):
    return pl.ds(pl.multiple_of(base + p * E, E), E)


def twice(x):
    return jnp.concatenate([x, x], axis=1)


def pair_at(ref, p):
    return ref[:, p * PAIR:(p + 1) * PAIR]


def rows_at(base, p):
    return pl.ds(pl.multiple_of(base + p * E, E), E)


def own_or_received(keep, received, own, p):
    return jnp.where(own, keep[rows_at(p)], received[rows_at(p)])


def state_pair(a, b):
    return fold(dot(a, b, 0, 0))


def edge(seg, table, last):
    row = seg[...]
    count = row.shape[1]
    own = row[:, count - 1:] if last else row[:, :1]
    size = jnp.sum((row == own).astype(F32), axis=1, keepdims=True)
    at = lax.broadcasted_iota(jnp.int32, (count, PAIR), 0).astype(F32)
    rows = at >= count - size if last else at < size
    ids = lax.broadcasted_iota(jnp.int32, table.shape, 1)
    flag = jnp.sum(jnp.where(ids == own, table[...], 0).astype(F32), axis=1, keepdims=True)
    return rows, own.astype(F32), flag


def lanes_at(base, p):
    return pl.ds(pl.multiple_of(base + p * PAIR, PAIR), PAIR)


def place(sel, core, lanes, sub):
    step = pl.program_id(0)
    group, part = step // sub, step % sub
    half = (sel + core[0]) % 2
    base = group * lanes + part * (lanes // sub)
    return group, base, base + (group + half) * lanes, base // PAIR * E


def states_kernel(core, ctx, dp, k_in, v_in, keep, send, zero, k, v, core_row, ctx_row, dp_row, sems):
    for row, index in ((core_row, core), (ctx_row, ctx), (dp_row, dp)):
        row[...] = jnp.full(row.shape, index[0], jnp.int32)
    lanes = k.shape[1] // GROUPS // 2
    count = lanes // PAIR
    copies = []
    for sel in (1, 0):
        for group in range(GROUPS):
            base = (2 * group + (sel + core[0]) % 2) * lanes
            at = pl.ds(pl.multiple_of(base, lanes), lanes)
            for i, (array, buf) in enumerate(((k_in, k), (v_in, v))):
                copies.append(pltpu.make_async_copy(array.at[:, at], buf.at[:, at], sems.at[2 * group + sel, i]))
    for copy in copies:
        copy.start()
    zero[...] = jnp.zeros_like(zero)
    for sel, out in ((1, send), (0, keep)):
        for group in range(GROUPS):
            copies.pop(0).wait()
            copies.pop(0).wait()
            base = (2 * group + (sel + core[0]) % 2) * lanes
            for p in range(count):
                at = lanes_at(base, p)
                row = (group * count + p) * E
                out[row:row + E] = state_pair(k[:, at], v[:, at])


def part_kernel(core, q_in, dy_in, k, v, seg, table, *rest):
    *outs, q, dy, token, sems = rest[-6:]
    copies = [pltpu.make_async_copy(a, b, sems.at[i]) for i, (a, b) in enumerate(((q_in, q), (dy_in, dy)))]
    for copy in copies:
        copy.start()
    token[...] = jnp.zeros_like(token)
    lanes = k.shape[1] // GROUPS // 2
    count = lanes // PAIR
    rows, own, _ = edge(seg, table, False)
    keep = rows.astype(BF16)
    for sel, out in enumerate(outs):
        for group in range(GROUPS):
            base = (2 * group + (sel + core[0]) % 2) * lanes
            for p in range(count):
                at = lanes_at(base, p)
                out[group, p * E:(p + 1) * E] = state_pair(k[:, at], v[:, at] * keep)
            out[group, count * E:] = jnp.broadcast_to(own, (EXTRA, PAIR))
    for copy in copies:
        copy.wait()


def local_kernel(sel, core, q, k, v, mask, mask_t, *rest):
    attn, probs, token = rest[-3:]
    lanes = attn.shape[1] // GROUPS
    group, base, wide, _ = place(sel, core, lanes, 1)
    m, mt = mask[...], mask_t[...]
    token[...] = jnp.zeros_like(token)
    for p in range(lanes // PAIR):
        at = lanes_at(wide, p)
        kp = k[:, at]
        total = None
        for h, (qh, vh) in enumerate(zip(heads_of(q[:, at]), heads_of(v[:, at]))):
            prob = dot(qh, kp, 1, 1).astype(BF16) * m
            probs[group * (lanes // E) + 2 * p + h] = dot(kp, qh, 1, 1).astype(BF16) * mt
            term = dot(prob, vh, 1, 0)
            total = term if total is None else total + term
        attn[:, lanes_at(base, p)] = total


def head_mean(x):
    high, low = split(x)
    ones = spread(jnp.full((E, PAIR), 1.0 / E, BF16))
    return dot(jnp.concatenate([high, low], axis=1), jnp.concatenate([ones, ones], axis=0), 1, 0)


def side_by_side(state, part):
    sh, sl = split(state)
    ph, pll = split(part)
    left = jnp.concatenate([spread(sh), spread(sl)], axis=0)
    right = jnp.concatenate([spread(ph), spread(pll)], axis=0)
    return jnp.concatenate([left, right], axis=1)


def stacked(state, part):
    sh, sl = split(state)
    ph, pll = split(part)
    top = jnp.concatenate([spread(sh), spread(sl)], axis=1)
    bottom = jnp.concatenate([spread(ph), spread(pll)], axis=1)
    return jnp.concatenate([top, bottom], axis=0)


def on_rows(seg, table, last, part):
    rows, own, flag = edge(seg, table, last)
    met = part[0, part.shape[1] - EXTRA:part.shape[1] - EXTRA + 1] == own
    if last:
        met = met & (flag == 1)
    return rows.astype(F32) * met.astype(F32)


def norm_kernel(sel, core, q, dy, local, gain, seg, table, prefix, nxt, *rest):
    out, dab, part, gsum, total, token = rest[-6:]
    token[...] = jnp.zeros_like(token)
    lanes = out.shape[1]
    count = lanes // PAIR
    _, base, wide, row = place(sel, core, lanes, 1)
    on_next = on_rows(seg, table, True, nxt)
    last, own, flag = edge(seg, table, True)
    last = (last.astype(F32) * jnp.where(flag == 1, 1.0, 0.0)).astype(BF16)
    pairs = [slice(p * PAIR, (p + 1) * PAIR) for p in range(count)]
    bases = [lanes_at(base, p) for p in range(count)]
    wides = [lanes_at(wide, p) for p in range(count)]
    fars = [
        dot(twice(q[:, at]), side_by_side(prefix[rows_at(row, p)], nxt[0, rows_at(0, p)]), 1, 0)
        for p, at in enumerate(wides)
    ]
    attns = [local[:, at] + far[:, :PAIR] + on_next * far[:, PAIR:] for at, far in zip(bases, fars)]
    squares = [head_mean(attn * attn) for attn in attns]
    scales = [lax.rsqrt(square + 1e-06) for square in squares]
    normeds = [attn * scale for attn, scale in zip(attns, scales)]
    gas = [dy[:, at].astype(F32) * gain[:, pair] for at, pair in zip(wides, pairs)]
    means = [head_mean(ga * normed) for ga, normed in zip(gas, normeds)]
    das = [
        (scale * (ga - normed * mean)).astype(BF16)
        for scale, ga, normed, mean in zip(scales, gas, normeds, means)
    ]
    states = [state_pair(q[:, at], jnp.concatenate([da, da * last], axis=1)) for at, da in zip(wides, das)]
    part[0, count * E:] = jnp.broadcast_to(own, (EXTRA, PAIR))
    for p, (at, normed, da) in enumerate(zip(pairs, normeds, das)):
        total[rows_at(row, p)] = states[p][:, :PAIR]
        part[0, p * E:(p + 1) * E] = states[p][:, PAIR:]
        dab[:, bases[p]] = da
        out[:, at] = (normed * gain[:, at]).astype(BF16)
        gsum[0, p:p + 1] = jnp.sum(dy[:, wides[p]].astype(F32) * normed, axis=0, keepdims=True)


def inner_kernel(sel, core, q, k, v, dab, probs, mask, seg, table, prefix, nxt, *rest):
    gq, gk, gv, token = rest[-4:]
    lanes = dab.shape[1] // GROUPS
    count = lanes // SUB // PAIR
    group, base, wide, row = place(sel, core, lanes, SUB)
    m = mask[...]
    token[...] = jnp.zeros_like(token)
    on_next = on_rows(seg, table, True, nxt)
    first = row - group * (lanes // 2)
    for p in range(count):
        at = lanes_at(wide, p)
        da = dab[:, lanes_at(base, p)]
        vp = v[:, at]
        far = dot(twice(da), stacked(prefix[rows_at(row, p)], nxt[0, rows_at(first, p)]), 1, 1)
        tq = far[:, :PAIR] + on_next * far[:, PAIR:]
        tk = tv = None
        for h, (qh, kh, dh) in enumerate(zip(heads_of(q[:, at]), heads_of(k[:, at]), heads_of(da))):
            dprob = dot(dh, vp, 1, 1).astype(BF16) * m
            tq = tq + dot(dprob, kh, 1, 0)
            a = dot(dprob, qh, 0, 0)
            b = dot(probs[row // (E // 2) + 2 * p + h], dh, 1, 0)
            tk = a if tk is None else tk + a
            tv = b if tv is None else tv + b
        gq[:, p * PAIR:(p + 1) * PAIR] = tq.astype(BF16)
        gk[:, lanes_at(base, p)] = tk
        gv[:, lanes_at(base, p)] = tv


def outer_kernel(sel, core, k, v, gk_in, gv_in, seg, table, suffix, prv, *rest):
    gk, gv, token = rest[-3:]
    lanes = gk_in.shape[1] // GROUPS
    count = lanes // SUB // PAIR
    group, base, wide, row = place(sel, core, lanes, SUB)
    token[...] = jnp.zeros_like(token)
    on_prev = on_rows(seg, table, False, prv)
    first = row - group * (lanes // 2)
    for p in range(count):
        here, own, at = slice(p * PAIR, (p + 1) * PAIR), lanes_at(base, p), lanes_at(wide, p)
        s = suffix[rows_at(row, p)]
        g = prv[0, rows_at(first, p)]
        far = dot(twice(v[:, at]), stacked(s, g), 1, 1)
        gk[:, here] = (gk_in[:, own] + far[:, :PAIR] + on_prev * far[:, PAIR:]).astype(BF16)
        far = dot(twice(k[:, at]), side_by_side(s, g), 1, 0)
        gv[:, here] = (gv_in[:, own] + far[:, :PAIR] + on_prev * far[:, PAIR:]).astype(BF16)


def partner(x, axis, bit):
    route = [(i, i ^ (1 << bit)) for i in range(lax.axis_size(axis))]
    return lax.ppermute(x, axis, route)


def shifted(x, distance):
    count = lax.axis_size("ctx")
    return lax.ppermute(x, "ctx", [(i, i + distance) for i in range(count) if 0 <= i + distance < count])


def nought(x):
    return jnp.minimum(jnp.abs(x), 0.0)


def within_chip(keep, send):
    received = partner(send, "ctx", 0)
    return keep, received, keep + received


def to_cores(core, before, piece, towards):
    keep, received, _ = piece
    is_source = core == (0 if towards == 1 else 1)
    mine = jnp.where(is_source, before, before + received)
    return mine, partner(jnp.where(is_source, before + keep, before), "ctx", 0)


def pinned(x, space):
    return pltpu.with_memory_space_constraint(x, space)


def scatter_step(x, at, axis, bit):
    low, high = jnp.split(x, 2, axis=0 if x.shape[0] > 1 else 1)
    upper = (at >> bit & 1 == 1)[:, :low.shape[-1]]
    return jnp.where(upper, high, low) + partner(jnp.where(upper, low, high), axis, bit)


def on_device(queries, keys, values, out_grad, segment_ids, image_flags, gain):
    rows, width = queries.shape[1:]
    q, k, v, dy = (x[0] for x in (queries, keys, values, out_grad))
    table = image_flags[0]
    gain_row = gain.reshape(1, width)
    ctx = lax.axis_index("ctx")
    core, ctx, dp = (x.reshape(1).astype(jnp.int32) for x in (ctx & 1, ctx, lax.axis_index("dp")))
    lanes = width // GROUPS // 2
    half_rows = lanes // PAIR * E
    heads = lanes // E

    def call(kernel, sel, ins, outs, after=(), alias=(), scratch=(), sub=1, steps=None, scalars=None):
        scalars = scalars or [core]

        def wide(i, c, *_):
            return (0, (i // sub * 2 + (sel + c[0]) % 2) * sub + i % sub)

        def whole(*args):
            return (0, 0)

        def part(i, c, *_):
            return (i // sub, 0, 0)

        specs = {
            "vmem": pl.BlockSpec(memory_space=pltpu.VMEM),
            "hbm": pl.BlockSpec(memory_space=pltpu.HBM),
            "wide": pl.BlockSpec((rows, lanes // sub), wide),
            "row": pl.BlockSpec((1, lanes // sub), wide),
            "sums": pl.BlockSpec((1, lanes // PAIR, PAIR), part),
            "zero": pl.BlockSpec((1, rows), whole),
            "all": pl.BlockSpec((GROUPS * half_rows, PAIR), whole),
            "part": pl.BlockSpec((1, half_rows + EXTRA, PAIR), part),
            "later": pl.BlockSpec((1, half_rows + EXTRA, PAIR), lambda i, *_: (GROUPS + i // sub, 0, 0)),
            "parts": pl.BlockSpec((GROUPS, half_rows + EXTRA, PAIR), lambda *args: (0, 0, 0)),
            "seg": pl.BlockSpec((1, rows), whole),
            "table": pl.BlockSpec((1, table.shape[0]), whole),
            "mask": pl.BlockSpec((rows, rows), whole),
            "token": pl.BlockSpec((1, PAIR), whole),
            "after2": pl.BlockSpec((8, PAIR), whole),
            "after3": pl.BlockSpec((1, 8, PAIR), lambda *args: (0, 0, 0)),
            "any": pl.BlockSpec(memory_space=pl.ANY),
        }
        shapes = {
            "wide": (rows, width),
            "sums": (GROUPS, lanes // PAIR, PAIR),
            "zero": (1, rows),
            "all": (GROUPS * half_rows, PAIR),
            "part": (GROUPS, half_rows + EXTRA, PAIR),
            "parts": (GROUPS, half_rows + EXTRA, PAIR),
            "token": (1, PAIR),
        }
        spaces = {"vmem": pltpu.VMEM, "hbm": pltpu.HBM}
        operands = [pinned(x, spaces[kind]) if kind in spaces else x for kind, x in ins] + list(after)
        kinds = [kind for kind, _ in ins] + [f"after{x.ndim}" for x in after]
        aliases = {}
        for out_at, x in alias:
            if x is not None:
                aliases[len(scalars) + len(operands)] = out_at
                operands.append(x)
                kinds.append("any")
        out_shape = [
            pltpu.VMEM(*shape, dtype) if kind == "vmem" else jax.ShapeDtypeStruct(shapes[kind], dtype)
            for kind, dtype, *shape in outs
        ]
        return pl.pallas_call(
            kernel,
            grid_spec=pltpu.PrefetchScalarGridSpec(
                num_scalar_prefetch=len(scalars),
                grid=steps or (GROUPS * sub,),
                in_specs=[specs[kind] for kind in kinds],
                out_specs=[specs[kind] for kind, *_ in outs],
                scratch_shapes=scratch,
            ),
            out_shape=out_shape,
            input_output_aliases=aliases,
            compiler_params=pltpu.CompilerParams(vmem_limit_bytes=VMEM),
            cost_estimate=pl.CostEstimate(flops=1, bytes_accessed=1, transcendentals=0),
        )(*scalars, *operands)

    edges = [("seg", segment_ids), ("table", image_flags)]
    chips = lax.axis_size("ctx") // 2
    whole, part_of = (rows, width), (rows, width // 2)

    def local_attn(sel, after):
        return call(
            functools.partial(local_kernel, sel), sel,
            [("vmem", q), ("vmem", k), ("vmem", v), ("mask", mask), ("mask", mask_t)],
            [("vmem", F32, part_of), ("vmem", BF16, (GROUPS * heads, rows, rows)), ("token", F32)], after=after)

    def norm(sel, before, after):
        return call(
            functools.partial(norm_kernel, sel), sel,
            [("vmem", q), ("vmem", dy), ("vmem", local[sel][0]), ("row", gain_row), *edges,
             ("all", prefix[sel]), ("part", nxt[sel])],
            [("wide", BF16), ("vmem", BF16, part_of), ("part", F32), ("sums", F32), ("all", F32), ("token", F32)],
            after=after, alias=[(0, before)])

    def inner(sel, before, after):
        return call(
            functools.partial(inner_kernel, sel), sel,
            [("vmem", q), ("vmem", k), ("vmem", v), ("vmem", norms[sel][1]), ("vmem", local[sel][1]), ("mask", mask),
             *edges, ("all", prefix[sel]), ("part", nxt[sel])],
            [("wide", BF16), ("vmem", F32, part_of), ("vmem", F32, part_of), ("token", F32)],
            after=after, alias=[(0, before)], sub=SUB)

    def outer(sel, before, after):
        return call(
            functools.partial(outer_kernel, sel), sel,
            [("vmem", k), ("vmem", v), ("vmem", inners[sel][1]), ("vmem", inners[sel][2]), *edges,
             ("all", suffix[sel]), ("later" if sel else "part", prv[0])],
            [("wide", BF16), ("wide", BF16), ("token", F32)], after=after, alias=list(enumerate(before)), sub=SUB)

    def summed_before(own, towards, works):
        load, before, span = own, None, 1
        while span < chips:
            arrived = shifted(load, 2 * towards * span)
            if works:
                arrived = arrived + works.pop(0)(load)
            before = arrived if before is None else before + arrived
            load = load + arrived
            span *= 2
        for work in works:
            before = before + work(load)
        return before

    keep, send, zero, k, v, core_row, ctx_row, dp_row = call(
        states_kernel, 0, [("hbm", k), ("hbm", v)],
        [("all", F32), ("all", F32), ("zero", jnp.int32), ("vmem", BF16, whole), ("vmem", BF16, whole)]
        + [("token", jnp.int32)] * 3,
        scratch=[pltpu.SemaphoreType.DMA((2 * GROUPS, 2))], steps=(1,), scalars=[core, ctx, dp])
    piece = within_chip(keep, send)
    seg = (segment_ids + zero)[0]
    onehot = seg[:, None] == jnp.arange(table.shape[0], dtype=jnp.int32)[None, :]
    img = jnp.sum(jnp.where(onehot, table[None, :], 0), axis=1)
    imgseg = jnp.where(img == 1, seg, -1)
    pos = jnp.arange(rows)
    mask = ((pos[:, None] >= pos[None, :]) | (imgseg[:, None] == seg[None, :])).astype(BF16)
    mask_t = ((pos[:, None] <= pos[None, :]) | (seg[:, None] == imgseg[None, :])).astype(BF16)

    parts = call(
        part_kernel, 0, [("hbm", q), ("hbm", dy), ("vmem", k), ("vmem", v), *edges],
        [("parts", F32)] * 2 + [("vmem", BF16, whole), ("vmem", BF16, whole), ("token", F32)],
        after=[piece[2]], scratch=[pltpu.SemaphoreType.DMA((2,))], steps=(1,))
    *parts, q, dy, _ = parts
    local, nxt = [], []

    def first_work(load):
        *made, token = local_attn(0, [parts[0]])
        local.append(made)
        return token

    def second_work(load):
        for part in reversed(parts):
            nxt.append(shifted(part + nought(load[:1]), -1))
        *made, token = local_attn(1, [load])
        local.append(made)
        return token

    before = summed_before(piece[2], 1, [first_work, second_work])
    prefix = to_cores(core_row, before, piece, 1)
    norms = [norm(0, None, [])]
    norms.append(norm(1, norms[0][0], [norms[0][4]]))
    output = norms[1][0]
    piece = within_chip(norms[0][4], norms[1][4])
    gain_sum = [jnp.concatenate([jnp.where(core_row == half, norms[0][3], norms[1][3]) for half in range(2)], axis=0)]
    gain_sum.append(scatter_step(gain_sum[-1], dp_row, "dp", 0))
    bits = list(reversed(range(lax.axis_size("ctx").bit_length() - 1)))
    inners, prv = [], []

    def third_work(load):
        x = scatter_step(gain_sum[-1] + nought(load[:1]), dp_row, "dp", 1)
        gain_sum.append(x.reshape(-1, PAIR))
        inners.append(inner(0, None, [load]))
        return inners[0][3]

    def fourth_work(load):
        gain_sum.append(scatter_step(gain_sum[-1] + nought(load[:1]), ctx_row, "ctx", bits[0]))
        both = jnp.concatenate([norms[1][2], norms[0][2]], axis=0) + nought(load[:1])
        prv.append(shifted(both, 1))
        inners.append(inner(1, inners[0][0], [load]))
        return inners[1][3]

    before = summed_before(piece[2], -1, [third_work, fourth_work])
    suffix = to_cores(core_row, before, piece, -1)
    grad_gain = scatter_step(gain_sum[-1] + nought(before[:1]), ctx_row, "ctx", bits[1])
    outers = outer(0, [None] * 2, [])
    grad_gain = grad_gain + outers[2]
    for bit in bits[2:]:
        grad_gain = scatter_step(grad_gain, ctx_row, "ctx", bit)
    grad_k, grad_v, _ = outer(1, outers[:2], [])
    grad_gain = grad_gain.reshape(-1)
    grad_q = inners[1][0]
    return output[None], grad_q[None], grad_k[None], grad_v[None], grad_gain


def solution(mesh):
    return jax.shard_map(
        on_device,
        mesh=mesh,
        in_specs=(
            P("dp", "ctx", None),
            P("dp", "ctx", None),
            P("dp", "ctx", None),
            P("dp", "ctx", None),
            P("dp", "ctx"),
            P("dp", None),
            P(),
        ),
        out_specs=(
            P("dp", "ctx", None),
            P("dp", "ctx", None),
            P("dp", "ctx", None),
            P("dp", "ctx", None),
            P(("dp", "ctx")),
        ),
        check_vma=False,
    )
```

```python
import functools

import jax
import jax.numpy as jnp
from jax import lax
from jax.experimental import pallas as pl
from jax.experimental.pallas import tpu as pltpu
from jax.sharding import PartitionSpec as P

E = 64
PAIR = 2 * E
GROUPS = 2
EXTRA = 8
VMEM = 10 * 2**20
SUB = 2
F32 = jnp.float32
BF16 = jnp.bfloat16


def dot(a, b, ca, cb):
    return lax.dot_general(a, b, (((ca,), (cb,)), ((), ())), preferred_element_type=F32)


def low_lanes(rows, cols):
    lane = lax.broadcasted_iota(jnp.int32, (rows, cols), 1)
    return lane % PAIR < E


def fold(product):
    return jnp.where(low_lanes(E, product.shape[1]), product[:E], product[E:])


def split(state):
    high = state.astype(BF16)
    return high, (state - high.astype(F32)).astype(BF16)


def spread(state):
    low = low_lanes(*state.shape)
    zero = jnp.zeros_like(state)
    return jnp.concatenate([jnp.where(low, state, zero), jnp.where(low, zero, state)], axis=0)


def heads_of(pair):
    low = low_lanes(*pair.shape)
    zero = jnp.zeros_like(pair)
    return jnp.where(low, pair, zero), jnp.where(low, zero, pair)


def twice(x):
    return jnp.concatenate([x, x], axis=1)


def pair_at(ref, p):
    return ref[:, p * PAIR:(p + 1) * PAIR]


def rows_at(base, p):
    return pl.ds(pl.multiple_of(base + p * E, E), E)


def twice(x):
    return jnp.concatenate([x, x], axis=1)


def pair_at(ref, p):
    return ref[:, p * PAIR:(p + 1) * PAIR]


def rows_at(base, p):
    return pl.ds(pl.multiple_of(base + p * E, E), E)


def own_or_received(keep, received, own, p):
    return jnp.where(own, keep[rows_at(p)], received[rows_at(p)])


def state_pair(a, b):
    return fold(dot(a, b, 0, 0))


def edge(seg, table, last):
    row = seg[...]
    count = row.shape[1]
    own = row[:, count - 1:] if last else row[:, :1]
    size = jnp.sum((row == own).astype(F32), axis=1, keepdims=True)
    at = lax.broadcasted_iota(jnp.int32, (count, PAIR), 0).astype(F32)
    rows = at >= count - size if last else at < size
    ids = lax.broadcasted_iota(jnp.int32, table.shape, 1)
    flag = jnp.sum(jnp.where(ids == own, table[...], 0).astype(F32), axis=1, keepdims=True)
    return rows, own.astype(F32), flag


def lanes_at(base, p):
    return pl.ds(pl.multiple_of(base + p * PAIR, PAIR), PAIR)


def place(group, core, lanes, sub):
    step = pl.program_id(0)
    sel, part = step // sub, step % sub
    half = (sel + core[0]) % 2
    inside = part * (lanes // sub)
    return sel, sel * lanes + inside, (2 * group + half) * lanes + inside, inside // PAIR * E


def own_or_received(keep, received, sel, at):
    return jnp.where(sel == 0, keep[at], received[at])


def states_kernel(core, ctx, dp, k_in, v_in, keep, send, zero, k, v, core_row, ctx_row, dp_row, sems):
    for row, index in ((core_row, core), (ctx_row, ctx), (dp_row, dp)):
        row[...] = jnp.full(row.shape, index[0], jnp.int32)
    lanes = k.shape[1] // GROUPS // 2
    count = lanes // PAIR
    copies = []
    for sel in (1, 0):
        for group in range(GROUPS):
            base = (2 * group + (sel + core[0]) % 2) * lanes
            at = pl.ds(pl.multiple_of(base, lanes), lanes)
            for i, (array, buf) in enumerate(((k_in, k), (v_in, v))):
                copies.append(pltpu.make_async_copy(array.at[:, at], buf.at[:, at], sems.at[2 * group + sel, i]))
    for copy in copies:
        copy.start()
    zero[...] = jnp.zeros_like(zero)
    for sel, out in ((1, send), (0, keep)):
        for group in range(GROUPS):
            copies.pop(0).wait()
            copies.pop(0).wait()
            base = (2 * group + (sel + core[0]) % 2) * lanes
            for p in range(count):
                at = lanes_at(base, p)
                row = (group * count + p) * E
                out[row:row + E] = state_pair(k[:, at], v[:, at])


def part_kernel(core, q_in, dy_in, k, v, seg, table, *rest):
    *outs, q, dy, token, sems = rest[-4 - GROUPS:]
    copies = [pltpu.make_async_copy(a, b, sems.at[i]) for i, (a, b) in enumerate(((q_in, q), (dy_in, dy)))]
    for copy in copies:
        copy.start()
    token[...] = jnp.zeros_like(token)
    lanes = k.shape[1] // GROUPS // 2
    count = lanes // PAIR
    rows, own, _ = edge(seg, table, False)
    keep = rows.astype(BF16)
    for group, out in enumerate(outs):
        for sel in range(2):
            base = (2 * group + (sel + core[0]) % 2) * lanes
            for p in range(count):
                at = lanes_at(base, p)
                out[sel, p * E:(p + 1) * E] = state_pair(k[:, at], v[:, at] * keep)
            out[sel, count * E:] = jnp.broadcast_to(own, (EXTRA, PAIR))
    for copy in copies:
        copy.wait()


def local_kernel(group, core, q, k, v, mask, mask_t, *rest):
    attn, probs, token = rest[-3:]
    lanes = attn.shape[1] // 2
    sel, base, wide, _ = place(group, core, lanes, 1)
    m, mt = mask[...], mask_t[...]
    token[...] = jnp.zeros_like(token)
    for p in range(lanes // PAIR):
        at = lanes_at(wide, p)
        kp = k[:, at]
        total = None
        for h, (qh, vh) in enumerate(zip(heads_of(q[:, at]), heads_of(v[:, at]))):
            prob = dot(qh, kp, 1, 1).astype(BF16) * m
            probs[sel * (lanes // E) + 2 * p + h] = dot(kp, qh, 1, 1).astype(BF16) * mt
            term = dot(prob, vh, 1, 0)
            total = term if total is None else total + term
        attn[:, lanes_at(base, p)] = total


def head_mean(x):
    high, low = split(x)
    ones = spread(jnp.full((E, PAIR), 1.0 / E, BF16))
    return dot(jnp.concatenate([high, low], axis=1), jnp.concatenate([ones, ones], axis=0), 1, 0)


def side_by_side(state, part):
    sh, sl = split(state)
    ph, pll = split(part)
    left = jnp.concatenate([spread(sh), spread(sl)], axis=0)
    right = jnp.concatenate([spread(ph), spread(pll)], axis=0)
    return jnp.concatenate([left, right], axis=1)


def stacked(state, part):
    sh, sl = split(state)
    ph, pll = split(part)
    top = jnp.concatenate([spread(sh), spread(sl)], axis=1)
    bottom = jnp.concatenate([spread(ph), spread(pll)], axis=1)
    return jnp.concatenate([top, bottom], axis=0)


def on_rows(seg, table, last, part):
    rows, own, flag = edge(seg, table, last)
    met = part[0, part.shape[1] - EXTRA:part.shape[1] - EXTRA + 1] == own
    if last:
        met = met & (flag == 1)
    return rows.astype(F32) * met.astype(F32)


def norm_kernel(group, core, q, dy, local, gain, seg, table, mine, theirs, nxt, *rest):
    out, dab, part, gsum, keep, send, token = rest[-7:]
    token[...] = jnp.zeros_like(token)
    lanes = out.shape[1]
    count = lanes // PAIR
    sel, base, wide, _ = place(group, core, lanes, 1)
    on_next = on_rows(seg, table, True, nxt)
    last, own, flag = edge(seg, table, True)
    last = (last.astype(F32) * jnp.where(flag == 1, 1.0, 0.0)).astype(BF16)
    pairs = [slice(p * PAIR, (p + 1) * PAIR) for p in range(count)]
    bases = [lanes_at(base, p) for p in range(count)]
    wides = [lanes_at(wide, p) for p in range(count)]
    fars = [
        dot(twice(q[:, at]), side_by_side(own_or_received(mine, theirs, sel, rows_at(0, p)), nxt[0, rows_at(0, p)]), 1, 0)
        for p, at in enumerate(wides)
    ]
    attns = [local[:, at] + far[:, :PAIR] + on_next * far[:, PAIR:] for at, far in zip(bases, fars)]
    squares = [head_mean(attn * attn) for attn in attns]
    scales = [lax.rsqrt(square + 1e-06) for square in squares]
    normeds = [attn * scale for attn, scale in zip(attns, scales)]
    gas = [dy[:, at].astype(F32) * gain[:, pair] for at, pair in zip(wides, pairs)]
    means = [head_mean(ga * normed) for ga, normed in zip(gas, normeds)]
    das = [
        (scale * (ga - normed * mean)).astype(BF16)
        for scale, ga, normed, mean in zip(scales, gas, normeds, means)
    ]
    states = [state_pair(q[:, at], jnp.concatenate([da, da * last], axis=1)) for at, da in zip(wides, das)]
    part[0, count * E:] = jnp.broadcast_to(own, (EXTRA, PAIR))
    for p, (at, normed, da) in enumerate(zip(pairs, normeds, das)):
        part[0, p * E:(p + 1) * E] = states[p][:, PAIR:]
        dab[:, bases[p]] = da
        out[:, at] = (normed * gain[:, at]).astype(BF16)
        gsum[0, p:p + 1] = jnp.sum(dy[:, wides[p]].astype(F32) * normed, axis=0, keepdims=True)

    @pl.when(sel == 0)
    def _():
        for p, state in enumerate(states):
            keep[rows_at(0, p)] = state[:, :PAIR]

    @pl.when(sel == 1)
    def _():
        for p, state in enumerate(states):
            send[rows_at(0, p)] = state[:, :PAIR]


def inner_kernel(group, core, q, k, v, dab, probs, mask, seg, table, mine, theirs, nxt, *rest):
    gq, gk, gv, token = rest[-4:]
    lanes = dab.shape[1] // 2
    count = lanes // SUB // PAIR
    sel, base, wide, row = place(group, core, lanes, SUB)
    m = mask[...]
    token[...] = jnp.zeros_like(token)
    on_next = on_rows(seg, table, True, nxt)
    for p in range(count):
        at = lanes_at(wide, p)
        da = dab[:, lanes_at(base, p)]
        vp = v[:, at]
        far = dot(twice(da), stacked(own_or_received(mine, theirs, sel, rows_at(row, p)), nxt[0, rows_at(row, p)]), 1, 1)
        tq = far[:, :PAIR] + on_next * far[:, PAIR:]
        tk = tv = None
        for h, (qh, kh, dh) in enumerate(zip(heads_of(q[:, at]), heads_of(k[:, at]), heads_of(da))):
            dprob = dot(dh, vp, 1, 1).astype(BF16) * m
            tq = tq + dot(dprob, kh, 1, 0)
            a = dot(dprob, qh, 0, 0)
            b = dot(probs[base // E + 2 * p + h], dh, 1, 0)
            tk = a if tk is None else tk + a
            tv = b if tv is None else tv + b
        gq[:, p * PAIR:(p + 1) * PAIR] = tq.astype(BF16)
        gk[:, lanes_at(base, p)] = tk
        gv[:, lanes_at(base, p)] = tv


def outer_kernel(group, core, k, v, gk_in, gv_in, seg, table, mine, theirs, prv, *rest):
    gk, gv, token = rest[-3:]
    lanes = gk_in.shape[1] // 2
    count = lanes // SUB // PAIR
    sel, base, wide, row = place(group, core, lanes, SUB)
    token[...] = jnp.zeros_like(token)
    on_prev = on_rows(seg, table, False, prv)
    for p in range(count):
        here, own, at = slice(p * PAIR, (p + 1) * PAIR), lanes_at(base, p), lanes_at(wide, p)
        s = own_or_received(mine, theirs, sel, rows_at(row, p))
        g = prv[0, rows_at(row, p)]
        far = dot(twice(v[:, at]), stacked(s, g), 1, 1)
        gk[:, here] = (gk_in[:, own] + far[:, :PAIR] + on_prev * far[:, PAIR:]).astype(BF16)
        far = dot(twice(k[:, at]), side_by_side(s, g), 1, 0)
        gv[:, here] = (gv_in[:, own] + far[:, :PAIR] + on_prev * far[:, PAIR:]).astype(BF16)


def partner(x, axis, bit):
    route = [(i, i ^ (1 << bit)) for i in range(lax.axis_size(axis))]
    return lax.ppermute(x, axis, route)


def shifted(x, distance):
    count = lax.axis_size("ctx")
    return lax.ppermute(x, "ctx", [(i, i + distance) for i in range(count) if 0 <= i + distance < count])


def nought(x):
    return jnp.minimum(jnp.abs(x), 0.0)


def within_chip(keep, send):
    received = partner(send, "ctx", 0)
    return keep, received, keep + received


def to_cores(core, before, piece, towards):
    keep, received, _ = piece
    is_source = core == (0 if towards == 1 else 1)
    mine = jnp.where(is_source, before, before + received)
    return mine, partner(jnp.where(is_source, before + keep, before), "ctx", 0)


def pinned(x, space):
    return pltpu.with_memory_space_constraint(x, space)


def scatter_step(x, at, axis, bit):
    low, high = jnp.split(x, 2, axis=0 if x.shape[0] > 1 else 1)
    upper = (at >> bit & 1 == 1)[:, :low.shape[-1]]
    return jnp.where(upper, high, low) + partner(jnp.where(upper, low, high), axis, bit)


def on_device(queries, keys, values, out_grad, segment_ids, image_flags, gain):
    rows, width = queries.shape[1:]
    q, k, v, dy = (x[0] for x in (queries, keys, values, out_grad))
    table = image_flags[0]
    gain_row = gain.reshape(1, width)
    ctx = lax.axis_index("ctx")
    core, ctx, dp = (x.reshape(1).astype(jnp.int32) for x in (ctx & 1, ctx, lax.axis_index("dp")))
    lanes = width // GROUPS // 2
    half_rows = lanes // PAIR * E
    heads = lanes // E

    def call(kernel, group, ins, outs, after=(), alias=(), scratch=(), sub=1, steps=None, scalars=None):
        scalars = scalars or [core]

        def wide(i, c, *_):
            return (0, (2 * group + (i // sub + c[0]) % 2) * sub + i % sub)

        def whole(*args):
            return (0, 0)

        def part(i, c, *_):
            return (i // sub, 0, 0)

        specs = {
            "vmem": pl.BlockSpec(memory_space=pltpu.VMEM),
            "hbm": pl.BlockSpec(memory_space=pltpu.HBM),
            "wide": pl.BlockSpec((rows, lanes // sub), wide),
            "row": pl.BlockSpec((1, lanes // sub), wide),
            "sums": pl.BlockSpec((1, lanes // PAIR, PAIR), part),
            "zero": pl.BlockSpec((1, rows), whole),
            "all": pl.BlockSpec((GROUPS * half_rows, PAIR), whole),
            "part": pl.BlockSpec((1, half_rows + EXTRA, PAIR), part),
            "got": pl.BlockSpec((1, half_rows + EXTRA, PAIR), lambda i, *_: (1 - i // sub, 0, 0)),
            "got1": pl.BlockSpec((1, half_rows + EXTRA, PAIR), lambda i, *_: (3 - i // sub, 0, 0)),
            "half": pl.BlockSpec((half_rows, PAIR), whole),
            "parts": pl.BlockSpec((2, half_rows + EXTRA, PAIR), lambda *args: (0, 0, 0)),
            "seg": pl.BlockSpec((1, rows), whole),
            "table": pl.BlockSpec((1, table.shape[0]), whole),
            "mask": pl.BlockSpec((rows, rows), whole),
            "token": pl.BlockSpec((1, PAIR), whole),
            "after2": pl.BlockSpec((8, PAIR), whole),
            "after3": pl.BlockSpec((1, 8, PAIR), lambda *args: (0, 0, 0)),
            "any": pl.BlockSpec(memory_space=pl.ANY),
        }
        shapes = {
            "wide": (rows, width),
            "sums": (2, lanes // PAIR, PAIR),
            "half": (half_rows, PAIR),
            "zero": (1, rows),
            "all": (GROUPS * half_rows, PAIR),
            "part": (2, half_rows + EXTRA, PAIR),
            "parts": (2, half_rows + EXTRA, PAIR),
            "token": (1, PAIR),
        }
        spaces = {"vmem": pltpu.VMEM, "hbm": pltpu.HBM}
        operands = [pinned(x, spaces[kind]) if kind in spaces else x for kind, x in ins] + list(after)
        kinds = [kind for kind, _ in ins] + [f"after{x.ndim}" for x in after]
        aliases = {}
        for out_at, x in alias:
            if x is not None:
                aliases[len(scalars) + len(operands)] = out_at
                operands.append(x)
                kinds.append("any")
        out_shape = [
            pltpu.VMEM(*shape, dtype) if kind == "vmem" else jax.ShapeDtypeStruct(shapes[kind], dtype)
            for kind, dtype, *shape in outs
        ]
        return pl.pallas_call(
            kernel,
            grid_spec=pltpu.PrefetchScalarGridSpec(
                num_scalar_prefetch=len(scalars),
                grid=steps or (2 * sub,),
                in_specs=[specs[kind] for kind in kinds],
                out_specs=[specs[kind] for kind, *_ in outs],
                scratch_shapes=scratch,
            ),
            out_shape=out_shape,
            input_output_aliases=aliases,
            compiler_params=pltpu.CompilerParams(vmem_limit_bytes=VMEM),
            cost_estimate=pl.CostEstimate(flops=1, bytes_accessed=1, transcendentals=0),
        )(*scalars, *operands)

    edges = [("seg", segment_ids), ("table", image_flags)]
    chips = lax.axis_size("ctx") // 2
    whole, group_of = (rows, width), (rows, 2 * lanes)
    groups = range(GROUPS)

    def local_attn(g, after):
        return call(
            functools.partial(local_kernel, g), g,
            [("vmem", q), ("vmem", k), ("vmem", v), ("mask", mask), ("mask", mask_t)],
            [("vmem", F32, group_of), ("vmem", BF16, (2 * heads, rows, rows)), ("token", F32)], after=after)

    def norm(g, before, after):
        return call(
            functools.partial(norm_kernel, g), g,
            [("vmem", q), ("vmem", dy), ("vmem", local[g][0]), ("row", gain_row), *edges,
             ("half", prefix[g][0]), ("half", prefix[g][1]), ("got", nxt[g])],
            [("wide", BF16), ("vmem", BF16, group_of), ("part", F32), ("sums", F32), ("half", F32), ("half", F32),
             ("token", F32)],
            after=after, alias=[(0, before)])

    def inner(g, before, after):
        return call(
            functools.partial(inner_kernel, g), g,
            [("vmem", q), ("vmem", k), ("vmem", v), ("vmem", norms[g][1]), ("vmem", local[g][1]), ("mask", mask),
             *edges, ("half", prefix[g][0]), ("half", prefix[g][1]), ("got", nxt[g])],
            [("wide", BF16), ("vmem", F32, group_of), ("vmem", F32, group_of), ("token", F32)],
            after=after, alias=[(0, before)], sub=SUB)

    def outer(g, before, after):
        return call(
            functools.partial(outer_kernel, g), g,
            [("vmem", k), ("vmem", v), ("vmem", inners[g][1]), ("vmem", inners[g][2]), *edges,
             ("half", suffix[g][0]), ("half", suffix[g][1]), ("got1" if g else "got", prv)],
            [("wide", BF16), ("wide", BF16), ("token", F32)], after=after, alias=list(enumerate(before)), sub=SUB)

    def hops_after_first(load, before, towards):
        span = 2
        while span < chips:
            arrived = shifted(load, 2 * towards * span)
            load, before = load + arrived, before + arrived
            span *= 2
        return before

    keep, send, zero, k, v, core_row, ctx_row, dp_row = call(
        states_kernel, 0, [("hbm", k), ("hbm", v)],
        [("all", F32), ("all", F32), ("zero", jnp.int32), ("vmem", BF16, whole), ("vmem", BF16, whole)]
        + [("token", jnp.int32)] * 3,
        scratch=[pltpu.SemaphoreType.DMA((2 * GROUPS, 2))], steps=(1,), scalars=[core, ctx, dp])
    piece = within_chip(keep, send)
    seg = (segment_ids + zero)[0]
    onehot = seg[:, None] == jnp.arange(table.shape[0], dtype=jnp.int32)[None, :]
    img = jnp.sum(jnp.where(onehot, table[None, :], 0), axis=1)
    imgseg = jnp.where(img == 1, seg, -1)
    pos = jnp.arange(rows)
    mask = ((pos[:, None] >= pos[None, :]) | (imgseg[:, None] == seg[None, :])).astype(BF16)
    mask_t = ((pos[:, None] <= pos[None, :]) | (seg[:, None] == imgseg[None, :])).astype(BF16)

    pieces = [tuple(x[g * half_rows:(g + 1) * half_rows] for x in piece) for g in groups]
    parts = call(
        part_kernel, 0, [("hbm", q), ("hbm", dy), ("vmem", k), ("vmem", v), *edges],
        [("parts", F32)] * GROUPS + [("vmem", BF16, whole), ("vmem", BF16, whole), ("token", F32)],
        after=[piece[2]], scratch=[pltpu.SemaphoreType.DMA((2,))], steps=(1,))
    *parts, q, dy, _ = parts

    local = [local_attn(0, [parts[0]])]
    first = shifted(piece[2], 2) + local[0][2]
    load = piece[2] + first
    arrived, loads = ([x[g * half_rows:(g + 1) * half_rows] for g in groups] for x in (first, load))
    nxt = [shifted(part + nought(load[:1]), -1) for part in parts]
    local.append(local_attn(1, [loads[1]]))
    befores = [hops_after_first(load, first, 1) for load, first in zip(loads, arrived)]
    befores[0] = befores[0] + local[1][2]
    prefix = [to_cores(core_row, befores[0], pieces[0], 1)]
    norms = [norm(0, None, [])]
    late = [within_chip(norms[0][4], norms[0][5])]
    befores[1] = befores[1] + norms[0][6]
    prefix.append(to_cores(core_row, befores[1], pieces[1], 1))
    norms.append(norm(1, norms[0][0], [late[0][2]]))
    output = norms[1][0]

    gain_sum = jnp.concatenate(
        [jnp.where(core_row == half, n[3][:1], n[3][1:]) for half in range(2) for n in norms], axis=0)
    gain_sum = scatter_step(gain_sum, dp_row, "dp", 0)
    bits = list(reversed(range(lax.axis_size("ctx").bit_length() - 1)))

    arrived = [shifted(late[0][2], -2) + norms[1][6]]
    loads = [late[0][2] + arrived[0]]
    keep, received, total = within_chip(norms[1][4], norms[1][5])
    late.append((keep, received, total + nought(loads[0][:1])))
    gain_sum = scatter_step(gain_sum + nought(late[1][2][:1]), dp_row, "dp", 1).reshape(-1, PAIR)
    inners = [inner(0, None, [late[1][2], loads[0]])]
    arrived.append(shifted(late[1][2], -2) + inners[0][3])
    loads.append(late[1][2] + arrived[1])
    gain_sum = scatter_step(gain_sum + nought(loads[1][:1]), ctx_row, "ctx", bits[0])
    prv = shifted(jnp.concatenate([n[2] for n in norms], axis=0) + nought(loads[1][:1]), 1)
    inners.append(inner(1, inners[0][0], [loads[1]]))
    grad_q = inners[1][0]
    befores = [hops_after_first(load, first, -1) for load, first in zip(loads, arrived)]
    befores[0] = befores[0] + inners[1][3]
    suffix = [to_cores(core_row, befores[0], late[0], -1)]
    grad_gain = scatter_step(gain_sum + nought(befores[0][:1]), ctx_row, "ctx", bits[1])
    outers = outer(0, [None] * 2, [])
    befores[1] = befores[1] + outers[2]
    suffix.append(to_cores(core_row, befores[1], late[1], -1))
    for bit in bits[2:]:
        grad_gain = scatter_step(grad_gain + nought(befores[1][:1])[:, :grad_gain.shape[1]], ctx_row, "ctx", bit)
    grad_k, grad_v, _ = outer(1, outers[:2], [])
    grad_gain = grad_gain.reshape(-1)
    return output[None], grad_q[None], grad_k[None], grad_v[None], grad_gain


def solution(mesh):
    return jax.shard_map(
        on_device,
        mesh=mesh,
        in_specs=(
            P("dp", "ctx", None),
            P("dp", "ctx", None),
            P("dp", "ctx", None),
            P("dp", "ctx", None),
            P("dp", "ctx"),
            P("dp", None),
            P(),
        ),
        out_specs=(
            P("dp", "ctx", None),
            P("dp", "ctx", None),
            P("dp", "ctx", None),
            P("dp", "ctx", None),
            P(("dp", "ctx")),
        ),
        check_vma=False,
    )
```

```python
import functools

import jax
import jax.numpy as jnp
from jax import lax
from jax.experimental import pallas as pl
from jax.experimental.pallas import tpu as pltpu
from jax.sharding import PartitionSpec as P

E = 64
PAIR = 2 * E
GROUPS = 2
EXTRA = 8
VMEM = 10 * 2**20
SUB = 2
F32 = jnp.float32
BF16 = jnp.bfloat16


def dot(a, b, ca, cb):
    return lax.dot_general(a, b, (((ca,), (cb,)), ((), ())), preferred_element_type=F32)


def low_lanes(rows, cols):
    lane = lax.broadcasted_iota(jnp.int32, (rows, cols), 1)
    return lane % PAIR < E


def fold(product):
    return jnp.where(low_lanes(E, product.shape[1]), product[:E], product[E:])


def split(state):
    high = state.astype(BF16)
    return high, (state - high.astype(F32)).astype(BF16)


def spread(state):
    low = low_lanes(*state.shape)
    zero = jnp.zeros_like(state)
    return jnp.concatenate([jnp.where(low, state, zero), jnp.where(low, zero, state)], axis=0)


def heads_of(pair):
    low = low_lanes(*pair.shape)
    zero = jnp.zeros_like(pair)
    return jnp.where(low, pair, zero), jnp.where(low, zero, pair)


def twice(x):
    return jnp.concatenate([x, x], axis=1)


def pair_at(ref, p):
    return ref[:, p * PAIR:(p + 1) * PAIR]


def rows_at(base, p):
    return pl.ds(pl.multiple_of(base + p * E, E), E)


def twice(x):
    return jnp.concatenate([x, x], axis=1)


def pair_at(ref, p):
    return ref[:, p * PAIR:(p + 1) * PAIR]


def rows_at(base, p):
    return pl.ds(pl.multiple_of(base + p * E, E), E)


def own_or_received(keep, received, own, p):
    return jnp.where(own, keep[rows_at(p)], received[rows_at(p)])


def state_pair(a, b):
    return fold(dot(a, b, 0, 0))


def edge(seg, table, last):
    row = seg[...]
    count = row.shape[1]
    own = row[:, count - 1:] if last else row[:, :1]
    size = jnp.sum((row == own).astype(F32), axis=1, keepdims=True)
    at = lax.broadcasted_iota(jnp.int32, (count, PAIR), 0).astype(F32)
    rows = at >= count - size if last else at < size
    ids = lax.broadcasted_iota(jnp.int32, table.shape, 1)
    flag = jnp.sum(jnp.where(ids == own, table[...], 0).astype(F32), axis=1, keepdims=True)
    return rows, own.astype(F32), flag


def lanes_at(base, p):
    return pl.ds(pl.multiple_of(base + p * PAIR, PAIR), PAIR)


def place(sel, group, core, lanes, sub):
    inside = pl.program_id(0) % sub * (lanes // sub)
    half = (sel + core[0]) % 2
    return inside, (2 * group + half) * lanes + inside, inside // PAIR * E


def states_kernel(core, ctx, dp, k_in, v_in, keep, send, zero, k, v, core_row, ctx_row, dp_row, sems):
    for row, index in ((core_row, core), (ctx_row, ctx), (dp_row, dp)):
        row[...] = jnp.full(row.shape, index[0], jnp.int32)
    lanes = k.shape[1] // GROUPS // 2
    count = lanes // PAIR
    copies = []
    for sel in (1, 0):
        for group in range(GROUPS):
            base = (2 * group + (sel + core[0]) % 2) * lanes
            at = pl.ds(pl.multiple_of(base, lanes), lanes)
            for i, (array, buf) in enumerate(((k_in, k), (v_in, v))):
                copies.append(pltpu.make_async_copy(array.at[:, at], buf.at[:, at], sems.at[2 * group + sel, i]))
    for copy in copies:
        copy.start()
    zero[...] = jnp.zeros_like(zero)
    for sel, out in ((1, send), (0, keep)):
        for group in range(GROUPS):
            copies.pop(0).wait()
            copies.pop(0).wait()
            base = (2 * group + (sel + core[0]) % 2) * lanes
            for p in range(count):
                at = lanes_at(base, p)
                row = (group * count + p) * E
                out[row:row + E] = state_pair(k[:, at], v[:, at])


def part_kernel(core, q_in, dy_in, k, v, seg, table, *rest):
    *outs, q, dy, token, sems = rest[-6:]
    copies = [pltpu.make_async_copy(a, b, sems.at[i]) for i, (a, b) in enumerate(((q_in, q), (dy_in, dy)))]
    for copy in copies:
        copy.start()
    token[...] = jnp.zeros_like(token)
    lanes = k.shape[1] // GROUPS // 2
    count = lanes // PAIR
    rows, own, _ = edge(seg, table, False)
    keep = rows.astype(BF16)
    for sel, out in enumerate(outs):
        for group in range(GROUPS):
            base = (2 * group + (sel + core[0]) % 2) * lanes
            for p in range(count):
                at = lanes_at(base, p)
                out[group, p * E:(p + 1) * E] = state_pair(k[:, at], v[:, at] * keep)
            out[group, count * E:] = jnp.broadcast_to(own, (EXTRA, PAIR))
    for copy in copies:
        copy.wait()


def local_kernel(sel, core, q, k, v, mask, mask_t, *rest):
    attn, probs, token = rest[-3:]
    lanes = attn.shape[1] // GROUPS
    group = pl.program_id(0)
    base = group * lanes
    wide = base + (group + (sel + core[0]) % 2) * lanes
    m, mt = mask[...], mask_t[...]
    token[...] = jnp.zeros_like(token)
    for p in range(lanes // PAIR):
        at = lanes_at(wide, p)
        kp = k[:, at]
        total = None
        for h, (qh, vh) in enumerate(zip(heads_of(q[:, at]), heads_of(v[:, at]))):
            prob = dot(qh, kp, 1, 1).astype(BF16) * m
            probs[group * (lanes // E) + 2 * p + h] = dot(kp, qh, 1, 1).astype(BF16) * mt
            term = dot(prob, vh, 1, 0)
            total = term if total is None else total + term
        attn[:, lanes_at(base, p)] = total


def head_mean(x):
    high, low = split(x)
    ones = spread(jnp.full((E, PAIR), 1.0 / E, BF16))
    return dot(jnp.concatenate([high, low], axis=1), jnp.concatenate([ones, ones], axis=0), 1, 0)


def side_by_side(state, part):
    sh, sl = split(state)
    ph, pll = split(part)
    left = jnp.concatenate([spread(sh), spread(sl)], axis=0)
    right = jnp.concatenate([spread(ph), spread(pll)], axis=0)
    return jnp.concatenate([left, right], axis=1)


def stacked(state, part):
    sh, sl = split(state)
    ph, pll = split(part)
    top = jnp.concatenate([spread(sh), spread(sl)], axis=1)
    bottom = jnp.concatenate([spread(ph), spread(pll)], axis=1)
    return jnp.concatenate([top, bottom], axis=0)


def on_rows(seg, table, last, part):
    rows, own, flag = edge(seg, table, last)
    met = part[0, part.shape[1] - EXTRA:part.shape[1] - EXTRA + 1] == own
    if last:
        met = met & (flag == 1)
    return rows.astype(F32) * met.astype(F32)


def norm_kernel(sel, group, core, q, dy, local, gain, seg, table, prefix, nxt, *rest):
    out, dab, part, gsum, total, token = rest[-6:]
    token[...] = jnp.zeros_like(token)
    lanes = out.shape[1]
    count = lanes // PAIR
    base, wide, row = place(sel, group, core, lanes, 1)
    on_next = on_rows(seg, table, True, nxt)
    last, own, flag = edge(seg, table, True)
    last = (last.astype(F32) * jnp.where(flag == 1, 1.0, 0.0)).astype(BF16)
    pairs = [slice(p * PAIR, (p + 1) * PAIR) for p in range(count)]
    bases = [lanes_at(base, p) for p in range(count)]
    wides = [lanes_at(wide, p) for p in range(count)]
    fars = [
        dot(twice(q[:, at]), side_by_side(prefix[rows_at(row, p)], nxt[0, rows_at(0, p)]), 1, 0)
        for p, at in enumerate(wides)
    ]
    attns = [
        local[:, lanes_at(group * lanes, p)] + far[:, :PAIR] + on_next * far[:, PAIR:] for p, far in enumerate(fars)
    ]
    squares = [head_mean(attn * attn) for attn in attns]
    scales = [lax.rsqrt(square + 1e-06) for square in squares]
    normeds = [attn * scale for attn, scale in zip(attns, scales)]
    gas = [dy[:, at].astype(F32) * gain[:, pair] for at, pair in zip(wides, pairs)]
    means = [head_mean(ga * normed) for ga, normed in zip(gas, normeds)]
    das = [
        (scale * (ga - normed * mean)).astype(BF16)
        for scale, ga, normed, mean in zip(scales, gas, normeds, means)
    ]
    states = [state_pair(q[:, at], jnp.concatenate([da, da * last], axis=1)) for at, da in zip(wides, das)]
    part[0, count * E:] = jnp.broadcast_to(own, (EXTRA, PAIR))
    for p, (at, normed, da) in enumerate(zip(pairs, normeds, das)):
        total[rows_at(row, p)] = states[p][:, :PAIR]
        part[0, p * E:(p + 1) * E] = states[p][:, PAIR:]
        dab[:, bases[p]] = da
        out[:, at] = (normed * gain[:, at]).astype(BF16)
        gsum[0, p:p + 1] = jnp.sum(dy[:, wides[p]].astype(F32) * normed, axis=0, keepdims=True)


def inner_kernel(sel, group, core, q, k, v, dab, probs, mask, seg, table, prefix, nxt, *rest):
    gq, gk, gv, token = rest[-4:]
    lanes = dab.shape[1]
    count = lanes // SUB // PAIR
    base, wide, row = place(sel, group, core, lanes, SUB)
    m = mask[...]
    token[...] = jnp.zeros_like(token)
    on_next = on_rows(seg, table, True, nxt)
    for p in range(count):
        at = lanes_at(wide, p)
        da = dab[:, lanes_at(base, p)]
        vp = v[:, at]
        far = dot(twice(da), stacked(prefix[rows_at(row, p)], nxt[0, rows_at(row, p)]), 1, 1)
        tq = far[:, :PAIR] + on_next * far[:, PAIR:]
        tk = tv = None
        for h, (qh, kh, dh) in enumerate(zip(heads_of(q[:, at]), heads_of(k[:, at]), heads_of(da))):
            dprob = dot(dh, vp, 1, 1).astype(BF16) * m
            tq = tq + dot(dprob, kh, 1, 0)
            a = dot(dprob, qh, 0, 0)
            b = dot(probs[group * (lanes // E) + base // E + 2 * p + h], dh, 1, 0)
            tk = a if tk is None else tk + a
            tv = b if tv is None else tv + b
        gq[:, p * PAIR:(p + 1) * PAIR] = tq.astype(BF16)
        gk[:, lanes_at(base, p)] = tk
        gv[:, lanes_at(base, p)] = tv


def outer_kernel(sel, group, core, k, v, gk_in, gv_in, seg, table, suffix, prv, *rest):
    gk, gv, token = rest[-3:]
    lanes = gk_in.shape[1]
    count = lanes // SUB // PAIR
    base, wide, row = place(sel, group, core, lanes, SUB)
    token[...] = jnp.zeros_like(token)
    on_prev = on_rows(seg, table, False, prv)
    for p in range(count):
        here, own, at = slice(p * PAIR, (p + 1) * PAIR), lanes_at(base, p), lanes_at(wide, p)
        s = suffix[rows_at(row, p)]
        g = prv[0, rows_at(row, p)]
        far = dot(twice(v[:, at]), stacked(s, g), 1, 1)
        gk[:, here] = (gk_in[:, own] + far[:, :PAIR] + on_prev * far[:, PAIR:]).astype(BF16)
        far = dot(twice(k[:, at]), side_by_side(s, g), 1, 0)
        gv[:, here] = (gv_in[:, own] + far[:, :PAIR] + on_prev * far[:, PAIR:]).astype(BF16)


def partner(x, axis, bit):
    route = [(i, i ^ (1 << bit)) for i in range(lax.axis_size(axis))]
    return lax.ppermute(x, axis, route)


def shifted(x, distance):
    count = lax.axis_size("ctx")
    return lax.ppermute(x, "ctx", [(i, i + distance) for i in range(count) if 0 <= i + distance < count])


def nought(x):
    return jnp.minimum(jnp.abs(x), 0.0)


def within_chip(keep, send):
    received = partner(send, "ctx", 0)
    return keep, received, keep + received


def to_cores(core, before, piece, towards):
    keep, received, _ = piece
    is_source = core == (0 if towards == 1 else 1)
    mine = jnp.where(is_source, before, before + received)
    return mine, partner(jnp.where(is_source, before + keep, before), "ctx", 0)


def pinned(x, space):
    return pltpu.with_memory_space_constraint(x, space)


def scatter_step(x, at, axis, bit):
    low, high = jnp.split(x, 2, axis=0 if x.shape[0] > 1 else 1)
    upper = (at >> bit & 1 == 1)[:, :low.shape[-1]]
    return jnp.where(upper, high, low) + partner(jnp.where(upper, low, high), axis, bit)


def on_device(queries, keys, values, out_grad, segment_ids, image_flags, gain):
    rows, width = queries.shape[1:]
    q, k, v, dy = (x[0] for x in (queries, keys, values, out_grad))
    table = image_flags[0]
    gain_row = gain.reshape(1, width)
    ctx = lax.axis_index("ctx")
    core, ctx, dp = (x.reshape(1).astype(jnp.int32) for x in (ctx & 1, ctx, lax.axis_index("dp")))
    lanes = width // GROUPS // 2
    half_rows = lanes // PAIR * E
    heads = lanes // E

    def call(kernel, sel, ins, outs, group=0, after=(), alias=(), scratch=(), sub=1, steps=None, scalars=None):
        scalars = scalars or [core]

        def wide(i, c, *_):
            return (0, (2 * group + (sel + c[0]) % 2) * sub + i % sub)

        def whole(*args):
            return (0, 0)

        def part(i, c, *_):
            return (group, 0, 0)

        def single(*args):
            return (0, 0, 0)

        specs = {
            "vmem": pl.BlockSpec(memory_space=pltpu.VMEM),
            "hbm": pl.BlockSpec(memory_space=pltpu.HBM),
            "wide": pl.BlockSpec((rows, lanes // sub), wide),
            "row": pl.BlockSpec((1, lanes // sub), wide),
            "sums": pl.BlockSpec((1, lanes // PAIR, PAIR), single),
            "zero": pl.BlockSpec((1, rows), whole),
            "all": pl.BlockSpec((GROUPS * half_rows, PAIR), whole),
            "part": pl.BlockSpec((1, half_rows + EXTRA, PAIR), part),
            "later": pl.BlockSpec((1, half_rows + EXTRA, PAIR), lambda *args: (GROUPS + group, 0, 0)),
            "one": pl.BlockSpec((1, half_rows + EXTRA, PAIR), single),
            "half": pl.BlockSpec((half_rows, PAIR), whole),
            "parts": pl.BlockSpec((GROUPS, half_rows + EXTRA, PAIR), lambda *args: (0, 0, 0)),
            "seg": pl.BlockSpec((1, rows), whole),
            "table": pl.BlockSpec((1, table.shape[0]), whole),
            "mask": pl.BlockSpec((rows, rows), whole),
            "token": pl.BlockSpec((1, PAIR), whole),
            "after2": pl.BlockSpec((8, PAIR), whole),
            "after3": pl.BlockSpec((1, 8, PAIR), lambda *args: (0, 0, 0)),
            "any": pl.BlockSpec(memory_space=pl.ANY),
        }
        shapes = {
            "wide": (rows, width),
            "sums": (1, lanes // PAIR, PAIR),
            "one": (1, half_rows + EXTRA, PAIR),
            "half": (half_rows, PAIR),
            "zero": (1, rows),
            "all": (GROUPS * half_rows, PAIR),
            "part": (GROUPS, half_rows + EXTRA, PAIR),
            "parts": (GROUPS, half_rows + EXTRA, PAIR),
            "token": (1, PAIR),
        }
        spaces = {"vmem": pltpu.VMEM, "hbm": pltpu.HBM}
        operands = [pinned(x, spaces[kind]) if kind in spaces else x for kind, x in ins] + list(after)
        kinds = [kind for kind, _ in ins] + [f"after{x.ndim}" for x in after]
        aliases = {}
        for out_at, x in alias:
            if x is not None:
                aliases[len(scalars) + len(operands)] = out_at
                operands.append(x)
                kinds.append("any")
        out_shape = [
            pltpu.VMEM(*shape, dtype) if kind == "vmem" else jax.ShapeDtypeStruct(shapes[kind], dtype)
            for kind, dtype, *shape in outs
        ]
        return pl.pallas_call(
            kernel,
            grid_spec=pltpu.PrefetchScalarGridSpec(
                num_scalar_prefetch=len(scalars),
                grid=steps or (sub,),
                in_specs=[specs[kind] for kind in kinds],
                out_specs=[specs[kind] for kind, *_ in outs],
                scratch_shapes=scratch,
            ),
            out_shape=out_shape,
            input_output_aliases=aliases,
            compiler_params=pltpu.CompilerParams(vmem_limit_bytes=VMEM),
            cost_estimate=pl.CostEstimate(flops=1, bytes_accessed=1, transcendentals=0),
        )(*scalars, *operands)

    edges = [("seg", segment_ids), ("table", image_flags)]
    chips = lax.axis_size("ctx") // 2
    whole, part_of, one_of = (rows, width), (rows, width // 2), (rows, lanes)
    groups = range(GROUPS)

    def local_attn(sel, after):
        return call(
            functools.partial(local_kernel, sel), sel,
            [("vmem", q), ("vmem", k), ("vmem", v), ("mask", mask), ("mask", mask_t)],
            [("vmem", F32, part_of), ("vmem", BF16, (GROUPS * heads, rows, rows)), ("token", F32)],
            after=after, steps=(GROUPS,))

    def norm(sel, g, before, after):
        return call(
            functools.partial(norm_kernel, sel, g), sel,
            [("vmem", q), ("vmem", dy), ("vmem", local[sel][0]), ("row", gain_row), *edges,
             ("half", prefix[g][sel]), ("part", nxt[sel])],
            [("wide", BF16), ("vmem", BF16, one_of), ("one", F32), ("sums", F32), ("half", F32), ("token", F32)],
            group=g, after=after, alias=[(0, before)])

    def inner(sel, g, before, after):
        return call(
            functools.partial(inner_kernel, sel, g), sel,
            [("vmem", q), ("vmem", k), ("vmem", v), ("vmem", norms[g][sel][1]), ("vmem", local[sel][1]), ("mask", mask),
             *edges, ("half", prefix[g][sel]), ("part", nxt[sel])],
            [("wide", BF16), ("vmem", F32, one_of), ("vmem", F32, one_of), ("token", F32)],
            group=g, after=after, alias=[(0, before)], sub=SUB)

    def outer(sel, g, before, after):
        return call(
            functools.partial(outer_kernel, sel, g), sel,
            [("vmem", k), ("vmem", v), ("vmem", inners[sel, g][1]), ("vmem", inners[sel, g][2]), *edges,
             ("half", suffix[g][sel]), ("later" if sel else "part", prv)],
            [("wide", BF16), ("wide", BF16), ("token", F32)],
            group=g, after=after, alias=list(enumerate(before)), sub=SUB)

    def rows_of_group(x, g):
        return x[g * half_rows:(g + 1) * half_rows]

    def more_hops(load, before, towards):
        span = 2
        while span < chips:
            arrived = shifted(load, 2 * towards * span)
            load, before = load + arrived, before + arrived
            span *= 2
        return before

    keep, send, zero, k, v, core_row, ctx_row, dp_row = call(
        states_kernel, 0, [("hbm", k), ("hbm", v)],
        [("all", F32), ("all", F32), ("zero", jnp.int32), ("vmem", BF16, whole), ("vmem", BF16, whole)]
        + [("token", jnp.int32)] * 3,
        scratch=[pltpu.SemaphoreType.DMA((2 * GROUPS, 2))], steps=(1,), scalars=[core, ctx, dp])
    piece = within_chip(keep, send)
    seg = (segment_ids + zero)[0]
    onehot = seg[:, None] == jnp.arange(table.shape[0], dtype=jnp.int32)[None, :]
    img = jnp.sum(jnp.where(onehot, table[None, :], 0), axis=1)
    imgseg = jnp.where(img == 1, seg, -1)
    pos = jnp.arange(rows)
    mask = ((pos[:, None] >= pos[None, :]) | (imgseg[:, None] == seg[None, :])).astype(BF16)
    mask_t = ((pos[:, None] <= pos[None, :]) | (seg[:, None] == imgseg[None, :])).astype(BF16)

    parts = call(
        part_kernel, 0, [("hbm", q), ("hbm", dy), ("vmem", k), ("vmem", v), *edges],
        [("parts", F32)] * 2 + [("vmem", BF16, whole), ("vmem", BF16, whole), ("token", F32)],
        after=[piece[2]], scratch=[pltpu.SemaphoreType.DMA((2,))], steps=(1,))
    *parts, q, dy, _ = parts
    local = [local_attn(0, [parts[0]])]
    local.append(local_attn(1, [parts[0]]))
    first = shifted(piece[2], 2) + local[0][2] + local[1][2]
    load = piece[2] + first
    loads = [rows_of_group(load, g) for g in groups]
    nxt = [shifted(part + nought(loads[1][:1]), -1) for part in reversed(parts)]
    prefix, norms, late, output, token = [], [], [], None, None
    for g in groups:
        before = more_hops(loads[g], rows_of_group(first, g), 1)
        if g:
            before = before + token
        prefix.append(to_cores(core_row, before, [rows_of_group(x, g) for x in piece], 1))
        norms.append([norm(0, g, output, [])])
        norms[g].append(norm(1, g, norms[g][0][0], [norms[g][0][4]]))
        output, token = norms[g][1][0], norms[g][1][5]
        late.append(within_chip(norms[g][0][4], norms[g][1][4]))

    gain_sum = jnp.concatenate(
        [jnp.where(core_row == half, n[0][3], n[1][3]) for half in range(2) for n in norms], axis=0)
    gain_sum = scatter_step(gain_sum, dp_row, "dp", 0)
    bits = list(reversed(range(lax.axis_size("ctx").bit_length() - 1)))

    load = jnp.concatenate([own for _, _, own in late], axis=0)
    first = shifted(load, -2)
    gain_sum = scatter_step(gain_sum + nought(load[:1]), dp_row, "dp", 1).reshape(-1, PAIR)
    inners = {(0, 0): inner(0, 0, None, [load])}
    inners[0, 1] = inner(0, 1, inners[0, 0][0], [load])
    first = first + inners[0, 1][3]
    load = load + first
    loads = [rows_of_group(load, 0)]
    inners[1, 0] = inner(1, 0, inners[0, 1][0], [loads[0]])
    loads.append(rows_of_group(load, 1) + inners[1, 0][3])
    gain_sum = scatter_step(gain_sum + nought(loads[1][:1]), ctx_row, "ctx", bits[0])
    both = jnp.concatenate([norms[g][sel][2] for sel in (1, 0) for g in groups], axis=0)
    prv = shifted(both + nought(loads[1][:1]), 1)
    inners[1, 1] = inner(1, 1, inners[1, 0][0], [loads[1]])
    grad_q, token = inners[1, 1][0], inners[1, 1][3]
    suffix, outers, grad_gain = [], [None] * 2, gain_sum
    for g in groups:
        before = more_hops(loads[g], rows_of_group(first, g), -1) + token
        if g:
            grad_gain = scatter_step(gain_sum + nought(before[:1]), ctx_row, "ctx", bits[1])
        suffix.append(to_cores(core_row, before, late[g], -1))
        outers = outer(0, g, outers[:2], [])
        if g:
            grad_gain = grad_gain + outers[2]
        outers = outer(1, g, outers[:2], [])
        token = outers[2]
    for bit in bits[2:]:
        grad_gain = scatter_step(grad_gain, ctx_row, "ctx", bit)
    grad_gain = grad_gain.reshape(-1)
    grad_k, grad_v, _ = outers
    return output[None], grad_q[None], grad_k[None], grad_v[None], grad_gain


def solution(mesh):
    return jax.shard_map(
        on_device,
        mesh=mesh,
        in_specs=(
            P("dp", "ctx", None),
            P("dp", "ctx", None),
            P("dp", "ctx", None),
            P("dp", "ctx", None),
            P("dp", "ctx"),
            P("dp", None),
            P(),
        ),
        out_specs=(
            P("dp", "ctx", None),
            P("dp", "ctx", None),
            P("dp", "ctx", None),
            P("dp", "ctx", None),
            P(("dp", "ctx")),
        ),
        check_vma=False,
    )
```

```python
import functools

import jax
import jax.numpy as jnp
from jax import lax
from jax.experimental import pallas as pl
from jax.experimental.pallas import tpu as pltpu
from jax.sharding import PartitionSpec as P

E = 64
PAIR = 2 * E
GROUPS = 2
EXTRA = 8
VMEM = 10 * 2**20
SUB = 2
F32 = jnp.float32
BF16 = jnp.bfloat16


def dot(a, b, ca, cb):
    return lax.dot_general(a, b, (((ca,), (cb,)), ((), ())), preferred_element_type=F32)


def low_lanes(rows, cols):
    lane = lax.broadcasted_iota(jnp.int32, (rows, cols), 1)
    return lane % PAIR < E


def fold(product):
    return jnp.where(low_lanes(E, product.shape[1]), product[:E], product[E:])


def split(state):
    high = state.astype(BF16)
    return high, (state - high.astype(F32)).astype(BF16)


def spread(state):
    low = low_lanes(*state.shape)
    zero = jnp.zeros_like(state)
    return jnp.concatenate([jnp.where(low, state, zero), jnp.where(low, zero, state)], axis=0)


def heads_of(pair):
    low = low_lanes(*pair.shape)
    zero = jnp.zeros_like(pair)
    return jnp.where(low, pair, zero), jnp.where(low, zero, pair)


def twice(x):
    return jnp.concatenate([x, x], axis=1)


def pair_at(ref, p):
    return ref[:, p * PAIR:(p + 1) * PAIR]


def rows_at(base, p):
    return pl.ds(pl.multiple_of(base + p * E, E), E)


def twice(x):
    return jnp.concatenate([x, x], axis=1)


def pair_at(ref, p):
    return ref[:, p * PAIR:(p + 1) * PAIR]


def rows_at(base, p):
    return pl.ds(pl.multiple_of(base + p * E, E), E)


def own_or_received(keep, received, own, p):
    return jnp.where(own, keep[rows_at(p)], received[rows_at(p)])


def state_pair(a, b):
    return fold(dot(a, b, 0, 0))


def edge(seg, table, last):
    row = seg[...]
    count = row.shape[1]
    own = row[:, count - 1:] if last else row[:, :1]
    size = jnp.sum((row == own).astype(F32), axis=1, keepdims=True)
    at = lax.broadcasted_iota(jnp.int32, (count, PAIR), 0).astype(F32)
    rows = at >= count - size if last else at < size
    ids = lax.broadcasted_iota(jnp.int32, table.shape, 1)
    flag = jnp.sum(jnp.where(ids == own, table[...], 0).astype(F32), axis=1, keepdims=True)
    return rows, own.astype(F32), flag


def lanes_at(base, p):
    return pl.ds(pl.multiple_of(base + p * PAIR, PAIR), PAIR)


def place(sel, core, lanes, sub):
    step = pl.program_id(0)
    group, part = step // sub, step % sub
    half = (sel + core[0]) % 2
    base = group * lanes + part * (lanes // sub)
    return group, base, base + (group + half) * lanes, base // PAIR * E


def put_half(sel, core, k, v, out):
    lanes = k.shape[1] // GROUPS // 2
    count = lanes // PAIR
    for group in range(GROUPS):
        base = (2 * group + (sel + core[0]) % 2) * lanes
        for p in range(count):
            at = lanes_at(base, p)
            row = (group * count + p) * E
            out[row:row + E] = state_pair(k[:, at], v[:, at])


def send_kernel(core, ctx, dp, k_in, v_in, send, zero, k, v, core_row, ctx_row, dp_row, sems):
    for row, index in ((core_row, core), (ctx_row, ctx), (dp_row, dp)):
        row[...] = jnp.full(row.shape, index[0], jnp.int32)
    lanes = k.shape[1] // GROUPS // 2
    copies = []
    for sel in (1, 0):
        for group in range(GROUPS):
            base = (2 * group + (sel + core[0]) % 2) * lanes
            at = pl.ds(pl.multiple_of(base, lanes), lanes)
            for i, (array, buf) in enumerate(((k_in, k), (v_in, v))):
                copies.append(pltpu.make_async_copy(array.at[:, at], buf.at[:, at], sems.at[2 * group + sel, i]))
    for copy in copies:
        copy.start()
    zero[...] = jnp.zeros_like(zero)
    for copy in copies[:2 * GROUPS]:
        copy.wait()
    put_half(1, core, k, v, send)
    for copy in copies[2 * GROUPS:]:
        copy.wait()


def keep_kernel(core, k, v, *rest):
    put_half(0, core, k, v, rest[-1])


def part_kernel(core, q_in, dy_in, k, v, seg, table, *rest):
    out, q, dy, token, sems = rest[-5:]
    copies = [pltpu.make_async_copy(a, b, sems.at[i]) for i, (a, b) in enumerate(((q_in, q), (dy_in, dy)))]
    for copy in copies:
        copy.start()
    token[...] = jnp.zeros_like(token)
    lanes = k.shape[1] // GROUPS // 2
    count = lanes // PAIR
    rows, own, _ = edge(seg, table, False)
    keep = rows.astype(BF16)
    for sel in range(2):
        for group in range(GROUPS):
            base = (2 * group + (sel + core[0]) % 2) * lanes
            place_at = (1 - sel) * GROUPS + group
            for p in range(count):
                at = lanes_at(base, p)
                out[place_at, p * E:(p + 1) * E] = state_pair(k[:, at], v[:, at] * keep)
            out[place_at, count * E:] = jnp.broadcast_to(own, (EXTRA, PAIR))
    for copy in copies:
        copy.wait()


def local_kernel(sel, core, q, k, v, mask, mask_t, *rest):
    attn, probs, token = rest[-3:]
    lanes = attn.shape[1] // GROUPS
    group, base, wide, _ = place(sel, core, lanes, 1)
    m, mt = mask[...], mask_t[...]
    token[...] = jnp.zeros_like(token)
    for p in range(lanes // PAIR):
        at = lanes_at(wide, p)
        kp = k[:, at]
        total = None
        for h, (qh, vh) in enumerate(zip(heads_of(q[:, at]), heads_of(v[:, at]))):
            prob = dot(qh, kp, 1, 1).astype(BF16) * m
            probs[group * (lanes // E) + 2 * p + h] = dot(kp, qh, 1, 1).astype(BF16) * mt
            term = dot(prob, vh, 1, 0)
            total = term if total is None else total + term
        attn[:, lanes_at(base, p)] = total


def head_mean(x):
    high, low = split(x)
    ones = spread(jnp.full((E, PAIR), 1.0 / E, BF16))
    return dot(jnp.concatenate([high, low], axis=1), jnp.concatenate([ones, ones], axis=0), 1, 0)


def side_by_side(state, part):
    sh, sl = split(state)
    ph, pll = split(part)
    left = jnp.concatenate([spread(sh), spread(sl)], axis=0)
    right = jnp.concatenate([spread(ph), spread(pll)], axis=0)
    return jnp.concatenate([left, right], axis=1)


def stacked(state, part):
    sh, sl = split(state)
    ph, pll = split(part)
    top = jnp.concatenate([spread(sh), spread(sl)], axis=1)
    bottom = jnp.concatenate([spread(ph), spread(pll)], axis=1)
    return jnp.concatenate([top, bottom], axis=0)


def on_rows(seg, table, last, part):
    rows, own, flag = edge(seg, table, last)
    met = part[0, part.shape[1] - EXTRA:part.shape[1] - EXTRA + 1] == own
    if last:
        met = met & (flag == 1)
    return rows.astype(F32) * met.astype(F32)


def norm_kernel(sel, group, core, q, dy, local, gain, seg, table, prefix, nxt, *rest):
    out, dab, part, gsum, total, token = rest[-6:]
    token[...] = jnp.zeros_like(token)
    lanes = out.shape[1]
    count = lanes // PAIR
    base = group * lanes
    wide = base + (group + (sel + core[0]) % 2) * lanes
    on_next = on_rows(seg, table, True, nxt)
    last, own, flag = edge(seg, table, True)
    last = (last.astype(F32) * jnp.where(flag == 1, 1.0, 0.0)).astype(BF16)
    pairs = [slice(p * PAIR, (p + 1) * PAIR) for p in range(count)]
    bases = [lanes_at(base, p) for p in range(count)]
    wides = [lanes_at(wide, p) for p in range(count)]
    fars = [
        dot(twice(q[:, at]), side_by_side(prefix[rows_at(0, p)], nxt[0, rows_at(0, p)]), 1, 0)
        for p, at in enumerate(wides)
    ]
    attns = [local[:, at] + far[:, :PAIR] + on_next * far[:, PAIR:] for at, far in zip(bases, fars)]
    squares = [head_mean(attn * attn) for attn in attns]
    scales = [lax.rsqrt(square + 1e-06) for square in squares]
    normeds = [attn * scale for attn, scale in zip(attns, scales)]
    gas = [dy[:, at].astype(F32) * gain[:, pair] for at, pair in zip(wides, pairs)]
    means = [head_mean(ga * normed) for ga, normed in zip(gas, normeds)]
    das = [
        (scale * (ga - normed * mean)).astype(BF16)
        for scale, ga, normed, mean in zip(scales, gas, normeds, means)
    ]
    states = [state_pair(q[:, at], jnp.concatenate([da, da * last], axis=1)) for at, da in zip(wides, das)]
    part[0, count * E:] = jnp.broadcast_to(own, (EXTRA, PAIR))
    for p, (at, normed, da) in enumerate(zip(pairs, normeds, das)):
        total[p * E:(p + 1) * E] = states[p][:, :PAIR]
        part[0, p * E:(p + 1) * E] = states[p][:, PAIR:]
        dab[:, bases[p]] = da
        out[:, at] = (normed * gain[:, at]).astype(BF16)
        gsum[0, p:p + 1] = jnp.sum(dy[:, wides[p]].astype(F32) * normed, axis=0, keepdims=True)


def inner_kernel(sel, core, q, k, v, dab, probs, mask, seg, table, prefix_a, prefix_b, nxt, *rest):
    gq, gk, gv, token = rest[-4:]
    lanes = dab.shape[1] // GROUPS
    count = lanes // SUB // PAIR
    group, base, wide, row = place(sel, core, lanes, SUB)
    m = mask[...]
    token[...] = jnp.zeros_like(token)
    on_next = on_rows(seg, table, True, nxt)
    first = row - group * (lanes // 2)
    for p in range(count):
        at = lanes_at(wide, p)
        da = dab[:, lanes_at(base, p)]
        vp = v[:, at]
        far = dot(twice(da), stacked(jnp.where(group == 0, prefix_a[rows_at(first, p)], prefix_b[rows_at(first, p)]), nxt[0, rows_at(first, p)]), 1, 1)
        tq = far[:, :PAIR] + on_next * far[:, PAIR:]
        tk = tv = None
        for h, (qh, kh, dh) in enumerate(zip(heads_of(q[:, at]), heads_of(k[:, at]), heads_of(da))):
            dprob = dot(dh, vp, 1, 1).astype(BF16) * m
            tq = tq + dot(dprob, kh, 1, 0)
            a = dot(dprob, qh, 0, 0)
            b = dot(probs[row // (E // 2) + 2 * p + h], dh, 1, 0)
            tk = a if tk is None else tk + a
            tv = b if tv is None else tv + b
        gq[:, p * PAIR:(p + 1) * PAIR] = tq.astype(BF16)
        gk[:, lanes_at(base, p)] = tk
        gv[:, lanes_at(base, p)] = tv


def outer_kernel(sel, core, k, v, gk_in, gv_in, seg, table, suffix, prv, *rest):
    gk, gv, token = rest[-3:]
    lanes = gk_in.shape[1] // GROUPS
    count = lanes // SUB // PAIR
    group, base, wide, row = place(sel, core, lanes, SUB)
    token[...] = jnp.zeros_like(token)
    on_prev = on_rows(seg, table, False, prv)
    first = row - group * (lanes // 2)
    for p in range(count):
        here, own, at = slice(p * PAIR, (p + 1) * PAIR), lanes_at(base, p), lanes_at(wide, p)
        s = suffix[rows_at(row, p)]
        g = prv[0, rows_at(first, p)]
        far = dot(twice(v[:, at]), stacked(s, g), 1, 1)
        gk[:, here] = (gk_in[:, own] + far[:, :PAIR] + on_prev * far[:, PAIR:]).astype(BF16)
        far = dot(twice(k[:, at]), side_by_side(s, g), 1, 0)
        gv[:, here] = (gv_in[:, own] + far[:, :PAIR] + on_prev * far[:, PAIR:]).astype(BF16)


def partner(x, axis, bit):
    route = [(i, i ^ (1 << bit)) for i in range(lax.axis_size(axis))]
    return lax.ppermute(x, axis, route)


def shifted(x, distance):
    count = lax.axis_size("ctx")
    return lax.ppermute(x, "ctx", [(i, i + distance) for i in range(count) if 0 <= i + distance < count])


def nought(x):
    return jnp.minimum(jnp.abs(x), 0.0)


def within_chip(keep, send):
    received = partner(send, "ctx", 0)
    return keep, received, keep + received


def to_cores(core, before, piece, towards):
    keep, received, _ = piece
    is_source = core == (0 if towards == 1 else 1)
    mine = jnp.where(is_source, before, before + received)
    return mine, partner(jnp.where(is_source, before + keep, before), "ctx", 0)


def pinned(x, space):
    return pltpu.with_memory_space_constraint(x, space)


def scatter_step(x, at, axis, bit):
    low, high = jnp.split(x, 2, axis=0 if x.shape[0] > 1 else 1)
    upper = (at >> bit & 1 == 1)[:, :low.shape[-1]]
    return jnp.where(upper, high, low) + partner(jnp.where(upper, low, high), axis, bit)


def on_device(queries, keys, values, out_grad, segment_ids, image_flags, gain):
    rows, width = queries.shape[1:]
    q, k, v, dy = (x[0] for x in (queries, keys, values, out_grad))
    table = image_flags[0]
    gain_row = gain.reshape(1, width)
    ctx = lax.axis_index("ctx")
    core, ctx, dp = (x.reshape(1).astype(jnp.int32) for x in (ctx & 1, ctx, lax.axis_index("dp")))
    lanes = width // GROUPS // 2
    half_rows = lanes // PAIR * E
    heads = lanes // E

    def call(kernel, sel, ins, outs, group=None, after=(), alias=(), scratch=(), sub=1, steps=None, scalars=None):
        scalars = scalars or [core]

        def group_at(i):
            return i // sub if group is None else group

        def wide(i, c, *_):
            return (0, (2 * group_at(i) + (sel + c[0]) % 2) * sub + i % sub)

        def whole(*args):
            return (0, 0)

        def part(i, c, *_):
            return (sel * GROUPS + group_at(i), 0, 0)

        def single(*args):
            return (0, 0, 0)

        specs = {
            "vmem": pl.BlockSpec(memory_space=pltpu.VMEM),
            "hbm": pl.BlockSpec(memory_space=pltpu.HBM),
            "wide": pl.BlockSpec((rows, lanes // sub), wide),
            "row": pl.BlockSpec((1, lanes // sub), wide),
            "sums": pl.BlockSpec((1, lanes // PAIR, PAIR), single),
            "zero": pl.BlockSpec((1, rows), whole),
            "all": pl.BlockSpec((GROUPS * half_rows, PAIR), whole),
            "part": pl.BlockSpec((1, half_rows + EXTRA, PAIR), part),
            "one": pl.BlockSpec((1, half_rows + EXTRA, PAIR), single),
            "half": pl.BlockSpec((half_rows, PAIR), whole),
            "parts": pl.BlockSpec((2 * GROUPS, half_rows + EXTRA, PAIR), lambda *args: (0, 0, 0)),
            "seg": pl.BlockSpec((1, rows), whole),
            "table": pl.BlockSpec((1, table.shape[0]), whole),
            "mask": pl.BlockSpec((rows, rows), whole),
            "token": pl.BlockSpec((1, PAIR), whole),
            "after2": pl.BlockSpec((8, PAIR), whole),
            "after3": pl.BlockSpec((1, 8, PAIR), lambda *args: (0, 0, 0)),
            "any": pl.BlockSpec(memory_space=pl.ANY),
        }
        shapes = {
            "wide": (rows, width),
            "sums": (1, lanes // PAIR, PAIR),
            "one": (1, half_rows + EXTRA, PAIR),
            "half": (half_rows, PAIR),
            "zero": (1, rows),
            "all": (GROUPS * half_rows, PAIR),
            "part": (GROUPS, half_rows + EXTRA, PAIR),
            "parts": (2 * GROUPS, half_rows + EXTRA, PAIR),
            "token": (1, PAIR),
        }
        spaces = {"vmem": pltpu.VMEM, "hbm": pltpu.HBM}
        operands = [pinned(x, spaces[kind]) if kind in spaces else x for kind, x in ins] + list(after)
        kinds = [kind for kind, _ in ins] + [f"after{x.ndim}" for x in after]
        aliases = {}
        for out_at, x in alias:
            if x is not None:
                aliases[len(scalars) + len(operands)] = out_at
                in_vmem = outs[out_at][0] == "vmem"
                operands.append(pinned(x, pltpu.VMEM) if in_vmem else x)
                kinds.append("vmem" if in_vmem else "any")
        out_shape = [
            pltpu.VMEM(*shape, dtype) if kind == "vmem" else jax.ShapeDtypeStruct(shapes[kind], dtype)
            for kind, dtype, *shape in outs
        ]
        return pl.pallas_call(
            kernel,
            grid_spec=pltpu.PrefetchScalarGridSpec(
                num_scalar_prefetch=len(scalars),
                grid=steps or ((GROUPS if group is None else 1) * sub,),
                in_specs=[specs[kind] for kind in kinds],
                out_specs=[specs[kind] for kind, *_ in outs],
                scratch_shapes=scratch,
            ),
            out_shape=out_shape,
            input_output_aliases=aliases,
            compiler_params=pltpu.CompilerParams(vmem_limit_bytes=VMEM),
            cost_estimate=pl.CostEstimate(flops=1, bytes_accessed=1, transcendentals=0),
        )(*scalars, *operands)

    edges = [("seg", segment_ids), ("table", image_flags)]
    chips = lax.axis_size("ctx") // 2
    whole, part_of = (rows, width), (rows, width // 2)
    groups = range(GROUPS)

    def local_attn(sel, after):
        return call(
            functools.partial(local_kernel, sel), sel,
            [("vmem", q), ("vmem", k), ("vmem", v), ("mask", mask), ("mask", mask_t)],
            [("vmem", F32, part_of), ("vmem", BF16, (GROUPS * heads, rows, rows)), ("token", F32)], after=after)

    def norm(sel, g, before, after):
        return call(
            functools.partial(norm_kernel, sel, g), sel,
            [("vmem", q), ("vmem", dy), ("vmem", local[sel][0]), ("row", gain_row), *edges,
             ("half", prefix[g][sel]), ("part", nxt)],
            [("wide", BF16), ("vmem", BF16, part_of), ("one", F32), ("sums", F32), ("half", F32), ("token", F32)],
            group=g, after=after, alias=list(enumerate(before)))

    def inner(sel, before, after):
        return call(
            functools.partial(inner_kernel, sel), sel,
            [("vmem", q), ("vmem", k), ("vmem", v), ("vmem", norms[sel][-1][1]), ("vmem", local[sel][1]),
             ("mask", mask), *edges, *[("half", p[sel]) for p in prefix], ("part", nxt)],
            [("wide", BF16), ("vmem", F32, part_of), ("vmem", F32, part_of), ("token", F32)],
            after=after, alias=[(0, before)], sub=SUB)

    def outer(sel, before, after):
        return call(
            functools.partial(outer_kernel, sel), sel,
            [("vmem", k), ("vmem", v), ("vmem", inners[sel][1]), ("vmem", inners[sel][2]), *edges,
             ("all", suffix[sel]), ("part", prv[0])],
            [("wide", BF16), ("wide", BF16), ("token", F32)], after=after, alias=list(enumerate(before)), sub=SUB)

    def summed_before(own, towards, works):
        load, before, span = own, None, 1
        while span < chips:
            arrived = shifted(load, 2 * towards * span)
            if works:
                arrived = arrived + works.pop(0)(load)
            before = arrived if before is None else before + arrived
            load = load + arrived
            span *= 2
        for work in works:
            before = before + work(load)
        return before

    send, zero, k, v, core_row, ctx_row, dp_row = call(
        send_kernel, 0, [("hbm", k), ("hbm", v)],
        [("all", F32), ("zero", jnp.int32), ("vmem", BF16, whole), ("vmem", BF16, whole)]
        + [("token", jnp.int32)] * 3,
        scratch=[pltpu.SemaphoreType.DMA((2 * GROUPS, 2))], steps=(1,), scalars=[core, ctx, dp])
    keep, = call(keep_kernel, 0, [("vmem", k), ("vmem", v)], [("all", F32)], steps=(1,))
    piece = within_chip(keep, send)
    seg = (segment_ids + zero)[0]
    onehot = seg[:, None] == jnp.arange(table.shape[0], dtype=jnp.int32)[None, :]
    img = jnp.sum(jnp.where(onehot, table[None, :], 0), axis=1)
    imgseg = jnp.where(img == 1, seg, -1)
    pos = jnp.arange(rows)
    mask = ((pos[:, None] >= pos[None, :]) | (imgseg[:, None] == seg[None, :])).astype(BF16)
    mask_t = ((pos[:, None] <= pos[None, :]) | (seg[:, None] == imgseg[None, :])).astype(BF16)

    parts = call(
        part_kernel, 0, [("hbm", q), ("hbm", dy), ("vmem", k), ("vmem", v), *edges],
        [("parts", F32)] + [("vmem", BF16, whole), ("vmem", BF16, whole), ("token", F32)],
        after=[piece[2]], scratch=[pltpu.SemaphoreType.DMA((2,))], steps=(1,))
    parts, q, dy, _ = parts

    def rows_of_group(x, g):
        return x[g * half_rows:(g + 1) * half_rows]

    local = [local_attn(0, [parts])]
    local.append(local_attn(1, [parts]))
    first = shifted(piece[2], 2) + local[0][2] + local[1][2]
    load = piece[2] + first
    nxt = shifted(parts + nought(load[:1]), -1)
    prefix, norms, before = [], [[], []], [None] * 2
    output, token = None, None
    for g in groups:
        summed, load_g, span = rows_of_group(first, g), rows_of_group(load, g), 2
        while span < chips:
            arrived = shifted(load_g, 2 * span)
            summed, load_g = summed + arrived, load_g + arrived
            span *= 2
        if g:
            summed = summed + token
        prefix.append(to_cores(core_row, summed, [rows_of_group(x, g) for x in piece], 1))
        for sel in range(2):
            made = norm(sel, g, [output, before[sel]], [])
            norms[sel].append(made)
            output, before[sel], token = made[0], made[1], made[5]
    piece = within_chip(*[jnp.concatenate([n[4] for n in norms[sel]], axis=0) for sel in range(2)])

    gain_sum = [jnp.concatenate(
        [jnp.where(core_row == half, norms[0][g][3], norms[1][g][3]) for half in range(2) for g in groups], axis=0)]
    gain_sum.append(scatter_step(gain_sum[-1], dp_row, "dp", 0))
    bits = list(reversed(range(lax.axis_size("ctx").bit_length() - 1)))
    inners, prv = [], []

    def third_work(load):
        x = scatter_step(gain_sum[-1] + nought(load[:1]), dp_row, "dp", 1)
        gain_sum.append(x.reshape(-1, PAIR))
        inners.append(inner(0, None, [load]))
        return inners[0][3]

    def fourth_work(load):
        gain_sum.append(scatter_step(gain_sum[-1] + nought(load[:1]), ctx_row, "ctx", bits[0]))
        both = jnp.concatenate([n[2] for n in norms[1] + norms[0]], axis=0) + nought(load[:1])
        prv.append(shifted(both, 1))
        inners.append(inner(1, inners[0][0], [load]))
        return inners[1][3]

    before = summed_before(piece[2], -1, [third_work, fourth_work])
    suffix = to_cores(core_row, before, piece, -1)
    grad_gain = scatter_step(gain_sum[-1] + nought(before[:1]), ctx_row, "ctx", bits[1])
    outers = outer(0, [None] * 2, [])
    grad_gain = grad_gain + outers[2]
    for bit in bits[2:]:
        grad_gain = scatter_step(grad_gain, ctx_row, "ctx", bit)
    grad_k, grad_v, _ = outer(1, outers[:2], [])
    grad_gain = grad_gain.reshape(-1)
    grad_q = inners[1][0]
    return output[None], grad_q[None], grad_k[None], grad_v[None], grad_gain


def solution(mesh):
    return jax.shard_map(
        on_device,
        mesh=mesh,
        in_specs=(
            P("dp", "ctx", None),
            P("dp", "ctx", None),
            P("dp", "ctx", None),
            P("dp", "ctx", None),
            P("dp", "ctx"),
            P("dp", None),
            P(),
        ),
        out_specs=(
            P("dp", "ctx", None),
            P("dp", "ctx", None),
            P("dp", "ctx", None),
            P("dp", "ctx", None),
            P(("dp", "ctx")),
        ),
        check_vma=False,
    )
```

```python
import functools

import jax
import jax.numpy as jnp
from jax import lax
from jax.experimental import pallas as pl
from jax.experimental.pallas import tpu as pltpu
from jax.sharding import PartitionSpec as P

E = 64
PAIR = 2 * E
GROUPS = 2
EXTRA = 8
VMEM = 10 * 2**20
SUB = 2
F32 = jnp.float32
BF16 = jnp.bfloat16


def dot(a, b, ca, cb):
    return lax.dot_general(a, b, (((ca,), (cb,)), ((), ())), preferred_element_type=F32)


def low_lanes(rows, cols):
    lane = lax.broadcasted_iota(jnp.int32, (rows, cols), 1)
    return lane % PAIR < E


def fold(product):
    return jnp.where(low_lanes(E, product.shape[1]), product[:E], product[E:])


def split(state):
    high = state.astype(BF16)
    return high, (state - high.astype(F32)).astype(BF16)


def spread(state):
    low = low_lanes(*state.shape)
    zero = jnp.zeros_like(state)
    return jnp.concatenate([jnp.where(low, state, zero), jnp.where(low, zero, state)], axis=0)


def heads_of(pair):
    low = low_lanes(*pair.shape)
    zero = jnp.zeros_like(pair)
    return jnp.where(low, pair, zero), jnp.where(low, zero, pair)


def twice(x):
    return jnp.concatenate([x, x], axis=1)


def pair_at(ref, p):
    return ref[:, p * PAIR:(p + 1) * PAIR]


def rows_at(base, p):
    return pl.ds(pl.multiple_of(base + p * E, E), E)


def twice(x):
    return jnp.concatenate([x, x], axis=1)


def pair_at(ref, p):
    return ref[:, p * PAIR:(p + 1) * PAIR]


def rows_at(base, p):
    return pl.ds(pl.multiple_of(base + p * E, E), E)


def own_or_received(keep, received, own, p):
    return jnp.where(own, keep[rows_at(p)], received[rows_at(p)])


def state_pair(a, b):
    return fold(dot(a, b, 0, 0))


def edge(seg, table, last):
    row = seg[...]
    count = row.shape[1]
    own = row[:, count - 1:] if last else row[:, :1]
    size = jnp.sum((row == own).astype(F32), axis=1, keepdims=True)
    at = lax.broadcasted_iota(jnp.int32, (count, PAIR), 0).astype(F32)
    rows = at >= count - size if last else at < size
    ids = lax.broadcasted_iota(jnp.int32, table.shape, 1)
    flag = jnp.sum(jnp.where(ids == own, table[...], 0).astype(F32), axis=1, keepdims=True)
    return rows, own.astype(F32), flag


def lanes_at(base, p):
    return pl.ds(pl.multiple_of(base + p * PAIR, PAIR), PAIR)


def place(sel, core, lanes, sub):
    step = pl.program_id(0)
    group, part = step // sub, step % sub
    half = (sel + core[0]) % 2
    base = group * lanes + part * (lanes // sub)
    return group, base, base + (group + half) * lanes, base // PAIR * E


def put_half(sel, core, k, v, out):
    lanes = k.shape[1] // GROUPS // 2
    count = lanes // PAIR
    for group in range(GROUPS):
        base = (2 * group + (sel + core[0]) % 2) * lanes
        for p in range(count):
            at = lanes_at(base, p)
            row = (group * count + p) * E
            out[row:row + E] = state_pair(k[:, at], v[:, at])


def send_kernel(core, ctx, dp, k_in, v_in, send, zero, k, v, core_row, ctx_row, dp_row, sems):
    for row, index in ((core_row, core), (ctx_row, ctx), (dp_row, dp)):
        row[...] = jnp.full(row.shape, index[0], jnp.int32)
    lanes = k.shape[1] // GROUPS // 2
    copies = []
    for sel in (1, 0):
        for group in range(GROUPS):
            base = (2 * group + (sel + core[0]) % 2) * lanes
            at = pl.ds(pl.multiple_of(base, lanes), lanes)
            for i, (array, buf) in enumerate(((k_in, k), (v_in, v))):
                copies.append(pltpu.make_async_copy(array.at[:, at], buf.at[:, at], sems.at[2 * group + sel, i]))
    for copy in copies:
        copy.start()
    zero[...] = jnp.zeros_like(zero)
    for copy in copies[:2 * GROUPS]:
        copy.wait()
    put_half(1, core, k, v, send)
    for copy in copies[2 * GROUPS:]:
        copy.wait()


def keep_kernel(core, k, v, *rest):
    put_half(0, core, k, v, rest[-1])


def part_kernel(core, q_in, dy_in, k, v, seg, table, *rest):
    *outs, q, dy, token, sems = rest[-6:]
    copies = [pltpu.make_async_copy(a, b, sems.at[i]) for i, (a, b) in enumerate(((q_in, q), (dy_in, dy)))]
    for copy in copies:
        copy.start()
    token[...] = jnp.zeros_like(token)
    lanes = k.shape[1] // GROUPS // 2
    count = lanes // PAIR
    rows, own, _ = edge(seg, table, False)
    keep = rows.astype(BF16)
    for sel, out in enumerate(outs):
        for group in range(GROUPS):
            base = (2 * group + (sel + core[0]) % 2) * lanes
            for p in range(count):
                at = lanes_at(base, p)
                out[group, p * E:(p + 1) * E] = state_pair(k[:, at], v[:, at] * keep)
            out[group, count * E:] = jnp.broadcast_to(own, (EXTRA, PAIR))
    for copy in copies:
        copy.wait()


def local_kernel(sel, core, q, k, v, mask, mask_t, *rest):
    attn, probs, token = rest[-3:]
    lanes = attn.shape[1] // GROUPS
    group, base, wide, _ = place(sel, core, lanes, 1)
    m, mt = mask[...], mask_t[...]
    token[...] = jnp.zeros_like(token)
    for p in range(lanes // PAIR):
        at = lanes_at(wide, p)
        kp = k[:, at]
        total = None
        for h, (qh, vh) in enumerate(zip(heads_of(q[:, at]), heads_of(v[:, at]))):
            prob = dot(qh, kp, 1, 1).astype(BF16) * m
            probs[group * (lanes // E) + 2 * p + h] = dot(kp, qh, 1, 1).astype(BF16) * mt
            term = dot(prob, vh, 1, 0)
            total = term if total is None else total + term
        attn[:, lanes_at(base, p)] = total


def head_mean(x):
    high, low = split(x)
    ones = spread(jnp.full((E, PAIR), 1.0 / E, BF16))
    return dot(jnp.concatenate([high, low], axis=1), jnp.concatenate([ones, ones], axis=0), 1, 0)


def side_by_side(state, part):
    sh, sl = split(state)
    ph, pll = split(part)
    left = jnp.concatenate([spread(sh), spread(sl)], axis=0)
    right = jnp.concatenate([spread(ph), spread(pll)], axis=0)
    return jnp.concatenate([left, right], axis=1)


def stacked(state, part):
    sh, sl = split(state)
    ph, pll = split(part)
    top = jnp.concatenate([spread(sh), spread(sl)], axis=1)
    bottom = jnp.concatenate([spread(ph), spread(pll)], axis=1)
    return jnp.concatenate([top, bottom], axis=0)


def on_rows(seg, table, last, part):
    rows, own, flag = edge(seg, table, last)
    met = part[0, part.shape[1] - EXTRA:part.shape[1] - EXTRA + 1] == own
    if last:
        met = met & (flag == 1)
    return rows.astype(F32) * met.astype(F32)


def norm_kernel(sel, core, q, dy, local, gain, seg, table, prefix, nxt, *rest):
    out, dab, part, gsum, total, token = rest[-6:]
    token[...] = jnp.zeros_like(token)
    lanes = out.shape[1]
    count = lanes // PAIR
    _, base, wide, row = place(sel, core, lanes, 1)
    on_next = on_rows(seg, table, True, nxt)
    last, own, flag = edge(seg, table, True)
    last = (last.astype(F32) * jnp.where(flag == 1, 1.0, 0.0)).astype(BF16)
    pairs = [slice(p * PAIR, (p + 1) * PAIR) for p in range(count)]
    bases = [lanes_at(base, p) for p in range(count)]
    wides = [lanes_at(wide, p) for p in range(count)]
    fars = [
        dot(twice(q[:, at]), side_by_side(prefix[rows_at(row, p)], nxt[0, rows_at(0, p)]), 1, 0)
        for p, at in enumerate(wides)
    ]
    attns = [local[:, at] + far[:, :PAIR] + on_next * far[:, PAIR:] for at, far in zip(bases, fars)]
    squares = [head_mean(attn * attn) for attn in attns]
    scales = [lax.rsqrt(square + 1e-06) for square in squares]
    normeds = [attn * scale for attn, scale in zip(attns, scales)]
    gas = [dy[:, at].astype(F32) * gain[:, pair] for at, pair in zip(wides, pairs)]
    means = [head_mean(ga * normed) for ga, normed in zip(gas, normeds)]
    das = [
        (scale * (ga - normed * mean)).astype(BF16)
        for scale, ga, normed, mean in zip(scales, gas, normeds, means)
    ]
    states = [state_pair(q[:, at], jnp.concatenate([da, da * last], axis=1)) for at, da in zip(wides, das)]
    part[0, count * E:] = jnp.broadcast_to(own, (EXTRA, PAIR))
    for p, (at, normed, da) in enumerate(zip(pairs, normeds, das)):
        total[rows_at(row, p)] = states[p][:, :PAIR]
        part[0, p * E:(p + 1) * E] = states[p][:, PAIR:]
        dab[:, bases[p]] = da
        out[:, at] = (normed * gain[:, at]).astype(BF16)
        gsum[0, p:p + 1] = jnp.sum(dy[:, wides[p]].astype(F32) * normed, axis=0, keepdims=True)


def inner_kernel(sel, core, q, k, v, dab, probs, mask, seg, table, prefix, nxt, *rest):
    gq, gk, gv, token = rest[-4:]
    lanes = dab.shape[1] // GROUPS
    count = lanes // SUB // PAIR
    group, base, wide, row = place(sel, core, lanes, SUB)
    m = mask[...]
    token[...] = jnp.zeros_like(token)
    on_next = on_rows(seg, table, True, nxt)
    first = row - group * (lanes // 2)
    for p in range(count):
        at = lanes_at(wide, p)
        da = dab[:, lanes_at(base, p)]
        vp = v[:, at]
        far = dot(twice(da), stacked(prefix[rows_at(row, p)], nxt[0, rows_at(first, p)]), 1, 1)
        tq = far[:, :PAIR] + on_next * far[:, PAIR:]
        tk = tv = None
        for h, (qh, kh, dh) in enumerate(zip(heads_of(q[:, at]), heads_of(k[:, at]), heads_of(da))):
            dprob = dot(dh, vp, 1, 1).astype(BF16) * m
            tq = tq + dot(dprob, kh, 1, 0)
            a = dot(dprob, qh, 0, 0)
            b = dot(probs[row // (E // 2) + 2 * p + h], dh, 1, 0)
            tk = a if tk is None else tk + a
            tv = b if tv is None else tv + b
        gq[:, p * PAIR:(p + 1) * PAIR] = tq.astype(BF16)
        gk[:, lanes_at(base, p)] = tk
        gv[:, lanes_at(base, p)] = tv


def outer_kernel(sel, core, k, v, gk_in, gv_in, seg, table, suffix, prv, *rest):
    gk, gv, token = rest[-3:]
    lanes = gk_in.shape[1] // GROUPS
    count = lanes // SUB // PAIR
    group, base, wide, row = place(sel, core, lanes, SUB)
    token[...] = jnp.zeros_like(token)
    on_prev = on_rows(seg, table, False, prv)
    first = row - group * (lanes // 2)
    for p in range(count):
        here, own, at = slice(p * PAIR, (p + 1) * PAIR), lanes_at(base, p), lanes_at(wide, p)
        s = suffix[rows_at(row, p)]
        g = prv[0, rows_at(first, p)]
        far = dot(twice(v[:, at]), stacked(s, g), 1, 1)
        gk[:, here] = (gk_in[:, own] + far[:, :PAIR] + on_prev * far[:, PAIR:]).astype(BF16)
        far = dot(twice(k[:, at]), side_by_side(s, g), 1, 0)
        gv[:, here] = (gv_in[:, own] + far[:, :PAIR] + on_prev * far[:, PAIR:]).astype(BF16)


def partner(x, axis, bit):
    route = [(i, i ^ (1 << bit)) for i in range(lax.axis_size(axis))]
    return lax.ppermute(x, axis, route)


def shifted(x, distance):
    count = lax.axis_size("ctx")
    return lax.ppermute(x, "ctx", [(i, i + distance) for i in range(count) if 0 <= i + distance < count])


def nought(x):
    return jnp.minimum(jnp.abs(x), 0.0)


def within_chip(keep, send):
    received = partner(send, "ctx", 0)
    return keep, received, keep + received


def to_cores(core, before, piece, towards):
    keep, received, _ = piece
    is_source = core == (0 if towards == 1 else 1)
    mine = jnp.where(is_source, before, before + received)
    return mine, partner(jnp.where(is_source, before + keep, before), "ctx", 0)


def pinned(x, space):
    return pltpu.with_memory_space_constraint(x, space)


def scatter_step(x, at, axis, bit):
    low, high = jnp.split(x, 2, axis=0 if x.shape[0] > 1 else 1)
    upper = (at >> bit & 1 == 1)[:, :low.shape[-1]]
    return jnp.where(upper, high, low) + partner(jnp.where(upper, low, high), axis, bit)


def on_device(queries, keys, values, out_grad, segment_ids, image_flags, gain):
    rows, width = queries.shape[1:]
    q, k, v, dy = (x[0] for x in (queries, keys, values, out_grad))
    table = image_flags[0]
    gain_row = gain.reshape(1, width)
    ctx = lax.axis_index("ctx")
    core, ctx, dp = (x.reshape(1).astype(jnp.int32) for x in (ctx & 1, ctx, lax.axis_index("dp")))
    lanes = width // GROUPS // 2
    half_rows = lanes // PAIR * E
    heads = lanes // E

    def call(kernel, sel, ins, outs, after=(), alias=(), scratch=(), sub=1, steps=None, scalars=None):
        scalars = scalars or [core]

        def wide(i, c, *_):
            return (0, (i // sub * 2 + (sel + c[0]) % 2) * sub + i % sub)

        def whole(*args):
            return (0, 0)

        def part(i, c, *_):
            return (i // sub, 0, 0)

        specs = {
            "vmem": pl.BlockSpec(memory_space=pltpu.VMEM),
            "hbm": pl.BlockSpec(memory_space=pltpu.HBM),
            "wide": pl.BlockSpec((rows, lanes // sub), wide),
            "row": pl.BlockSpec((1, lanes // sub), wide),
            "sums": pl.BlockSpec((1, lanes // PAIR, PAIR), part),
            "zero": pl.BlockSpec((1, rows), whole),
            "all": pl.BlockSpec((GROUPS * half_rows, PAIR), whole),
            "part": pl.BlockSpec((1, half_rows + EXTRA, PAIR), part),
            "later": pl.BlockSpec((1, half_rows + EXTRA, PAIR), lambda i, *_: (GROUPS + i // sub, 0, 0)),
            "parts": pl.BlockSpec((GROUPS, half_rows + EXTRA, PAIR), lambda *args: (0, 0, 0)),
            "seg": pl.BlockSpec((1, rows), whole),
            "table": pl.BlockSpec((1, table.shape[0]), whole),
            "mask": pl.BlockSpec((rows, rows), whole),
            "token": pl.BlockSpec((1, PAIR), whole),
            "after2": pl.BlockSpec((8, PAIR), whole),
            "after3": pl.BlockSpec((1, 8, PAIR), lambda *args: (0, 0, 0)),
            "any": pl.BlockSpec(memory_space=pl.ANY),
        }
        shapes = {
            "wide": (rows, width),
            "sums": (GROUPS, lanes // PAIR, PAIR),
            "zero": (1, rows),
            "all": (GROUPS * half_rows, PAIR),
            "part": (GROUPS, half_rows + EXTRA, PAIR),
            "parts": (GROUPS, half_rows + EXTRA, PAIR),
            "token": (1, PAIR),
        }
        spaces = {"vmem": pltpu.VMEM, "hbm": pltpu.HBM}
        operands = [pinned(x, spaces[kind]) if kind in spaces else x for kind, x in ins] + list(after)
        kinds = [kind for kind, _ in ins] + [f"after{x.ndim}" for x in after]
        aliases = {}
        for out_at, x in alias:
            if x is not None:
                aliases[len(scalars) + len(operands)] = out_at
                operands.append(x)
                kinds.append("any")
        out_shape = [
            pltpu.VMEM(*shape, dtype) if kind == "vmem" else jax.ShapeDtypeStruct(shapes[kind], dtype)
            for kind, dtype, *shape in outs
        ]
        return pl.pallas_call(
            kernel,
            grid_spec=pltpu.PrefetchScalarGridSpec(
                num_scalar_prefetch=len(scalars),
                grid=steps or (GROUPS * sub,),
                in_specs=[specs[kind] for kind in kinds],
                out_specs=[specs[kind] for kind, *_ in outs],
                scratch_shapes=scratch,
            ),
            out_shape=out_shape,
            input_output_aliases=aliases,
            compiler_params=pltpu.CompilerParams(vmem_limit_bytes=VMEM),
            cost_estimate=pl.CostEstimate(flops=1, bytes_accessed=1, transcendentals=0),
        )(*scalars, *operands)

    edges = [("seg", segment_ids), ("table", image_flags)]
    chips = lax.axis_size("ctx") // 2
    whole, part_of = (rows, width), (rows, width // 2)

    def local_attn(sel, after):
        return call(
            functools.partial(local_kernel, sel), sel,
            [("vmem", q), ("vmem", k), ("vmem", v), ("mask", mask), ("mask", mask_t)],
            [("vmem", F32, part_of), ("vmem", BF16, (GROUPS * heads, rows, rows)), ("token", F32)], after=after)

    def norm(sel, before, after):
        return call(
            functools.partial(norm_kernel, sel), sel,
            [("vmem", q), ("vmem", dy), ("vmem", local[sel][0]), ("row", gain_row), *edges,
             ("all", prefix[sel]), ("part", nxt[sel])],
            [("wide", BF16), ("vmem", BF16, part_of), ("part", F32), ("sums", F32), ("all", F32), ("token", F32)],
            after=after, alias=[(0, before)])

    def inner(sel, before, after):
        return call(
            functools.partial(inner_kernel, sel), sel,
            [("vmem", q), ("vmem", k), ("vmem", v), ("vmem", norms[sel][1]), ("vmem", local[sel][1]), ("mask", mask),
             *edges, ("all", prefix[sel]), ("part", nxt[sel])],
            [("wide", BF16), ("vmem", F32, part_of), ("vmem", F32, part_of), ("token", F32)],
            after=after, alias=[(0, before)], sub=SUB)

    def outer(sel, before, after):
        return call(
            functools.partial(outer_kernel, sel), sel,
            [("vmem", k), ("vmem", v), ("vmem", inners[sel][1]), ("vmem", inners[sel][2]), *edges,
             ("all", suffix[sel]), ("later" if sel else "part", prv[0])],
            [("wide", BF16), ("wide", BF16), ("token", F32)], after=after, alias=list(enumerate(before)), sub=SUB)

    def summed_before(own, towards, works):
        load, before, span = own, None, 1
        while span < chips:
            arrived = shifted(load, 2 * towards * span)
            if works:
                arrived = arrived + works.pop(0)(load)
            before = arrived if before is None else before + arrived
            load = load + arrived
            span *= 2
        for work in works:
            before = before + work(load)
        return before

    send, zero, k, v, core_row, ctx_row, dp_row = call(
        send_kernel, 0, [("hbm", k), ("hbm", v)],
        [("all", F32), ("zero", jnp.int32), ("vmem", BF16, whole), ("vmem", BF16, whole)]
        + [("token", jnp.int32)] * 3,
        scratch=[pltpu.SemaphoreType.DMA((2 * GROUPS, 2))], steps=(1,), scalars=[core, ctx, dp])
    keep, = call(keep_kernel, 0, [("vmem", k), ("vmem", v)], [("all", F32)], steps=(1,))
    piece = within_chip(keep, send)
    seg = (segment_ids + zero)[0]
    onehot = seg[:, None] == jnp.arange(table.shape[0], dtype=jnp.int32)[None, :]
    img = jnp.sum(jnp.where(onehot, table[None, :], 0), axis=1)
    imgseg = jnp.where(img == 1, seg, -1)
    pos = jnp.arange(rows)
    mask = ((pos[:, None] >= pos[None, :]) | (imgseg[:, None] == seg[None, :])).astype(BF16)
    mask_t = ((pos[:, None] <= pos[None, :]) | (seg[:, None] == imgseg[None, :])).astype(BF16)

    parts = call(
        part_kernel, 0, [("hbm", q), ("hbm", dy), ("vmem", k), ("vmem", v), *edges],
        [("parts", F32)] * 2 + [("vmem", BF16, whole), ("vmem", BF16, whole), ("token", F32)],
        after=[piece[2]], scratch=[pltpu.SemaphoreType.DMA((2,))], steps=(1,))
    *parts, q, dy, _ = parts
    local, nxt = [], []

    def first_work(load):
        tokens = []
        for sel in range(2):
            *made, token = local_attn(sel, [parts[0]])
            local.append(made)
            tokens.append(token)
        return sum(tokens)

    def second_work(load):
        for part in reversed(parts):
            nxt.append(shifted(part + nought(load[:1]), -1))
        return jnp.zeros((1, PAIR), F32)

    before = summed_before(piece[2], 1, [first_work, second_work])
    prefix = to_cores(core_row, before, piece, 1)
    norms = [norm(0, None, [])]
    norms.append(norm(1, norms[0][0], [norms[0][4]]))
    output = norms[1][0]
    piece = within_chip(norms[0][4], norms[1][4])
    gain_sum = [jnp.concatenate([jnp.where(core_row == half, norms[0][3], norms[1][3]) for half in range(2)], axis=0)]
    gain_sum.append(scatter_step(gain_sum[-1], dp_row, "dp", 0))
    bits = list(reversed(range(lax.axis_size("ctx").bit_length() - 1)))
    inners, prv = [], []

    def third_work(load):
        x = scatter_step(gain_sum[-1] + nought(load[:1]), dp_row, "dp", 1)
        gain_sum.append(x.reshape(-1, PAIR))
        inners.append(inner(0, None, [load]))
        return inners[0][3]

    def fourth_work(load):
        gain_sum.append(scatter_step(gain_sum[-1] + nought(load[:1]), ctx_row, "ctx", bits[0]))
        both = jnp.concatenate([norms[1][2], norms[0][2]], axis=0) + nought(load[:1])
        prv.append(shifted(both, 1))
        inners.append(inner(1, inners[0][0], [load]))
        return inners[1][3]

    before = summed_before(piece[2], -1, [third_work, fourth_work])
    suffix = to_cores(core_row, before, piece, -1)
    grad_gain = scatter_step(gain_sum[-1] + nought(before[:1]), ctx_row, "ctx", bits[1])
    outers = outer(0, [None] * 2, [])
    grad_gain = grad_gain + outers[2]
    for bit in bits[2:]:
        grad_gain = scatter_step(grad_gain, ctx_row, "ctx", bit)
    grad_k, grad_v, _ = outer(1, outers[:2], [])
    grad_gain = grad_gain.reshape(-1)
    grad_q = inners[1][0]
    return output[None], grad_q[None], grad_k[None], grad_v[None], grad_gain


def solution(mesh):
    return jax.shard_map(
        on_device,
        mesh=mesh,
        in_specs=(
            P("dp", "ctx", None),
            P("dp", "ctx", None),
            P("dp", "ctx", None),
            P("dp", "ctx", None),
            P("dp", "ctx"),
            P("dp", None),
            P(),
        ),
        out_specs=(
            P("dp", "ctx", None),
            P("dp", "ctx", None),
            P("dp", "ctx", None),
            P("dp", "ctx", None),
            P(("dp", "ctx")),
        ),
        check_vma=False,
    )
```

```python
import functools

import jax
import jax.numpy as jnp
from jax import lax
from jax.experimental import pallas as pl
from jax.experimental.pallas import tpu as pltpu
from jax.sharding import PartitionSpec as P

E = 64
PAIR = 2 * E
GROUPS = 2
EXTRA = 8
VMEM = 10 * 2**20
SUB = 2
F32 = jnp.float32
BF16 = jnp.bfloat16


def dot(a, b, ca, cb):
    return lax.dot_general(a, b, (((ca,), (cb,)), ((), ())), preferred_element_type=F32)


def low_lanes(rows, cols):
    lane = lax.broadcasted_iota(jnp.int32, (rows, cols), 1)
    return lane % PAIR < E


def fold(product):
    return jnp.where(low_lanes(E, product.shape[1]), product[:E], product[E:])


def split(state):
    high = state.astype(BF16)
    return high, (state - high.astype(F32)).astype(BF16)


def spread(state):
    low = low_lanes(*state.shape)
    zero = jnp.zeros_like(state)
    return jnp.concatenate([jnp.where(low, state, zero), jnp.where(low, zero, state)], axis=0)


def heads_of(pair):
    low = low_lanes(*pair.shape)
    zero = jnp.zeros_like(pair)
    return jnp.where(low, pair, zero), jnp.where(low, zero, pair)


def twice(x):
    return jnp.concatenate([x, x], axis=1)


def pair_at(ref, p):
    return ref[:, p * PAIR:(p + 1) * PAIR]


def rows_at(base, p):
    return pl.ds(pl.multiple_of(base + p * E, E), E)


def twice(x):
    return jnp.concatenate([x, x], axis=1)


def pair_at(ref, p):
    return ref[:, p * PAIR:(p + 1) * PAIR]


def rows_at(base, p):
    return pl.ds(pl.multiple_of(base + p * E, E), E)


def own_or_received(keep, received, own, p):
    return jnp.where(own, keep[rows_at(p)], received[rows_at(p)])


def state_pair(a, b):
    return fold(dot(a, b, 0, 0))


def edge(seg, table, last):
    row = seg[...]
    count = row.shape[1]
    own = row[:, count - 1:] if last else row[:, :1]
    size = jnp.sum((row == own).astype(F32), axis=1, keepdims=True)
    at = lax.broadcasted_iota(jnp.int32, (count, PAIR), 0).astype(F32)
    rows = at >= count - size if last else at < size
    ids = lax.broadcasted_iota(jnp.int32, table.shape, 1)
    flag = jnp.sum(jnp.where(ids == own, table[...], 0).astype(F32), axis=1, keepdims=True)
    return rows, own.astype(F32), flag


def lanes_at(base, p):
    return pl.ds(pl.multiple_of(base + p * PAIR, PAIR), PAIR)


def place(sel, core, lanes, sub):
    step = pl.program_id(0)
    group, part = step // sub, step % sub
    half = (sel + core[0]) % 2
    base = group * lanes + part * (lanes // sub)
    return group, base, base + (group + half) * lanes, base // PAIR * E


def put_half(sel, core, k_in, v_in, k, v, out, sems):
    lanes = k.shape[1] // GROUPS // 2
    count = lanes // PAIR
    bases = [(2 * group + (sel + core[0]) % 2) * lanes for group in range(GROUPS)]
    copies = []
    for group, base in enumerate(bases):
        at = pl.ds(pl.multiple_of(base, lanes), lanes)
        for i, (array, buf) in enumerate(((k_in, k), (v_in, v))):
            copies.append(pltpu.make_async_copy(array.at[:, at], buf.at[:, at], sems.at[group, i]))
    for copy in copies:
        copy.start()
    for group, base in enumerate(bases):
        copies[2 * group].wait()
        copies[2 * group + 1].wait()
        for p in range(count):
            at = lanes_at(base, p)
            row = (group * count + p) * E
            out[row:row + E] = state_pair(k[:, at], v[:, at])


def send_kernel(core, ctx, dp, k_in, v_in, send, zero, k, v, core_row, ctx_row, dp_row, sems):
    for row, index in ((core_row, core), (ctx_row, ctx), (dp_row, dp)):
        row[...] = jnp.full(row.shape, index[0], jnp.int32)
    zero[...] = jnp.zeros_like(zero)
    put_half(1, core, k_in, v_in, k, v, send, sems)


def keep_kernel(core, k_in, v_in, *rest):
    keep, k, v, sems = rest[-4:]
    put_half(0, core, k_in, v_in, k, v, keep, sems)


def part_kernel(core, q_in, dy_in, k, v, seg, table, *rest):
    *outs, q, dy, token, sems = rest[-6:]
    copies = [pltpu.make_async_copy(a, b, sems.at[i]) for i, (a, b) in enumerate(((q_in, q), (dy_in, dy)))]
    for copy in copies:
        copy.start()
    token[...] = jnp.zeros_like(token)
    lanes = k.shape[1] // GROUPS // 2
    count = lanes // PAIR
    rows, own, _ = edge(seg, table, False)
    keep = rows.astype(BF16)
    for sel, out in enumerate(outs):
        for group in range(GROUPS):
            base = (2 * group + (sel + core[0]) % 2) * lanes
            for p in range(count):
                at = lanes_at(base, p)
                out[group, p * E:(p + 1) * E] = state_pair(k[:, at], v[:, at] * keep)
            out[group, count * E:] = jnp.broadcast_to(own, (EXTRA, PAIR))
    for copy in copies:
        copy.wait()


def local_kernel(sel, core, q, k, v, mask, mask_t, *rest):
    attn, probs, token = rest[-3:]
    lanes = attn.shape[1] // GROUPS
    group, base, wide, _ = place(sel, core, lanes, 1)
    m, mt = mask[...], mask_t[...]
    token[...] = jnp.zeros_like(token)
    for p in range(lanes // PAIR):
        at = lanes_at(wide, p)
        kp = k[:, at]
        total = None
        for h, (qh, vh) in enumerate(zip(heads_of(q[:, at]), heads_of(v[:, at]))):
            prob = dot(qh, kp, 1, 1).astype(BF16) * m
            probs[group * (lanes // E) + 2 * p + h] = dot(kp, qh, 1, 1).astype(BF16) * mt
            term = dot(prob, vh, 1, 0)
            total = term if total is None else total + term
        attn[:, lanes_at(base, p)] = total


def head_mean(x):
    high, low = split(x)
    ones = spread(jnp.full((E, PAIR), 1.0 / E, BF16))
    return dot(jnp.concatenate([high, low], axis=1), jnp.concatenate([ones, ones], axis=0), 1, 0)


def side_by_side(state, part):
    sh, sl = split(state)
    ph, pll = split(part)
    left = jnp.concatenate([spread(sh), spread(sl)], axis=0)
    right = jnp.concatenate([spread(ph), spread(pll)], axis=0)
    return jnp.concatenate([left, right], axis=1)


def stacked(state, part):
    sh, sl = split(state)
    ph, pll = split(part)
    top = jnp.concatenate([spread(sh), spread(sl)], axis=1)
    bottom = jnp.concatenate([spread(ph), spread(pll)], axis=1)
    return jnp.concatenate([top, bottom], axis=0)


def on_rows(seg, table, last, part):
    rows, own, flag = edge(seg, table, last)
    met = part[0, part.shape[1] - EXTRA:part.shape[1] - EXTRA + 1] == own
    if last:
        met = met & (flag == 1)
    return rows.astype(F32) * met.astype(F32)


def norm_kernel(sel, core, q, dy, local, gain, seg, table, prefix, nxt, *rest):
    out, dab, part, gsum, total, token = rest[-6:]
    token[...] = jnp.zeros_like(token)
    lanes = out.shape[1]
    count = lanes // PAIR
    _, base, wide, row = place(sel, core, lanes, 1)
    on_next = on_rows(seg, table, True, nxt)
    last, own, flag = edge(seg, table, True)
    last = (last.astype(F32) * jnp.where(flag == 1, 1.0, 0.0)).astype(BF16)
    pairs = [slice(p * PAIR, (p + 1) * PAIR) for p in range(count)]
    bases = [lanes_at(base, p) for p in range(count)]
    wides = [lanes_at(wide, p) for p in range(count)]
    fars = [
        dot(twice(q[:, at]), side_by_side(prefix[rows_at(row, p)], nxt[0, rows_at(0, p)]), 1, 0)
        for p, at in enumerate(wides)
    ]
    attns = [local[:, at] + far[:, :PAIR] + on_next * far[:, PAIR:] for at, far in zip(bases, fars)]
    squares = [head_mean(attn * attn) for attn in attns]
    scales = [lax.rsqrt(square + 1e-06) for square in squares]
    normeds = [attn * scale for attn, scale in zip(attns, scales)]
    gas = [dy[:, at].astype(F32) * gain[:, pair] for at, pair in zip(wides, pairs)]
    means = [head_mean(ga * normed) for ga, normed in zip(gas, normeds)]
    das = [
        (scale * (ga - normed * mean)).astype(BF16)
        for scale, ga, normed, mean in zip(scales, gas, normeds, means)
    ]
    states = [state_pair(q[:, at], jnp.concatenate([da, da * last], axis=1)) for at, da in zip(wides, das)]
    part[0, count * E:] = jnp.broadcast_to(own, (EXTRA, PAIR))
    for p, (at, normed, da) in enumerate(zip(pairs, normeds, das)):
        total[rows_at(row, p)] = states[p][:, :PAIR]
        part[0, p * E:(p + 1) * E] = states[p][:, PAIR:]
        dab[:, bases[p]] = da
        out[:, at] = (normed * gain[:, at]).astype(BF16)
        gsum[0, p:p + 1] = jnp.sum(dy[:, wides[p]].astype(F32) * normed, axis=0, keepdims=True)


def inner_kernel(sel, core, q, k, v, dab, probs, mask, seg, table, prefix, nxt, *rest):
    gq, gk, gv, token = rest[-4:]
    lanes = dab.shape[1] // GROUPS
    count = lanes // SUB // PAIR
    group, base, wide, row = place(sel, core, lanes, SUB)
    m = mask[...]
    token[...] = jnp.zeros_like(token)
    on_next = on_rows(seg, table, True, nxt)
    first = row - group * (lanes // 2)
    for p in range(count):
        at = lanes_at(wide, p)
        da = dab[:, lanes_at(base, p)]
        vp = v[:, at]
        far = dot(twice(da), stacked(prefix[rows_at(row, p)], nxt[0, rows_at(first, p)]), 1, 1)
        tq = far[:, :PAIR] + on_next * far[:, PAIR:]
        tk = tv = None
        for h, (qh, kh, dh) in enumerate(zip(heads_of(q[:, at]), heads_of(k[:, at]), heads_of(da))):
            dprob = dot(dh, vp, 1, 1).astype(BF16) * m
            tq = tq + dot(dprob, kh, 1, 0)
            a = dot(dprob, qh, 0, 0)
            b = dot(probs[row // (E // 2) + 2 * p + h], dh, 1, 0)
            tk = a if tk is None else tk + a
            tv = b if tv is None else tv + b
        gq[:, p * PAIR:(p + 1) * PAIR] = tq.astype(BF16)
        gk[:, lanes_at(base, p)] = tk
        gv[:, lanes_at(base, p)] = tv


def outer_kernel(sel, core, k, v, gk_in, gv_in, seg, table, suffix, prv, *rest):
    gk, gv, token = rest[-3:]
    lanes = gk_in.shape[1] // GROUPS
    count = lanes // SUB // PAIR
    group, base, wide, row = place(sel, core, lanes, SUB)
    token[...] = jnp.zeros_like(token)
    on_prev = on_rows(seg, table, False, prv)
    first = row - group * (lanes // 2)
    for p in range(count):
        here, own, at = slice(p * PAIR, (p + 1) * PAIR), lanes_at(base, p), lanes_at(wide, p)
        s = suffix[rows_at(row, p)]
        g = prv[0, rows_at(first, p)]
        far = dot(twice(v[:, at]), stacked(s, g), 1, 1)
        gk[:, here] = (gk_in[:, own] + far[:, :PAIR] + on_prev * far[:, PAIR:]).astype(BF16)
        far = dot(twice(k[:, at]), side_by_side(s, g), 1, 0)
        gv[:, here] = (gv_in[:, own] + far[:, :PAIR] + on_prev * far[:, PAIR:]).astype(BF16)


def partner(x, axis, bit):
    route = [(i, i ^ (1 << bit)) for i in range(lax.axis_size(axis))]
    return lax.ppermute(x, axis, route)


def shifted(x, distance):
    count = lax.axis_size("ctx")
    return lax.ppermute(x, "ctx", [(i, i + distance) for i in range(count) if 0 <= i + distance < count])


def nought(x):
    return jnp.minimum(jnp.abs(x), 0.0)


def cycled(x, distance):
    count = lax.axis_size("ctx")
    return lax.ppermute(x, "ctx", [(i, (i + distance) % count) for i in range(count)])


def within_chip(keep, send):
    received = partner(send, "ctx", 0)
    return keep, received, keep + received


def to_cores(core, before, piece, towards):
    keep, received, _ = piece
    is_source = core == (0 if towards == 1 else 1)
    mine = jnp.where(is_source, before, before + received)
    return mine, partner(jnp.where(is_source, before + keep, before), "ctx", 0)


def pinned(x, space):
    return pltpu.with_memory_space_constraint(x, space)


def scatter_step(x, at, axis, bit):
    low, high = jnp.split(x, 2, axis=0 if x.shape[0] > 1 else 1)
    upper = (at >> bit & 1 == 1)[:, :low.shape[-1]]
    return jnp.where(upper, high, low) + partner(jnp.where(upper, low, high), axis, bit)


def on_device(queries, keys, values, out_grad, segment_ids, image_flags, gain):
    rows, width = queries.shape[1:]
    q, k, v, dy = (x[0] for x in (queries, keys, values, out_grad))
    table = image_flags[0]
    gain_row = gain.reshape(1, width)
    ctx = lax.axis_index("ctx")
    core, ctx, dp = (x.reshape(1).astype(jnp.int32) for x in (ctx & 1, ctx, lax.axis_index("dp")))
    lanes = width // GROUPS // 2
    half_rows = lanes // PAIR * E
    heads = lanes // E

    def call(kernel, sel, ins, outs, after=(), alias=(), scratch=(), sub=1, steps=None, scalars=None):
        scalars = scalars or [core]

        def wide(i, c, *_):
            return (0, (i // sub * 2 + (sel + c[0]) % 2) * sub + i % sub)

        def whole(*args):
            return (0, 0)

        def part(i, c, *_):
            return (i // sub, 0, 0)

        specs = {
            "vmem": pl.BlockSpec(memory_space=pltpu.VMEM),
            "hbm": pl.BlockSpec(memory_space=pltpu.HBM),
            "wide": pl.BlockSpec((rows, lanes // sub), wide),
            "row": pl.BlockSpec((1, lanes // sub), wide),
            "sums": pl.BlockSpec((1, lanes // PAIR, PAIR), part),
            "zero": pl.BlockSpec((1, rows), whole),
            "all": pl.BlockSpec((GROUPS * half_rows, PAIR), whole),
            "part": pl.BlockSpec((1, half_rows + EXTRA, PAIR), part),
            "later": pl.BlockSpec((1, half_rows + EXTRA, PAIR), lambda i, *_: (GROUPS + i // sub, 0, 0)),
            "parts": pl.BlockSpec((GROUPS, half_rows + EXTRA, PAIR), lambda *args: (0, 0, 0)),
            "seg": pl.BlockSpec((1, rows), whole),
            "table": pl.BlockSpec((1, table.shape[0]), whole),
            "mask": pl.BlockSpec((rows, rows), whole),
            "token": pl.BlockSpec((1, PAIR), whole),
            "after2": pl.BlockSpec((8, PAIR), whole),
            "after3": pl.BlockSpec((1, 8, PAIR), lambda *args: (0, 0, 0)),
            "any": pl.BlockSpec(memory_space=pl.ANY),
        }
        shapes = {
            "wide": (rows, width),
            "sums": (GROUPS, lanes // PAIR, PAIR),
            "zero": (1, rows),
            "all": (GROUPS * half_rows, PAIR),
            "part": (GROUPS, half_rows + EXTRA, PAIR),
            "parts": (GROUPS, half_rows + EXTRA, PAIR),
            "token": (1, PAIR),
        }
        spaces = {"vmem": pltpu.VMEM, "hbm": pltpu.HBM}
        operands = [pinned(x, spaces[kind]) if kind in spaces else x for kind, x in ins] + list(after)
        kinds = [kind for kind, _ in ins] + [f"after{x.ndim}" for x in after]
        aliases = {}
        for out_at, x in alias:
            if x is not None:
                aliases[len(scalars) + len(operands)] = out_at
                in_vmem = outs[out_at][0] == "vmem"
                operands.append(pinned(x, pltpu.VMEM) if in_vmem else x)
                kinds.append("vmem" if in_vmem else "any")
        out_shape = [
            pltpu.VMEM(*shape, dtype) if kind == "vmem" else jax.ShapeDtypeStruct(shapes[kind], dtype)
            for kind, dtype, *shape in outs
        ]
        return pl.pallas_call(
            kernel,
            grid_spec=pltpu.PrefetchScalarGridSpec(
                num_scalar_prefetch=len(scalars),
                grid=steps or (GROUPS * sub,),
                in_specs=[specs[kind] for kind in kinds],
                out_specs=[specs[kind] for kind, *_ in outs],
                scratch_shapes=scratch,
            ),
            out_shape=out_shape,
            input_output_aliases=aliases,
            compiler_params=pltpu.CompilerParams(vmem_limit_bytes=VMEM),
            cost_estimate=pl.CostEstimate(flops=1, bytes_accessed=1, transcendentals=0),
        )(*scalars, *operands)

    edges = [("seg", segment_ids), ("table", image_flags)]
    chips = lax.axis_size("ctx") // 2
    whole, part_of = (rows, width), (rows, width // 2)

    def local_attn(sel, after):
        return call(
            functools.partial(local_kernel, sel), sel,
            [("vmem", q), ("vmem", k), ("vmem", v), ("mask", mask), ("mask", mask_t)],
            [("vmem", F32, part_of), ("vmem", BF16, (GROUPS * heads, rows, rows)), ("token", F32)], after=after)

    def norm(sel, before, after):
        return call(
            functools.partial(norm_kernel, sel), sel,
            [("vmem", q), ("vmem", dy), ("vmem", local[sel][0]), ("row", gain_row), *edges,
             ("all", prefix[sel]), ("part", nxt[sel])],
            [("wide", BF16), ("vmem", BF16, part_of), ("part", F32), ("sums", F32), ("all", F32), ("token", F32)],
            after=after, alias=[(0, before)])

    def inner(sel, before, after):
        return call(
            functools.partial(inner_kernel, sel), sel,
            [("vmem", q), ("vmem", k), ("vmem", v), ("vmem", norms[sel][1]), ("vmem", local[sel][1]), ("mask", mask),
             *edges, ("all", prefix[sel]), ("part", nxt[sel])],
            [("wide", BF16), ("vmem", F32, part_of), ("vmem", F32, part_of), ("token", F32)],
            after=after, alias=[(0, before)], sub=SUB)

    def outer(sel, before, after):
        return call(
            functools.partial(outer_kernel, sel), sel,
            [("vmem", k), ("vmem", v), ("vmem", inners[sel][1]), ("vmem", inners[sel][2]), *edges,
             ("all", suffix[sel]), ("later" if sel else "part", prv[0])],
            [("wide", BF16), ("wide", BF16), ("token", F32)], after=after, alias=list(enumerate(before)), sub=SUB)

    def summed_before(own, towards, works):
        load, before, span = own, None, 1
        while span < chips:
            if span == 1:
                first = ctx_row >> 1 == (0 if towards == 1 else chips - 1)
                arrived = jnp.where(first, 0.0, cycled(load, 2 * towards))
            else:
                arrived = shifted(load, 2 * towards * span)
            if works:
                arrived = arrived + works.pop(0)(load)
            before = arrived if before is None else before + arrived
            load = load + arrived
            span *= 2
        for work in works:
            before = before + work(load)
        return before

    in_hbm = [("hbm", k), ("hbm", v)]
    semaphores = [pltpu.SemaphoreType.DMA((GROUPS, 2))]
    send, zero, k, v, core_row, ctx_row, dp_row = call(
        send_kernel, 0, in_hbm,
        [("all", F32), ("zero", jnp.int32), ("vmem", BF16, whole), ("vmem", BF16, whole)]
        + [("token", jnp.int32)] * 3,
        scratch=semaphores, steps=(1,), scalars=[core, ctx, dp])
    keep, k, v = call(
        keep_kernel, 0, in_hbm, [("all", F32), ("vmem", BF16, whole), ("vmem", BF16, whole)],
        alias=[(1, k), (2, v)], scratch=semaphores, steps=(1,))
    piece = within_chip(keep, send)
    seg = (segment_ids + zero)[0]
    onehot = seg[:, None] == jnp.arange(table.shape[0], dtype=jnp.int32)[None, :]
    img = jnp.sum(jnp.where(onehot, table[None, :], 0), axis=1)
    imgseg = jnp.where(img == 1, seg, -1)
    pos = jnp.arange(rows)
    mask = ((pos[:, None] >= pos[None, :]) | (imgseg[:, None] == seg[None, :])).astype(BF16)
    mask_t = ((pos[:, None] <= pos[None, :]) | (seg[:, None] == imgseg[None, :])).astype(BF16)

    parts = call(
        part_kernel, 0, [("hbm", q), ("hbm", dy), ("vmem", k), ("vmem", v), *edges],
        [("parts", F32)] * 2 + [("vmem", BF16, whole), ("vmem", BF16, whole), ("token", F32)],
        after=[piece[2]], scratch=[pltpu.SemaphoreType.DMA((2,))], steps=(1,))
    *parts, q, dy, _ = parts
    local, nxt = [], []

    def first_work(load):
        tokens = []
        for sel in range(2):
            *made, token = local_attn(sel, [parts[0]])
            local.append(made)
            tokens.append(token)
        return sum(tokens)

    def second_work(load):
        for part in reversed(parts):
            nxt.append(shifted(part + nought(load[:1]), -1))
        return jnp.zeros((1, PAIR), F32)

    before = summed_before(piece[2], 1, [first_work, second_work])
    prefix = to_cores(core_row, before, piece, 1)
    norms = [norm(0, None, [])]
    norms.append(norm(1, norms[0][0], [norms[0][4]]))
    output = norms[1][0]
    piece = within_chip(norms[0][4], norms[1][4])
    gain_sum = [jnp.concatenate([jnp.where(core_row == half, norms[0][3], norms[1][3]) for half in range(2)], axis=0)]
    gain_sum.append(scatter_step(gain_sum[-1], dp_row, "dp", 0))
    bits = list(reversed(range(lax.axis_size("ctx").bit_length() - 1)))
    inners, prv = [], []

    def third_work(load):
        x = scatter_step(gain_sum[-1] + nought(load[:1]), dp_row, "dp", 1)
        gain_sum.append(x.reshape(-1, PAIR))
        inners.append(inner(0, None, [load]))
        return inners[0][3]

    def fourth_work(load):
        gain_sum.append(scatter_step(gain_sum[-1] + nought(load[:1]), ctx_row, "ctx", bits[0]))
        both = jnp.concatenate([norms[1][2], norms[0][2]], axis=0) + nought(load[:1])
        prv.append(shifted(both, 1))
        inners.append(inner(1, inners[0][0], [load]))
        return inners[1][3]

    before = summed_before(piece[2], -1, [third_work, fourth_work])
    suffix = to_cores(core_row, before, piece, -1)
    grad_gain = scatter_step(gain_sum[-1] + nought(before[:1]), ctx_row, "ctx", bits[1])
    outers = outer(0, [None] * 2, [])
    grad_gain = grad_gain + outers[2]
    for bit in bits[2:]:
        grad_gain = scatter_step(grad_gain, ctx_row, "ctx", bit)
    grad_k, grad_v, _ = outer(1, outers[:2], [])
    grad_gain = grad_gain.reshape(-1)
    grad_q = inners[1][0]
    return output[None], grad_q[None], grad_k[None], grad_v[None], grad_gain


def solution(mesh):
    return jax.shard_map(
        on_device,
        mesh=mesh,
        in_specs=(
            P("dp", "ctx", None),
            P("dp", "ctx", None),
            P("dp", "ctx", None),
            P("dp", "ctx", None),
            P("dp", "ctx"),
            P("dp", None),
            P(),
        ),
        out_specs=(
            P("dp", "ctx", None),
            P("dp", "ctx", None),
            P("dp", "ctx", None),
            P("dp", "ctx", None),
            P(("dp", "ctx")),
        ),
        check_vma=False,
    )
```

```python
import functools

import jax
import jax.numpy as jnp
from jax import lax
from jax.experimental import pallas as pl
from jax.experimental.pallas import tpu as pltpu
from jax.sharding import PartitionSpec as P

E = 64
PAIR = 2 * E
GROUPS = 2
EXTRA = 8
VMEM = 10 * 2**20
SUB = 2
F32 = jnp.float32
BF16 = jnp.bfloat16


def dot(a, b, ca, cb):
    return lax.dot_general(a, b, (((ca,), (cb,)), ((), ())), preferred_element_type=F32)


def low_lanes(rows, cols):
    lane = lax.broadcasted_iota(jnp.int32, (rows, cols), 1)
    return lane % PAIR < E


def fold(product):
    return jnp.where(low_lanes(E, product.shape[1]), product[:E], product[E:])


def split(state):
    high = state.astype(BF16)
    return high, (state - high.astype(F32)).astype(BF16)


def spread(state):
    low = low_lanes(*state.shape)
    zero = jnp.zeros_like(state)
    return jnp.concatenate([jnp.where(low, state, zero), jnp.where(low, zero, state)], axis=0)


def heads_of(pair):
    low = low_lanes(*pair.shape)
    zero = jnp.zeros_like(pair)
    return jnp.where(low, pair, zero), jnp.where(low, zero, pair)


def twice(x):
    return jnp.concatenate([x, x], axis=1)


def pair_at(ref, p):
    return ref[:, p * PAIR:(p + 1) * PAIR]


def rows_at(base, p):
    return pl.ds(pl.multiple_of(base + p * E, E), E)


def twice(x):
    return jnp.concatenate([x, x], axis=1)


def pair_at(ref, p):
    return ref[:, p * PAIR:(p + 1) * PAIR]


def rows_at(base, p):
    return pl.ds(pl.multiple_of(base + p * E, E), E)


def own_or_received(keep, received, own, p):
    return jnp.where(own, keep[rows_at(p)], received[rows_at(p)])


def state_pair(a, b):
    return fold(dot(a, b, 0, 0))


def edge(seg, table, last):
    row = seg[...]
    count = row.shape[1]
    own = row[:, count - 1:] if last else row[:, :1]
    size = jnp.sum((row == own).astype(F32), axis=1, keepdims=True)
    at = lax.broadcasted_iota(jnp.int32, (count, PAIR), 0).astype(F32)
    rows = at >= count - size if last else at < size
    ids = lax.broadcasted_iota(jnp.int32, table.shape, 1)
    flag = jnp.sum(jnp.where(ids == own, table[...], 0).astype(F32), axis=1, keepdims=True)
    return rows, own.astype(F32), flag


def lanes_at(base, p):
    return pl.ds(pl.multiple_of(base + p * PAIR, PAIR), PAIR)


def place(sel, core, lanes, sub):
    step = pl.program_id(0)
    group, part = step // sub, step % sub
    half = (sel + core[0]) % 2
    base = group * lanes + part * (lanes // sub)
    return group, base, base + (group + half) * lanes, base // PAIR * E


def put_half(sel, core, k, v, out):
    lanes = k.shape[1] // GROUPS // 2
    count = lanes // PAIR
    for group in range(GROUPS):
        base = (2 * group + (sel + core[0]) % 2) * lanes
        for p in range(count):
            at = lanes_at(base, p)
            row = (group * count + p) * E
            out[row:row + E] = state_pair(k[:, at], v[:, at])


def send_kernel(core, ctx, dp, k_in, v_in, send, zero, k, v, core_row, ctx_row, dp_row, sems):
    for row, index in ((core_row, core), (ctx_row, ctx), (dp_row, dp)):
        row[...] = jnp.full(row.shape, index[0], jnp.int32)
    lanes = k.shape[1] // GROUPS // 2
    copies = []
    for sel in (1, 0):
        for group in range(GROUPS):
            base = (2 * group + (sel + core[0]) % 2) * lanes
            at = pl.ds(pl.multiple_of(base, lanes), lanes)
            for i, (array, buf) in enumerate(((k_in, k), (v_in, v))):
                copies.append(pltpu.make_async_copy(array.at[:, at], buf.at[:, at], sems.at[2 * group + sel, i]))
    for copy in copies:
        copy.start()
    zero[...] = jnp.zeros_like(zero)
    for copy in copies[:2 * GROUPS]:
        copy.wait()
    put_half(1, core, k, v, send)
    for copy in copies[2 * GROUPS:]:
        copy.wait()


def keep_kernel(core, k, v, *rest):
    put_half(0, core, k, v, rest[-1])


def part_kernel(core, q_in, dy_in, k, v, seg, table, *rest):
    *outs, q, dy, token, sems = rest[-6:]
    copies = [pltpu.make_async_copy(a, b, sems.at[i]) for i, (a, b) in enumerate(((q_in, q), (dy_in, dy)))]
    for copy in copies:
        copy.start()
    token[...] = jnp.zeros_like(token)
    lanes = k.shape[1] // GROUPS // 2
    count = lanes // PAIR
    rows, own, _ = edge(seg, table, False)
    keep = rows.astype(BF16)
    for sel, out in enumerate(outs):
        for group in range(GROUPS):
            base = (2 * group + (sel + core[0]) % 2) * lanes
            for p in range(count):
                at = lanes_at(base, p)
                out[group, p * E:(p + 1) * E] = state_pair(k[:, at], v[:, at] * keep)
            out[group, count * E:] = jnp.broadcast_to(own, (EXTRA, PAIR))
    for copy in copies:
        copy.wait()


def local_kernel(sel, core, q, k, v, mask, mask_t, *rest):
    attn, probs, token = rest[-3:]
    lanes = attn.shape[1] // GROUPS
    group, base, wide, _ = place(sel, core, lanes, 1)
    m, mt = mask[...], mask_t[...]
    token[...] = jnp.zeros_like(token)
    for p in range(lanes // PAIR):
        at = lanes_at(wide, p)
        kp = k[:, at]
        total = None
        for h, (qh, vh) in enumerate(zip(heads_of(q[:, at]), heads_of(v[:, at]))):
            prob = dot(qh, kp, 1, 1).astype(BF16) * m
            probs[group * (lanes // E) + 2 * p + h] = dot(kp, qh, 1, 1).astype(BF16) * mt
            term = dot(prob, vh, 1, 0)
            total = term if total is None else total + term
        attn[:, lanes_at(base, p)] = total


def head_mean(x):
    high, low = split(x)
    ones = spread(jnp.full((E, PAIR), 1.0 / E, BF16))
    return dot(jnp.concatenate([high, low], axis=1), jnp.concatenate([ones, ones], axis=0), 1, 0)


def side_by_side(state, part):
    sh, sl = split(state)
    ph, pll = split(part)
    left = jnp.concatenate([spread(sh), spread(sl)], axis=0)
    right = jnp.concatenate([spread(ph), spread(pll)], axis=0)
    return jnp.concatenate([left, right], axis=1)


def stacked(state, part):
    sh, sl = split(state)
    ph, pll = split(part)
    top = jnp.concatenate([spread(sh), spread(sl)], axis=1)
    bottom = jnp.concatenate([spread(ph), spread(pll)], axis=1)
    return jnp.concatenate([top, bottom], axis=0)


def on_rows(seg, table, last, part):
    rows, own, flag = edge(seg, table, last)
    met = part[0, part.shape[1] - EXTRA:part.shape[1] - EXTRA + 1] == own
    if last:
        met = met & (flag == 1)
    return rows.astype(F32) * met.astype(F32)


def norm_kernel(sel, core, q, dy, local, gain, seg, table, prefix, nxt, *rest):
    out, dab, part, gsum, total, token = rest[-6:]
    token[...] = jnp.zeros_like(token)
    lanes = out.shape[1]
    count = lanes // PAIR
    _, base, wide, row = place(sel, core, lanes, 1)
    on_next = on_rows(seg, table, True, nxt)
    last, own, flag = edge(seg, table, True)
    last = (last.astype(F32) * jnp.where(flag == 1, 1.0, 0.0)).astype(BF16)
    pairs = [slice(p * PAIR, (p + 1) * PAIR) for p in range(count)]
    bases = [lanes_at(base, p) for p in range(count)]
    wides = [lanes_at(wide, p) for p in range(count)]
    fars = [
        dot(twice(q[:, at]), side_by_side(prefix[rows_at(row, p)], nxt[0, rows_at(0, p)]), 1, 0)
        for p, at in enumerate(wides)
    ]
    attns = [local[:, at] + far[:, :PAIR] + on_next * far[:, PAIR:] for at, far in zip(bases, fars)]
    squares = [head_mean(attn * attn) for attn in attns]
    scales = [lax.rsqrt(square + 1e-06) for square in squares]
    normeds = [attn * scale for attn, scale in zip(attns, scales)]
    gas = [dy[:, at].astype(F32) * gain[:, pair] for at, pair in zip(wides, pairs)]
    means = [head_mean(ga * normed) for ga, normed in zip(gas, normeds)]
    das = [
        (scale * (ga - normed * mean)).astype(BF16)
        for scale, ga, normed, mean in zip(scales, gas, normeds, means)
    ]
    states = [state_pair(q[:, at], jnp.concatenate([da, da * last], axis=1)) for at, da in zip(wides, das)]
    part[0, count * E:] = jnp.broadcast_to(own, (EXTRA, PAIR))
    for p, (at, normed, da) in enumerate(zip(pairs, normeds, das)):
        total[rows_at(row, p)] = states[p][:, :PAIR]
        part[0, p * E:(p + 1) * E] = states[p][:, PAIR:]
        dab[:, bases[p]] = da
        out[:, at] = (normed * gain[:, at]).astype(BF16)
        gsum[0, p:p + 1] = jnp.sum(dy[:, wides[p]].astype(F32) * normed, axis=0, keepdims=True)


def inner_kernel(sel, core, q, k, v, dab, probs, mask, seg, table, prefix, nxt, *rest):
    gq, gk, gv, token = rest[-4:]
    lanes = dab.shape[1] // GROUPS
    count = lanes // SUB // PAIR
    group, base, wide, row = place(sel, core, lanes, SUB)
    m = mask[...]
    token[...] = jnp.zeros_like(token)
    on_next = on_rows(seg, table, True, nxt)
    first = row - group * (lanes // 2)
    for p in range(count):
        at = lanes_at(wide, p)
        da = dab[:, lanes_at(base, p)]
        vp = v[:, at]
        far = dot(twice(da), stacked(prefix[rows_at(row, p)], nxt[0, rows_at(first, p)]), 1, 1)
        tq = far[:, :PAIR] + on_next * far[:, PAIR:]
        tk = tv = None
        for h, (qh, kh, dh) in enumerate(zip(heads_of(q[:, at]), heads_of(k[:, at]), heads_of(da))):
            dprob = dot(dh, vp, 1, 1).astype(BF16) * m
            tq = tq + dot(dprob, kh, 1, 0)
            a = dot(dprob, qh, 0, 0)
            b = dot(probs[row // (E // 2) + 2 * p + h], dh, 1, 0)
            tk = a if tk is None else tk + a
            tv = b if tv is None else tv + b
        gq[:, p * PAIR:(p + 1) * PAIR] = tq.astype(BF16)
        gk[:, lanes_at(base, p)] = tk
        gv[:, lanes_at(base, p)] = tv


def outer_kernel(sel, core, k, v, gk_in, gv_in, seg, table, suffix, prv, *rest):
    gk, gv, token = rest[-3:]
    lanes = gk_in.shape[1] // GROUPS
    count = lanes // SUB // PAIR
    group, base, wide, row = place(sel, core, lanes, SUB)
    token[...] = jnp.zeros_like(token)
    on_prev = on_rows(seg, table, False, prv)
    first = row - group * (lanes // 2)
    for p in range(count):
        here, own, at = slice(p * PAIR, (p + 1) * PAIR), lanes_at(base, p), lanes_at(wide, p)
        s = suffix[rows_at(row, p)]
        g = prv[0, rows_at(first, p)]
        far = dot(twice(v[:, at]), stacked(s, g), 1, 1)
        gk[:, here] = (gk_in[:, own] + far[:, :PAIR] + on_prev * far[:, PAIR:]).astype(BF16)
        far = dot(twice(k[:, at]), side_by_side(s, g), 1, 0)
        gv[:, here] = (gv_in[:, own] + far[:, :PAIR] + on_prev * far[:, PAIR:]).astype(BF16)


def partner(x, axis, bit):
    route = [(i, i ^ (1 << bit)) for i in range(lax.axis_size(axis))]
    return lax.ppermute(x, axis, route)


def shifted(x, distance):
    count = lax.axis_size("ctx")
    return lax.ppermute(x, "ctx", [(i, i + distance) for i in range(count) if 0 <= i + distance < count])


def nought(x):
    return jnp.minimum(jnp.abs(x), 0.0)


def cycled(x, distance):
    count = lax.axis_size("ctx")
    return lax.ppermute(x, "ctx", [(i, (i + distance) % count) for i in range(count)])


def within_chip(keep, send):
    received = partner(send, "ctx", 0)
    return keep, received, keep + received


def to_cores(core, before, piece, towards):
    keep, received, _ = piece
    is_source = core == (0 if towards == 1 else 1)
    mine = jnp.where(is_source, before, before + received)
    return mine, partner(jnp.where(is_source, before + keep, before), "ctx", 0)


def pinned(x, space):
    return pltpu.with_memory_space_constraint(x, space)


def scatter_step(x, at, axis, bit):
    low, high = jnp.split(x, 2, axis=0 if x.shape[0] > 1 else 1)
    upper = (at >> bit & 1 == 1)[:, :low.shape[-1]]
    return jnp.where(upper, high, low) + partner(jnp.where(upper, low, high), axis, bit)


def on_device(queries, keys, values, out_grad, segment_ids, image_flags, gain):
    rows, width = queries.shape[1:]
    q, k, v, dy = (x[0] for x in (queries, keys, values, out_grad))
    table = image_flags[0]
    gain_row = gain.reshape(1, width)
    ctx = lax.axis_index("ctx")
    core, ctx, dp = (x.reshape(1).astype(jnp.int32) for x in (ctx & 1, ctx, lax.axis_index("dp")))
    lanes = width // GROUPS // 2
    half_rows = lanes // PAIR * E
    heads = lanes // E

    def call(kernel, sel, ins, outs, after=(), alias=(), scratch=(), sub=1, steps=None, scalars=None):
        scalars = scalars or [core]

        def wide(i, c, *_):
            return (0, (i // sub * 2 + (sel + c[0]) % 2) * sub + i % sub)

        def whole(*args):
            return (0, 0)

        def part(i, c, *_):
            return (i // sub, 0, 0)

        specs = {
            "vmem": pl.BlockSpec(memory_space=pltpu.VMEM),
            "hbm": pl.BlockSpec(memory_space=pltpu.HBM),
            "wide": pl.BlockSpec((rows, lanes // sub), wide),
            "row": pl.BlockSpec((1, lanes // sub), wide),
            "sums": pl.BlockSpec((1, lanes // PAIR, PAIR), part),
            "zero": pl.BlockSpec((1, rows), whole),
            "all": pl.BlockSpec((GROUPS * half_rows, PAIR), whole),
            "part": pl.BlockSpec((1, half_rows + EXTRA, PAIR), part),
            "later": pl.BlockSpec((1, half_rows + EXTRA, PAIR), lambda i, *_: (GROUPS + i // sub, 0, 0)),
            "parts": pl.BlockSpec((GROUPS, half_rows + EXTRA, PAIR), lambda *args: (0, 0, 0)),
            "seg": pl.BlockSpec((1, rows), whole),
            "table": pl.BlockSpec((1, table.shape[0]), whole),
            "mask": pl.BlockSpec((rows, rows), whole),
            "token": pl.BlockSpec((1, PAIR), whole),
            "after2": pl.BlockSpec((8, PAIR), whole),
            "after3": pl.BlockSpec((1, 8, PAIR), lambda *args: (0, 0, 0)),
            "any": pl.BlockSpec(memory_space=pl.ANY),
        }
        shapes = {
            "wide": (rows, width),
            "sums": (GROUPS, lanes // PAIR, PAIR),
            "zero": (1, rows),
            "all": (GROUPS * half_rows, PAIR),
            "part": (GROUPS, half_rows + EXTRA, PAIR),
            "parts": (GROUPS, half_rows + EXTRA, PAIR),
            "token": (1, PAIR),
        }
        spaces = {"vmem": pltpu.VMEM, "hbm": pltpu.HBM}
        operands = [pinned(x, spaces[kind]) if kind in spaces else x for kind, x in ins] + list(after)
        kinds = [kind for kind, _ in ins] + [f"after{x.ndim}" for x in after]
        aliases = {}
        for out_at, x in alias:
            if x is not None:
                aliases[len(scalars) + len(operands)] = out_at
                operands.append(x)
                kinds.append("any")
        out_shape = [
            pltpu.VMEM(*shape, dtype) if kind == "vmem" else jax.ShapeDtypeStruct(shapes[kind], dtype)
            for kind, dtype, *shape in outs
        ]
        return pl.pallas_call(
            kernel,
            grid_spec=pltpu.PrefetchScalarGridSpec(
                num_scalar_prefetch=len(scalars),
                grid=steps or (GROUPS * sub,),
                in_specs=[specs[kind] for kind in kinds],
                out_specs=[specs[kind] for kind, *_ in outs],
                scratch_shapes=scratch,
            ),
            out_shape=out_shape,
            input_output_aliases=aliases,
            compiler_params=pltpu.CompilerParams(vmem_limit_bytes=VMEM),
            cost_estimate=pl.CostEstimate(flops=1, bytes_accessed=1, transcendentals=0),
        )(*scalars, *operands)

    edges = [("seg", segment_ids), ("table", image_flags)]
    chips = lax.axis_size("ctx") // 2
    whole, part_of = (rows, width), (rows, width // 2)

    def local_attn(sel, after):
        return call(
            functools.partial(local_kernel, sel), sel,
            [("vmem", q), ("vmem", k), ("vmem", v), ("mask", mask), ("mask", mask_t)],
            [("vmem", F32, part_of), ("vmem", BF16, (GROUPS * heads, rows, rows)), ("token", F32)], after=after)

    def norm(sel, before, after):
        return call(
            functools.partial(norm_kernel, sel), sel,
            [("vmem", q), ("vmem", dy), ("vmem", local[sel][0]), ("row", gain_row), *edges,
             ("all", prefix[sel]), ("part", nxt[sel])],
            [("wide", BF16), ("vmem", BF16, part_of), ("part", F32), ("sums", F32), ("all", F32), ("token", F32)],
            after=after, alias=[(0, before)])

    def inner(sel, before, after):
        return call(
            functools.partial(inner_kernel, sel), sel,
            [("vmem", q), ("vmem", k), ("vmem", v), ("vmem", norms[sel][1]), ("vmem", local[sel][1]), ("mask", mask),
             *edges, ("all", prefix[sel]), ("part", nxt[sel])],
            [("wide", BF16), ("vmem", F32, part_of), ("vmem", F32, part_of), ("token", F32)],
            after=after, alias=[(0, before)], sub=SUB)

    def outer(sel, before, after):
        return call(
            functools.partial(outer_kernel, sel), sel,
            [("vmem", k), ("vmem", v), ("vmem", inners[sel][1]), ("vmem", inners[sel][2]), *edges,
             ("all", suffix[sel]), ("later" if sel else "part", prv[0])],
            [("wide", BF16), ("wide", BF16), ("token", F32)], after=after, alias=list(enumerate(before)), sub=SUB)

    def summed_before(own, towards, works):
        load, before, span = own, None, 1
        while span < chips:
            if span == 1 and towards == 1:
                arrived = jnp.where(ctx_row < 2, 0.0, cycled(load, 2))
            else:
                arrived = shifted(load, 2 * towards * span)
            if works:
                arrived = arrived + works.pop(0)(load)
            before = arrived if before is None else before + arrived
            load = load + arrived
            span *= 2
        for work in works:
            before = before + work(load)
        return before

    send, zero, k, v, core_row, ctx_row, dp_row = call(
        send_kernel, 0, [("hbm", k), ("hbm", v)],
        [("all", F32), ("zero", jnp.int32), ("vmem", BF16, whole), ("vmem", BF16, whole)]
        + [("token", jnp.int32)] * 3,
        scratch=[pltpu.SemaphoreType.DMA((2 * GROUPS, 2))], steps=(1,), scalars=[core, ctx, dp])
    keep, = call(keep_kernel, 0, [("vmem", k), ("vmem", v)], [("all", F32)], steps=(1,))
    piece = within_chip(keep, send)
    seg = (segment_ids + zero)[0]
    onehot = seg[:, None] == jnp.arange(table.shape[0], dtype=jnp.int32)[None, :]
    img = jnp.sum(jnp.where(onehot, table[None, :], 0), axis=1)
    imgseg = jnp.where(img == 1, seg, -1)
    pos = jnp.arange(rows)
    mask = ((pos[:, None] >= pos[None, :]) | (imgseg[:, None] == seg[None, :])).astype(BF16)
    mask_t = ((pos[:, None] <= pos[None, :]) | (seg[:, None] == imgseg[None, :])).astype(BF16)

    parts = call(
        part_kernel, 0, [("hbm", q), ("hbm", dy), ("vmem", k), ("vmem", v), *edges],
        [("parts", F32)] * 2 + [("vmem", BF16, whole), ("vmem", BF16, whole), ("token", F32)],
        after=[piece[2]], scratch=[pltpu.SemaphoreType.DMA((2,))], steps=(1,))
    *parts, q, dy, _ = parts
    local, nxt = [], []

    def first_work(load):
        tokens = []
        for sel in range(2):
            *made, token = local_attn(sel, [parts[0]])
            local.append(made)
            tokens.append(token)
        return sum(tokens)

    def second_work(load):
        for part in reversed(parts):
            nxt.append(shifted(part + nought(load[:1]), -1))
        return jnp.zeros((1, PAIR), F32)

    before = summed_before(piece[2], 1, [first_work, second_work])
    prefix = to_cores(core_row, before, piece, 1)
    norms = [norm(0, None, [])]
    norms.append(norm(1, norms[0][0], [norms[0][4]]))
    output = norms[1][0]
    piece = within_chip(norms[0][4], norms[1][4])
    gain_sum = [jnp.concatenate([jnp.where(core_row == half, norms[0][3], norms[1][3]) for half in range(2)], axis=0)]
    gain_sum.append(scatter_step(gain_sum[-1], dp_row, "dp", 0))
    bits = list(reversed(range(lax.axis_size("ctx").bit_length() - 1)))
    inners, prv = [], []

    def third_work(load):
        x = scatter_step(gain_sum[-1] + nought(load[:1]), dp_row, "dp", 1)
        gain_sum.append(x.reshape(-1, PAIR))
        inners.append(inner(0, None, [load]))
        return inners[0][3]

    def fourth_work(load):
        gain_sum.append(scatter_step(gain_sum[-1] + nought(load[:1]), ctx_row, "ctx", bits[0]))
        both = jnp.concatenate([norms[1][2], norms[0][2]], axis=0) + nought(load[:1])
        prv.append(shifted(both, 1))
        inners.append(inner(1, inners[0][0], [load]))
        return inners[1][3]

    before = summed_before(piece[2], -1, [third_work, fourth_work])
    suffix = to_cores(core_row, before, piece, -1)
    grad_gain = scatter_step(gain_sum[-1] + nought(before[:1]), ctx_row, "ctx", bits[1])
    outers = outer(0, [None] * 2, [])
    grad_gain = grad_gain + outers[2]
    for bit in bits[2:]:
        grad_gain = scatter_step(grad_gain, ctx_row, "ctx", bit)
    grad_k, grad_v, _ = outer(1, outers[:2], [])
    grad_gain = grad_gain.reshape(-1)
    grad_q = inners[1][0]
    return output[None], grad_q[None], grad_k[None], grad_v[None], grad_gain


def solution(mesh):
    return jax.shard_map(
        on_device,
        mesh=mesh,
        in_specs=(
            P("dp", "ctx", None),
            P("dp", "ctx", None),
            P("dp", "ctx", None),
            P("dp", "ctx", None),
            P("dp", "ctx"),
            P("dp", None),
            P(),
        ),
        out_specs=(
            P("dp", "ctx", None),
            P("dp", "ctx", None),
            P("dp", "ctx", None),
            P("dp", "ctx", None),
            P(("dp", "ctx")),
        ),
        check_vma=False,
    )
```

```python
import functools

import jax
import jax.numpy as jnp
from jax import lax
from jax.experimental import pallas as pl
from jax.experimental.pallas import tpu as pltpu
from jax.sharding import PartitionSpec as P

E = 64
PAIR = 2 * E
GROUPS = 2
EXTRA = 8
VMEM = 10 * 2**20
SUB = 2
F32 = jnp.float32
BF16 = jnp.bfloat16


def dot(a, b, ca, cb):
    return lax.dot_general(a, b, (((ca,), (cb,)), ((), ())), preferred_element_type=F32)


def low_lanes(rows, cols):
    lane = lax.broadcasted_iota(jnp.int32, (rows, cols), 1)
    return lane % PAIR < E


def fold(product):
    return jnp.where(low_lanes(E, product.shape[1]), product[:E], product[E:])


def split(state):
    high = state.astype(BF16)
    return high, (state - high.astype(F32)).astype(BF16)


def spread(state):
    low = low_lanes(*state.shape)
    zero = jnp.zeros_like(state)
    return jnp.concatenate([jnp.where(low, state, zero), jnp.where(low, zero, state)], axis=0)


def heads_of(pair):
    low = low_lanes(*pair.shape)
    zero = jnp.zeros_like(pair)
    return jnp.where(low, pair, zero), jnp.where(low, zero, pair)


def twice(x):
    return jnp.concatenate([x, x], axis=1)


def pair_at(ref, p):
    return ref[:, p * PAIR:(p + 1) * PAIR]


def rows_at(base, p):
    return pl.ds(pl.multiple_of(base + p * E, E), E)


def twice(x):
    return jnp.concatenate([x, x], axis=1)


def pair_at(ref, p):
    return ref[:, p * PAIR:(p + 1) * PAIR]


def rows_at(base, p):
    return pl.ds(pl.multiple_of(base + p * E, E), E)


def own_or_received(keep, received, own, p):
    return jnp.where(own, keep[rows_at(p)], received[rows_at(p)])


def state_pair(a, b):
    return fold(dot(a, b, 0, 0))


def edge(seg, table, last):
    row = seg[...]
    count = row.shape[1]
    own = row[:, count - 1:] if last else row[:, :1]
    size = jnp.sum((row == own).astype(F32), axis=1, keepdims=True)
    at = lax.broadcasted_iota(jnp.int32, (count, PAIR), 0).astype(F32)
    rows = at >= count - size if last else at < size
    ids = lax.broadcasted_iota(jnp.int32, table.shape, 1)
    flag = jnp.sum(jnp.where(ids == own, table[...], 0).astype(F32), axis=1, keepdims=True)
    return rows, own.astype(F32), flag


def lanes_at(base, p):
    return pl.ds(pl.multiple_of(base + p * PAIR, PAIR), PAIR)


def place(sel, core, lanes, sub, first=0):
    step = pl.program_id(0)
    group, part = first + step // sub, step % sub
    half = (sel + core[0]) % 2
    base = group * lanes + part * (lanes // sub)
    return group, base, base + (group + half) * lanes, base // PAIR * E


def put_half(sel, core, k, v, out):
    lanes = k.shape[1] // GROUPS // 2
    count = lanes // PAIR
    for group in range(GROUPS):
        base = (2 * group + (sel + core[0]) % 2) * lanes
        for p in range(count):
            at = lanes_at(base, p)
            row = (group * count + p) * E
            out[row:row + E] = state_pair(k[:, at], v[:, at])


def send_kernel(core, ctx, dp, k_in, v_in, send, zero, k, v, core_row, ctx_row, dp_row, sems):
    for row, index in ((core_row, core), (ctx_row, ctx), (dp_row, dp)):
        row[...] = jnp.full(row.shape, index[0], jnp.int32)
    lanes = k.shape[1] // GROUPS // 2
    copies = []
    for sel in (1, 0):
        for group in range(GROUPS):
            base = (2 * group + (sel + core[0]) % 2) * lanes
            at = pl.ds(pl.multiple_of(base, lanes), lanes)
            for i, (array, buf) in enumerate(((k_in, k), (v_in, v))):
                copies.append(pltpu.make_async_copy(array.at[:, at], buf.at[:, at], sems.at[2 * group + sel, i]))
    for copy in copies:
        copy.start()
    zero[...] = jnp.zeros_like(zero)
    for copy in copies[:2 * GROUPS]:
        copy.wait()
    put_half(1, core, k, v, send)
    for copy in copies[2 * GROUPS:]:
        copy.wait()


def keep_kernel(core, k, v, *rest):
    put_half(0, core, k, v, rest[-1])


def part_kernel(core, q_in, dy_in, k, v, seg, table, *rest):
    *outs, q, dy, token, sems = rest[-6:]
    copies = [pltpu.make_async_copy(a, b, sems.at[i]) for i, (a, b) in enumerate(((q_in, q), (dy_in, dy)))]
    for copy in copies:
        copy.start()
    token[...] = jnp.zeros_like(token)
    lanes = k.shape[1] // GROUPS // 2
    count = lanes // PAIR
    rows, own, _ = edge(seg, table, False)
    keep = rows.astype(BF16)
    for sel, out in enumerate(outs):
        for group in range(GROUPS):
            base = (2 * group + (sel + core[0]) % 2) * lanes
            for p in range(count):
                at = lanes_at(base, p)
                out[group, p * E:(p + 1) * E] = state_pair(k[:, at], v[:, at] * keep)
            out[group, count * E:] = jnp.broadcast_to(own, (EXTRA, PAIR))
    for copy in copies:
        copy.wait()


def local_kernel(sel, core, q, k, v, mask, mask_t, *rest):
    attn, probs, token = rest[-3:]
    lanes = attn.shape[1] // GROUPS
    group, base, wide, _ = place(sel, core, lanes, 1)
    m, mt = mask[...], mask_t[...]
    token[...] = jnp.zeros_like(token)
    for p in range(lanes // PAIR):
        at = lanes_at(wide, p)
        kp = k[:, at]
        total = None
        for h, (qh, vh) in enumerate(zip(heads_of(q[:, at]), heads_of(v[:, at]))):
            prob = dot(qh, kp, 1, 1).astype(BF16) * m
            probs[group * (lanes // E) + 2 * p + h] = dot(kp, qh, 1, 1).astype(BF16) * mt
            term = dot(prob, vh, 1, 0)
            total = term if total is None else total + term
        attn[:, lanes_at(base, p)] = total


def head_mean(x):
    high, low = split(x)
    ones = spread(jnp.full((E, PAIR), 1.0 / E, BF16))
    return dot(jnp.concatenate([high, low], axis=1), jnp.concatenate([ones, ones], axis=0), 1, 0)


def side_by_side(state, part):
    sh, sl = split(state)
    ph, pll = split(part)
    left = jnp.concatenate([spread(sh), spread(sl)], axis=0)
    right = jnp.concatenate([spread(ph), spread(pll)], axis=0)
    return jnp.concatenate([left, right], axis=1)


def stacked(state, part):
    sh, sl = split(state)
    ph, pll = split(part)
    top = jnp.concatenate([spread(sh), spread(sl)], axis=1)
    bottom = jnp.concatenate([spread(ph), spread(pll)], axis=1)
    return jnp.concatenate([top, bottom], axis=0)


def on_rows(seg, table, last, part):
    rows, own, flag = edge(seg, table, last)
    met = part[0, part.shape[1] - EXTRA:part.shape[1] - EXTRA + 1] == own
    if last:
        met = met & (flag == 1)
    return rows.astype(F32) * met.astype(F32)


def norm_kernel(sel, core, q, dy, local, gain, seg, table, prefix, nxt, *rest):
    out, dab, part, gsum, total, token = rest[-6:]
    token[...] = jnp.zeros_like(token)
    lanes = out.shape[1]
    count = lanes // PAIR
    _, base, wide, row = place(sel, core, lanes, 1)
    on_next = on_rows(seg, table, True, nxt)
    last, own, flag = edge(seg, table, True)
    last = (last.astype(F32) * jnp.where(flag == 1, 1.0, 0.0)).astype(BF16)
    pairs = [slice(p * PAIR, (p + 1) * PAIR) for p in range(count)]
    bases = [lanes_at(base, p) for p in range(count)]
    wides = [lanes_at(wide, p) for p in range(count)]
    fars = [
        dot(twice(q[:, at]), side_by_side(prefix[rows_at(row, p)], nxt[0, rows_at(0, p)]), 1, 0)
        for p, at in enumerate(wides)
    ]
    attns = [local[:, at] + far[:, :PAIR] + on_next * far[:, PAIR:] for at, far in zip(bases, fars)]
    squares = [head_mean(attn * attn) for attn in attns]
    scales = [lax.rsqrt(square + 1e-06) for square in squares]
    normeds = [attn * scale for attn, scale in zip(attns, scales)]
    gas = [dy[:, at].astype(F32) * gain[:, pair] for at, pair in zip(wides, pairs)]
    means = [head_mean(ga * normed) for ga, normed in zip(gas, normeds)]
    das = [
        (scale * (ga - normed * mean)).astype(BF16)
        for scale, ga, normed, mean in zip(scales, gas, normeds, means)
    ]
    states = [state_pair(q[:, at], jnp.concatenate([da, da * last], axis=1)) for at, da in zip(wides, das)]
    part[0, count * E:] = jnp.broadcast_to(own, (EXTRA, PAIR))
    for p, (at, normed, da) in enumerate(zip(pairs, normeds, das)):
        total[rows_at(row, p)] = states[p][:, :PAIR]
        part[0, p * E:(p + 1) * E] = states[p][:, PAIR:]
        dab[:, bases[p]] = da
        out[:, at] = (normed * gain[:, at]).astype(BF16)
        gsum[0, p:p + 1] = jnp.sum(dy[:, wides[p]].astype(F32) * normed, axis=0, keepdims=True)


def inner_kernel(sel, start, core, q, k, v, dab, probs, mask, seg, table, prefix, nxt, *rest):
    gq, gk, gv, token = rest[-4:]
    lanes = dab.shape[1] // GROUPS
    count = lanes // SUB // PAIR
    group, base, wide, row = place(sel, core, lanes, SUB, start)
    m = mask[...]
    token[...] = jnp.zeros_like(token)
    on_next = on_rows(seg, table, True, nxt)
    first = row - group * (lanes // 2)
    for p in range(count):
        at = lanes_at(wide, p)
        da = dab[:, lanes_at(base, p)]
        vp = v[:, at]
        far = dot(twice(da), stacked(prefix[rows_at(row, p)], nxt[0, rows_at(first, p)]), 1, 1)
        tq = far[:, :PAIR] + on_next * far[:, PAIR:]
        tk = tv = None
        for h, (qh, kh, dh) in enumerate(zip(heads_of(q[:, at]), heads_of(k[:, at]), heads_of(da))):
            dprob = dot(dh, vp, 1, 1).astype(BF16) * m
            tq = tq + dot(dprob, kh, 1, 0)
            a = dot(dprob, qh, 0, 0)
            b = dot(probs[row // (E // 2) + 2 * p + h], dh, 1, 0)
            tk = a if tk is None else tk + a
            tv = b if tv is None else tv + b
        gq[:, p * PAIR:(p + 1) * PAIR] = tq.astype(BF16)
        gk[:, lanes_at(base, p)] = tk
        gv[:, lanes_at(base, p)] = tv


def outer_kernel(sel, core, k, v, gk_in, gv_in, seg, table, suffix, prv, *rest):
    gk, gv, token = rest[-3:]
    lanes = gk_in.shape[1] // GROUPS
    count = lanes // SUB // PAIR
    group, base, wide, row = place(sel, core, lanes, SUB)
    token[...] = jnp.zeros_like(token)
    on_prev = on_rows(seg, table, False, prv)
    first = row - group * (lanes // 2)
    for p in range(count):
        here, own, at = slice(p * PAIR, (p + 1) * PAIR), lanes_at(base, p), lanes_at(wide, p)
        s = suffix[rows_at(row, p)]
        g = prv[0, rows_at(first, p)]
        far = dot(twice(v[:, at]), stacked(s, g), 1, 1)
        gk[:, here] = (gk_in[:, own] + far[:, :PAIR] + on_prev * far[:, PAIR:]).astype(BF16)
        far = dot(twice(k[:, at]), side_by_side(s, g), 1, 0)
        gv[:, here] = (gv_in[:, own] + far[:, :PAIR] + on_prev * far[:, PAIR:]).astype(BF16)


def partner(x, axis, bit):
    route = [(i, i ^ (1 << bit)) for i in range(lax.axis_size(axis))]
    return lax.ppermute(x, axis, route)


def shifted(x, distance):
    count = lax.axis_size("ctx")
    return lax.ppermute(x, "ctx", [(i, i + distance) for i in range(count) if 0 <= i + distance < count])


def nought(x):
    return jnp.minimum(jnp.abs(x), 0.0)


def cycled(x, distance):
    count = lax.axis_size("ctx")
    return lax.ppermute(x, "ctx", [(i, (i + distance) % count) for i in range(count)])


def within_chip(keep, send):
    received = partner(send, "ctx", 0)
    return keep, received, keep + received


def to_cores(core, before, piece, towards):
    keep, received, _ = piece
    is_source = core == (0 if towards == 1 else 1)
    mine = jnp.where(is_source, before, before + received)
    return mine, partner(jnp.where(is_source, before + keep, before), "ctx", 0)


def pinned(x, space):
    return pltpu.with_memory_space_constraint(x, space)


def scatter_step(x, at, axis, bit):
    low, high = jnp.split(x, 2, axis=0 if x.shape[0] > 1 else 1)
    upper = (at >> bit & 1 == 1)[:, :low.shape[-1]]
    return jnp.where(upper, high, low) + partner(jnp.where(upper, low, high), axis, bit)


def on_device(queries, keys, values, out_grad, segment_ids, image_flags, gain):
    rows, width = queries.shape[1:]
    q, k, v, dy = (x[0] for x in (queries, keys, values, out_grad))
    table = image_flags[0]
    gain_row = gain.reshape(1, width)
    ctx = lax.axis_index("ctx")
    core, ctx, dp = (x.reshape(1).astype(jnp.int32) for x in (ctx & 1, ctx, lax.axis_index("dp")))
    lanes = width // GROUPS // 2
    half_rows = lanes // PAIR * E
    heads = lanes // E

    def call(kernel, sel, ins, outs, first=0, after=(), alias=(), scratch=(), sub=1, steps=None, scalars=None):
        scalars = scalars or [core]

        def wide(i, c, *_):
            return (0, ((first + i // sub) * 2 + (sel + c[0]) % 2) * sub + i % sub)

        def whole(*args):
            return (0, 0)

        def part(i, c, *_):
            return (first + i // sub, 0, 0)

        specs = {
            "vmem": pl.BlockSpec(memory_space=pltpu.VMEM),
            "hbm": pl.BlockSpec(memory_space=pltpu.HBM),
            "wide": pl.BlockSpec((rows, lanes // sub), wide),
            "row": pl.BlockSpec((1, lanes // sub), wide),
            "sums": pl.BlockSpec((1, lanes // PAIR, PAIR), part),
            "zero": pl.BlockSpec((1, rows), whole),
            "all": pl.BlockSpec((GROUPS * half_rows, PAIR), whole),
            "part": pl.BlockSpec((1, half_rows + EXTRA, PAIR), part),
            "later": pl.BlockSpec((1, half_rows + EXTRA, PAIR), lambda i, *_: (GROUPS + i // sub, 0, 0)),
            "parts": pl.BlockSpec((GROUPS, half_rows + EXTRA, PAIR), lambda *args: (0, 0, 0)),
            "seg": pl.BlockSpec((1, rows), whole),
            "table": pl.BlockSpec((1, table.shape[0]), whole),
            "mask": pl.BlockSpec((rows, rows), whole),
            "token": pl.BlockSpec((1, PAIR), whole),
            "after2": pl.BlockSpec((8, PAIR), whole),
            "after3": pl.BlockSpec((1, 8, PAIR), lambda *args: (0, 0, 0)),
            "any": pl.BlockSpec(memory_space=pl.ANY),
        }
        shapes = {
            "wide": (rows, width),
            "sums": (GROUPS, lanes // PAIR, PAIR),
            "zero": (1, rows),
            "all": (GROUPS * half_rows, PAIR),
            "part": (GROUPS, half_rows + EXTRA, PAIR),
            "parts": (GROUPS, half_rows + EXTRA, PAIR),
            "token": (1, PAIR),
        }
        spaces = {"vmem": pltpu.VMEM, "hbm": pltpu.HBM}
        operands = [pinned(x, spaces[kind]) if kind in spaces else x for kind, x in ins] + list(after)
        kinds = [kind for kind, _ in ins] + [f"after{x.ndim}" for x in after]
        aliases = {}
        for out_at, x in alias:
            if x is not None:
                aliases[len(scalars) + len(operands)] = out_at
                in_vmem = outs[out_at][0] == "vmem"
                operands.append(pinned(x, pltpu.VMEM) if in_vmem else x)
                kinds.append("vmem" if in_vmem else "any")
        out_shape = [
            pltpu.VMEM(*shape, dtype) if kind == "vmem" else jax.ShapeDtypeStruct(shapes[kind], dtype)
            for kind, dtype, *shape in outs
        ]
        return pl.pallas_call(
            kernel,
            grid_spec=pltpu.PrefetchScalarGridSpec(
                num_scalar_prefetch=len(scalars),
                grid=steps or (GROUPS * sub,),
                in_specs=[specs[kind] for kind in kinds],
                out_specs=[specs[kind] for kind, *_ in outs],
                scratch_shapes=scratch,
            ),
            out_shape=out_shape,
            input_output_aliases=aliases,
            compiler_params=pltpu.CompilerParams(vmem_limit_bytes=VMEM),
            cost_estimate=pl.CostEstimate(flops=1, bytes_accessed=1, transcendentals=0),
        )(*scalars, *operands)

    edges = [("seg", segment_ids), ("table", image_flags)]
    chips = lax.axis_size("ctx") // 2
    whole, part_of = (rows, width), (rows, width // 2)

    def local_attn(sel, after):
        return call(
            functools.partial(local_kernel, sel), sel,
            [("vmem", q), ("vmem", k), ("vmem", v), ("mask", mask), ("mask", mask_t)],
            [("vmem", F32, part_of), ("vmem", BF16, (GROUPS * heads, rows, rows)), ("token", F32)], after=after)

    def norm(sel, before, after):
        return call(
            functools.partial(norm_kernel, sel), sel,
            [("vmem", q), ("vmem", dy), ("vmem", local[sel][0]), ("row", gain_row), *edges,
             ("all", prefix[sel]), ("part", nxt[sel])],
            [("wide", BF16), ("vmem", BF16, part_of), ("part", F32), ("sums", F32), ("all", F32), ("token", F32)],
            after=after, alias=[(0, before)])

    def inner(sel, start, before, after):
        count = 1 if sel == 0 else GROUPS
        return call(
            functools.partial(inner_kernel, sel, start), sel,
            [("vmem", q), ("vmem", k), ("vmem", v), ("vmem", norms[sel][1]), ("vmem", local[sel][1]), ("mask", mask),
             *edges, ("all", prefix[sel]), ("part", nxt[sel])],
            [("wide", BF16), ("vmem", F32, part_of), ("vmem", F32, part_of), ("token", F32)],
            first=start, after=after, alias=list(enumerate(before)), sub=SUB, steps=(count * SUB,))

    def outer(sel, before, after):
        return call(
            functools.partial(outer_kernel, sel), sel,
            [("vmem", k), ("vmem", v), ("vmem", inners[sel][1]), ("vmem", inners[sel][2]), *edges,
             ("all", suffix[sel]), ("later" if sel else "part", prv[0])],
            [("wide", BF16), ("wide", BF16), ("token", F32)], after=after, alias=list(enumerate(before)), sub=SUB)

    def summed_before(own, towards, works):
        load, before, span = own, None, 1
        while span < chips:
            if span == 1:
                first = ctx_row >> 1 == (0 if towards == 1 else chips - 1)
                arrived = jnp.where(first, 0.0, cycled(load, 2 * towards))
            else:
                arrived = shifted(load, 2 * towards * span)
            if works:
                arrived = arrived + works.pop(0)(load)
            before = arrived if before is None else before + arrived
            load = load + arrived
            span *= 2
        for work in works:
            before = before + work(load)
        return before

    send, zero, k, v, core_row, ctx_row, dp_row = call(
        send_kernel, 0, [("hbm", k), ("hbm", v)],
        [("all", F32), ("zero", jnp.int32), ("vmem", BF16, whole), ("vmem", BF16, whole)]
        + [("token", jnp.int32)] * 3,
        scratch=[pltpu.SemaphoreType.DMA((2 * GROUPS, 2))], steps=(1,), scalars=[core, ctx, dp])
    keep, = call(keep_kernel, 0, [("vmem", k), ("vmem", v)], [("all", F32)], steps=(1,))
    piece = within_chip(keep, send)
    seg = (segment_ids + zero)[0]
    onehot = seg[:, None] == jnp.arange(table.shape[0], dtype=jnp.int32)[None, :]
    img = jnp.sum(jnp.where(onehot, table[None, :], 0), axis=1)
    imgseg = jnp.where(img == 1, seg, -1)
    pos = jnp.arange(rows)
    mask = ((pos[:, None] >= pos[None, :]) | (imgseg[:, None] == seg[None, :])).astype(BF16)
    mask_t = ((pos[:, None] <= pos[None, :]) | (seg[:, None] == imgseg[None, :])).astype(BF16)

    parts = call(
        part_kernel, 0, [("hbm", q), ("hbm", dy), ("vmem", k), ("vmem", v), *edges],
        [("parts", F32)] * 2 + [("vmem", BF16, whole), ("vmem", BF16, whole), ("token", F32)],
        after=[piece[2]], scratch=[pltpu.SemaphoreType.DMA((2,))], steps=(1,))
    *parts, q, dy, _ = parts
    local, nxt = [], []

    def first_work(load):
        tokens = []
        for sel in range(2):
            *made, token = local_attn(sel, [parts[0]])
            local.append(made)
            tokens.append(token)
        return sum(tokens)

    def second_work(load):
        for part in reversed(parts):
            nxt.append(shifted(part + nought(load[:1]), -1))
        return jnp.zeros((1, PAIR), F32)

    before = summed_before(piece[2], 1, [first_work, second_work])
    prefix = to_cores(core_row, before, piece, 1)
    norms = [norm(0, None, [])]
    norms.append(norm(1, norms[0][0], [norms[0][4]]))
    output = norms[1][0]
    piece = within_chip(norms[0][4], norms[1][4])
    gain_sum = [jnp.concatenate([jnp.where(core_row == half, norms[0][3], norms[1][3]) for half in range(2)], axis=0)]
    gain_sum.append(scatter_step(gain_sum[-1], dp_row, "dp", 0))
    bits = list(reversed(range(lax.axis_size("ctx").bit_length() - 1)))
    inners, prv = [], []

    def third_work(load):
        x = scatter_step(gain_sum[-1] + nought(load[:1]), dp_row, "dp", 1)
        gain_sum.append(x.reshape(-1, PAIR))
        inners.append(inner(0, 0, [None] * 3, [load]))
        return inners[0][3]

    def fourth_work(load):
        gain_sum.append(scatter_step(gain_sum[-1] + nought(load[:1]), ctx_row, "ctx", bits[0]))
        both = jnp.concatenate([norms[1][2], norms[0][2]], axis=0) + nought(load[:1])
        prv.append(shifted(both, 1))
        inners[0] = inner(0, 1, inners[0][:3], [load])
        inners.append(inner(1, 0, [inners[0][0], None, None], [load]))
        return inners[0][3] + inners[1][3]

    before = summed_before(piece[2], -1, [third_work, fourth_work])
    suffix = to_cores(core_row, before, piece, -1)
    grad_gain = scatter_step(gain_sum[-1] + nought(before[:1]), ctx_row, "ctx", bits[1])
    outers = outer(0, [None] * 2, [])
    grad_gain = grad_gain + outers[2]
    for bit in bits[2:]:
        grad_gain = scatter_step(grad_gain, ctx_row, "ctx", bit)
    grad_k, grad_v, _ = outer(1, outers[:2], [])
    grad_gain = grad_gain.reshape(-1)
    grad_q = inners[1][0]
    return output[None], grad_q[None], grad_k[None], grad_v[None], grad_gain


def solution(mesh):
    return jax.shard_map(
        on_device,
        mesh=mesh,
        in_specs=(
            P("dp", "ctx", None),
            P("dp", "ctx", None),
            P("dp", "ctx", None),
            P("dp", "ctx", None),
            P("dp", "ctx"),
            P("dp", None),
            P(),
        ),
        out_specs=(
            P("dp", "ctx", None),
            P("dp", "ctx", None),
            P("dp", "ctx", None),
            P("dp", "ctx", None),
            P(("dp", "ctx")),
        ),
        check_vma=False,
    )
```

```python
import functools

import jax
import jax.numpy as jnp
from jax import lax
from jax.experimental import pallas as pl
from jax.experimental.pallas import tpu as pltpu
from jax.sharding import PartitionSpec as P

E = 64
PAIR = 2 * E
GROUPS = 2
EXTRA = 8
VMEM = 10 * 2**20
SUB = 2
F32 = jnp.float32
BF16 = jnp.bfloat16


def dot(a, b, ca, cb):
    return lax.dot_general(a, b, (((ca,), (cb,)), ((), ())), preferred_element_type=F32)


def low_lanes(rows, cols):
    lane = lax.broadcasted_iota(jnp.int32, (rows, cols), 1)
    return lane % PAIR < E


def fold(product):
    return jnp.where(low_lanes(E, product.shape[1]), product[:E], product[E:])


def split(state):
    high = state.astype(BF16)
    return high, (state - high.astype(F32)).astype(BF16)


def spread(state):
    low = low_lanes(*state.shape)
    zero = jnp.zeros_like(state)
    return jnp.concatenate([jnp.where(low, state, zero), jnp.where(low, zero, state)], axis=0)


def heads_of(pair):
    low = low_lanes(*pair.shape)
    zero = jnp.zeros_like(pair)
    return jnp.where(low, pair, zero), jnp.where(low, zero, pair)


def twice(x):
    return jnp.concatenate([x, x], axis=1)


def pair_at(ref, p):
    return ref[:, p * PAIR:(p + 1) * PAIR]


def rows_at(base, p):
    return pl.ds(pl.multiple_of(base + p * E, E), E)


def twice(x):
    return jnp.concatenate([x, x], axis=1)


def pair_at(ref, p):
    return ref[:, p * PAIR:(p + 1) * PAIR]


def rows_at(base, p):
    return pl.ds(pl.multiple_of(base + p * E, E), E)


def own_or_received(keep, received, own, p):
    return jnp.where(own, keep[rows_at(p)], received[rows_at(p)])


def state_pair(a, b):
    return fold(dot(a, b, 0, 0))


def edge(seg, table, last):
    row = seg[...]
    count = row.shape[1]
    own = row[:, count - 1:] if last else row[:, :1]
    size = jnp.sum((row == own).astype(F32), axis=1, keepdims=True)
    at = lax.broadcasted_iota(jnp.int32, (count, PAIR), 0).astype(F32)
    rows = at >= count - size if last else at < size
    ids = lax.broadcasted_iota(jnp.int32, table.shape, 1)
    flag = jnp.sum(jnp.where(ids == own, table[...], 0).astype(F32), axis=1, keepdims=True)
    return rows, own.astype(F32), flag


def lanes_at(base, p):
    return pl.ds(pl.multiple_of(base + p * PAIR, PAIR), PAIR)


def place(sel, core, lanes, sub, first=0):
    step = pl.program_id(0)
    group, part = first + step // sub, step % sub
    half = (sel + core[0]) % 2
    base = group * lanes + part * (lanes // sub)
    return group, base, base + (group + half) * lanes, base // PAIR * E


def put_half(sel, core, k, v, out):
    lanes = k.shape[1] // GROUPS // 2
    count = lanes // PAIR
    for group in range(GROUPS):
        base = (2 * group + (sel + core[0]) % 2) * lanes
        for p in range(count):
            at = lanes_at(base, p)
            row = (group * count + p) * E
            out[row:row + E] = state_pair(k[:, at], v[:, at])


def send_kernel(core, ctx, dp, k_in, v_in, send, zero, k, v, core_row, ctx_row, dp_row, sems):
    for row, index in ((core_row, core), (ctx_row, ctx), (dp_row, dp)):
        row[...] = jnp.full(row.shape, index[0], jnp.int32)
    lanes = k.shape[1] // GROUPS // 2
    copies = []
    for sel in (1, 0):
        for group in range(GROUPS):
            base = (2 * group + (sel + core[0]) % 2) * lanes
            at = pl.ds(pl.multiple_of(base, lanes), lanes)
            for i, (array, buf) in enumerate(((k_in, k), (v_in, v))):
                copies.append(pltpu.make_async_copy(array.at[:, at], buf.at[:, at], sems.at[2 * group + sel, i]))
    for copy in copies:
        copy.start()
    zero[...] = jnp.zeros_like(zero)
    for copy in copies[:2 * GROUPS]:
        copy.wait()
    put_half(1, core, k, v, send)
    for copy in copies[2 * GROUPS:]:
        copy.wait()


def keep_kernel(core, k, v, *rest):
    put_half(0, core, k, v, rest[-1])


def part_kernel(core, q_in, dy_in, k, v, seg, table, *rest):
    *outs, q, dy, token, sems = rest[-6:]
    copies = [pltpu.make_async_copy(a, b, sems.at[i]) for i, (a, b) in enumerate(((q_in, q), (dy_in, dy)))]
    for copy in copies:
        copy.start()
    token[...] = jnp.zeros_like(token)
    lanes = k.shape[1] // GROUPS // 2
    count = lanes // PAIR
    rows, own, _ = edge(seg, table, False)
    keep = rows.astype(BF16)
    for sel, out in enumerate(outs):
        for group in range(GROUPS):
            base = (2 * group + (sel + core[0]) % 2) * lanes
            for p in range(count):
                at = lanes_at(base, p)
                out[group, p * E:(p + 1) * E] = state_pair(k[:, at], v[:, at] * keep)
            out[group, count * E:] = jnp.broadcast_to(own, (EXTRA, PAIR))
    for copy in copies:
        copy.wait()


def local_kernel(sel, core, q, k, v, mask, mask_t, *rest):
    attn, probs, token = rest[-3:]
    lanes = attn.shape[1] // GROUPS
    group, base, wide, _ = place(sel, core, lanes, 1)
    m, mt = mask[...], mask_t[...]
    token[...] = jnp.zeros_like(token)
    for p in range(lanes // PAIR):
        at = lanes_at(wide, p)
        kp = k[:, at]
        total = None
        for h, (qh, vh) in enumerate(zip(heads_of(q[:, at]), heads_of(v[:, at]))):
            prob = dot(qh, kp, 1, 1).astype(BF16) * m
            probs[group * (lanes // E) + 2 * p + h] = dot(kp, qh, 1, 1).astype(BF16) * mt
            term = dot(prob, vh, 1, 0)
            total = term if total is None else total + term
        attn[:, lanes_at(base, p)] = total


def head_mean(x):
    high, low = split(x)
    ones = spread(jnp.full((E, PAIR), 1.0 / E, BF16))
    return dot(jnp.concatenate([high, low], axis=1), jnp.concatenate([ones, ones], axis=0), 1, 0)


def side_by_side(state, part):
    sh, sl = split(state)
    ph, pll = split(part)
    left = jnp.concatenate([spread(sh), spread(sl)], axis=0)
    right = jnp.concatenate([spread(ph), spread(pll)], axis=0)
    return jnp.concatenate([left, right], axis=1)


def stacked(state, part):
    sh, sl = split(state)
    ph, pll = split(part)
    top = jnp.concatenate([spread(sh), spread(sl)], axis=1)
    bottom = jnp.concatenate([spread(ph), spread(pll)], axis=1)
    return jnp.concatenate([top, bottom], axis=0)


def on_rows(seg, table, last, part):
    rows, own, flag = edge(seg, table, last)
    met = part[0, part.shape[1] - EXTRA:part.shape[1] - EXTRA + 1] == own
    if last:
        met = met & (flag == 1)
    return rows.astype(F32) * met.astype(F32)


def norm_kernel(sel, core, q, dy, local, gain, seg, table, prefix, nxt, *rest):
    out, dab, part, gsum, total, token = rest[-6:]
    token[...] = jnp.zeros_like(token)
    lanes = out.shape[1]
    count = lanes // PAIR
    _, base, wide, row = place(sel, core, lanes, 1)
    on_next = on_rows(seg, table, True, nxt)
    last, own, flag = edge(seg, table, True)
    last = (last.astype(F32) * jnp.where(flag == 1, 1.0, 0.0)).astype(BF16)
    pairs = [slice(p * PAIR, (p + 1) * PAIR) for p in range(count)]
    bases = [lanes_at(base, p) for p in range(count)]
    wides = [lanes_at(wide, p) for p in range(count)]
    fars = [
        dot(twice(q[:, at]), side_by_side(prefix[rows_at(row, p)], nxt[0, rows_at(0, p)]), 1, 0)
        for p, at in enumerate(wides)
    ]
    attns = [local[:, at] + far[:, :PAIR] + on_next * far[:, PAIR:] for at, far in zip(bases, fars)]
    squares = [head_mean(attn * attn) for attn in attns]
    scales = [lax.rsqrt(square + 1e-06) for square in squares]
    normeds = [attn * scale for attn, scale in zip(attns, scales)]
    gas = [dy[:, at].astype(F32) * gain[:, pair] for at, pair in zip(wides, pairs)]
    means = [head_mean(ga * normed) for ga, normed in zip(gas, normeds)]
    das = [
        (scale * (ga - normed * mean)).astype(BF16)
        for scale, ga, normed, mean in zip(scales, gas, normeds, means)
    ]
    states = [state_pair(q[:, at], jnp.concatenate([da, da * last], axis=1)) for at, da in zip(wides, das)]
    part[0, count * E:] = jnp.broadcast_to(own, (EXTRA, PAIR))
    for p, (at, normed, da) in enumerate(zip(pairs, normeds, das)):
        total[rows_at(row, p)] = states[p][:, :PAIR]
        part[0, p * E:(p + 1) * E] = states[p][:, PAIR:]
        dab[:, bases[p]] = da
        out[:, at] = (normed * gain[:, at]).astype(BF16)
        gsum[0, p:p + 1] = jnp.sum(dy[:, wides[p]].astype(F32) * normed, axis=0, keepdims=True)


def inner_kernel(sel, start, core, q, k, v, dab, probs, mask, seg, table, prefix, nxt, *rest):
    gq, gk, gv, token = rest[-4:]
    lanes = dab.shape[1] // GROUPS
    count = lanes // SUB // PAIR
    group, base, wide, row = place(sel, core, lanes, SUB, start)
    m = mask[...]
    token[...] = jnp.zeros_like(token)
    on_next = on_rows(seg, table, True, nxt)
    first = row - group * (lanes // 2)
    for p in range(count):
        at = lanes_at(wide, p)
        da = dab[:, lanes_at(base, p)]
        vp = v[:, at]
        far = dot(twice(da), stacked(prefix[rows_at(row, p)], nxt[0, rows_at(first, p)]), 1, 1)
        tq = far[:, :PAIR] + on_next * far[:, PAIR:]
        tk = tv = None
        for h, (qh, kh, dh) in enumerate(zip(heads_of(q[:, at]), heads_of(k[:, at]), heads_of(da))):
            dprob = dot(dh, vp, 1, 1).astype(BF16) * m
            tq = tq + dot(dprob, kh, 1, 0)
            a = dot(dprob, qh, 0, 0)
            b = dot(probs[row // (E // 2) + 2 * p + h], dh, 1, 0)
            tk = a if tk is None else tk + a
            tv = b if tv is None else tv + b
        gq[:, p * PAIR:(p + 1) * PAIR] = tq.astype(BF16)
        gk[:, lanes_at(base, p)] = tk
        gv[:, lanes_at(base, p)] = tv


def outer_kernel(sel, core, k, v, gk_in, gv_in, seg, table, suffix, prv, *rest):
    gk, gv, token = rest[-3:]
    lanes = gk_in.shape[1] // GROUPS
    count = lanes // PAIR
    group, base, wide, row = place(sel, core, lanes, 1)
    token[...] = jnp.zeros_like(token)
    on_prev = on_rows(seg, table, False, prv)
    first = row - group * (lanes // 2)
    wides = [lanes_at(wide, p) for p in range(count)]
    states = [(suffix[rows_at(row, p)], prv[0, rows_at(first, p)]) for p in range(count)]
    fars_k = [dot(twice(v[:, at]), stacked(*state), 1, 1) for at, state in zip(wides, states)]
    fars_v = [dot(twice(k[:, at]), side_by_side(*state), 1, 0) for at, state in zip(wides, states)]
    for fars, inside, out in ((fars_k, gk_in, gk), (fars_v, gv_in, gv)):
        for p, far in enumerate(fars):
            total = inside[:, lanes_at(base, p)] + far[:, :PAIR] + on_prev * far[:, PAIR:]
            out[:, p * PAIR:(p + 1) * PAIR] = total.astype(BF16)


def partner(x, axis, bit):
    route = [(i, i ^ (1 << bit)) for i in range(lax.axis_size(axis))]
    return lax.ppermute(x, axis, route)


def shifted(x, distance):
    count = lax.axis_size("ctx")
    return lax.ppermute(x, "ctx", [(i, i + distance) for i in range(count) if 0 <= i + distance < count])


def nought(x):
    return jnp.minimum(jnp.abs(x), 0.0)


def cycled(x, distance):
    count = lax.axis_size("ctx")
    return lax.ppermute(x, "ctx", [(i, (i + distance) % count) for i in range(count)])


def within_chip(keep, send):
    received = partner(send, "ctx", 0)
    return keep, received, keep + received


def to_cores(core, before, piece, towards):
    keep, received, _ = piece
    is_source = core == (0 if towards == 1 else 1)
    mine = jnp.where(is_source, before, before + received)
    return mine, partner(jnp.where(is_source, before + keep, before), "ctx", 0)


def pinned(x, space):
    return pltpu.with_memory_space_constraint(x, space)


def scatter_step(x, at, axis, bit):
    low, high = jnp.split(x, 2, axis=0 if x.shape[0] > 1 else 1)
    upper = (at >> bit & 1 == 1)[:, :low.shape[-1]]
    return jnp.where(upper, high, low) + partner(jnp.where(upper, low, high), axis, bit)


def on_device(queries, keys, values, out_grad, segment_ids, image_flags, gain):
    rows, width = queries.shape[1:]
    q, k, v, dy = (x[0] for x in (queries, keys, values, out_grad))
    table = image_flags[0]
    gain_row = gain.reshape(1, width)
    ctx = lax.axis_index("ctx")
    core, ctx, dp = (x.reshape(1).astype(jnp.int32) for x in (ctx & 1, ctx, lax.axis_index("dp")))
    lanes = width // GROUPS // 2
    half_rows = lanes // PAIR * E
    heads = lanes // E

    def call(kernel, sel, ins, outs, first=0, after=(), alias=(), scratch=(), sub=1, steps=None, scalars=None):
        scalars = scalars or [core]

        def wide(i, c, *_):
            return (0, ((first + i // sub) * 2 + (sel + c[0]) % 2) * sub + i % sub)

        def whole(*args):
            return (0, 0)

        def part(i, c, *_):
            return (first + i // sub, 0, 0)

        specs = {
            "vmem": pl.BlockSpec(memory_space=pltpu.VMEM),
            "hbm": pl.BlockSpec(memory_space=pltpu.HBM),
            "wide": pl.BlockSpec((rows, lanes // sub), wide),
            "row": pl.BlockSpec((1, lanes // sub), wide),
            "sums": pl.BlockSpec((1, lanes // PAIR, PAIR), part),
            "zero": pl.BlockSpec((1, rows), whole),
            "all": pl.BlockSpec((GROUPS * half_rows, PAIR), whole),
            "part": pl.BlockSpec((1, half_rows + EXTRA, PAIR), part),
            "later": pl.BlockSpec((1, half_rows + EXTRA, PAIR), lambda i, *_: (GROUPS + i // sub, 0, 0)),
            "parts": pl.BlockSpec((GROUPS, half_rows + EXTRA, PAIR), lambda *args: (0, 0, 0)),
            "seg": pl.BlockSpec((1, rows), whole),
            "table": pl.BlockSpec((1, table.shape[0]), whole),
            "mask": pl.BlockSpec((rows, rows), whole),
            "token": pl.BlockSpec((1, PAIR), whole),
            "after2": pl.BlockSpec((8, PAIR), whole),
            "after3": pl.BlockSpec((1, 8, PAIR), lambda *args: (0, 0, 0)),
            "any": pl.BlockSpec(memory_space=pl.ANY),
        }
        shapes = {
            "wide": (rows, width),
            "sums": (GROUPS, lanes // PAIR, PAIR),
            "zero": (1, rows),
            "all": (GROUPS * half_rows, PAIR),
            "part": (GROUPS, half_rows + EXTRA, PAIR),
            "parts": (GROUPS, half_rows + EXTRA, PAIR),
            "token": (1, PAIR),
        }
        spaces = {"vmem": pltpu.VMEM, "hbm": pltpu.HBM}
        operands = [pinned(x, spaces[kind]) if kind in spaces else x for kind, x in ins] + list(after)
        kinds = [kind for kind, _ in ins] + [f"after{x.ndim}" for x in after]
        aliases = {}
        for out_at, x in alias:
            if x is not None:
                aliases[len(scalars) + len(operands)] = out_at
                in_vmem = outs[out_at][0] == "vmem"
                operands.append(pinned(x, pltpu.VMEM) if in_vmem else x)
                kinds.append("vmem" if in_vmem else "any")
        out_shape = [
            pltpu.VMEM(*shape, dtype) if kind == "vmem" else jax.ShapeDtypeStruct(shapes[kind], dtype)
            for kind, dtype, *shape in outs
        ]
        return pl.pallas_call(
            kernel,
            grid_spec=pltpu.PrefetchScalarGridSpec(
                num_scalar_prefetch=len(scalars),
                grid=steps or (GROUPS * sub,),
                in_specs=[specs[kind] for kind in kinds],
                out_specs=[specs[kind] for kind, *_ in outs],
                scratch_shapes=scratch,
            ),
            out_shape=out_shape,
            input_output_aliases=aliases,
            compiler_params=pltpu.CompilerParams(vmem_limit_bytes=VMEM),
            cost_estimate=pl.CostEstimate(flops=1, bytes_accessed=1, transcendentals=0),
        )(*scalars, *operands)

    edges = [("seg", segment_ids), ("table", image_flags)]
    chips = lax.axis_size("ctx") // 2
    whole, part_of = (rows, width), (rows, width // 2)

    def local_attn(sel, after):
        return call(
            functools.partial(local_kernel, sel), sel,
            [("vmem", q), ("vmem", k), ("vmem", v), ("mask", mask), ("mask", mask_t)],
            [("vmem", F32, part_of), ("vmem", BF16, (GROUPS * heads, rows, rows)), ("token", F32)], after=after)

    def norm(sel, before, after):
        return call(
            functools.partial(norm_kernel, sel), sel,
            [("vmem", q), ("vmem", dy), ("vmem", local[sel][0]), ("row", gain_row), *edges,
             ("all", prefix[sel]), ("part", nxt[sel])],
            [("wide", BF16), ("vmem", BF16, part_of), ("part", F32), ("sums", F32), ("all", F32), ("token", F32)],
            after=after, alias=[(0, before)])

    def inner(sel, start, before, after):
        count = 1 if sel == 0 else GROUPS
        return call(
            functools.partial(inner_kernel, sel, start), sel,
            [("vmem", q), ("vmem", k), ("vmem", v), ("vmem", norms[sel][1]), ("vmem", local[sel][1]), ("mask", mask),
             *edges, ("all", prefix[sel]), ("part", nxt[sel])],
            [("wide", BF16), ("vmem", F32, part_of), ("vmem", F32, part_of), ("token", F32)],
            first=start, after=after, alias=list(enumerate(before)), sub=SUB, steps=(count * SUB,))

    def outer(sel, before, after):
        return call(
            functools.partial(outer_kernel, sel), sel,
            [("vmem", k), ("vmem", v), ("vmem", inners[sel][1]), ("vmem", inners[sel][2]), *edges,
             ("all", suffix[sel]), ("later" if sel else "part", prv[0])],
            [("wide", BF16), ("wide", BF16), ("token", F32)], after=after, alias=list(enumerate(before)))

    def summed_before(own, towards, works):
        load, before, span = own, None, 1
        while span < chips:
            if span == 1:
                first = ctx_row >> 1 == (0 if towards == 1 else chips - 1)
                arrived = jnp.where(first, 0.0, cycled(load, 2 * towards))
            else:
                arrived = shifted(load, 2 * towards * span)
            if works:
                arrived = arrived + works.pop(0)(load)
            before = arrived if before is None else before + arrived
            load = load + arrived
            span *= 2
        for work in works:
            before = before + work(load)
        return before

    send, zero, k, v, core_row, ctx_row, dp_row = call(
        send_kernel, 0, [("hbm", k), ("hbm", v)],
        [("all", F32), ("zero", jnp.int32), ("vmem", BF16, whole), ("vmem", BF16, whole)]
        + [("token", jnp.int32)] * 3,
        scratch=[pltpu.SemaphoreType.DMA((2 * GROUPS, 2))], steps=(1,), scalars=[core, ctx, dp])
    keep, = call(keep_kernel, 0, [("vmem", k), ("vmem", v)], [("all", F32)], steps=(1,))
    piece = within_chip(keep, send)
    seg = (segment_ids + zero)[0]
    onehot = seg[:, None] == jnp.arange(table.shape[0], dtype=jnp.int32)[None, :]
    img = jnp.sum(jnp.where(onehot, table[None, :], 0), axis=1)
    imgseg = jnp.where(img == 1, seg, -1)
    pos = jnp.arange(rows)
    mask = ((pos[:, None] >= pos[None, :]) | (imgseg[:, None] == seg[None, :])).astype(BF16)
    mask_t = ((pos[:, None] <= pos[None, :]) | (seg[:, None] == imgseg[None, :])).astype(BF16)

    parts = call(
        part_kernel, 0, [("hbm", q), ("hbm", dy), ("vmem", k), ("vmem", v), *edges],
        [("parts", F32)] * 2 + [("vmem", BF16, whole), ("vmem", BF16, whole), ("token", F32)],
        after=[piece[2]], scratch=[pltpu.SemaphoreType.DMA((2,))], steps=(1,))
    *parts, q, dy, _ = parts
    local, nxt = [], []

    def first_work(load):
        tokens = []
        for sel in range(2):
            *made, token = local_attn(sel, [parts[0]])
            local.append(made)
            tokens.append(token)
        return sum(tokens)

    def second_work(load):
        for part in reversed(parts):
            nxt.append(shifted(part + nought(load[:1]), -1))
        return jnp.zeros((1, PAIR), F32)

    before = summed_before(piece[2], 1, [first_work, second_work])
    prefix = to_cores(core_row, before, piece, 1)
    norms = [norm(0, None, [])]
    norms.append(norm(1, norms[0][0], [norms[0][4]]))
    output = norms[1][0]
    piece = within_chip(norms[0][4], norms[1][4])
    gain_sum = [jnp.concatenate([jnp.where(core_row == half, norms[0][3], norms[1][3]) for half in range(2)], axis=0)]
    gain_sum.append(scatter_step(gain_sum[-1], dp_row, "dp", 0))
    bits = list(reversed(range(lax.axis_size("ctx").bit_length() - 1)))
    inners, prv = [], []

    def third_work(load):
        x = scatter_step(gain_sum[-1] + nought(load[:1]), dp_row, "dp", 1)
        gain_sum.append(x.reshape(-1, PAIR))
        inners.append(inner(0, 0, [None] * 3, [load]))
        return inners[0][3]

    def fourth_work(load):
        gain_sum.append(scatter_step(gain_sum[-1] + nought(load[:1]), ctx_row, "ctx", bits[0]))
        both = jnp.concatenate([norms[1][2], norms[0][2]], axis=0) + nought(load[:1])
        prv.append(shifted(both, 1))
        inners[0] = inner(0, 1, inners[0][:3], [load])
        inners.append(inner(1, 0, [inners[0][0], None, None], [load]))
        return inners[0][3] + inners[1][3]

    before = summed_before(piece[2], -1, [third_work, fourth_work])
    suffix = to_cores(core_row, before, piece, -1)
    grad_gain = scatter_step(gain_sum[-1] + nought(before[:1]), ctx_row, "ctx", bits[1])
    outers = outer(0, [None] * 2, [])
    grad_gain = grad_gain + outers[2]
    for bit in bits[2:]:
        grad_gain = scatter_step(grad_gain, ctx_row, "ctx", bit)
    grad_k, grad_v, _ = outer(1, outers[:2], [])
    grad_gain = grad_gain.reshape(-1)
    grad_q = inners[1][0]
    return output[None], grad_q[None], grad_k[None], grad_v[None], grad_gain


def solution(mesh):
    return jax.shard_map(
        on_device,
        mesh=mesh,
        in_specs=(
            P("dp", "ctx", None),
            P("dp", "ctx", None),
            P("dp", "ctx", None),
            P("dp", "ctx", None),
            P("dp", "ctx"),
            P("dp", None),
            P(),
        ),
        out_specs=(
            P("dp", "ctx", None),
            P("dp", "ctx", None),
            P("dp", "ctx", None),
            P("dp", "ctx", None),
            P(("dp", "ctx")),
        ),
        check_vma=False,
    )
```

```python
import functools

import jax
import jax.numpy as jnp
from jax import lax
from jax.experimental import pallas as pl
from jax.experimental.pallas import tpu as pltpu
from jax.sharding import PartitionSpec as P

E = 64
PAIR = 2 * E
GROUPS = 2
EXTRA = 8
VMEM = 10 * 2**20
SUB = 2
F32 = jnp.float32
BF16 = jnp.bfloat16


def dot(a, b, ca, cb):
    return lax.dot_general(a, b, (((ca,), (cb,)), ((), ())), preferred_element_type=F32)


def low_lanes(rows, cols):
    lane = lax.broadcasted_iota(jnp.int32, (rows, cols), 1)
    return lane % PAIR < E


def fold(product):
    return jnp.where(low_lanes(E, product.shape[1]), product[:E], product[E:])


def split(state):
    high = state.astype(BF16)
    return high, (state - high.astype(F32)).astype(BF16)


def spread(state):
    low = low_lanes(*state.shape)
    zero = jnp.zeros_like(state)
    return jnp.concatenate([jnp.where(low, state, zero), jnp.where(low, zero, state)], axis=0)


def heads_of(pair):
    low = low_lanes(*pair.shape)
    zero = jnp.zeros_like(pair)
    return jnp.where(low, pair, zero), jnp.where(low, zero, pair)


def twice(x):
    return jnp.concatenate([x, x], axis=1)


def pair_at(ref, p):
    return ref[:, p * PAIR:(p + 1) * PAIR]


def rows_at(base, p):
    return pl.ds(pl.multiple_of(base + p * E, E), E)


def twice(x):
    return jnp.concatenate([x, x], axis=1)


def pair_at(ref, p):
    return ref[:, p * PAIR:(p + 1) * PAIR]


def rows_at(base, p):
    return pl.ds(pl.multiple_of(base + p * E, E), E)


def own_or_received(keep, received, own, p):
    return jnp.where(own, keep[rows_at(p)], received[rows_at(p)])


def state_pair(a, b):
    return fold(dot(a, b, 0, 0))


def edge(seg, table, last):
    row = seg[...]
    count = row.shape[1]
    own = row[:, count - 1:] if last else row[:, :1]
    size = jnp.sum((row == own).astype(F32), axis=1, keepdims=True)
    at = lax.broadcasted_iota(jnp.int32, (count, PAIR), 0).astype(F32)
    rows = at >= count - size if last else at < size
    ids = lax.broadcasted_iota(jnp.int32, table.shape, 1)
    flag = jnp.sum(jnp.where(ids == own, table[...], 0).astype(F32), axis=1, keepdims=True)
    return rows, own.astype(F32), flag


def lanes_at(base, p):
    return pl.ds(pl.multiple_of(base + p * PAIR, PAIR), PAIR)


def place(sel, core, lanes, sub, first=0):
    step = pl.program_id(0)
    group, part = first + step // sub, step % sub
    half = (sel + core[0]) % 2
    base = group * lanes + part * (lanes // sub)
    return group, base, base + (group + half) * lanes, base // PAIR * E


def put_half(sel, core, k, v, out):
    lanes = k.shape[1] // GROUPS // 2
    count = lanes // PAIR
    bases = [(2 * group + (sel + core[0]) % 2) * lanes for group in range(GROUPS)]
    ats = [lanes_at(base, p) for base in bases for p in range(count)]
    products = [dot(k[:, at], v[:, at], 0, 0) for at in ats]
    for i, product in enumerate(products):
        out[i * E:(i + 1) * E] = fold(product)


def send_kernel(core, ctx, dp, k_in, v_in, send, zero, k, v, core_row, ctx_row, dp_row, sems):
    for row, index in ((core_row, core), (ctx_row, ctx), (dp_row, dp)):
        row[...] = jnp.full(row.shape, index[0], jnp.int32)
    lanes = k.shape[1] // GROUPS // 2
    copies = []
    for sel in (1, 0):
        for group in range(GROUPS):
            base = (2 * group + (sel + core[0]) % 2) * lanes
            at = pl.ds(pl.multiple_of(base, lanes), lanes)
            for i, (array, buf) in enumerate(((k_in, k), (v_in, v))):
                copies.append(pltpu.make_async_copy(array.at[:, at], buf.at[:, at], sems.at[2 * group + sel, i]))
    for copy in copies:
        copy.start()
    zero[...] = jnp.zeros_like(zero)
    for copy in copies[:2 * GROUPS]:
        copy.wait()
    put_half(1, core, k, v, send)
    for copy in copies[2 * GROUPS:]:
        copy.wait()


def keep_kernel(core, k, v, *rest):
    put_half(0, core, k, v, rest[-1])


def part_kernel(core, q_in, dy_in, k, v, seg, table, *rest):
    *outs, q, dy, token, sems = rest[-6:]
    copies = [pltpu.make_async_copy(a, b, sems.at[i]) for i, (a, b) in enumerate(((q_in, q), (dy_in, dy)))]
    for copy in copies:
        copy.start()
    token[...] = jnp.zeros_like(token)
    lanes = k.shape[1] // GROUPS // 2
    count = lanes // PAIR
    rows, own, _ = edge(seg, table, False)
    keep = rows.astype(BF16)
    for sel, out in enumerate(outs):
        for group in range(GROUPS):
            base = (2 * group + (sel + core[0]) % 2) * lanes
            for p in range(count):
                at = lanes_at(base, p)
                out[group, p * E:(p + 1) * E] = state_pair(k[:, at], v[:, at] * keep)
            out[group, count * E:] = jnp.broadcast_to(own, (EXTRA, PAIR))
    for copy in copies:
        copy.wait()


def local_kernel(sel, core, q, k, v, mask, mask_t, *rest):
    attn, probs, token = rest[-3:]
    lanes = attn.shape[1] // GROUPS
    group, base, wide, _ = place(sel, core, lanes, 1)
    m, mt = mask[...], mask_t[...]
    token[...] = jnp.zeros_like(token)
    for p in range(lanes // PAIR):
        at = lanes_at(wide, p)
        kp = k[:, at]
        total = None
        for h, (qh, vh) in enumerate(zip(heads_of(q[:, at]), heads_of(v[:, at]))):
            prob = dot(qh, kp, 1, 1).astype(BF16) * m
            probs[group * (lanes // E) + 2 * p + h] = dot(kp, qh, 1, 1).astype(BF16) * mt
            term = dot(prob, vh, 1, 0)
            total = term if total is None else total + term
        attn[:, lanes_at(base, p)] = total


def head_mean(x):
    high, low = split(x)
    ones = spread(jnp.full((E, PAIR), 1.0 / E, BF16))
    return dot(jnp.concatenate([high, low], axis=1), jnp.concatenate([ones, ones], axis=0), 1, 0)


def side_by_side(state, part):
    sh, sl = split(state)
    ph, pll = split(part)
    left = jnp.concatenate([spread(sh), spread(sl)], axis=0)
    right = jnp.concatenate([spread(ph), spread(pll)], axis=0)
    return jnp.concatenate([left, right], axis=1)


def stacked(state, part):
    sh, sl = split(state)
    ph, pll = split(part)
    top = jnp.concatenate([spread(sh), spread(sl)], axis=1)
    bottom = jnp.concatenate([spread(ph), spread(pll)], axis=1)
    return jnp.concatenate([top, bottom], axis=0)


def on_rows(seg, table, last, part):
    rows, own, flag = edge(seg, table, last)
    met = part[0, part.shape[1] - EXTRA:part.shape[1] - EXTRA + 1] == own
    if last:
        met = met & (flag == 1)
    return rows.astype(F32) * met.astype(F32)


def norm_kernel(sel, core, q, dy, local, gain, seg, table, prefix, nxt, *rest):
    out, dab, part, gsum, total, token = rest[-6:]
    token[...] = jnp.zeros_like(token)
    lanes = out.shape[1]
    count = lanes // PAIR
    _, base, wide, row = place(sel, core, lanes, 1)
    on_next = on_rows(seg, table, True, nxt)
    last, own, flag = edge(seg, table, True)
    last = (last.astype(F32) * jnp.where(flag == 1, 1.0, 0.0)).astype(BF16)
    pairs = [slice(p * PAIR, (p + 1) * PAIR) for p in range(count)]
    bases = [lanes_at(base, p) for p in range(count)]
    wides = [lanes_at(wide, p) for p in range(count)]
    fars = [
        dot(twice(q[:, at]), side_by_side(prefix[rows_at(row, p)], nxt[0, rows_at(0, p)]), 1, 0)
        for p, at in enumerate(wides)
    ]
    attns = [local[:, at] + far[:, :PAIR] + on_next * far[:, PAIR:] for at, far in zip(bases, fars)]
    squares = [head_mean(attn * attn) for attn in attns]
    scales = [lax.rsqrt(square + 1e-06) for square in squares]
    normeds = [attn * scale for attn, scale in zip(attns, scales)]
    gas = [dy[:, at].astype(F32) * gain[:, pair] for at, pair in zip(wides, pairs)]
    means = [head_mean(ga * normed) for ga, normed in zip(gas, normeds)]
    das = [
        (scale * (ga - normed * mean)).astype(BF16)
        for scale, ga, normed, mean in zip(scales, gas, normeds, means)
    ]
    states = [state_pair(q[:, at], jnp.concatenate([da, da * last], axis=1)) for at, da in zip(wides, das)]
    part[0, count * E:] = jnp.broadcast_to(own, (EXTRA, PAIR))
    for p, (at, normed, da) in enumerate(zip(pairs, normeds, das)):
        total[rows_at(row, p)] = states[p][:, :PAIR]
        part[0, p * E:(p + 1) * E] = states[p][:, PAIR:]
        dab[:, bases[p]] = da
        out[:, at] = (normed * gain[:, at]).astype(BF16)
        gsum[0, p:p + 1] = jnp.sum(dy[:, wides[p]].astype(F32) * normed, axis=0, keepdims=True)


def inner_kernel(sel, start, core, q, k, v, dab, probs, mask, seg, table, prefix, nxt, *rest):
    gq, gk, gv, token = rest[-4:]
    lanes = dab.shape[1] // GROUPS
    count = lanes // SUB // PAIR
    group, base, wide, row = place(sel, core, lanes, SUB, start)
    m = mask[...]
    token[...] = jnp.zeros_like(token)
    on_next = on_rows(seg, table, True, nxt)
    first = row - group * (lanes // 2)
    for p in range(count):
        at = lanes_at(wide, p)
        da = dab[:, lanes_at(base, p)]
        vp = v[:, at]
        far = dot(twice(da), stacked(prefix[rows_at(row, p)], nxt[0, rows_at(first, p)]), 1, 1)
        tq = far[:, :PAIR] + on_next * far[:, PAIR:]
        tk = tv = None
        heads = list(zip(heads_of(q[:, at]), heads_of(k[:, at]), heads_of(da)))
        dprobs = [dot(dh, vp, 1, 1).astype(BF16) * m for _, _, dh in heads]
        for h, ((qh, kh, dh), dprob) in enumerate(zip(heads, dprobs)):
            tq = tq + dot(dprob, kh, 1, 0)
            a = dot(dprob, qh, 0, 0)
            b = dot(probs[row // (E // 2) + 2 * p + h], dh, 1, 0)
            tk = a if tk is None else tk + a
            tv = b if tv is None else tv + b
        gq[:, p * PAIR:(p + 1) * PAIR] = tq.astype(BF16)
        gk[:, lanes_at(base, p)] = tk
        gv[:, lanes_at(base, p)] = tv


def outer_kernel(sel, core, k, v, gk_in, gv_in, seg, table, suffix, prv, *rest):
    gk, gv, token = rest[-3:]
    lanes = gk_in.shape[1] // GROUPS
    count = lanes // PAIR
    group, base, wide, row = place(sel, core, lanes, 1)
    token[...] = jnp.zeros_like(token)
    on_prev = on_rows(seg, table, False, prv)
    first = row - group * (lanes // 2)
    wides = [lanes_at(wide, p) for p in range(count)]
    states = [(suffix[rows_at(row, p)], prv[0, rows_at(first, p)]) for p in range(count)]
    fars_k = [dot(twice(v[:, at]), stacked(*state), 1, 1) for at, state in zip(wides, states)]
    fars_v = [dot(twice(k[:, at]), side_by_side(*state), 1, 0) for at, state in zip(wides, states)]
    for fars, inside, out in ((fars_k, gk_in, gk), (fars_v, gv_in, gv)):
        for p, far in enumerate(fars):
            total = inside[:, lanes_at(base, p)] + far[:, :PAIR] + on_prev * far[:, PAIR:]
            out[:, p * PAIR:(p + 1) * PAIR] = total.astype(BF16)


def partner(x, axis, bit):
    route = [(i, i ^ (1 << bit)) for i in range(lax.axis_size(axis))]
    return lax.ppermute(x, axis, route)


def shifted(x, distance):
    count = lax.axis_size("ctx")
    return lax.ppermute(x, "ctx", [(i, i + distance) for i in range(count) if 0 <= i + distance < count])


def nought(x):
    return jnp.minimum(jnp.abs(x), 0.0)


def cycled(x, distance):
    count = lax.axis_size("ctx")
    return lax.ppermute(x, "ctx", [(i, (i + distance) % count) for i in range(count)])


def within_chip(keep, send):
    received = partner(send, "ctx", 0)
    return keep, received, keep + received


def to_cores(core, before, piece, towards):
    keep, received, _ = piece
    is_source = core == (0 if towards == 1 else 1)
    mine = jnp.where(is_source, before, before + received)
    return mine, partner(jnp.where(is_source, before + keep, before), "ctx", 0)


def pinned(x, space):
    return pltpu.with_memory_space_constraint(x, space)


def scatter_step(x, at, axis, bit):
    low, high = jnp.split(x, 2, axis=0 if x.shape[0] > 1 else 1)
    upper = (at >> bit & 1 == 1)[:, :low.shape[-1]]
    return jnp.where(upper, high, low) + partner(jnp.where(upper, low, high), axis, bit)


def on_device(queries, keys, values, out_grad, segment_ids, image_flags, gain):
    rows, width = queries.shape[1:]
    q, k, v, dy = (x[0] for x in (queries, keys, values, out_grad))
    table = image_flags[0]
    gain_row = gain.reshape(1, width)
    ctx = lax.axis_index("ctx")
    core, ctx, dp = (x.reshape(1).astype(jnp.int32) for x in (ctx & 1, ctx, lax.axis_index("dp")))
    lanes = width // GROUPS // 2
    half_rows = lanes // PAIR * E
    heads = lanes // E

    def call(kernel, sel, ins, outs, first=0, after=(), alias=(), scratch=(), sub=1, steps=None, scalars=None):
        scalars = scalars or [core]

        def wide(i, c, *_):
            return (0, ((first + i // sub) * 2 + (sel + c[0]) % 2) * sub + i % sub)

        def whole(*args):
            return (0, 0)

        def part(i, c, *_):
            return (first + i // sub, 0, 0)

        specs = {
            "vmem": pl.BlockSpec(memory_space=pltpu.VMEM),
            "hbm": pl.BlockSpec(memory_space=pltpu.HBM),
            "wide": pl.BlockSpec((rows, lanes // sub), wide),
            "row": pl.BlockSpec((1, lanes // sub), wide),
            "sums": pl.BlockSpec((1, lanes // PAIR, PAIR), part),
            "zero": pl.BlockSpec((1, rows), whole),
            "all": pl.BlockSpec((GROUPS * half_rows, PAIR), whole),
            "part": pl.BlockSpec((1, half_rows + EXTRA, PAIR), part),
            "later": pl.BlockSpec((1, half_rows + EXTRA, PAIR), lambda i, *_: (GROUPS + i // sub, 0, 0)),
            "parts": pl.BlockSpec((GROUPS, half_rows + EXTRA, PAIR), lambda *args: (0, 0, 0)),
            "seg": pl.BlockSpec((1, rows), whole),
            "table": pl.BlockSpec((1, table.shape[0]), whole),
            "mask": pl.BlockSpec((rows, rows), whole),
            "token": pl.BlockSpec((1, PAIR), whole),
            "after2": pl.BlockSpec((8, PAIR), whole),
            "after3": pl.BlockSpec((1, 8, PAIR), lambda *args: (0, 0, 0)),
            "any": pl.BlockSpec(memory_space=pl.ANY),
        }
        shapes = {
            "wide": (rows, width),
            "sums": (GROUPS, lanes // PAIR, PAIR),
            "zero": (1, rows),
            "all": (GROUPS * half_rows, PAIR),
            "part": (GROUPS, half_rows + EXTRA, PAIR),
            "parts": (GROUPS, half_rows + EXTRA, PAIR),
            "token": (1, PAIR),
        }
        spaces = {"vmem": pltpu.VMEM, "hbm": pltpu.HBM}
        operands = [pinned(x, spaces[kind]) if kind in spaces else x for kind, x in ins] + list(after)
        kinds = [kind for kind, _ in ins] + [f"after{x.ndim}" for x in after]
        aliases = {}
        for out_at, x in alias:
            if x is not None:
                aliases[len(scalars) + len(operands)] = out_at
                in_vmem = outs[out_at][0] == "vmem"
                operands.append(pinned(x, pltpu.VMEM) if in_vmem else x)
                kinds.append("vmem" if in_vmem else "any")
        out_shape = [
            pltpu.VMEM(*shape, dtype) if kind == "vmem" else jax.ShapeDtypeStruct(shapes[kind], dtype)
            for kind, dtype, *shape in outs
        ]
        return pl.pallas_call(
            kernel,
            grid_spec=pltpu.PrefetchScalarGridSpec(
                num_scalar_prefetch=len(scalars),
                grid=steps or (GROUPS * sub,),
                in_specs=[specs[kind] for kind in kinds],
                out_specs=[specs[kind] for kind, *_ in outs],
                scratch_shapes=scratch,
            ),
            out_shape=out_shape,
            input_output_aliases=aliases,
            compiler_params=pltpu.CompilerParams(vmem_limit_bytes=VMEM),
            cost_estimate=pl.CostEstimate(flops=1, bytes_accessed=1, transcendentals=0),
        )(*scalars, *operands)

    edges = [("seg", segment_ids), ("table", image_flags)]
    chips = lax.axis_size("ctx") // 2
    whole, part_of = (rows, width), (rows, width // 2)

    def local_attn(sel, after):
        return call(
            functools.partial(local_kernel, sel), sel,
            [("vmem", q), ("vmem", k), ("vmem", v), ("mask", mask), ("mask", mask_t)],
            [("vmem", F32, part_of), ("vmem", BF16, (GROUPS * heads, rows, rows)), ("token", F32)], after=after)

    def norm(sel, before, after):
        return call(
            functools.partial(norm_kernel, sel), sel,
            [("vmem", q), ("vmem", dy), ("vmem", local[sel][0]), ("row", gain_row), *edges,
             ("all", prefix[sel]), ("part", nxt[sel])],
            [("wide", BF16), ("vmem", BF16, part_of), ("part", F32), ("sums", F32), ("all", F32), ("token", F32)],
            after=after, alias=[(0, before)])

    def inner(sel, start, before, after):
        count = 1 if sel == 0 else GROUPS
        return call(
            functools.partial(inner_kernel, sel, start), sel,
            [("vmem", q), ("vmem", k), ("vmem", v), ("vmem", norms[sel][1]), ("vmem", local[sel][1]), ("mask", mask),
             *edges, ("all", prefix[sel]), ("part", nxt[sel])],
            [("wide", BF16), ("vmem", F32, part_of), ("vmem", F32, part_of), ("token", F32)],
            first=start, after=after, alias=list(enumerate(before)), sub=SUB, steps=(count * SUB,))

    def outer(sel, before, after):
        return call(
            functools.partial(outer_kernel, sel), sel,
            [("vmem", k), ("vmem", v), ("vmem", inners[sel][1]), ("vmem", inners[sel][2]), *edges,
             ("all", suffix[sel]), ("later" if sel else "part", prv[0])],
            [("wide", BF16), ("wide", BF16), ("token", F32)], after=after, alias=list(enumerate(before)))

    def summed_before(own, towards, works):
        load, before, span = own, None, 1
        while span < chips:
            if span == 1:
                first = ctx_row >> 1 == (0 if towards == 1 else chips - 1)
                arrived = jnp.where(first, 0.0, cycled(load, 2 * towards))
            else:
                arrived = shifted(load, 2 * towards * span)
            if works:
                arrived = arrived + works.pop(0)(load)
            before = arrived if before is None else before + arrived
            load = load + arrived
            span *= 2
        for work in works:
            before = before + work(load)
        return before

    send, zero, k, v, core_row, ctx_row, dp_row = call(
        send_kernel, 0, [("hbm", k), ("hbm", v)],
        [("all", F32), ("zero", jnp.int32), ("vmem", BF16, whole), ("vmem", BF16, whole)]
        + [("token", jnp.int32)] * 3,
        scratch=[pltpu.SemaphoreType.DMA((2 * GROUPS, 2))], steps=(1,), scalars=[core, ctx, dp])
    keep, = call(keep_kernel, 0, [("vmem", k), ("vmem", v)], [("all", F32)], steps=(1,))
    piece = within_chip(keep, send)
    seg = (segment_ids + zero)[0]
    onehot = seg[:, None] == jnp.arange(table.shape[0], dtype=jnp.int32)[None, :]
    img = jnp.sum(jnp.where(onehot, table[None, :], 0), axis=1)
    imgseg = jnp.where(img == 1, seg, -1)
    pos = jnp.arange(rows)
    mask = ((pos[:, None] >= pos[None, :]) | (imgseg[:, None] == seg[None, :])).astype(BF16)
    mask_t = ((pos[:, None] <= pos[None, :]) | (seg[:, None] == imgseg[None, :])).astype(BF16)

    parts = call(
        part_kernel, 0, [("hbm", q), ("hbm", dy), ("vmem", k), ("vmem", v), *edges],
        [("parts", F32)] * 2 + [("vmem", BF16, whole), ("vmem", BF16, whole), ("token", F32)],
        after=[piece[2]], scratch=[pltpu.SemaphoreType.DMA((2,))], steps=(1,))
    *parts, q, dy, _ = parts
    local, nxt = [], []

    def first_work(load):
        tokens = []
        for sel in range(2):
            *made, token = local_attn(sel, [parts[0]])
            local.append(made)
            tokens.append(token)
        return sum(tokens)

    def second_work(load):
        for part in reversed(parts):
            nxt.append(shifted(part + nought(load[:1]), -1))
        return jnp.zeros((1, PAIR), F32)

    before = summed_before(piece[2], 1, [first_work, second_work])
    prefix = to_cores(core_row, before, piece, 1)
    norms = [norm(0, None, [])]
    norms.append(norm(1, norms[0][0], [norms[0][4]]))
    output = norms[1][0]
    piece = within_chip(norms[0][4], norms[1][4])
    gain_sum = [jnp.concatenate([jnp.where(core_row == half, norms[0][3], norms[1][3]) for half in range(2)], axis=0)]
    gain_sum.append(scatter_step(gain_sum[-1], dp_row, "dp", 0))
    bits = list(reversed(range(lax.axis_size("ctx").bit_length() - 1)))
    inners, prv = [], []

    def third_work(load):
        x = scatter_step(gain_sum[-1] + nought(load[:1]), dp_row, "dp", 1)
        gain_sum.append(x.reshape(-1, PAIR))
        inners.append(inner(0, 0, [None] * 3, [load]))
        return inners[0][3]

    def fourth_work(load):
        gain_sum.append(scatter_step(gain_sum[-1] + nought(load[:1]), ctx_row, "ctx", bits[0]))
        both = jnp.concatenate([norms[1][2], norms[0][2]], axis=0) + nought(load[:1])
        prv.append(shifted(both, 1))
        inners[0] = inner(0, 1, inners[0][:3], [load])
        inners.append(inner(1, 0, [inners[0][0], None, None], [load]))
        return inners[0][3] + inners[1][3]

    before = summed_before(piece[2], -1, [third_work, fourth_work])
    suffix = to_cores(core_row, before, piece, -1)
    grad_gain = scatter_step(gain_sum[-1] + nought(before[:1]), ctx_row, "ctx", bits[1])
    outers = outer(0, [None] * 2, [])
    grad_gain = grad_gain + outers[2]
    for bit in bits[2:]:
        grad_gain = scatter_step(grad_gain, ctx_row, "ctx", bit)
    grad_k, grad_v, _ = outer(1, outers[:2], [])
    grad_gain = grad_gain.reshape(-1)
    grad_q = inners[1][0]
    return output[None], grad_q[None], grad_k[None], grad_v[None], grad_gain


def solution(mesh):
    return jax.shard_map(
        on_device,
        mesh=mesh,
        in_specs=(
            P("dp", "ctx", None),
            P("dp", "ctx", None),
            P("dp", "ctx", None),
            P("dp", "ctx", None),
            P("dp", "ctx"),
            P("dp", None),
            P(),
        ),
        out_specs=(
            P("dp", "ctx", None),
            P("dp", "ctx", None),
            P("dp", "ctx", None),
            P("dp", "ctx", None),
            P(("dp", "ctx")),
        ),
        check_vma=False,
    )
```
